128 devices in a mesh: dp: 32 (over y, x, core), tensor: 4 (over z).
Axes of the slice: x: 4, y: 4, z: 4, core: 2. Of those that a mesh axis runs over, the one named last changes fastest.
Arguments:
- tokens: bfloat16 [32768, 1536], P(('dp', 'tensor')), may hold values from -6 to 6
- cotangent: bfloat16 [32768, 1536], P(('dp', 'tensor')), may hold values from -6 to 6
- segments: int32 [32768], replicated, may hold values from 0 to 32767, as said below
- adapter_ids: int32 [16], replicated, may hold values from 0 to 7
- norm_gains: float32 [2, 1536], replicated, may hold values from 0.5 to 1.5
- q_weight: bfloat16 [1536, 1536], P('dp', 'tensor'), may hold values from -0.15625 to 0.15625
- kv_weight: bfloat16 [2, 1536, 128], P(None, 'dp'), may hold values from -0.15625 to 0.15625
- out_weight: bfloat16 [1536, 1536], P('tensor', 'dp'), may hold values from -0.625 to 0.625
- gate_up_weight: bfloat16 [2, 1536, 4608], P(None, 'dp', 'tensor'), may hold values from -0.15625 to 0.15625
- down_weight: bfloat16 [4608, 1536], P('tensor', 'dp'), may hold values from -0.125 to 0.125
- wide_adapters: bfloat16 [7, 1536, 128], P(None, 'dp'), may hold values from -0.359375 to 0.359375
- kv_adapter: bfloat16 [2, 128, 128], replicated, may hold values from -0.59765625 to 0.59765625
- q_adapter: bfloat16 [128, 1536], P(None, 'tensor'), may hold values from -0.59765625 to 0.59765625
- out_adapter: bfloat16 [1536, 128], P('tensor'), may hold values from -0.625 to 0.625
- gate_up_adapter: bfloat16 [2, 128, 4608], P(None, None, 'tensor'), may hold values from -0.59765625 to 0.59765625
- down_adapter: bfloat16 [4608, 128], P('tensor'), may hold values from -0.375 to 0.375
Outputs:
- block_output: bfloat16 [32768, 1536], P(('dp', 'tensor'))
- input_grad: float32 [32768, 1536], P(('dp', 'tensor'))
- wide_grad: float32 [7, 1536, 128], P(None, ('dp', 'tensor'))
- kv_adapter_grad: float32 [2, 128, 128], P(None, ('dp', 'tensor'))
- q_adapter_grad: float32 [128, 1536], P(None, 'tensor')
- out_adapter_grad: float32 [1536, 128], P('tensor')
- gate_up_adapter_grad: float32 [2, 128, 4608], P(None, None, 'tensor')
- down_adapter_grad: float32 [4608, 128], P('tensor')
The draws below stay inside these ranges and needn't reach their ends.
Inputs may be any that keep to these rules, and one draw needn't show every extreme that they name: `segments`: A token's segment number is the index of the first token of its document, so the numbers never fall; a new document begins at the first token of each sequence of 2048 tokens, each sequence holds one document of exactly 1537 tokens that begins among its first 256 tokens, and the last token of all is a document of its own.
All inputs are finite; a program needn't handle non-finite values.
Results may differ from the reference program's by a relative error of at most 0.025.
Values may be sent and summed in bfloat16 or wider, within the bound.
No kernel may reach another device: no remote copies, remote signals or barrier semaphores. Data moves between devices by JAX's collectives and lax.ppermute only.
A program may use at most 192 MiB of HBM per device.

```python
import jax
import jax.numpy as jnp
from jax import lax

D = 1536
H = 12
HD = 128
FF = 4608
WINDOW = 1024
ADAPTERS = 8
RANK = 16
GROUP = 1024
SEQ_LEN = 2048
SEQS = 16
TOKENS = 32768


def draw_segments(key, part):
    key = jax.random.fold_in(key, 7)
    rate_key, mark_key, start_key = jax.random.split(key, 3)
    seq_count = TOKENS // SEQ_LEN
    periods = jnp.array([8, 32, 128], dtype=jnp.int32)
    levels = jax.random.randint(rate_key, (seq_count, 2), 0, 3)
    period = jnp.repeat(jnp.take(periods, levels), GROUP, axis=1)
    boundary = jax.random.randint(mark_key, (seq_count, SEQ_LEN), 0, 1 << 20) % period == 0
    long_start = jax.random.randint(start_key, (seq_count,), 1, GROUP // 4)
    long_span = GROUP * 3 // 2 + 1
    offsets = jnp.arange(SEQ_LEN)[None, :]
    inside = (offsets > long_start[:, None]) & (offsets < long_start[:, None] + long_span)
    boundary = jnp.where(inside, False, boundary)
    boundary = boundary | (offsets == long_start[:, None]) | (offsets == long_start[:, None] + long_span) | (offsets == 0)
    flat = boundary.reshape(-1)
    index = jnp.arange(TOKENS).astype(jnp.int32)
    flat = flat | (index == TOKENS - 1)
    starts = jnp.where(flat, index, jnp.zeros_like(index))
    return lax.cummax(starts, axis=0).astype(jnp.int32)


def touch_ends(drawn, stream_key, low, high):
    extent = drawn.shape
    index_at = [jax.random.randint(jax.random.fold_in(stream_key, axis), (), 0, extent[axis]) for axis in range(len(extent))]
    drawn = drawn.at[tuple(index_at)].set(low)
    longest = extent.index(max(extent))
    index_at[longest] = (index_at[longest] + 1) % extent[longest]
    return drawn.at[tuple(index_at)].set(high)


def steps_of(stream_key, extent, shards, smallest, high):
    gain, own = 1.0, jax.random.fold_in(stream_key, 6)
    for dim, shards_of in shards:
        draws = jnp.exp(jax.random.uniform(jax.random.fold_in(own, dim), (shards_of,), jnp.float32, smallest / len(shards), high / len(shards)))
        gain = gain * jnp.repeat(draws, extent[dim] // shards_of).reshape([-1 if axis == dim else 1 for axis in range(len(extent))])
    return gain


def scatter_about(own_key, extent, spread, most, cuts=(), kind=jnp.bfloat16):
    gain = steps_of(own_key, extent, cuts, -0.22, 0.18) if cuts else 1.0
    drawn = jax.random.normal(own_key, extent, jnp.float32) * spread * gain
    return jnp.minimum(jnp.maximum(drawn, -most), most).astype(kind)


def setup_inputs(seed: int = 0) -> dict:
    arg_keys = jax.random.split(jax.random.key(seed), 17)
    return {
        "tokens": scatter_about(arg_keys[0], (TOKENS, D), 1.0, 6.0, ((0, 128),)),
        "cotangent": scatter_about(arg_keys[1], (TOKENS, D), 1.0, 6.0, ((0, 128),)),
        "segments": draw_segments(jax.random.fold_in(arg_keys[16], 71), 0),
        "adapter_ids": touch_ends(jax.random.randint(arg_keys[3], (SEQS,), 0, ADAPTERS), jax.random.fold_in(arg_keys[3], 1), 0, ADAPTERS - 1).astype(jnp.int32),
        "norm_gains": jnp.clip(1.0 + 0.1 * jax.random.normal(arg_keys[4], (2, D), jnp.float32), 0.5, 1.5),
        "q_weight": scatter_about(arg_keys[5], (D, H * HD), D ** -0.5, 0.15625, ((0, 32), (1, 4))),
        "kv_weight": scatter_about(arg_keys[6], (2, D, HD), D ** -0.5, 0.15625, ((1, 32),)),
        "out_weight": scatter_about(arg_keys[7], (H * HD, D), (H * HD // 16) ** -0.5, 0.625, ((0, 4), (1, 32))),
        "gate_up_weight": scatter_about(arg_keys[8], (2, D, FF), D ** -0.5, 0.15625, ((1, 32), (2, 4))),
        "down_weight": scatter_about(arg_keys[9], (FF, D), (FF // 2) ** -0.5, 0.125, ((0, 4), (1, 32))),
        "wide_adapters": scatter_about(arg_keys[10], (7, D, ADAPTERS * RANK), 0.06, 0.359375, ((1, 32),)),
        "kv_adapter": scatter_about(arg_keys[11], (2, ADAPTERS * RANK, HD), 0.1, 0.59765625),
        "q_adapter": scatter_about(arg_keys[12], (ADAPTERS * RANK, H * HD), 0.1, 0.59765625, ((1, 4),)),
        "out_adapter": scatter_about(arg_keys[13], (H * HD, ADAPTERS * RANK), (H * HD // 16) ** -0.5, 0.625, ((0, 4),)),
        "gate_up_adapter": scatter_about(arg_keys[14], (2, ADAPTERS * RANK, FF), 0.1, 0.59765625, ((2, 4),)),
        "down_adapter": scatter_about(arg_keys[15], (FF, ADAPTERS * RANK), (FF // 16) ** -0.5, 0.375, ((0, 4),)),
    }


@jax.custom_vjp
def low(v):
    return lax.optimization_barrier(v.astype(jnp.bfloat16)).astype(jnp.float32)

@jax.custom_vjp
def low_back(v):
    return v

def low_keep(v):
    return (low(v), None)

def low_pass(kept, grad):
    return (grad,)

def back_keep(v):
    return (v, None)

def back_low(kept, grad):
    return (low(grad),)
low.defvjp(low_keep, low_pass)
low_back.defvjp(back_keep, back_low)
epsilon = 1e-06
highest = lax.Precision.HIGHEST
masked_score = -1e+30

def product(left_side, right_side):
    return jnp.dot(left_side, right_side, precision=highest)

def rms_norm(vector, gain_row):
    return vector * lax.rsqrt(lax.optimization_barrier(jnp.mean(vector * vector, axis=-1, keepdims=True)) + epsilon) * gain_row

def rope_tables(positions, head_width):
    half_width = head_width // 2
    frequency = 10000.0 ** (-(jnp.arange(half_width).astype(jnp.float32) / half_width))
    angles = positions.astype(jnp.float32)[:, None] * frequency[None, :]
    return (jnp.cos(angles), jnp.sin(angles))

def rotate(vector, cosine_table, sine_table):
    half_width = vector.shape[-1] // 2
    first_half = vector[..., :half_width]
    second_half = vector[..., half_width:]
    return jnp.concatenate([first_half * cosine_table - second_half * sine_table, second_half * cosine_table + first_half * sine_table], axis=-1)

def attend(queries, key_rows, values, segment_ids):
    seq_length = queries.shape[0]
    block_rows = min(512, seq_length // 2)
    score_scale = HD ** (-0.5)
    pad_keys = jnp.concatenate([jnp.zeros((WINDOW, HD), key_rows.dtype), key_rows])
    pad_values = jnp.concatenate([jnp.zeros((WINDOW, HD), values.dtype), values])
    pad_segments = jnp.concatenate([jnp.full((WINDOW,), -1, jnp.int32), segment_ids.astype(jnp.int32)])

    def one_block(begin_row):
        query_block = lax.dynamic_slice_in_dim(queries, begin_row, block_rows, 0)
        key_block = lax.dynamic_slice_in_dim(pad_keys, begin_row, block_rows + WINDOW, 0)
        value_block = lax.dynamic_slice_in_dim(pad_values, begin_row, block_rows + WINDOW, 0)
        query_seg = lax.dynamic_slice_in_dim(segment_ids.astype(jnp.int32), begin_row, block_rows, 0)
        near_seg = lax.dynamic_slice_in_dim(pad_segments, begin_row, block_rows + WINDOW, 0)
        distance = jnp.arange(block_rows)[:, None] + WINDOW - jnp.arange(block_rows + WINDOW)[None, :]
        allowed = (distance >= 0) & (distance <= WINDOW) & (query_seg[:, None] == near_seg[None, :])
        scores = low_back(jnp.einsum('bhd,kd->hbk', query_block, key_block, precision=highest) * score_scale)
        scores = jnp.where(allowed[None], scores, masked_score)
        shifted = jnp.exp(scores - lax.optimization_barrier(jnp.max(scores, axis=-1, keepdims=True)))
        probs = shifted / lax.optimization_barrier(jnp.sum(shifted, axis=-1, keepdims=True))
        mixed_heads = jnp.einsum('hbk,kd->bhd', low(probs), value_block, precision=highest)
        return low(low_back(mixed_heads)).reshape(block_rows, H * HD)
    begins = (jnp.arange(seq_length // block_rows) * block_rows).astype(jnp.int32)
    return lax.map(jax.checkpoint(one_block), begins).reshape(seq_length, H * HD)

def block_forward(vector_in, segment_ids, adapter, frozen, adapters):
    norm_gains, q_weight, kv_weight, out_weight, gate_up_weight, down_weight = frozen
    wide_adapters, kv_adapter, q_adapter, out_adapter, gate_up_adapter, down_adapter = adapters
    column = (adapter * RANK).astype(jnp.int32)

    def take_cols(matrix):
        return lax.dynamic_slice_in_dim(matrix, column, RANK, matrix.ndim - 1)

    def take_rows(matrix):
        return lax.dynamic_slice_in_dim(matrix, column, RANK, matrix.ndim - 2)
    seq_length = vector_in.shape[0]
    cosine_table, sine_table = rope_tables(jnp.arange(seq_length), HD)
    normed_one = low(rms_norm(vector_in, norm_gains[0]))
    rank_q = low(product(normed_one, take_cols(wide_adapters[0])))
    rank_k = low(product(normed_one, take_cols(wide_adapters[1])))
    rank_v = low(product(normed_one, take_cols(wide_adapters[2])))
    query_lin = low_back(product(normed_one, q_weight) + product(rank_q, take_rows(q_adapter)))
    key_lin = product(normed_one, kv_weight[0]) + product(rank_k, take_rows(kv_adapter[0]))
    values = low(product(normed_one, kv_weight[1]) + product(rank_v, take_rows(kv_adapter[1])))
    queries = low(rotate(query_lin.reshape(seq_length, H, HD), cosine_table[:, None, :], sine_table[:, None, :]))
    key_rows = low(rotate(key_lin, cosine_table, sine_table))
    mixed_heads = attend(queries, key_rows, values, segment_ids)
    rank_out = low_back(product(mixed_heads, take_cols(out_adapter)))
    branch = low_back(product(mixed_heads, out_weight) + product(rank_out, take_cols(wide_adapters[5]).T))
    residual = vector_in + branch
    normed_two = low(rms_norm(residual, norm_gains[1]))
    rank_g = low(product(normed_two, take_cols(wide_adapters[3])))
    rank_u = low(product(normed_two, take_cols(wide_adapters[4])))
    gate = low_back(product(normed_two, gate_up_weight[0]) + product(rank_g, take_rows(gate_up_adapter[0])))
    upper = low_back(product(normed_two, gate_up_weight[1]) + product(rank_u, take_rows(gate_up_adapter[1])))
    hidden = low(low_back(jax.nn.gelu(gate, approximate=True) * upper))
    rank_down = low_back(product(hidden, take_cols(down_adapter)))
    ffn = low_back(product(hidden, down_weight) + product(rank_down, take_cols(wide_adapters[6]).T))
    return residual + ffn

def reference(tokens, cotangent, segments, adapter_ids, norm_gains, q_weight, kv_weight, out_weight, gate_up_weight, down_weight, wide_adapters, kv_adapter, q_adapter, out_adapter, gate_up_adapter, down_adapter):
    frozen = tuple((weight.astype(jnp.float32) for weight in (norm_gains, q_weight, kv_weight, out_weight, gate_up_weight, down_weight)))
    adapters = tuple((weight.astype(jnp.float32) for weight in (wide_adapters, kv_adapter, q_adapter, out_adapter, gate_up_adapter, down_adapter)))
    seq_inputs = tokens.astype(jnp.float32).reshape(SEQS, SEQ_LEN, D)
    seq_grads = cotangent.astype(jnp.float32).reshape(SEQS, SEQ_LEN, D)
    seq_segments = segments.reshape(SEQS, SEQ_LEN)

    def one_sequence(totals, packed):
        vector_in, grad_out, segment_ids, adapter = packed

        def forward(inputs, weights):
            return block_forward(inputs, segment_ids, adapter, frozen, weights)
        outcome, pullback = jax.vjp(forward, vector_in, adapters)
        grad_in, grad_adapters = pullback(grad_out)
        totals = jax.tree.map(lambda left_sum, right_term: left_sum + right_term, totals, grad_adapters)
        return (totals, (outcome, grad_in))
    start_totals = jax.tree.map(jnp.zeros_like, adapters)
    totals, (outcomes, grads_in) = lax.scan(one_sequence, start_totals, (seq_inputs, seq_grads, seq_segments, adapter_ids))
    return (outcomes.reshape(TOKENS, D).astype(jnp.bfloat16), grads_in.reshape(TOKENS, D), totals[0], totals[1], totals[2], totals[3], totals[4], totals[5])
```

```python
import jax
import jax.numpy as jnp
from jax import lax
from jax.experimental import pallas as pl
from jax.experimental.pallas import tpu as pltpu
from jax.sharding import PartitionSpec as P

HD = 128
WINDOW = 1024
RANK = 16
LANES = 128
EPS = 1e-06
MASKED = -1e30
SCALE = HD ** (-0.5)
GELU_C = 0.7978845608028654
GELU_A = 0.044715
VMEM_LIMIT = 58 * 1024 * 1024
BF = jnp.bfloat16
F32 = jnp.float32
BOTH = ("dp", "tensor")

SLOT_Q, SLOT_K, SLOT_V, SLOT_G, SLOT_U, SLOT_O, SLOT_D = range(7)


def rows_of(slot):
    return slice(slot * RANK, (slot + 1) * RANK)


def mm(a, b):
    return lax.dot_general(a, b, (((1,), (0,)), ((), ())), preferred_element_type=F32)


def mm_nt(a, b):
    return lax.dot_general(a, b, (((1,), (1,)), ((), ())), preferred_element_type=F32)


def rope(v, cos, sin):
    return v * cos + pltpu.roll(v, HD // 2, 1) * sin


def rope_back(g, cos, sin):
    return g * cos - pltpu.roll(g, HD // 2, 1) * sin


def flat(ref):
    block = ref[...]
    return block.reshape(block.shape[0] * block.shape[2], block.shape[3])


def rms(v, gain):
    return v * lax.rsqrt(jnp.mean(v * v, axis=-1, keepdims=True) + EPS) * gain


def rms_back(v, gain, grad):
    inv = lax.rsqrt(jnp.mean(v * v, axis=-1, keepdims=True) + EPS)
    scaled = grad * gain
    dot = jnp.mean(v * scaled, axis=-1, keepdims=True)
    return inv * scaled - v * (inv * inv * inv * dot)


def pre_kernel(
    x_ref, gain_ref, a_ref, kvw_ref, bkv_ref, cos_ref, sin_ref, wq_ref, bq_ref,
    n1_ref, r1_ref, kv_ref, q_ref,
):
    @pl.when(pl.program_id(0) == 0)
    def _():
        n1 = rms(x_ref[...].astype(F32), gain_ref[...]).astype(BF)
        n1_ref[...] = n1
        r1 = mm(n1, a_ref[...]).astype(BF)
        r1_ref[...] = r1
        key = mm(n1, kvw_ref[0]) + mm(r1, bkv_ref[0])
        kv_ref[:, :HD] = rope(key, cos_ref[...], sin_ref[...]).astype(BF)
        kv_ref[:, HD:] = (mm(n1, kvw_ref[1]) + mm(r1, bkv_ref[1])).astype(BF)

    lin = mm(n1_ref[...], flat(wq_ref)) + mm(r1_ref[...], bq_ref[0])
    for h in range(lin.shape[1] // HD):
        part = slice(h * HD, (h + 1) * HD)
        q_ref[:, part] = rope(lin[:, part], cos_ref[...], sin_ref[...]).astype(BF)


def fill_bias(bias_ref, kseg_ref, qseg_ref):
    shape = bias_ref.shape
    key = lax.broadcasted_iota(jnp.int32, shape, 0)
    query = lax.broadcasted_iota(jnp.int32, shape, 1)
    allowed = (key >= query) & (key <= query + WINDOW) & (kseg_ref[...] == qseg_ref[...])
    bias_ref[...] = jnp.where(allowed, 0.0, MASKED)


def attn_kernel(
    kv_ref, kseg_ref, qseg_ref, x_ref, gain_ref, a_ref, q_ref, wo_ref, bo_ref,
    mixed_ref, lse_ref, res_ref, n2_ref, r2_ref, ro_ref,
    bias_ref, s_ref, p_ref, acc_ref, vt_ref, rank_ref,
):
    step = pl.program_id(0)
    rows = q_ref.shape[0]
    chunks = kv_ref.shape[0] // rows

    @pl.when(step == 0)
    def _():
        fill_bias(bias_ref, kseg_ref, qseg_ref)
        vt_ref[...] = kv_ref[:, HD:].astype(F32).T.astype(BF)
        acc_ref[...] = jnp.zeros_like(acc_ref)
        rank_ref[...] = jnp.zeros_like(rank_ref)

    for h in range(q_ref.shape[1] // HD):
        part = slice(h * HD, (h + 1) * HD)
        query = q_ref[:, part]
        top = jnp.full((1, rows), MASKED, F32)
        for c in range(chunks):
            span = slice(c * rows, (c + 1) * rows)
            s = mm_nt(kv_ref[span, :HD], query) * SCALE + bias_ref[span]
            s_ref[span] = s
            top = jnp.maximum(top, jnp.max(s, axis=0, keepdims=True))
        total = jnp.zeros((1, rows), F32)
        for c in range(chunks):
            span = slice(c * rows, (c + 1) * rows)
            p = jnp.exp(s_ref[span] - top)
            total = total + jnp.sum(p, axis=0, keepdims=True)
            p_ref[span] = p.astype(BF)
        out = mm(vt_ref[...], p_ref[...]) / total
        mixed_ref[:, part] = out.T.astype(BF)
        lse_ref[0, h : h + 1] = top + jnp.log(total)

    mixed = mixed_ref[...]
    acc_ref[...] += mm_nt(mixed, flat(wo_ref))
    rank_ref[...] += mm_nt(mixed, bo_ref[0])

    @pl.when(step == pl.num_programs(0) - 1)
    def _():
        ro = rank_ref[...].astype(BF)
        ro_ref[...] = ro
        res = x_ref[...].astype(F32) + (acc_ref[...] + mm_nt(ro, a_ref[...]))
        res_ref[...] = res
        n2 = rms(res, gain_ref[...]).astype(BF)
        n2_ref[...] = n2
        r2_ref[...] = mm(n2, a_ref[...]).astype(BF)


def ffn_kernel(
    res_ref, n2_ref, r2_ref, cot_ref, gain_ref, a_ref,
    g_ref, u_ref, d_ref, bg_ref, bu_ref, bd_ref,
    out_ref, gres_ref, gb_ref, wide_ref, gbg_ref, gbu_ref, gbd_ref,
    ffn_ref, g2_ref, rd_ref, gr_ref, r2t_ref, grd_ref, grdt_ref,
):
    step = pl.program_id(0)

    @pl.when(step == 0)
    def _():
        ffn_ref[...] = jnp.zeros_like(ffn_ref)
        g2_ref[...] = jnp.zeros_like(g2_ref)
        rd_ref[...] = jnp.zeros_like(rd_ref)
        gr_ref[...] = jnp.zeros_like(gr_ref)
        r2t_ref[...] = r2_ref[...].astype(F32).T.astype(BF)
        grd = mm(cot_ref[...], a_ref[...]).astype(BF)
        grd_ref[...] = grd
        grdt_ref[...] = grd.astype(F32).T.astype(BF)

    n2, r2, cot = n2_ref[...], r2_ref[...], cot_ref[...]
    w_g, w_u, w_d = flat(g_ref), flat(u_ref), flat(d_ref)
    gate = mm(n2, w_g) + mm(r2, bg_ref[0])
    up = mm(n2, w_u) + mm(r2, bu_ref[0])
    grad_hidden = (mm(cot, w_d) + mm(grd_ref[...], bd_ref[0])).astype(BF).astype(F32)
    square = gate * gate
    th = jnp.tanh(GELU_C * (gate + GELU_A * square * gate))
    half = 0.5 * (1.0 + th)
    act = gate * half
    slope = half + 0.5 * gate * (1.0 - th * th) * (GELU_C * (1.0 + 3.0 * GELU_A * square))
    hidden = (act * up).astype(BF)
    grad_gate = (grad_hidden * up * slope).astype(BF)
    grad_up = (grad_hidden * act).astype(BF)
    ffn_ref[...] += mm_nt(hidden, w_d)
    rd_ref[...] += mm_nt(hidden, bd_ref[0])
    g2_ref[...] += mm_nt(grad_gate, w_g) + mm_nt(grad_up, w_u)
    gr_ref[...] += mm_nt(grad_gate, bg_ref[0]) + mm_nt(grad_up, bu_ref[0])
    gbg_ref[0] = mm(r2t_ref[rows_of(SLOT_G)], grad_gate).astype(BF)
    gbu_ref[0] = mm(r2t_ref[rows_of(SLOT_U)], grad_up).astype(BF)
    gbd_ref[0] = mm(grdt_ref[rows_of(SLOT_D)], hidden).astype(BF)

    @pl.when(step == pl.num_programs(0) - 1)
    def _():
        rd = rd_ref[...].astype(BF)
        gr = gr_ref[...].astype(BF)
        res = res_ref[...]
        out_ref[...] = (res + (ffn_ref[...] + mm_nt(rd, a_ref[...]))).astype(BF)
        grad_two = g2_ref[...] + mm_nt(gr, a_ref[...])
        grad_res = cot_ref[...].astype(F32) + rms_back(res, gain_ref[...], grad_two)
        gres_ref[...] = grad_res
        gb_ref[...] = grad_res.astype(BF)
        wide_ref[...] = mm(gr_ref[...].T.astype(BF), n2) + mm(rd_ref[...].T.astype(BF), cot)


def attn_back_kernel(
    kv_ref, kseg_ref, qseg_ref, gb_ref, a_ref, r1_ref, ro_ref, cos_ref, sin_ref,
    q_ref, mixed_ref, lse_ref, wo_ref, bo_ref, wq_ref, bq_ref,
    dkv_ref, g1_ref, gr_ref, wide_ref, gbo_ref, gbq_ref,
    bias_ref, ds_ref, dk_ref, dv_ref, kt_ref, r1t_ref, gro_ref, grot_ref, gq_ref, gm_ref,
):
    step = pl.program_id(0)
    rows = q_ref.shape[0]
    chunks = kv_ref.shape[0] // rows

    @pl.when(step == 0)
    def _():
        fill_bias(bias_ref, kseg_ref, qseg_ref)
        kt_ref[...] = kv_ref[:, :HD].astype(F32).T.astype(BF)
        r1t_ref[...] = r1_ref[...].astype(F32).T.astype(BF)
        gro = mm(gb_ref[...], a_ref[...]).astype(BF)
        gro_ref[...] = gro
        grot_ref[...] = gro.astype(F32).T.astype(BF)
        dk_ref[...] = jnp.zeros_like(dk_ref)
        dv_ref[...] = jnp.zeros_like(dv_ref)
        g1_ref[...] = jnp.zeros_like(g1_ref)
        gr_ref[...] = jnp.zeros_like(gr_ref)

    gm_ref[...] = (mm(gb_ref[...], flat(wo_ref)) + mm(gro_ref[...], bo_ref[0])).astype(BF)
    gbo_ref[0] = mm(grot_ref[rows_of(SLOT_O)], mixed_ref[...]).astype(BF)
    for h in range(q_ref.shape[1] // HD):
        part = slice(h * HD, (h + 1) * HD)
        query, grad = q_ref[:, part], gm_ref[:, part]
        delta = grad.astype(F32) * mixed_ref[:, part].astype(F32)
        delta = jnp.sum(delta.T, axis=0, keepdims=True)
        lse = lse_ref[0, h : h + 1]
        for c in range(chunks):
            span = slice(c * rows, (c + 1) * rows)
            s = mm_nt(kv_ref[span, :HD], query) * SCALE + bias_ref[span]
            p = jnp.exp(s - lse)
            dp = mm_nt(kv_ref[span, HD:], grad)
            ds = (p * (dp - delta)).astype(BF)
            ds_ref[span] = ds
            dk_ref[span] += mm(ds, query)
            dv_ref[span] += mm(p.astype(BF), grad)
        dq = mm(kt_ref[...], ds_ref[...]) * SCALE
        gq_ref[:, part] = rope_back(dq.T, cos_ref[...], sin_ref[...]).astype(BF)

    gq = gq_ref[...]
    gbq_ref[0] = mm(r1t_ref[rows_of(SLOT_Q)], gq).astype(BF)
    gr_ref[...] += mm_nt(gq, bq_ref[0])
    g1_ref[...] += mm_nt(gq, flat(wq_ref))

    @pl.when(step == pl.num_programs(0) - 1)
    def _():
        dkv_ref[:, :HD] = (dk_ref[...] * SCALE).astype(BF)
        dkv_ref[:, HD:] = dv_ref[...].astype(BF)
        wide_ref[...] = mm(ro_ref[...].astype(F32).T.astype(BF), gb_ref[...])


def final_kernel(
    x_ref, gain_ref, a_ref, n1_ref, r1_ref, kvw_ref, bkv_ref, cos_ref, sin_ref,
    gkv_ref, g1_ref, gr_ref, gres_ref, widef_ref, wideo_ref,
    grad_ref, wide_ref, kvg_ref,
):
    gk = rope_back(gkv_ref[:, :HD].astype(F32), cos_ref[...], sin_ref[...]).astype(BF)
    gv = gkv_ref[:, HD:].astype(BF)
    gr = gr_ref[...] + mm_nt(gk, bkv_ref[0]) + mm_nt(gv, bkv_ref[1])
    wide = mm(gr.T.astype(BF), n1_ref[...]) + widef_ref[...] + wideo_ref[...]
    wide_ref[...] = wide.T.astype(BF)
    r1t = r1_ref[...].astype(F32).T.astype(BF)
    kvg_ref[0] = mm(r1t[rows_of(SLOT_K)], gk).astype(BF)
    kvg_ref[1] = mm(r1t[rows_of(SLOT_V)], gv).astype(BF)
    g1 = g1_ref[...] + mm_nt(gk, kvw_ref[0]) + mm_nt(gv, kvw_ref[1])
    g1 = g1 + mm_nt(gr.astype(BF), a_ref[...])
    x = x_ref[...].astype(F32)
    grad_ref[...] = gres_ref[...] + rms_back(x, gain_ref[...], g1)


def whole(array):
    rank = len(array.shape)
    return pl.BlockSpec(array.shape, lambda *_: (0,) * rank)


def out_whole(shape):
    rank = len(shape)
    return pl.BlockSpec(shape, lambda *_: (0,) * rank)


def call(kernel, name, steps, args, specs, outs, out_specs, scratch, flops, nbytes):
    return pl.pallas_call(
        kernel,
        name=name,
        grid=(steps,),
        in_specs=specs,
        out_specs=out_specs,
        out_shape=outs,
        scratch_shapes=scratch,
        compiler_params=pltpu.CompilerParams(
            dimension_semantics=("arbitrary",), vmem_limit_bytes=VMEM_LIMIT
        ),
        cost_estimate=pl.CostEstimate(flops=flops, bytes_accessed=nbytes, transcendentals=0),
    )(*args)


def on_device(
    tokens, cotangent, segments, adapter_ids, norm_gains, q_weight, kv_weight, out_weight,
    gate_up_weight, down_weight, wide_adapters, kv_adapter, q_adapter, out_adapter,
    gate_up_adapter, down_adapter,
):
    rows, width = tokens.shape
    dp_count, tensor_count = lax.axis_size("dp"), lax.axis_size("tensor")
    devices = dp_count * tensor_count
    group_rows = rows * tensor_count
    seq_length = 2 * group_rows
    shard_rows = q_weight.shape[0]
    q_cols, ff_cols = q_weight.shape[1], gate_up_weight.shape[2]
    pack_cols = 3 * ff_cols + 2 * q_cols
    seqs = adapter_ids.shape[0]
    adapters = wide_adapters.shape[2] // RANK
    q_block = 3 * ff_cols // q_cols
    dp = lax.axis_index("dp")
    tensor = lax.axis_index("tensor")
    adapter = lax.dynamic_index_in_dim(adapter_ids, dp // 2, keepdims=False)
    column = adapter * RANK

    def sds(shape, dtype):
        return jax.ShapeDtypeStruct(shape, dtype)

    pack = jnp.concatenate(
        [gate_up_weight[0], gate_up_weight[1], down_weight.T, q_weight, out_weight.T], axis=1
    )
    weights = lax.all_gather(pack, BOTH, axis=0, tiled=False)
    weights = weights.reshape(dp_count, tensor_count, shard_rows, pack_cols)
    kv_full = lax.all_gather(kv_weight, "dp", axis=1, tiled=True)

    wide = wide_adapters.reshape(7, shard_rows, adapters, RANK)
    wide = jnp.take(wide, adapter_ids, axis=2).transpose(2, 1, 0, 3)
    wide = wide.reshape(seqs, shard_rows, 7 * RANK)
    wide = jnp.pad(wide, ((0, 0), (0, 0), (0, LANES - 7 * RANK)))
    wide = jnp.repeat(wide, dp_count // seqs, axis=0)
    a_all = lax.all_to_all(wide, "dp", 0, 0, tiled=True).reshape(width, LANES)

    def take_rows(matrix):
        return lax.dynamic_slice_in_dim(matrix, column, RANK, matrix.ndim - 2)

    def take_cols(matrix):
        return lax.dynamic_slice_in_dim(matrix, column, RANK, matrix.ndim - 1)

    gu_rows = take_rows(gate_up_adapter)
    b_own = jnp.concatenate(
        [gu_rows[0], gu_rows[1], take_cols(down_adapter).T, take_rows(q_adapter), take_cols(out_adapter).T],
        axis=1,
    )
    b_all = lax.all_gather(b_own, "tensor", axis=0, tiled=False)

    def in_slot(block, slot):
        pads = [(0, 0)] * block.ndim
        pads[-2] = (slot * RANK, LANES - (slot + 1) * RANK)
        return jnp.pad(block, pads)

    f1, f2, f3 = ff_cols, 2 * ff_cols, 3 * ff_cols
    b_pad = jnp.concatenate(
        [
            in_slot(b_all[:, :, :f1], SLOT_G),
            in_slot(b_all[:, :, f1:f2], SLOT_U),
            in_slot(b_all[:, :, f2:f3], SLOT_D),
            in_slot(b_all[:, :, f3 : f3 + q_cols], SLOT_Q),
            in_slot(b_all[:, :, f3 + q_cols :], SLOT_O),
        ],
        axis=2,
    )
    kv_rows = take_rows(kv_adapter)
    b_kv = jnp.stack([in_slot(kv_rows[0], SLOT_K), in_slot(kv_rows[1], SLOT_V)])

    start = dp * group_rows + tensor * rows
    positions = (start + jnp.arange(rows)) % seq_length
    half = HD // 2
    frequency = 10000.0 ** (-(jnp.arange(half).astype(F32) / half))
    angles = positions.astype(F32)[:, None] * frequency[None, :]
    cos, sin = jnp.cos(angles), jnp.sin(angles)
    cos = jnp.concatenate([cos, cos], axis=1)
    sin = jnp.concatenate([-sin, sin], axis=1)

    padded = jnp.concatenate([jnp.full((WINDOW,), -1, jnp.int32), segments])
    kseg = lax.dynamic_slice_in_dim(padded, start, WINDOW + rows, 0)
    qseg = kseg[WINDOW:].reshape(1, rows)
    kseg = kseg.reshape(WINDOW + rows, 1)
    span = WINDOW + rows

    gain_one, gain_two = norm_gains[0:1], norm_gains[1:2]

    def weight_spec(cols, block):
        return pl.BlockSpec((dp_count, 1, shard_rows, cols), lambda t: (0, t, 0, block))

    def adapter_spec(cols, block):
        return pl.BlockSpec((1, LANES, cols), lambda t: (t, 0, block))

    def token_cols(cols):
        return pl.BlockSpec((rows, cols), lambda t: (0, t))

    def by_step(*shape):
        return pl.BlockSpec((1,) + shape, lambda t: (t,) + (0,) * len(shape))

    heads_cols = tensor_count * q_cols
    q_spec, qb_spec = weight_spec(q_cols, q_block), adapter_spec(q_cols, q_block)
    o_spec, ob_spec = weight_spec(q_cols, q_block + 1), adapter_spec(q_cols, q_block + 1)

    args = (tokens, gain_one, a_all, kv_full, b_kv, cos, sin, weights, b_pad)
    normed_one, rank_one, kv_own, queries = call(
        pre_kernel, "qkv", tensor_count, args,
        [whole(v) for v in args[:7]] + [q_spec, qb_spec],
        (sds((rows, width), BF), sds((rows, LANES), BF), sds((rows, 2 * HD), BF), sds((rows, heads_cols), BF)),
        (out_whole((rows, width)), out_whole((rows, LANES)), out_whole((rows, 2 * HD)), token_cols(q_cols)),
        [], 2 * rows * width * (heads_cols + 384), 2 * width * heads_cols,
    )

    kv_half = lax.all_gather(kv_own, "tensor", axis=0, tiled=True)
    kv_prev = lax.ppermute(kv_half, "dp", [(2 * s, 2 * s + 1) for s in range(dp_count // 2)])
    kv_window = lax.dynamic_slice_in_dim(jnp.concatenate([kv_prev, kv_half]), tensor * rows, span, 0)

    args = (kv_window, kseg, qseg, tokens, gain_two, a_all, queries, weights, b_pad)
    mixed, lse, residual, normed_two, rank_two, rank_out = call(
        attn_kernel, "attention", tensor_count, args,
        [whole(v) for v in args[:6]] + [token_cols(q_cols), o_spec, ob_spec],
        (
            sds((rows, heads_cols), BF), sds((tensor_count, 8, rows), F32), sds((rows, width), F32),
            sds((rows, width), BF), sds((rows, LANES), BF), sds((rows, LANES), BF),
        ),
        (
            token_cols(q_cols), by_step(8, rows), out_whole((rows, width)),
            out_whole((rows, width)), out_whole((rows, LANES)), out_whole((rows, LANES)),
        ),
        [
            pltpu.VMEM((span, rows), F32), pltpu.VMEM((span, rows), F32), pltpu.VMEM((span, rows), BF),
            pltpu.VMEM((rows, width), F32), pltpu.VMEM((HD, span), BF), pltpu.VMEM((rows, LANES), F32),
        ],
        2 * rows * heads_cols * (2 * span + width), 2 * width * heads_cols,
    )

    args = (residual, normed_two, rank_two, cotangent, gain_two, a_all, weights, weights, weights, b_pad, b_pad, b_pad)
    block_output, grad_residual, grad_branch, wide_ffn, grad_bg, grad_bu, grad_bd = call(
        ffn_kernel, "feed_forward", tensor_count, args,
        [whole(v) for v in args[:6]]
        + [weight_spec(ff_cols, j) for j in range(3)]
        + [adapter_spec(ff_cols, j) for j in range(3)],
        (sds((rows, width), BF), sds((rows, width), F32), sds((rows, width), BF), sds((LANES, width), F32))
        + (sds((tensor_count, RANK, ff_cols), BF),) * 3,
        (out_whole((rows, width)), out_whole((rows, width)), out_whole((rows, width)), out_whole((LANES, width)))
        + (by_step(RANK, ff_cols),) * 3,
        [
            pltpu.VMEM((rows, width), F32), pltpu.VMEM((rows, width), F32),
            pltpu.VMEM((rows, LANES), F32), pltpu.VMEM((rows, LANES), F32),
            pltpu.VMEM((LANES, rows), BF), pltpu.VMEM((rows, LANES), BF), pltpu.VMEM((LANES, rows), BF),
        ],
        12 * rows * width * tensor_count * ff_cols, 6 * width * tensor_count * ff_cols,
    )

    args = (
        kv_window, kseg, qseg, grad_branch, a_all, rank_one, rank_out, cos, sin,
        queries, mixed, lse, weights, b_pad, weights, b_pad,
    )
    dkv, grad_one, grad_rank, wide_out, grad_bo, grad_bq = call(
        attn_back_kernel, "attention_back", tensor_count, args,
        [whole(v) for v in args[:9]]
        + [token_cols(q_cols), token_cols(q_cols), by_step(8, rows), o_spec, ob_spec, q_spec, qb_spec],
        (
            sds((span, 2 * HD), BF), sds((rows, width), F32), sds((rows, LANES), F32), sds((LANES, width), F32),
            sds((tensor_count, RANK, q_cols), BF), sds((tensor_count, RANK, q_cols), BF),
        ),
        (
            out_whole((span, 2 * HD)), out_whole((rows, width)), out_whole((rows, LANES)), out_whole((LANES, width)),
            by_step(RANK, q_cols), by_step(RANK, q_cols),
        ),
        [
            pltpu.VMEM((span, rows), F32), pltpu.VMEM((span, rows), BF),
            pltpu.VMEM((span, HD), F32), pltpu.VMEM((span, HD), F32), pltpu.VMEM((HD, span), BF),
            pltpu.VMEM((LANES, rows), BF), pltpu.VMEM((rows, LANES), BF), pltpu.VMEM((LANES, rows), BF),
            pltpu.VMEM((rows, q_cols), BF), pltpu.VMEM((rows, q_cols), BF),
        ],
        2 * rows * heads_cols * (5 * span + 2 * width), 4 * width * heads_cols,
    )

    placed = lax.dynamic_update_slice_in_dim(jnp.zeros((seq_length, 2 * HD), BF), dkv, tensor * rows, 0)
    returned = lax.ppermute(placed[:group_rows], "dp", [(2 * s + 1, 2 * s) for s in range(dp_count // 2)])
    gathered = placed[group_rows:].astype(F32) + returned.astype(F32)
    grad_kv = lax.psum_scatter(gathered.astype(BF), "tensor", scatter_dimension=0, tiled=True)

    args = (
        tokens, gain_one, a_all, normed_one, rank_one, kv_full, b_kv, cos, sin,
        grad_kv, grad_one, grad_rank, grad_residual, wide_ffn, wide_out,
    )
    input_grad, wide_term, kv_term = call(
        final_kernel, "input_gradient", 1, args, [whole(v) for v in args],
        (sds((rows, width), F32), sds((width, LANES), BF), sds((2, RANK, HD), BF)),
        (out_whole((rows, width)), out_whole((width, LANES)), out_whole((2, RANK, HD))),
        [], 2 * rows * width * 640, 8 * rows * width,
    )

    own_rows = width // devices
    kv_rows_out = jnp.tile(kv_term.transpose(1, 0, 2), (devices // RANK, 1, 1))
    payload = jnp.concatenate(
        [wide_term.reshape(devices, own_rows, LANES), kv_rows_out, jnp.zeros((devices, 2, LANES), BF)], axis=1
    )
    received = lax.all_to_all(payload, BOTH, 0, 0, tiled=True)
    sent_rows = own_rows + 4
    source_adapter = jnp.repeat(adapter_ids, devices // seqs)
    pick = (jnp.arange(adapters)[:, None] == source_adapter[None, :]).astype(BF)
    summed = mm(pick, received.reshape(devices, sent_rows * LANES)).reshape(adapters, sent_rows, LANES)
    wide_grad = summed[:, :own_rows, : 7 * RANK].reshape(adapters, own_rows, 7, RANK)
    wide_grad = wide_grad.transpose(2, 1, 0, 3).reshape(7, own_rows, adapters * RANK)
    own_row = dp * tensor_count + tensor
    kv_adapter_grad = lax.dynamic_index_in_dim(
        summed[:, own_rows : own_rows + 2], own_row // RANK, 0, keepdims=False
    ).reshape(2, 1, HD)

    pick_dp = (jnp.arange(adapters)[:, None] == jnp.repeat(adapter_ids, dp_count // seqs)[None, :]).astype(BF)

    def by_adapter(terms):
        own = lax.psum_scatter(terms, "tensor", scatter_dimension=0, tiled=True)
        every = lax.all_gather(own.reshape(RANK, -1), "dp", axis=0, tiled=False)
        cols = every.shape[2]
        return mm(pick_dp, every.reshape(dp_count, RANK * cols)).reshape(adapters * RANK, cols)

    early = by_adapter(jnp.concatenate([grad_bg, grad_bu, grad_bd, grad_bo], axis=2))
    q_adapter_grad = by_adapter(grad_bq)
    gate_up_adapter_grad = jnp.stack([early[:, :f1], early[:, f1:f2]])
    down_adapter_grad = early[:, f2:f3].T
    out_adapter_grad = early[:, f3:].T
    return (
        block_output, input_grad, wide_grad, kv_adapter_grad,
        q_adapter_grad, out_adapter_grad, gate_up_adapter_grad, down_adapter_grad,
    )


def solution(mesh):
    return jax.shard_map(
        on_device,
        mesh=mesh,
        in_specs=(
            P(BOTH, None), P(BOTH, None), P(), P(), P(), P("dp", "tensor"), P(None, "dp", None),
            P("tensor", "dp"), P(None, "dp", "tensor"), P("tensor", "dp"), P(None, "dp", None), P(),
            P(None, "tensor"), P("tensor", None), P(None, None, "tensor"), P("tensor", None),
        ),
        out_specs=(
            P(BOTH, None), P(BOTH, None), P(None, BOTH, None), P(None, BOTH, None),
            P(None, "tensor"), P("tensor", None), P(None, None, "tensor"), P("tensor", None),
        ),
        check_vma=False,
    )
```

```python
import jax
import jax.numpy as jnp
from jax import lax
from jax.experimental import pallas as pl
from jax.experimental.pallas import tpu as pltpu
from jax.sharding import PartitionSpec as P

HD = 128
WINDOW = 1024
RANK = 16
LANES = 128
EPS = 1e-06
MASKED = -1e30
SCALE = HD ** (-0.5)
GELU_C = 0.7978845608028654
GELU_A = 0.044715
VMEM_LIMIT = 58 * 1024 * 1024
BF = jnp.bfloat16
F32 = jnp.float32
BOTH = ("dp", "tensor")

SLOT_Q, SLOT_K, SLOT_V, SLOT_G, SLOT_U, SLOT_O, SLOT_D = range(7)


def rows_of(slot):
    return slice(slot * RANK, (slot + 1) * RANK)


def mm(a, b):
    return lax.dot_general(a, b, (((1,), (0,)), ((), ())), preferred_element_type=F32)


def mm_nt(a, b):
    return lax.dot_general(a, b, (((1,), (1,)), ((), ())), preferred_element_type=F32)


def rope(v, cos, sin):
    return v * cos + pltpu.roll(v, HD // 2, 1) * sin


def rope_back(g, cos, sin):
    return g * cos - pltpu.roll(g, HD // 2, 1) * sin


def flat(ref):
    block = ref[...]
    return block.reshape(block.shape[0] * block.shape[2], block.shape[3])


def rms(v, gain):
    return v * lax.rsqrt(jnp.mean(v * v, axis=-1, keepdims=True) + EPS) * gain


def rms_back(v, gain, grad):
    inv = lax.rsqrt(jnp.mean(v * v, axis=-1, keepdims=True) + EPS)
    scaled = grad * gain
    dot = jnp.mean(v * scaled, axis=-1, keepdims=True)
    return inv * scaled - v * (inv * inv * inv * dot)


def pre_kernel(
    x_ref, gain_ref, a_ref, wk_ref, wv_ref, bkv_ref, cos_ref, sin_ref, wq_ref, bq_ref,
    n1_ref, r1_ref, kv_ref, q_ref,
):
    @pl.when(pl.program_id(0) == 0)
    def _():
        n1 = rms(x_ref[...].astype(F32), gain_ref[...]).astype(BF)
        n1_ref[...] = n1
        r1 = mm(n1, a_ref[...]).astype(BF)
        r1_ref[...] = r1
        key = mm(n1, wk_ref[...]) + mm(r1, bkv_ref[0])
        kv_ref[:, :HD] = rope(key, cos_ref[...], sin_ref[...]).astype(BF)
        kv_ref[:, HD:] = (mm(n1, wv_ref[...]) + mm(r1, bkv_ref[1])).astype(BF)

    lin = mm(n1_ref[...], flat(wq_ref)) + mm(r1_ref[...], bq_ref[0])
    for h in range(lin.shape[1] // HD):
        part = slice(h * HD, (h + 1) * HD)
        q_ref[:, part] = rope(lin[:, part], cos_ref[...], sin_ref[...]).astype(BF)


def fill_bias(bias_ref, kseg_ref, qseg_ref):
    shape = bias_ref.shape
    key = lax.broadcasted_iota(jnp.int32, shape, 0)
    query = lax.broadcasted_iota(jnp.int32, shape, 1)
    allowed = (key >= query) & (key <= query + WINDOW) & (kseg_ref[...] == qseg_ref[...])
    bias_ref[...] = jnp.where(allowed, 0.0, MASKED)


def attn_kernel(
    kv_ref, kseg_ref, qseg_ref, x_ref, gain_ref, a_ref, q_ref, wo_ref, bo_ref,
    mixed_ref, p_ref, res_ref, n2_ref, r2_ref, ro_ref,
    bias_ref, s_ref, acc_ref, vt_ref, rank_ref,
):
    step = pl.program_id(0)
    rows = q_ref.shape[0]
    chunks = kv_ref.shape[0] // rows

    @pl.when(step == 0)
    def _():
        fill_bias(bias_ref, kseg_ref, qseg_ref)
        vt_ref[...] = kv_ref[:, HD:].astype(F32).T.astype(BF)
        acc_ref[...] = jnp.zeros_like(acc_ref)
        rank_ref[...] = jnp.zeros_like(rank_ref)

    for h in range(q_ref.shape[1] // HD):
        part = slice(h * HD, (h + 1) * HD)
        query = q_ref[:, part]
        top = jnp.full((1, rows), MASKED, F32)
        for c in range(chunks):
            span = slice(c * rows, (c + 1) * rows)
            s = mm_nt(kv_ref[span, :HD], query) * SCALE + bias_ref[span]
            s_ref[span] = s
            top = jnp.maximum(top, jnp.max(s, axis=0, keepdims=True))
        total = jnp.zeros((1, rows), F32)
        for c in range(chunks):
            span = slice(c * rows, (c + 1) * rows)
            p = jnp.exp(s_ref[span] - top)
            total = total + jnp.sum(p, axis=0, keepdims=True)
            s_ref[span] = p
        inv = 1.0 / total
        for c in range(chunks):
            span = slice(c * rows, (c + 1) * rows)
            p_ref[h, span] = (s_ref[span] * inv).astype(BF)
        mixed_ref[:, part] = mm(vt_ref[...], p_ref[h]).T.astype(BF)

    mixed = mixed_ref[...]
    acc_ref[...] += mm_nt(mixed, flat(wo_ref))
    rank_ref[...] += mm_nt(mixed, bo_ref[0])

    @pl.when(step == pl.num_programs(0) - 1)
    def _():
        ro = rank_ref[...].astype(BF)
        ro_ref[...] = ro
        res = x_ref[...].astype(F32) + (acc_ref[...] + mm_nt(ro, a_ref[...]))
        res_ref[...] = res
        n2 = rms(res, gain_ref[...]).astype(BF)
        n2_ref[...] = n2
        r2_ref[...] = mm(n2, a_ref[...]).astype(BF)


def ffn_kernel(
    res_ref, n2_ref, r2_ref, cot_ref, gain_ref, mixed_ref, ro_ref, a_ref,
    g_ref, u_ref, d_ref, bg_ref, bu_ref, bd_ref,
    out_ref, gres_ref, gb_ref, wide_ref, gro_ref, gbo_ref, gbg_ref, gbu_ref, gbd_ref,
    ffn_ref, g2_ref, rd_ref, gr_ref, r2t_ref, grd_ref, grdt_ref,
):
    step = pl.program_id(0)

    @pl.when(step == 0)
    def _():
        ffn_ref[...] = jnp.zeros_like(ffn_ref)
        g2_ref[...] = jnp.zeros_like(g2_ref)
        rd_ref[...] = jnp.zeros_like(rd_ref)
        gr_ref[...] = jnp.zeros_like(gr_ref)
        r2t_ref[...] = r2_ref[...].astype(F32).T.astype(BF)
        grd = mm(cot_ref[...], a_ref[...]).astype(BF)
        grd_ref[...] = grd
        grdt_ref[...] = grd.astype(F32).T.astype(BF)

    n2, r2, cot = n2_ref[...], r2_ref[...], cot_ref[...]
    w_g, w_u, w_d = flat(g_ref), flat(u_ref), flat(d_ref)
    gate = mm(n2, w_g) + mm(r2, bg_ref[0])
    up = mm(n2, w_u) + mm(r2, bu_ref[0])
    grad_hidden = (mm(cot, w_d) + mm(grd_ref[...], bd_ref[0])).astype(BF).astype(F32)
    square = gate * gate
    th = jnp.tanh(GELU_C * (gate + GELU_A * square * gate))
    half = 0.5 * (1.0 + th)
    act = gate * half
    slope = half + 0.5 * gate * (1.0 - th * th) * (GELU_C * (1.0 + 3.0 * GELU_A * square))
    hidden = (act * up).astype(BF)
    grad_gate = (grad_hidden * up * slope).astype(BF)
    grad_up = (grad_hidden * act).astype(BF)
    ffn_ref[...] += mm_nt(hidden, w_d)
    rd_ref[...] += mm_nt(hidden, bd_ref[0])
    g2_ref[...] += mm_nt(grad_gate, w_g) + mm_nt(grad_up, w_u)
    gr_ref[...] += mm_nt(grad_gate, bg_ref[0]) + mm_nt(grad_up, bu_ref[0])
    gbg_ref[0] = mm(r2t_ref[rows_of(SLOT_G)], grad_gate).astype(BF)
    gbu_ref[0] = mm(r2t_ref[rows_of(SLOT_U)], grad_up).astype(BF)
    gbd_ref[0] = mm(grdt_ref[rows_of(SLOT_D)], hidden).astype(BF)

    @pl.when(step == pl.num_programs(0) - 1)
    def _():
        rd = rd_ref[...].astype(BF)
        gr = gr_ref[...].astype(BF)
        res = res_ref[...]
        out_ref[...] = (res + (ffn_ref[...] + mm_nt(rd, a_ref[...]))).astype(BF)
        grad_two = g2_ref[...] + mm_nt(gr, a_ref[...])
        grad_res = cot_ref[...].astype(F32) + rms_back(res, gain_ref[...], grad_two)
        gres_ref[...] = grad_res
        grad_branch = grad_res.astype(BF)
        gb_ref[...] = grad_branch
        gro = mm(grad_branch, a_ref[...])
        gro_ref[...] = gro.astype(BF)
        grot = gro.T[rows_of(SLOT_O)].astype(BF)
        cols = gbo_ref.shape[2]
        for t in range(gbo_ref.shape[0]):
            gbo_ref[t] = mm(grot, mixed_ref[:, t * cols : (t + 1) * cols]).astype(BF)
        wide = mm(gr_ref[...].T.astype(BF), n2) + mm(rd_ref[...].T.astype(BF), cot)
        wide_ref[...] = wide + mm(ro_ref[...].astype(F32).T.astype(BF), grad_branch)


def attn_back_kernel(
    kv_ref, gb_ref, gro_ref, r1_ref, cos_ref, sin_ref,
    q_ref, mixed_ref, p_ref, wo_ref, bo_ref, wq_ref, bq_ref,
    dkv_ref, g1_ref, gr_ref, gbq_ref,
    ds_ref, dk_ref, dv_ref, kt_ref, r1t_ref, gq_ref, gm_ref,
):
    step = pl.program_id(0)
    rows = q_ref.shape[0]
    chunks = kv_ref.shape[0] // rows

    @pl.when(step == 0)
    def _():
        kt_ref[...] = kv_ref[:, :HD].astype(F32).T.astype(BF)
        r1t_ref[...] = r1_ref[...].astype(F32).T.astype(BF)
        dk_ref[...] = jnp.zeros_like(dk_ref)
        dv_ref[...] = jnp.zeros_like(dv_ref)
        g1_ref[...] = jnp.zeros_like(g1_ref)
        gr_ref[...] = jnp.zeros_like(gr_ref)

    gm_ref[...] = (mm(gb_ref[...], flat(wo_ref)) + mm(gro_ref[...], bo_ref[0])).astype(BF)
    for h in range(q_ref.shape[1] // HD):
        part = slice(h * HD, (h + 1) * HD)
        query, grad = q_ref[:, part], gm_ref[:, part]
        delta = grad.astype(F32) * mixed_ref[:, part].astype(F32)
        delta = jnp.sum(delta.T, axis=0, keepdims=True)
        for c in range(chunks):
            span = slice(c * rows, (c + 1) * rows)
            p = p_ref[h, span]
            dp = mm_nt(kv_ref[span, HD:], grad)
            ds = (p.astype(F32) * (dp - delta)).astype(BF)
            ds_ref[span] = ds
            dk_ref[span] += mm(ds, query)
            dv_ref[span] += mm(p, grad)
        dq = mm(kt_ref[...], ds_ref[...]) * SCALE
        gq_ref[:, part] = rope_back(dq.T, cos_ref[...], sin_ref[...]).astype(BF)

    gq = gq_ref[...]
    gbq_ref[0] = mm(r1t_ref[rows_of(SLOT_Q)], gq).astype(BF)
    gr_ref[...] += mm_nt(gq, bq_ref[0])
    g1_ref[...] += mm_nt(gq, flat(wq_ref))

    @pl.when(step == pl.num_programs(0) - 1)
    def _():
        dkv_ref[:, :HD] = (dk_ref[...] * SCALE).astype(BF)
        dkv_ref[:, HD:] = dv_ref[...].astype(BF)


def final_kernel(
    x_ref, gain_ref, a_ref, wk_ref, wv_ref, n1_ref, r1_ref, bkv_ref, cos_ref, sin_ref,
    own_ref, back1_ref, back2_ref, back3_ref, back4_ref, g1_ref, gr_ref, gres_ref, widef_ref,
    grad_ref, wide_ref, kvg_ref,
):
    gkv = own_ref[...].astype(F32)
    for back_ref in (back1_ref, back2_ref, back3_ref, back4_ref):
        gkv = gkv + back_ref[...].astype(F32)
    gk = rope_back(gkv[:, :HD], cos_ref[...], sin_ref[...]).astype(BF)
    gv = gkv[:, HD:].astype(BF)
    gr = gr_ref[...] + mm_nt(gk, bkv_ref[0]) + mm_nt(gv, bkv_ref[1])
    wide = mm(gr.T.astype(BF), n1_ref[...]) + widef_ref[...]
    wide_ref[...] = wide.T.astype(BF)
    r1t = r1_ref[...].astype(F32).T.astype(BF)
    kvg_ref[0] = mm(r1t[rows_of(SLOT_K)], gk).astype(BF)
    kvg_ref[1] = mm(r1t[rows_of(SLOT_V)], gv).astype(BF)
    g1 = g1_ref[...] + mm_nt(gk, wk_ref[...]) + mm_nt(gv, wv_ref[...])
    g1 = g1 + mm_nt(gr.astype(BF), a_ref[...])
    x = x_ref[...].astype(F32)
    grad_ref[...] = gres_ref[...] + rms_back(x, gain_ref[...], g1)


def whole(array):
    rank = len(array.shape)
    return pl.BlockSpec(array.shape, lambda *_: (0,) * rank)


def out_whole(shape):
    rank = len(shape)
    return pl.BlockSpec(shape, lambda *_: (0,) * rank)


def call(kernel, name, steps, args, specs, outs, out_specs, scratch, flops, nbytes):
    return pl.pallas_call(
        kernel,
        name=name,
        grid=(steps,),
        in_specs=specs,
        out_specs=out_specs,
        out_shape=outs,
        scratch_shapes=scratch,
        compiler_params=pltpu.CompilerParams(
            dimension_semantics=("arbitrary",), vmem_limit_bytes=VMEM_LIMIT
        ),
        cost_estimate=pl.CostEstimate(flops=flops, bytes_accessed=nbytes, transcendentals=0),
    )(*args)


def on_device(
    tokens, cotangent, segments, adapter_ids, norm_gains, q_weight, kv_weight, out_weight,
    gate_up_weight, down_weight, wide_adapters, kv_adapter, q_adapter, out_adapter,
    gate_up_adapter, down_adapter,
):
    rows, width = tokens.shape
    dp_count, tensor_count = lax.axis_size("dp"), lax.axis_size("tensor")
    devices = dp_count * tensor_count
    group_rows = rows * tensor_count
    seq_length = 2 * group_rows
    shard_rows = q_weight.shape[0]
    q_cols, ff_cols = q_weight.shape[1], gate_up_weight.shape[2]
    pack_cols = 3 * ff_cols + 2 * q_cols
    seqs = adapter_ids.shape[0]
    adapters = wide_adapters.shape[2] // RANK
    q_block = 3 * ff_cols // q_cols
    dp = lax.axis_index("dp")
    tensor = lax.axis_index("tensor")
    adapter = lax.dynamic_index_in_dim(adapter_ids, dp // 2, keepdims=False)
    column = adapter * RANK

    def sds(shape, dtype):
        return jax.ShapeDtypeStruct(shape, dtype)

    pack = jnp.concatenate(
        [gate_up_weight[0], gate_up_weight[1], down_weight.T, q_weight, out_weight.T], axis=1
    )
    weights = lax.all_gather(pack, BOTH, axis=0, tiled=False)
    weights = weights.reshape(dp_count, tensor_count, shard_rows, pack_cols)

    wide = wide_adapters.reshape(7, shard_rows, adapters, RANK)
    wide = jnp.take(wide, adapter_ids, axis=2).transpose(2, 1, 0, 3)
    wide = wide.reshape(seqs, shard_rows, 7 * RANK)
    wide = jnp.pad(wide, ((0, 0), (0, 0), (0, LANES - 7 * RANK)))
    wide = jnp.repeat(wide, dp_count // seqs, axis=0)
    shared = jnp.broadcast_to(kv_weight[:, None], (2, dp_count, shard_rows, HD))
    wide = jnp.concatenate([wide, shared[0], shared[1]], axis=2)
    a_all = lax.all_to_all(wide, "dp", 0, 0, tiled=True).reshape(width, 3 * LANES)

    def take_rows(matrix):
        return lax.dynamic_slice_in_dim(matrix, column, RANK, matrix.ndim - 2)

    def take_cols(matrix):
        return lax.dynamic_slice_in_dim(matrix, column, RANK, matrix.ndim - 1)

    gu_rows = take_rows(gate_up_adapter)
    b_own = jnp.concatenate(
        [gu_rows[0], gu_rows[1], take_cols(down_adapter).T, take_rows(q_adapter), take_cols(out_adapter).T],
        axis=1,
    )
    b_all = lax.all_gather(b_own, "tensor", axis=0, tiled=False)

    def in_slot(block, slot):
        pads = [(0, 0)] * block.ndim
        pads[-2] = (slot * RANK, LANES - (slot + 1) * RANK)
        return jnp.pad(block, pads)

    f1, f2, f3 = ff_cols, 2 * ff_cols, 3 * ff_cols
    b_pad = jnp.concatenate(
        [
            in_slot(b_all[:, :, :f1], SLOT_G),
            in_slot(b_all[:, :, f1:f2], SLOT_U),
            in_slot(b_all[:, :, f2:f3], SLOT_D),
            in_slot(b_all[:, :, f3 : f3 + q_cols], SLOT_Q),
            in_slot(b_all[:, :, f3 + q_cols :], SLOT_O),
        ],
        axis=2,
    )
    kv_rows = take_rows(kv_adapter)
    b_kv = jnp.stack([in_slot(kv_rows[0], SLOT_K), in_slot(kv_rows[1], SLOT_V)])

    start = dp * group_rows + tensor * rows
    positions = (start + jnp.arange(rows)) % seq_length
    half = HD // 2
    frequency = 10000.0 ** (-(jnp.arange(half).astype(F32) / half))
    angles = positions.astype(F32)[:, None] * frequency[None, :]
    cos, sin = jnp.cos(angles), jnp.sin(angles)
    cos = jnp.concatenate([cos, cos], axis=1)
    sin = jnp.concatenate([-sin, sin], axis=1)

    padded = jnp.concatenate([jnp.full((WINDOW,), -1, jnp.int32), segments])
    kseg = lax.dynamic_slice_in_dim(padded, start, WINDOW + rows, 0)
    qseg = kseg[WINDOW:].reshape(1, rows)
    kseg = kseg.reshape(WINDOW + rows, 1)
    span = WINDOW + rows

    gain_one, gain_two = norm_gains[0:1], norm_gains[1:2]

    def weight_spec(cols, block):
        return pl.BlockSpec((dp_count, 1, shard_rows, cols), lambda t: (0, t, 0, block))

    def adapter_spec(cols, block):
        return pl.BlockSpec((1, LANES, cols), lambda t: (t, 0, block))

    def token_cols(cols):
        return pl.BlockSpec((rows, cols), lambda t: (0, t))

    def by_step(*shape):
        return pl.BlockSpec((1,) + shape, lambda t: (t,) + (0,) * len(shape))

    heads_cols = tensor_count * q_cols
    q_spec, qb_spec = weight_spec(q_cols, q_block), adapter_spec(q_cols, q_block)
    o_spec, ob_spec = weight_spec(q_cols, q_block + 1), adapter_spec(q_cols, q_block + 1)

    def lane_block(block):
        return pl.BlockSpec((width, LANES), lambda *_: (0, block))

    a_spec, wk_spec, wv_spec = lane_block(0), lane_block(1), lane_block(2)

    def wholes(*arrays):
        return [whole(v) for v in arrays]

    args = (tokens, gain_one, a_all, a_all, a_all, b_kv, cos, sin, weights, b_pad)
    normed_one, rank_one, kv_own, queries = call(
        pre_kernel, "qkv", tensor_count, args,
        wholes(tokens, gain_one) + [a_spec, wk_spec, wv_spec] + wholes(b_kv, cos, sin) + [q_spec, qb_spec],
        (sds((rows, width), BF), sds((rows, LANES), BF), sds((rows, 2 * HD), BF), sds((rows, heads_cols), BF)),
        (out_whole((rows, width)), out_whole((rows, LANES)), out_whole((rows, 2 * HD)), token_cols(q_cols)),
        [], 2 * rows * width * (heads_cols + 384), 2 * width * heads_cols,
    )

    parts = seq_length // rows
    reach = WINDOW // rows

    def moved(value, steps):
        pairs = [
            (s * parts + c, s * parts + c + steps)
            for s in range(devices // parts) for c in range(parts) if 0 <= c + steps < parts
        ]
        return lax.ppermute(value, BOTH, pairs)

    kv_window = jnp.concatenate([moved(kv_own, d) for d in range(reach, 0, -1)] + [kv_own])

    args = (kv_window, kseg, qseg, tokens, gain_two, a_all, queries, weights, b_pad)
    q_heads = q_cols // HD
    mixed, probs, residual, normed_two, rank_two, rank_out = call(
        attn_kernel, "attention", tensor_count, args,
        wholes(*args[:5]) + [a_spec, token_cols(q_cols), o_spec, ob_spec],
        (
            sds((rows, heads_cols), BF), sds((tensor_count * q_heads, span, rows), BF), sds((rows, width), F32),
            sds((rows, width), BF), sds((rows, LANES), BF), sds((rows, LANES), BF),
        ),
        (
            token_cols(q_cols), pl.BlockSpec((q_heads, span, rows), lambda t: (t, 0, 0)), out_whole((rows, width)),
            out_whole((rows, width)), out_whole((rows, LANES)), out_whole((rows, LANES)),
        ),
        [
            pltpu.VMEM((span, rows), F32), pltpu.VMEM((span, rows), F32),
            pltpu.VMEM((rows, width), F32), pltpu.VMEM((HD, span), BF), pltpu.VMEM((rows, LANES), F32),
        ],
        2 * rows * heads_cols * (2 * span + width), 2 * width * heads_cols,
    )

    args = (
        residual, normed_two, rank_two, cotangent, gain_two, mixed, rank_out, a_all,
        weights, weights, weights, b_pad, b_pad, b_pad,
    )
    block_output, grad_residual, grad_branch, wide_ffn, grad_ro, grad_bo, grad_bg, grad_bu, grad_bd = call(
        ffn_kernel, "feed_forward", tensor_count, args,
        wholes(*args[:7]) + [a_spec]
        + [weight_spec(ff_cols, j) for j in range(3)]
        + [adapter_spec(ff_cols, j) for j in range(3)],
        (
            sds((rows, width), BF), sds((rows, width), F32), sds((rows, width), BF), sds((LANES, width), F32),
            sds((rows, LANES), BF), sds((tensor_count, RANK, q_cols), BF),
        )
        + (sds((tensor_count, RANK, ff_cols), BF),) * 3,
        (
            out_whole((rows, width)), out_whole((rows, width)), out_whole((rows, width)), out_whole((LANES, width)),
            out_whole((rows, LANES)), out_whole((tensor_count, RANK, q_cols)),
        )
        + (by_step(RANK, ff_cols),) * 3,
        [
            pltpu.VMEM((rows, width), F32), pltpu.VMEM((rows, width), F32),
            pltpu.VMEM((rows, LANES), F32), pltpu.VMEM((rows, LANES), F32),
            pltpu.VMEM((LANES, rows), BF), pltpu.VMEM((rows, LANES), BF), pltpu.VMEM((LANES, rows), BF),
        ],
        12 * rows * width * tensor_count * ff_cols, 6 * width * tensor_count * ff_cols,
    )

    args = (
        kv_window, grad_branch, grad_ro, rank_one, cos, sin,
        queries, mixed, probs, weights, b_pad, weights, b_pad,
    )
    dkv, grad_one, grad_rank, grad_bq = call(
        attn_back_kernel, "attention_back", tensor_count, args,
        wholes(*args[:6])
        + [
            token_cols(q_cols), token_cols(q_cols), pl.BlockSpec((q_heads, span, rows), lambda t: (t, 0, 0)),
            o_spec, ob_spec, q_spec, qb_spec,
        ],
        (
            sds((span, 2 * HD), BF), sds((rows, width), F32), sds((rows, LANES), F32),
            sds((tensor_count, RANK, q_cols), BF),
        ),
        (
            out_whole((span, 2 * HD)), out_whole((rows, width)), out_whole((rows, LANES)), by_step(RANK, q_cols),
        ),
        [
            pltpu.VMEM((span, rows), BF),
            pltpu.VMEM((span, HD), F32), pltpu.VMEM((span, HD), F32), pltpu.VMEM((HD, span), BF),
            pltpu.VMEM((LANES, rows), BF),
            pltpu.VMEM((rows, q_cols), BF), pltpu.VMEM((rows, q_cols), BF),
        ],
        2 * rows * heads_cols * (4 * span + 2 * width), 4 * width * heads_cols,
    )

    backs = [
        moved(dkv[(reach - d) * rows : (reach - d + 1) * rows], -d) for d in range(1, reach + 1)
    ]
    args = (
        tokens, gain_one, a_all, a_all, a_all, normed_one, rank_one, b_kv, cos, sin,
        dkv, *backs, grad_one, grad_rank, grad_residual, wide_ffn,
    )
    input_grad, wide_term, kv_term = call(
        final_kernel, "input_gradient", 1, args,
        wholes(*args[:2]) + [a_spec, wk_spec, wv_spec] + wholes(*args[5:10])
        + [pl.BlockSpec((rows, 2 * HD), lambda *_: (reach, 0))] + wholes(*args[11:]),
        (sds((rows, width), F32), sds((width, LANES), BF), sds((2, RANK, HD), BF)),
        (out_whole((rows, width)), out_whole((width, LANES)), out_whole((2, RANK, HD))),
        [], 2 * rows * width * 640, 8 * rows * width,
    )

    own_rows = width // devices
    kv_rows_out = jnp.tile(kv_term.transpose(1, 0, 2), (devices // RANK, 1, 1))
    payload = jnp.concatenate(
        [wide_term.reshape(devices, own_rows, LANES), kv_rows_out, jnp.zeros((devices, 2, LANES), BF)], axis=1
    )
    received = lax.all_to_all(payload, BOTH, 0, 0, tiled=True)
    sent_rows = own_rows + 4
    source_adapter = jnp.repeat(adapter_ids, devices // seqs)
    pick = (jnp.arange(adapters)[:, None] == source_adapter[None, :]).astype(BF)
    summed = mm(pick, received.reshape(devices, sent_rows * LANES)).reshape(adapters, sent_rows, LANES)
    wide_grad = summed[:, :own_rows, : 7 * RANK].reshape(adapters, own_rows, 7, RANK)
    wide_grad = wide_grad.transpose(2, 1, 0, 3).reshape(7, own_rows, adapters * RANK)
    own_row = dp * tensor_count + tensor
    kv_adapter_grad = lax.dynamic_index_in_dim(
        summed[:, own_rows : own_rows + 2], own_row // RANK, 0, keepdims=False
    ).reshape(2, 1, HD)

    early = jnp.concatenate([grad_bg, grad_bu, grad_bd, grad_bo], axis=2)
    early = lax.psum_scatter(early, "tensor", scatter_dimension=0, tiled=True).reshape(RANK, -1)
    early = lax.all_gather(early, "dp", axis=0, tiled=False)
    pick_dp = (jnp.arange(adapters)[:, None] == jnp.repeat(adapter_ids, dp_count // seqs)[None, :]).astype(BF)
    early = mm(pick_dp, early.reshape(dp_count, -1)).reshape(adapters * RANK, f3 + q_cols)

    late = jnp.broadcast_to(grad_bq[None], (dp_count, tensor_count, RANK, q_cols))
    late = lax.all_to_all(late.reshape(devices, RANK, q_cols), BOTH, 0, 0, tiled=True)
    q_adapter_grad = mm(pick, late.reshape(devices, RANK * q_cols)).reshape(adapters * RANK, q_cols)
    gate_up_adapter_grad = jnp.stack([early[:, :f1], early[:, f1:f2]])
    down_adapter_grad = early[:, f2:f3].T
    out_adapter_grad = early[:, f3:].T
    return (
        block_output, input_grad, wide_grad, kv_adapter_grad,
        q_adapter_grad, out_adapter_grad, gate_up_adapter_grad, down_adapter_grad,
    )


def solution(mesh):
    return jax.shard_map(
        on_device,
        mesh=mesh,
        in_specs=(
            P(BOTH, None), P(BOTH, None), P(), P(), P(), P("dp", "tensor"), P(None, "dp", None),
            P("tensor", "dp"), P(None, "dp", "tensor"), P("tensor", "dp"), P(None, "dp", None), P(),
            P(None, "tensor"), P("tensor", None), P(None, None, "tensor"), P("tensor", None),
        ),
        out_specs=(
            P(BOTH, None), P(BOTH, None), P(None, BOTH, None), P(None, BOTH, None),
            P(None, "tensor"), P("tensor", None), P(None, None, "tensor"), P("tensor", None),
        ),
        check_vma=False,
    )
```

```python
import jax
import jax.numpy as jnp
from jax import lax
from jax.experimental import pallas as pl
from jax.experimental.pallas import tpu as pltpu
from jax.sharding import PartitionSpec as P

HD = 128
WINDOW = 1024
RANK = 16
LANES = 128
EPS = 1e-06
MASKED = -1e30
SCALE = HD ** (-0.5)
GELU_C = 0.7978845608028654
GELU_A = 0.044715
VMEM_LIMIT = 58 * 1024 * 1024
BF = jnp.bfloat16
F32 = jnp.float32
BOTH = ("dp", "tensor")

SLOT_Q, SLOT_K, SLOT_V, SLOT_G, SLOT_U, SLOT_O, SLOT_D = range(7)


def rows_of(slot):
    return slice(slot * RANK, (slot + 1) * RANK)


def mm(a, b):
    return lax.dot_general(a, b, (((1,), (0,)), ((), ())), preferred_element_type=F32)


def mm_nt(a, b):
    return lax.dot_general(a, b, (((1,), (1,)), ((), ())), preferred_element_type=F32)


def rope(v, cos, sin):
    return v * cos + pltpu.roll(v, HD // 2, 1) * sin


def rope_back(g, cos, sin):
    return g * cos - pltpu.roll(g, HD // 2, 1) * sin


def flat(ref):
    block = ref[...]
    return block.reshape(block.shape[0] * block.shape[2], block.shape[3])


def rms(v, gain):
    return v * lax.rsqrt(jnp.mean(v * v, axis=-1, keepdims=True) + EPS) * gain


def rms_back(v, gain, grad):
    inv = lax.rsqrt(jnp.mean(v * v, axis=-1, keepdims=True) + EPS)
    scaled = grad * gain
    dot = jnp.mean(v * scaled, axis=-1, keepdims=True)
    return inv * scaled - v * (inv * inv * inv * dot)


def pre_kernel(place_ref, x_ref, gain_ref, a_ref, wk_ref, wv_ref, bkv_ref, cos_ref, sin_ref, bq_ref, *rest):
    pieces, (n1_ref, r1_ref, kv_ref, q_ref, wq_ref) = rest[:-5], rest[-5:]
    y_count = len(pieces) // 2
    x_count, tensor_count, shard_rows, _ = pieces[0].shape
    step = pl.program_id(0)

    @pl.when(step == 0)
    def _():
        my_y, my_x, my_core, my_z = (place_ref[axis] for axis in range(4))
        for number, piece in enumerate(pieces):
            y = lax.rem(my_y + number % y_count, y_count)
            core = my_core if number < y_count else 1 - my_core
            for away_x in range(x_count):
                x = lax.rem(my_x + away_x, x_count)
                row = pl.multiple_of(((y * x_count + x) * 2 + core) * shard_rows, 16)
                for away_z in range(tensor_count):
                    z = lax.rem(my_z + away_z, tensor_count)
                    wq_ref[z, pl.ds(row, shard_rows)] = piece[away_x, away_z]
        n1 = rms(x_ref[...].astype(F32), gain_ref[...]).astype(BF)
        n1_ref[...] = n1
        r1 = mm(n1, a_ref[...]).astype(BF)
        r1_ref[...] = r1
        key = mm(n1, wk_ref[...]) + mm(r1, bkv_ref[0])
        kv_ref[:, :HD] = rope(key, cos_ref[...], sin_ref[...]).astype(BF)
        kv_ref[:, HD:] = (mm(n1, wv_ref[...]) + mm(r1, bkv_ref[1])).astype(BF)

    lin = mm(n1_ref[...], wq_ref[step]) + mm(r1_ref[...], bq_ref[0])
    for h in range(lin.shape[1] // HD):
        part = slice(h * HD, (h + 1) * HD)
        q_ref[:, part] = rope(lin[:, part], cos_ref[...], sin_ref[...]).astype(BF)


def fill_bias(bias_ref, kseg_ref, qseg_ref):
    shape = bias_ref.shape
    key = lax.broadcasted_iota(jnp.int32, shape, 0)
    query = lax.broadcasted_iota(jnp.int32, shape, 1)
    allowed = (key >= query) & (key <= query + WINDOW) & (kseg_ref[...] == qseg_ref[...])
    bias_ref[...] = jnp.where(allowed, 0.0, MASKED)


def attn_kernel(kv_ref, kseg_ref, qseg_ref, q_ref, mixed_ref, p_ref, bias_ref, s_ref, vt_ref):
    step = pl.program_id(0)
    rows = q_ref.shape[0]
    chunks = kv_ref.shape[0] // rows

    @pl.when(step == 0)
    def _():
        fill_bias(bias_ref, kseg_ref, qseg_ref)
        vt_ref[...] = kv_ref[:, HD:].astype(F32).T.astype(BF)

    for h in range(q_ref.shape[1] // HD):
        part = slice(h * HD, (h + 1) * HD)
        query = q_ref[:, part]
        top = jnp.full((1, rows), MASKED, F32)
        for c in range(chunks):
            span = slice(c * rows, (c + 1) * rows)
            s = mm_nt(kv_ref[span, :HD], query) * SCALE + bias_ref[span]
            s_ref[span] = s
            top = jnp.maximum(top, jnp.max(s, axis=0, keepdims=True))
        total = jnp.zeros((1, rows), F32)
        for c in range(chunks):
            span = slice(c * rows, (c + 1) * rows)
            p = jnp.exp(s_ref[span] - top)
            total = total + jnp.sum(p, axis=0, keepdims=True)
            s_ref[span] = p
        inv = 1.0 / total
        for c in range(chunks):
            span = slice(c * rows, (c + 1) * rows)
            p_ref[h, span] = (s_ref[span] * inv).astype(BF)
        mixed_ref[:, part] = mm(vt_ref[...], p_ref[h]).T.astype(BF)


def out_kernel(
    x_ref, gain_ref, a_ref, mixed_ref, wo_ref, bo_ref, res_ref, n2_ref, r2_ref, ro_ref, acc_ref, rank_ref,
):
    step = pl.program_id(0)

    @pl.when(step == 0)
    def _():
        acc_ref[...] = jnp.zeros_like(acc_ref)
        rank_ref[...] = jnp.zeros_like(rank_ref)

    mixed = mixed_ref[...]
    acc_ref[...] += mm_nt(mixed, flat(wo_ref))
    rank_ref[...] += mm_nt(mixed, bo_ref[0])

    @pl.when(step == pl.num_programs(0) - 1)
    def _():
        ro = rank_ref[...].astype(BF)
        ro_ref[...] = ro
        res = x_ref[...].astype(F32) + (acc_ref[...] + mm_nt(ro, a_ref[...]))
        res_ref[...] = res
        n2 = rms(res, gain_ref[...]).astype(BF)
        n2_ref[...] = n2
        r2_ref[...] = mm(n2, a_ref[...]).astype(BF)


def ffn_kernel(
    res_ref, n2_ref, r2_ref, cot_ref, gain_ref, mixed_ref, ro_ref, a_ref,
    g_ref, u_ref, d_ref, bg_ref, bu_ref, bd_ref,
    out_ref, gres_ref, gb_ref, wide_ref, gro_ref, gbo_ref, gbg_ref, gbu_ref, gbd_ref,
    ffn_ref, g2_ref, rd_ref, gr_ref, r2t_ref, grd_ref, grdt_ref,
):
    step = pl.program_id(0)

    @pl.when(step == 0)
    def _():
        ffn_ref[...] = jnp.zeros_like(ffn_ref)
        g2_ref[...] = jnp.zeros_like(g2_ref)
        rd_ref[...] = jnp.zeros_like(rd_ref)
        gr_ref[...] = jnp.zeros_like(gr_ref)
        r2t_ref[...] = r2_ref[...].astype(F32).T.astype(BF)
        grd = mm(cot_ref[...], a_ref[...]).astype(BF)
        grd_ref[...] = grd
        grdt_ref[...] = grd.astype(F32).T.astype(BF)

    n2, r2, cot = n2_ref[...], r2_ref[...], cot_ref[...]
    w_g, w_u, w_d = flat(g_ref), flat(u_ref), flat(d_ref)
    gate = mm(n2, w_g) + mm(r2, bg_ref[0])
    up = mm(n2, w_u) + mm(r2, bu_ref[0])
    grad_hidden = (mm(cot, w_d) + mm(grd_ref[...], bd_ref[0])).astype(BF).astype(F32)
    square = gate * gate
    th = jnp.tanh(GELU_C * (gate + GELU_A * square * gate))
    half = 0.5 * (1.0 + th)
    act = gate * half
    slope = half + 0.5 * gate * (1.0 - th * th) * (GELU_C * (1.0 + 3.0 * GELU_A * square))
    hidden = (act * up).astype(BF)
    grad_gate = (grad_hidden * up * slope).astype(BF)
    grad_up = (grad_hidden * act).astype(BF)
    ffn_ref[...] += mm_nt(hidden, w_d)
    rd_ref[...] += mm_nt(hidden, bd_ref[0])
    g2_ref[...] += mm_nt(grad_gate, w_g) + mm_nt(grad_up, w_u)
    gr_ref[...] += mm_nt(grad_gate, bg_ref[0]) + mm_nt(grad_up, bu_ref[0])
    gbg_ref[0] = mm(r2t_ref[rows_of(SLOT_G)], grad_gate).astype(BF)
    gbu_ref[0] = mm(r2t_ref[rows_of(SLOT_U)], grad_up).astype(BF)
    gbd_ref[0] = mm(grdt_ref[rows_of(SLOT_D)], hidden).astype(BF)

    @pl.when(step == pl.num_programs(0) - 1)
    def _():
        rd = rd_ref[...].astype(BF)
        gr = gr_ref[...].astype(BF)
        res = res_ref[...]
        out_ref[...] = (res + (ffn_ref[...] + mm_nt(rd, a_ref[...]))).astype(BF)
        grad_two = g2_ref[...] + mm_nt(gr, a_ref[...])
        grad_res = cot_ref[...].astype(F32) + rms_back(res, gain_ref[...], grad_two)
        gres_ref[...] = grad_res
        grad_branch = grad_res.astype(BF)
        gb_ref[...] = grad_branch
        gro = mm(grad_branch, a_ref[...])
        gro_ref[...] = gro.astype(BF)
        grot = gro.T[rows_of(SLOT_O)].astype(BF)
        cols = gbo_ref.shape[2]
        for t in range(gbo_ref.shape[0]):
            gbo_ref[t] = mm(grot, mixed_ref[:, t * cols : (t + 1) * cols]).astype(BF)
        wide = mm(gr_ref[...].T.astype(BF), n2) + mm(rd_ref[...].T.astype(BF), cot)
        wide_ref[...] = wide + mm(ro_ref[...].astype(F32).T.astype(BF), grad_branch)


def attn_back_kernel(
    kv_ref, gb_ref, gro_ref, r1_ref, cos_ref, sin_ref,
    q_ref, mixed_ref, p_ref, wo_ref, bo_ref, wq_ref, bq_ref,
    dkv_ref, g1_ref, gr_ref, gbq_ref,
    ds_ref, dk_ref, dv_ref, kt_ref, r1t_ref, gq_ref, gm_ref,
):
    step = pl.program_id(0)
    rows = q_ref.shape[0]
    chunks = kv_ref.shape[0] // rows

    @pl.when(step == 0)
    def _():
        kt_ref[...] = kv_ref[:, :HD].astype(F32).T.astype(BF)
        r1t_ref[...] = r1_ref[...].astype(F32).T.astype(BF)
        dk_ref[...] = jnp.zeros_like(dk_ref)
        dv_ref[...] = jnp.zeros_like(dv_ref)
        g1_ref[...] = jnp.zeros_like(g1_ref)
        gr_ref[...] = jnp.zeros_like(gr_ref)

    gm_ref[...] = (mm(gb_ref[...], flat(wo_ref)) + mm(gro_ref[...], bo_ref[0])).astype(BF)
    for h in range(q_ref.shape[1] // HD):
        part = slice(h * HD, (h + 1) * HD)
        query, grad = q_ref[:, part], gm_ref[:, part]
        delta = grad.astype(F32) * mixed_ref[:, part].astype(F32)
        delta = jnp.sum(delta.T, axis=0, keepdims=True)
        for c in range(chunks):
            span = slice(c * rows, (c + 1) * rows)
            p = p_ref[h, span]
            dp = mm_nt(kv_ref[span, HD:], grad)
            ds = (p.astype(F32) * (dp - delta)).astype(BF)
            ds_ref[span] = ds
            dk_ref[span] += mm(ds, query)
            dv_ref[span] += mm(p, grad)
        dq = mm(kt_ref[...], ds_ref[...]) * SCALE
        gq_ref[:, part] = rope_back(dq.T, cos_ref[...], sin_ref[...]).astype(BF)

    gq = gq_ref[...]
    gbq_ref[0] = mm(r1t_ref[rows_of(SLOT_Q)], gq).astype(BF)
    gr_ref[...] += mm_nt(gq, bq_ref[0])
    g1_ref[...] += mm_nt(gq, wq_ref[0])

    @pl.when(step == pl.num_programs(0) - 1)
    def _():
        dkv_ref[:, :HD] = (dk_ref[...] * SCALE).astype(BF)
        dkv_ref[:, HD:] = dv_ref[...].astype(BF)


def final_kernel(
    x_ref, gain_ref, a_ref, wk_ref, wv_ref, n1_ref, r1_ref, bkv_ref, cos_ref, sin_ref,
    own_ref, back1_ref, back2_ref, back3_ref, back4_ref, g1_ref, gr_ref, gres_ref, widef_ref,
    grad_ref, wide_ref, kvg_ref,
):
    gkv = own_ref[...].astype(F32)
    for back_ref in (back1_ref, back2_ref, back3_ref, back4_ref):
        gkv = gkv + back_ref[...].astype(F32)
    gk = rope_back(gkv[:, :HD], cos_ref[...], sin_ref[...]).astype(BF)
    gv = gkv[:, HD:].astype(BF)
    gr = gr_ref[...] + mm_nt(gk, bkv_ref[0]) + mm_nt(gv, bkv_ref[1])
    wide = mm(gr.T.astype(BF), n1_ref[...]) + widef_ref[...]
    wide_ref[...] = wide.T.astype(BF)
    r1t = r1_ref[...].astype(F32).T.astype(BF)
    kvg_ref[0] = mm(r1t[rows_of(SLOT_K)], gk).astype(BF)
    kvg_ref[1] = mm(r1t[rows_of(SLOT_V)], gv).astype(BF)
    g1 = g1_ref[...] + mm_nt(gk, wk_ref[...]) + mm_nt(gv, wv_ref[...])
    g1 = g1 + mm_nt(gr.astype(BF), a_ref[...])
    x = x_ref[...].astype(F32)
    grad_ref[...] = gres_ref[...] + rms_back(x, gain_ref[...], g1)


def sum_hidden_kernel(ids_ref, terms_ref, gu_ref, down_ref, out_ref, acc_ref):
    acc_ref[...] = jnp.zeros_like(acc_ref)
    for s in range(terms_ref.shape[0] // 2):
        acc_ref[ids_ref[s]] += terms_ref[2 * s].astype(F32) + terms_ref[2 * s + 1].astype(F32)
    adapters, rank, cols = acc_ref.shape
    ff = gu_ref.shape[2]

    def taken(first, last):
        return acc_ref[:, :, first:last].reshape(adapters * rank, last - first)

    gu_ref[0] = taken(0, ff)
    gu_ref[1] = taken(ff, 2 * ff)
    down_ref[...] = taken(2 * ff, 3 * ff).T
    out_ref[...] = taken(3 * ff, cols).T


def sum_wide_kernel(ids_ref, own_ref, terms_ref, wide_ref, kv_ref, q_ref, acc_ref):
    acc_ref[...] = jnp.zeros_like(acc_ref)
    seqs, parts = terms_ref.shape[:2]
    for s in range(seqs):
        term = terms_ref[s, 0].astype(F32)
        for part in range(1, parts):
            term = term + terms_ref[s, part].astype(F32)
        acc_ref[ids_ref[s]] += term
    adapters, rank, _ = acc_ref.shape
    q_ref[...] = acc_ref[:, :, LANES:].reshape(q_ref.shape)
    lane = lax.broadcasted_iota(jnp.int32, (rank, LANES), 1) // RANK
    slots, own_rows = wide_ref.shape[:2]
    for j in range(slots):
        total = jnp.zeros((rank, LANES), F32)
        for a in range(adapters):
            turned = pltpu.roll(acc_ref[a, :, :LANES], ((a - j) * RANK) % LANES, 1)
            total = jnp.where(lane == a, turned, total)
        wide_ref[j] = total[:own_rows]
    mine = acc_ref[own_ref[0], :, :LANES]
    for j in range(2):
        kv_ref[j] = mine[own_rows + j : own_rows + j + 1]


def scalars():
    return pl.BlockSpec(memory_space=pltpu.SMEM)


def whole(array):
    rank = len(array.shape)
    return pl.BlockSpec(array.shape, lambda *_: (0,) * rank)


def out_whole(shape):
    rank = len(shape)
    return pl.BlockSpec(shape, lambda *_: (0,) * rank)


def call(kernel, name, steps, args, specs, outs, out_specs, scratch, flops, nbytes):
    return pl.pallas_call(
        kernel,
        name=name,
        grid=(steps,),
        in_specs=specs,
        out_specs=out_specs,
        out_shape=outs,
        scratch_shapes=scratch,
        compiler_params=pltpu.CompilerParams(
            dimension_semantics=("arbitrary",), vmem_limit_bytes=VMEM_LIMIT
        ),
        cost_estimate=pl.CostEstimate(flops=flops, bytes_accessed=nbytes, transcendentals=0),
    )(*args)


def on_device(
    tokens, cotangent, segments, adapter_ids, norm_gains, q_weight, kv_weight, out_weight,
    gate_up_weight, down_weight, wide_adapters, kv_adapter, q_adapter, out_adapter,
    gate_up_adapter, down_adapter,
):
    rows, width = tokens.shape
    dp_count, tensor_count = lax.axis_size("dp"), lax.axis_size("tensor")
    devices = dp_count * tensor_count
    group_rows = rows * tensor_count
    seq_length = 2 * group_rows
    shard_rows = q_weight.shape[0]
    q_cols, ff_cols = q_weight.shape[1], gate_up_weight.shape[2]
    pack_cols = 3 * ff_cols + q_cols
    seqs = adapter_ids.shape[0]
    adapters = wide_adapters.shape[2] // RANK
    o_block = 3 * ff_cols // q_cols
    dp = lax.axis_index("dp")
    tensor = lax.axis_index("tensor")
    adapter = lax.dynamic_index_in_dim(adapter_ids, dp // 2, keepdims=False)
    column = adapter * RANK

    def sds(shape, dtype):
        return jax.ShapeDtypeStruct(shape, dtype)

    pack = jnp.concatenate(
        [gate_up_weight[0], gate_up_weight[1], down_weight.T, out_weight.T], axis=1
    )
    weights = lax.all_gather(pack, BOTH, axis=0, tiled=False)
    weights = weights.reshape(dp_count, tensor_count, shard_rows, pack_cols)

    chips = dp_count // 2
    x_count = 4 if chips % 4 == 0 else chips
    y_count = chips // x_count
    my_core, my_x, my_y = dp % 2, (dp // 2) % x_count, dp // (2 * x_count)

    def from_z(value, away):
        return lax.ppermute(value, "tensor", [((z + away) % tensor_count, z) for z in range(tensor_count)])

    def from_dp(value, away_y, away_x, away_core):
        pairs = []
        for y in range(y_count):
            for x in range(x_count):
                for c in range(2):
                    source = (((y + away_y) % y_count) * x_count + (x + away_x) % x_count) * 2 + (c ^ away_core)
                    pairs.append((source, (y * x_count + x) * 2 + c))
        return lax.ppermute(value, "dp", pairs)

    q_z = jnp.stack([q_weight] + [from_z(q_weight, d) for d in range(1, tensor_count)])
    q_x = jnp.stack([q_z] + [from_dp(q_z, 0, d, 0) for d in range(1, x_count)])
    q_y = [q_x] + [from_dp(q_x, d, 0, 0) for d in range(1, y_count)]
    q_pieces = q_y + [from_dp(piece, 0, 0, 1) for piece in q_y]
    place = jnp.stack([my_y, my_x, my_core, tensor]).astype(jnp.int32)

    wide = wide_adapters.reshape(7, shard_rows, adapters, RANK)
    wide = jnp.take(wide, adapter_ids, axis=2).transpose(2, 1, 0, 3)
    wide = wide.reshape(seqs, shard_rows, 7 * RANK)
    wide = jnp.pad(wide, ((0, 0), (0, 0), (0, LANES - 7 * RANK)))
    wide = jnp.repeat(wide, dp_count // seqs, axis=0)
    shared = jnp.broadcast_to(kv_weight[:, None], (2, dp_count, shard_rows, HD))
    wide = jnp.concatenate([wide, shared[0], shared[1]], axis=2)
    a_all = lax.all_to_all(wide, "dp", 0, 0, tiled=True).reshape(width, 3 * LANES)

    def take_rows(matrix):
        return lax.dynamic_slice_in_dim(matrix, column, RANK, matrix.ndim - 2)

    def take_cols(matrix):
        return lax.dynamic_slice_in_dim(matrix, column, RANK, matrix.ndim - 1)

    gu_rows = take_rows(gate_up_adapter)
    b_own = jnp.concatenate(
        [gu_rows[0], gu_rows[1], take_cols(down_adapter).T, take_cols(out_adapter).T, take_rows(q_adapter)],
        axis=1,
    )
    b_all = lax.all_gather(b_own, "tensor", axis=0, tiled=False)

    def in_slot(block, slot):
        pads = [(0, 0)] * block.ndim
        pads[-2] = (slot * RANK, LANES - (slot + 1) * RANK)
        return jnp.pad(block, pads)

    f1, f2, f3 = ff_cols, 2 * ff_cols, 3 * ff_cols
    b_pad = jnp.concatenate(
        [
            in_slot(b_all[:, :, :f1], SLOT_G),
            in_slot(b_all[:, :, f1:f2], SLOT_U),
            in_slot(b_all[:, :, f2:f3], SLOT_D),
            in_slot(b_all[:, :, f3 : f3 + q_cols], SLOT_O),
            in_slot(b_all[:, :, f3 + q_cols :], SLOT_Q),
        ],
        axis=2,
    )
    kv_rows = take_rows(kv_adapter)
    b_kv = jnp.stack([in_slot(kv_rows[0], SLOT_K), in_slot(kv_rows[1], SLOT_V)])

    start = dp * group_rows + tensor * rows
    positions = (start + jnp.arange(rows)) % seq_length
    half = HD // 2
    frequency = 10000.0 ** (-(jnp.arange(half).astype(F32) / half))
    angles = positions.astype(F32)[:, None] * frequency[None, :]
    cos, sin = jnp.cos(angles), jnp.sin(angles)
    cos = jnp.concatenate([cos, cos], axis=1)
    sin = jnp.concatenate([-sin, sin], axis=1)

    padded = jnp.concatenate([jnp.full((WINDOW,), -1, jnp.int32), segments])
    kseg = lax.dynamic_slice_in_dim(padded, start, WINDOW + rows, 0)
    qseg = kseg[WINDOW:].reshape(1, rows)
    kseg = kseg.reshape(WINDOW + rows, 1)
    span = WINDOW + rows

    gain_one, gain_two = norm_gains[0:1], norm_gains[1:2]

    def weight_spec(cols, block):
        return pl.BlockSpec((dp_count, 1, shard_rows, cols), lambda t: (0, t, 0, block))

    def adapter_spec(cols, block):
        return pl.BlockSpec((1, LANES, cols), lambda t: (t, 0, block))

    def token_cols(cols):
        return pl.BlockSpec((rows, cols), lambda t: (0, t))

    def by_step(*shape):
        return pl.BlockSpec((1,) + shape, lambda t: (t,) + (0,) * len(shape))

    heads_cols = tensor_count * q_cols
    o_spec, ob_spec = weight_spec(q_cols, o_block), adapter_spec(q_cols, o_block)
    q_spec, qb_spec = by_step(width, q_cols), adapter_spec(q_cols, o_block + 1)

    def lane_block(block):
        return pl.BlockSpec((width, LANES), lambda *_: (0, block))

    a_spec, wk_spec, wv_spec = lane_block(0), lane_block(1), lane_block(2)

    def wholes(*arrays):
        return [whole(v) for v in arrays]

    args = (place, tokens, gain_one, a_all, a_all, a_all, b_kv, cos, sin, b_pad, *q_pieces)
    normed_one, rank_one, kv_own, queries, w_query = call(
        pre_kernel, "qkv", tensor_count, args,
        [scalars()] + wholes(tokens, gain_one) + [a_spec, wk_spec, wv_spec] + wholes(b_kv, cos, sin) + [qb_spec]
        + wholes(*q_pieces),
        (
            sds((rows, width), BF), sds((rows, LANES), BF), sds((rows, 2 * HD), BF), sds((rows, heads_cols), BF),
            sds((tensor_count, width, q_cols), BF),
        ),
        (
            out_whole((rows, width)), out_whole((rows, LANES)), out_whole((rows, 2 * HD)), token_cols(q_cols),
            out_whole((tensor_count, width, q_cols)),
        ),
        [], 2 * rows * width * (heads_cols + 384), 2 * width * heads_cols,
    )

    parts = seq_length // rows
    reach = WINDOW // rows

    def moved(value, steps):
        pairs = [
            (s * parts + c, s * parts + c + steps)
            for s in range(devices // parts) for c in range(parts) if 0 <= c + steps < parts
        ]
        return lax.ppermute(value, BOTH, pairs)

    kv_window = jnp.concatenate([moved(kv_own, d) for d in range(reach, 0, -1)] + [kv_own])

    args = (kv_window, kseg, qseg, queries)
    q_heads = q_cols // HD
    p_spec = pl.BlockSpec((q_heads, span, rows), lambda t: (t, 0, 0))
    mixed, probs = call(
        attn_kernel, "attention", tensor_count, args,
        wholes(*args[:3]) + [token_cols(q_cols)],
        (sds((rows, heads_cols), BF), sds((tensor_count * q_heads, span, rows), BF)),
        (token_cols(q_cols), p_spec),
        [pltpu.VMEM((span, rows), F32), pltpu.VMEM((span, rows), F32), pltpu.VMEM((HD, span), BF)],
        4 * rows * heads_cols * span, 2 * rows * heads_cols * span // HD,
    )

    args = (tokens, gain_two, a_all, mixed, weights, b_pad)
    residual, normed_two, rank_two, rank_out = call(
        out_kernel, "out_projection", tensor_count, args,
        wholes(*args[:2]) + [a_spec, token_cols(q_cols), o_spec, ob_spec],
        (sds((rows, width), F32), sds((rows, width), BF), sds((rows, LANES), BF), sds((rows, LANES), BF)),
        (out_whole((rows, width)), out_whole((rows, width)), out_whole((rows, LANES)), out_whole((rows, LANES))),
        [pltpu.VMEM((rows, width), F32), pltpu.VMEM((rows, LANES), F32)],
        2 * rows * heads_cols * width, 2 * width * heads_cols,
    )

    args = (
        residual, normed_two, rank_two, cotangent, gain_two, mixed, rank_out, a_all,
        weights, weights, weights, b_pad, b_pad, b_pad,
    )
    block_output, grad_residual, grad_branch, wide_ffn, grad_ro, grad_bo, grad_bg, grad_bu, grad_bd = call(
        ffn_kernel, "feed_forward", tensor_count, args,
        wholes(*args[:7]) + [a_spec]
        + [weight_spec(ff_cols, j) for j in range(3)]
        + [adapter_spec(ff_cols, j) for j in range(3)],
        (
            sds((rows, width), BF), sds((rows, width), F32), sds((rows, width), BF), sds((LANES, width), F32),
            sds((rows, LANES), BF), sds((tensor_count, RANK, q_cols), BF),
        )
        + (sds((tensor_count, RANK, ff_cols), BF),) * 3,
        (
            out_whole((rows, width)), out_whole((rows, width)), out_whole((rows, width)), out_whole((LANES, width)),
            out_whole((rows, LANES)), out_whole((tensor_count, RANK, q_cols)),
        )
        + (by_step(RANK, ff_cols),) * 3,
        [
            pltpu.VMEM((rows, width), F32), pltpu.VMEM((rows, width), F32),
            pltpu.VMEM((rows, LANES), F32), pltpu.VMEM((rows, LANES), F32),
            pltpu.VMEM((LANES, rows), BF), pltpu.VMEM((rows, LANES), BF), pltpu.VMEM((LANES, rows), BF),
        ],
        12 * rows * width * tensor_count * ff_cols, 6 * width * tensor_count * ff_cols,
    )

    args = (
        kv_window, grad_branch, grad_ro, rank_one, cos, sin,
        queries, mixed, probs, weights, b_pad, w_query, b_pad,
    )
    dkv, grad_one, grad_rank, grad_bq = call(
        attn_back_kernel, "attention_back", tensor_count, args,
        wholes(*args[:6])
        + [
            token_cols(q_cols), token_cols(q_cols), p_spec,
            o_spec, ob_spec, q_spec, qb_spec,
        ],
        (
            sds((span, 2 * HD), BF), sds((rows, width), F32), sds((rows, LANES), F32),
            sds((tensor_count, RANK, q_cols), BF),
        ),
        (
            out_whole((span, 2 * HD)), out_whole((rows, width)), out_whole((rows, LANES)), by_step(RANK, q_cols),
        ),
        [
            pltpu.VMEM((span, rows), BF),
            pltpu.VMEM((span, HD), F32), pltpu.VMEM((span, HD), F32), pltpu.VMEM((HD, span), BF),
            pltpu.VMEM((LANES, rows), BF),
            pltpu.VMEM((rows, q_cols), BF), pltpu.VMEM((rows, q_cols), BF),
        ],
        2 * rows * heads_cols * (4 * span + 2 * width), 4 * width * heads_cols,
    )

    backs = [
        moved(dkv[(reach - d) * rows : (reach - d + 1) * rows], -d) for d in range(1, reach + 1)
    ]
    args = (
        tokens, gain_one, a_all, a_all, a_all, normed_one, rank_one, b_kv, cos, sin,
        dkv, *backs, grad_one, grad_rank, grad_residual, wide_ffn,
    )
    input_grad, wide_term, kv_term = call(
        final_kernel, "input_gradient", 1, args,
        wholes(*args[:2]) + [a_spec, wk_spec, wv_spec] + wholes(*args[5:10])
        + [pl.BlockSpec((rows, 2 * HD), lambda *_: (reach, 0))] + wholes(*args[11:]),
        (sds((rows, width), F32), sds((width, LANES), BF), sds((2, RANK, HD), BF)),
        (out_whole((rows, width)), out_whole((width, LANES)), out_whole((2, RANK, HD))),
        [], 2 * rows * width * 640, 8 * rows * width,
    )

    early = jnp.concatenate([grad_bg, grad_bu, grad_bd, grad_bo], axis=2)
    early = lax.psum_scatter(early, "tensor", scatter_dimension=0, tiled=True).reshape(RANK, -1)
    early, grad_bq = lax.optimization_barrier((early, grad_bq))
    early = lax.all_gather(early, "dp", axis=0, tiled=False)
    gate_up_adapter_grad, down_adapter_grad, out_adapter_grad = pl.pallas_call(
        sum_hidden_kernel,
        name="sum_hidden",
        in_specs=[scalars()] + wholes(early),
        out_specs=(out_whole((2, LANES, ff_cols)), out_whole((ff_cols, LANES)), out_whole((q_cols, LANES))),
        out_shape=(sds((2, LANES, ff_cols), F32), sds((ff_cols, LANES), F32), sds((q_cols, LANES), F32)),
        scratch_shapes=[pltpu.VMEM((adapters, RANK, f3 + q_cols), F32)],
        compiler_params=pltpu.CompilerParams(vmem_limit_bytes=VMEM_LIMIT),
    )(adapter_ids, early)

    own_rows = width // devices
    kv_terms = jnp.tile(kv_term.transpose(1, 0, 2), (devices // RANK, 1, 1))
    owned = jnp.concatenate(
        [wide_term.reshape(devices, own_rows, LANES), kv_terms, jnp.zeros((devices, 2, LANES), BF)], axis=1
    )
    every = jnp.broadcast_to(grad_bq[None], (dp_count, tensor_count, RANK, q_cols)).reshape(devices, RANK, q_cols)
    terms = lax.all_to_all(jnp.concatenate([owned, every], axis=2), BOTH, 0, 0, tiled=True)
    terms = terms.reshape(seqs, devices // seqs, RANK, LANES + q_cols)
    own_adapter = ((dp * tensor_count + tensor) // RANK).astype(jnp.int32).reshape(1)
    wide_grad, kv_adapter_grad, q_adapter_grad = pl.pallas_call(
        sum_wide_kernel,
        name="sum_wide",
        in_specs=[scalars(), scalars()] + wholes(terms),
        out_specs=(out_whole((7, own_rows, LANES)), out_whole((2, 1, HD)), out_whole((LANES, q_cols))),
        out_shape=(sds((7, own_rows, LANES), F32), sds((2, 1, HD), F32), sds((LANES, q_cols), F32)),
        scratch_shapes=[pltpu.VMEM((adapters, RANK, LANES + q_cols), F32)],
        compiler_params=pltpu.CompilerParams(vmem_limit_bytes=VMEM_LIMIT),
    )(adapter_ids, own_adapter, terms)
    return (
        block_output, input_grad, wide_grad, kv_adapter_grad,
        q_adapter_grad, out_adapter_grad, gate_up_adapter_grad, down_adapter_grad,
    )


def solution(mesh):
    return jax.shard_map(
        on_device,
        mesh=mesh,
        in_specs=(
            P(BOTH, None), P(BOTH, None), P(), P(), P(), P("dp", "tensor"), P(None, "dp", None),
            P("tensor", "dp"), P(None, "dp", "tensor"), P("tensor", "dp"), P(None, "dp", None), P(),
            P(None, "tensor"), P("tensor", None), P(None, None, "tensor"), P("tensor", None),
        ),
        out_specs=(
            P(BOTH, None), P(BOTH, None), P(None, BOTH, None), P(None, BOTH, None),
            P(None, "tensor"), P("tensor", None), P(None, None, "tensor"), P("tensor", None),
        ),
        check_vma=False,
    )
```

```python
import math

import jax
import jax.numpy as jnp
from jax import lax
from jax.experimental import pallas as pl
from jax.experimental.pallas import tpu as pltpu
from jax.sharding import Mesh, PartitionSpec as P

HD = 128
WINDOW = 1024
RANK = 16
LANES = 128
EPS = 1e-06
MASKED = -1e30
SCALE = HD ** (-0.5)
GELU_C = 0.7978845608028654
GELU_A = 0.044715
VMEM_LIMIT = 58 * 1024 * 1024
BF = jnp.bfloat16
F32 = jnp.float32
DP = ("y", "x", "core")
SEQ = ("core", "tensor")
ALL = ("y", "x", "core", "tensor")

SLOT_Q, SLOT_K, SLOT_V, SLOT_G, SLOT_U, SLOT_O, SLOT_D = range(7)


def rows_of(slot):
    return slice(slot * RANK, (slot + 1) * RANK)


def mm(a, b):
    return lax.dot_general(a, b, (((1,), (0,)), ((), ())), preferred_element_type=F32)


def mm_nt(a, b):
    return lax.dot_general(a, b, (((1,), (1,)), ((), ())), preferred_element_type=F32)


def rope(v, cos, sin):
    return v * cos + pltpu.roll(v, HD // 2, 1) * sin


def rope_back(g, cos, sin):
    return g * cos - pltpu.roll(g, HD // 2, 1) * sin


def flat(ref):
    block = ref[...]
    return block.reshape(block.shape[0] * block.shape[2], block.shape[3])


def rms(v, gain):
    return v * lax.rsqrt(jnp.mean(v * v, axis=-1, keepdims=True) + EPS) * gain


def rms_back(v, gain, grad):
    inv = lax.rsqrt(jnp.mean(v * v, axis=-1, keepdims=True) + EPS)
    scaled = grad * gain
    dot = jnp.mean(v * scaled, axis=-1, keepdims=True)
    return inv * scaled - v * (inv * inv * inv * dot)


def place_weight(place_ref, own_ref, other_ref, whole_ref, x_first):
    shard_rows = own_ref.shape[3]
    my_y, my_x, my_core, my_z = (place_ref[axis] for axis in range(4))
    tensor_count = own_ref.shape[2]
    x_count, y_count = (own_ref.shape[0], own_ref.shape[1]) if x_first else (own_ref.shape[1], own_ref.shape[0])
    for away_y in range(y_count):
        y = lax.rem(my_y + away_y, y_count)
        for away_x in range(x_count):
            x = lax.rem(my_x + away_x, x_count)
            first, second = (away_x, away_y) if x_first else (away_y, away_x)
            for ref, core in ((own_ref, my_core), (other_ref, 1 - my_core)):
                row = pl.multiple_of(((y * x_count + x) * 2 + core) * shard_rows, 16)
                for away_z in range(tensor_count):
                    z = lax.rem(my_z + away_z, tensor_count)
                    whole_ref[z, pl.ds(row, shard_rows)] = ref[first, second, away_z]


def pre_kernel(
    place_ref, x_ref, gain_ref, a_ref, wk_ref, wv_ref, bkv_ref, cos_ref, sin_ref, bq_ref, own_ref, other_ref,
    n1_ref, r1_ref, kv_ref, q_ref, wq_ref,
):
    step = pl.program_id(0)

    @pl.when(step == 0)
    def _():
        place_weight(place_ref, own_ref, other_ref, wq_ref, False)
        n1 = rms(x_ref[...].astype(F32), gain_ref[...]).astype(BF)
        n1_ref[...] = n1
        r1 = mm(n1, a_ref[...]).astype(BF)
        r1_ref[...] = r1
        key = mm(n1, wk_ref[...]) + mm(r1, bkv_ref[0])
        kv_ref[:, :HD] = rope(key, cos_ref[...], sin_ref[...]).astype(BF)
        kv_ref[:, HD:] = (mm(n1, wv_ref[...]) + mm(r1, bkv_ref[1])).astype(BF)

    lin = mm(n1_ref[...], wq_ref[step]) + mm(r1_ref[...], bq_ref[0])
    for h in range(lin.shape[1] // HD):
        part = slice(h * HD, (h + 1) * HD)
        q_ref[:, part] = rope(lin[:, part], cos_ref[...], sin_ref[...]).astype(BF)


def fill_bias(bias_ref, kseg_ref, qseg_ref):
    shape = bias_ref.shape
    key = lax.broadcasted_iota(jnp.int32, shape, 0)
    query = lax.broadcasted_iota(jnp.int32, shape, 1)
    allowed = (key >= query) & (key <= query + WINDOW) & (kseg_ref[...] == qseg_ref[...])
    bias_ref[...] = jnp.where(allowed, 0.0, MASKED)


def attn_kernel(kv_ref, kseg_ref, qseg_ref, q_ref, mixed_ref, p_ref, bias_ref, s_ref, vt_ref):
    step = pl.program_id(0)
    rows = q_ref.shape[0]
    chunks = kv_ref.shape[0] // rows

    @pl.when(step == 0)
    def _():
        fill_bias(bias_ref, kseg_ref, qseg_ref)
        vt_ref[...] = kv_ref[:, HD:].astype(F32).T.astype(BF)

    for h in range(q_ref.shape[1] // HD):
        part = slice(h * HD, (h + 1) * HD)
        query = q_ref[:, part]
        top = jnp.full((1, rows), MASKED, F32)
        for c in range(chunks):
            span = slice(c * rows, (c + 1) * rows)
            s = mm_nt(kv_ref[span, :HD], query) * SCALE + bias_ref[span]
            s_ref[span] = s
            top = jnp.maximum(top, jnp.max(s, axis=0, keepdims=True))
        total = jnp.zeros((1, rows), F32)
        for c in range(chunks):
            span = slice(c * rows, (c + 1) * rows)
            p = jnp.exp(s_ref[span] - top)
            total = total + jnp.sum(p, axis=0, keepdims=True)
            s_ref[span] = p
        inv = 1.0 / total
        for c in range(chunks):
            span = slice(c * rows, (c + 1) * rows)
            p_ref[h, span] = (s_ref[span] * inv).astype(BF)
        mixed_ref[:, part] = mm(vt_ref[...], p_ref[h]).T.astype(BF)


def out_kernel(
    place_ref, x_ref, gain_ref, a_ref, mixed_ref, bo_ref, own_ref, other_ref,
    res_ref, n2_ref, r2_ref, ro_ref, wo_ref, acc_ref, rank_ref,
):
    step = pl.program_id(0)

    @pl.when(step == 0)
    def _():
        place_weight(place_ref, own_ref, other_ref, wo_ref, True)
        acc_ref[...] = jnp.zeros_like(acc_ref)
        rank_ref[...] = jnp.zeros_like(rank_ref)

    mixed = mixed_ref[...]
    acc_ref[...] += mm_nt(mixed, wo_ref[step])
    rank_ref[...] += mm_nt(mixed, bo_ref[0])

    @pl.when(step == pl.num_programs(0) - 1)
    def _():
        ro = rank_ref[...].astype(BF)
        ro_ref[...] = ro
        res = x_ref[...].astype(F32) + (acc_ref[...] + mm_nt(ro, a_ref[...]))
        res_ref[...] = res
        n2 = rms(res, gain_ref[...]).astype(BF)
        n2_ref[...] = n2
        r2_ref[...] = mm(n2, a_ref[...]).astype(BF)


def ffn_kernel(
    res_ref, n2_ref, r2_ref, cot_ref, gain_ref, mixed_ref, ro_ref, a_ref,
    g_ref, u_ref, d_ref, bg_ref, bu_ref, bd_ref,
    out_ref, gres_ref, gb_ref, wide_ref, gro_ref, gbo_ref, gbg_ref, gbu_ref, gbd_ref,
    ffn_ref, g2_ref, rd_ref, gr_ref, r2t_ref, grd_ref, grdt_ref,
):
    step = pl.program_id(0)

    @pl.when(step == 0)
    def _():
        ffn_ref[...] = jnp.zeros_like(ffn_ref)
        g2_ref[...] = jnp.zeros_like(g2_ref)
        rd_ref[...] = jnp.zeros_like(rd_ref)
        gr_ref[...] = jnp.zeros_like(gr_ref)
        r2t_ref[...] = r2_ref[...].astype(F32).T.astype(BF)
        grd = mm(cot_ref[...], a_ref[...]).astype(BF)
        grd_ref[...] = grd
        grdt_ref[...] = grd.astype(F32).T.astype(BF)

    n2, r2, cot = n2_ref[...], r2_ref[...], cot_ref[...]
    w_g, w_u, w_d = flat(g_ref), flat(u_ref), flat(d_ref)
    gate = mm(n2, w_g) + mm(r2, bg_ref[0])
    up = mm(n2, w_u) + mm(r2, bu_ref[0])
    grad_hidden = (mm(cot, w_d) + mm(grd_ref[...], bd_ref[0])).astype(BF).astype(F32)
    square = gate * gate
    th = jnp.tanh(GELU_C * (gate + GELU_A * square * gate))
    half = 0.5 * (1.0 + th)
    act = gate * half
    slope = half + 0.5 * gate * (1.0 - th * th) * (GELU_C * (1.0 + 3.0 * GELU_A * square))
    hidden = (act * up).astype(BF)
    grad_gate = (grad_hidden * up * slope).astype(BF)
    grad_up = (grad_hidden * act).astype(BF)
    ffn_ref[...] += mm_nt(hidden, w_d)
    rd_ref[...] += mm_nt(hidden, bd_ref[0])
    g2_ref[...] += mm_nt(grad_gate, w_g) + mm_nt(grad_up, w_u)
    gr_ref[...] += mm_nt(grad_gate, bg_ref[0]) + mm_nt(grad_up, bu_ref[0])
    gbg_ref[0] = mm(r2t_ref[rows_of(SLOT_G)], grad_gate).astype(BF)
    gbu_ref[0] = mm(r2t_ref[rows_of(SLOT_U)], grad_up).astype(BF)
    gbd_ref[0] = mm(grdt_ref[rows_of(SLOT_D)], hidden).astype(BF)

    @pl.when(step == pl.num_programs(0) - 1)
    def _():
        rd = rd_ref[...].astype(BF)
        gr = gr_ref[...].astype(BF)
        res = res_ref[...]
        out_ref[...] = (res + (ffn_ref[...] + mm_nt(rd, a_ref[...]))).astype(BF)
        grad_two = g2_ref[...] + mm_nt(gr, a_ref[...])
        grad_res = cot_ref[...].astype(F32) + rms_back(res, gain_ref[...], grad_two)
        gres_ref[...] = grad_res
        grad_branch = grad_res.astype(BF)
        gb_ref[...] = grad_branch
        gro = mm(grad_branch, a_ref[...])
        gro_ref[...] = gro.astype(BF)
        grot = gro.T[rows_of(SLOT_O)].astype(BF)
        cols = gbo_ref.shape[2]
        for t in range(gbo_ref.shape[0]):
            gbo_ref[t] = mm(grot, mixed_ref[:, t * cols : (t + 1) * cols]).astype(BF)
        wide = mm(gr_ref[...].T.astype(BF), n2) + mm(rd_ref[...].T.astype(BF), cot)
        wide_ref[...] = wide + mm(ro_ref[...].astype(F32).T.astype(BF), grad_branch)


def attn_back_kernel(
    place_ref, kv_ref, gb_ref, gro_ref, r1_ref, cos_ref, sin_ref,
    q_ref, mixed_ref, p_ref, wo_ref, bo_ref, wq_ref, bq_ref,
    send_ref, g1_ref, gr_ref,
    ds_ref, dk_ref, dv_ref, kt_ref, r1t_ref, gq_ref, gm_ref,
):
    step = pl.program_id(0)
    rows = q_ref.shape[0]
    chunks = kv_ref.shape[0] // rows

    @pl.when(step == 0)
    def _():
        kt_ref[...] = kv_ref[:, :HD].astype(F32).T.astype(BF)
        r1t_ref[...] = r1_ref[...].astype(F32).T.astype(BF)
        send_ref[...] = jnp.zeros_like(send_ref)
        dk_ref[...] = jnp.zeros_like(dk_ref)
        dv_ref[...] = jnp.zeros_like(dv_ref)
        g1_ref[...] = jnp.zeros_like(g1_ref)
        gr_ref[...] = jnp.zeros_like(gr_ref)

    gm_ref[...] = (mm(gb_ref[...], wo_ref[0]) + mm(gro_ref[...], bo_ref[0])).astype(BF)
    for h in range(q_ref.shape[1] // HD):
        part = slice(h * HD, (h + 1) * HD)
        query, grad = q_ref[:, part], gm_ref[:, part]
        delta = grad.astype(F32) * mixed_ref[:, part].astype(F32)
        delta = jnp.sum(delta.T, axis=0, keepdims=True)
        for c in range(chunks):
            span = slice(c * rows, (c + 1) * rows)
            p = p_ref[h, span]
            dp = mm_nt(kv_ref[span, HD:], grad)
            ds = (p.astype(F32) * (dp - delta)).astype(BF)
            ds_ref[span] = ds
            dk_ref[span] += mm(ds, query)
            dv_ref[span] += mm(p, grad)
        dq = mm(kt_ref[...], ds_ref[...]) * SCALE
        gq_ref[:, part] = rope_back(dq.T, cos_ref[...], sin_ref[...]).astype(BF)

    gq = gq_ref[...]
    grad_bq = mm(r1t_ref[rows_of(SLOT_Q)], gq).astype(BF)
    for core in range(2):
        target = core * pl.num_programs(0) + step
        send_ref[target, rows : rows + RANK] = grad_bq[:, : 2 * HD]
        send_ref[target, rows + RANK :, :HD] = grad_bq[:, 2 * HD :]
    gr_ref[...] += mm_nt(gq, bq_ref[0])
    g1_ref[...] += mm_nt(gq, wq_ref[0])

    @pl.when(step == pl.num_programs(0) - 1)
    def _():
        own = place_ref[2] * pl.num_programs(0) + place_ref[3]
        for w in range(chunks):
            target = own - (chunks - 1) + w
            span = slice(w * rows, (w + 1) * rows)

            @pl.when(target >= 0)
            def _(target=target, span=span):
                send_ref[target, :rows, :HD] = (dk_ref[span] * SCALE).astype(BF)
                send_ref[target, :rows, HD:] = dv_ref[span].astype(BF)


def shared_kernel(
    n1_ref, r1_ref, bkv_ref, cos_ref, sin_ref, terms_ref, gr_ref, widef_ref,
    wide_ref, kvg_ref, gq_ref, gk_ref, gv_ref, grt_ref,
):
    rows = n1_ref.shape[0]
    total = terms_ref[0].astype(F32)
    for source in range(1, terms_ref.shape[0]):
        total = total + terms_ref[source].astype(F32)
    gq_ref[:, : 2 * HD] = total[rows : rows + RANK].astype(BF)
    gq_ref[:, 2 * HD :] = total[rows + RANK :, :HD].astype(BF)
    gk = rope_back(total[:rows, :HD], cos_ref[...], sin_ref[...]).astype(BF)
    gv = total[:rows, HD:].astype(BF)
    gk_ref[...] = gk
    gv_ref[...] = gv
    gr = gr_ref[...] + mm_nt(gk, bkv_ref[0]) + mm_nt(gv, bkv_ref[1])
    grt_ref[...] = gr.astype(BF)
    wide = mm(gr.T.astype(BF), n1_ref[...]) + widef_ref[...]
    wide_ref[...] = wide.T.astype(BF)
    r1t = r1_ref[...].astype(F32).T.astype(BF)
    kvg_ref[0] = mm(r1t[rows_of(SLOT_K)], gk).astype(BF)
    kvg_ref[1] = mm(r1t[rows_of(SLOT_V)], gv).astype(BF)


def input_kernel(
    x_ref, gain_ref, a_ref, wk_ref, wv_ref, gk_ref, gv_ref, gr_ref, g1_ref, gres_ref, grad_ref,
):
    g1 = g1_ref[...] + mm_nt(gk_ref[...], wk_ref[...]) + mm_nt(gv_ref[...], wv_ref[...])
    g1 = g1 + mm_nt(gr_ref[...], a_ref[...])
    x = x_ref[...].astype(F32)
    grad_ref[...] = gres_ref[...] + rms_back(x, gain_ref[...], g1)


def sum_hidden_kernel(ids_ref, first_ref, second_ref, gu_ref, down_ref, out_ref, acc_ref):
    acc_ref[...] = jnp.zeros_like(acc_ref)
    adapters, rank, cols = acc_ref.shape
    for half, terms_ref in enumerate((first_ref, second_ref)):
        part = slice(half * (cols // 2), (half + 1) * (cols // 2))
        for s in range(terms_ref.shape[0]):
            acc_ref[ids_ref[s], :, part] += terms_ref[s].astype(F32)
    ff = gu_ref.shape[2]

    def taken(first, last):
        return acc_ref[:, :, first:last].reshape(adapters * rank, last - first)

    gu_ref[0] = taken(0, ff)
    gu_ref[1] = taken(ff, 2 * ff)
    down_ref[...] = taken(2 * ff, 3 * ff).T
    out_ref[...] = taken(3 * ff, cols).T


def sum_wide_kernel(ids_ref, own_ref, terms_ref, queries_ref, wide_ref, kv_ref, q_ref, acc_ref, accq_ref):
    acc_ref[...] = jnp.zeros_like(acc_ref)
    accq_ref[...] = jnp.zeros_like(accq_ref)
    seqs, parts = terms_ref.shape[:2]
    for s in range(seqs):
        term = terms_ref[s, 0].astype(F32)
        for part in range(1, parts):
            term = term + terms_ref[s, part].astype(F32)
        acc_ref[ids_ref[s]] += term
        accq_ref[ids_ref[s]] += queries_ref[s].astype(F32)
    adapters, rank, _ = acc_ref.shape
    q_ref[...] = accq_ref[...].reshape(q_ref.shape)
    lane = lax.broadcasted_iota(jnp.int32, (rank, LANES), 1) // RANK
    slots, own_rows = wide_ref.shape[:2]
    for j in range(slots):
        total = jnp.zeros((rank, LANES), F32)
        for a in range(adapters):
            turned = pltpu.roll(acc_ref[a], ((a - j) * RANK) % LANES, 1)
            total = jnp.where(lane == a, turned, total)
        wide_ref[j] = total[:own_rows]
    mine = acc_ref[own_ref[0]]
    for j in range(2):
        kv_ref[j] = mine[own_rows + j : own_rows + j + 1]


def scalars():
    return pl.BlockSpec(memory_space=pltpu.SMEM)


def whole(array):
    rank = len(array.shape)
    return pl.BlockSpec(array.shape, lambda *_: (0,) * rank)


def out_whole(shape):
    rank = len(shape)
    return pl.BlockSpec(shape, lambda *_: (0,) * rank)


def call(kernel, name, steps, args, specs, outs, out_specs, scratch, flops, nbytes):
    return pl.pallas_call(
        kernel,
        name=name,
        grid=(steps,),
        in_specs=specs,
        out_specs=out_specs,
        out_shape=outs,
        scratch_shapes=scratch,
        compiler_params=pltpu.CompilerParams(
            dimension_semantics=("arbitrary",), vmem_limit_bytes=VMEM_LIMIT
        ),
        cost_estimate=pl.CostEstimate(flops=flops, bytes_accessed=nbytes, transcendentals=0),
    )(*args)


def on_device(
    tokens, cotangent, segments, adapter_ids, norm_gains, q_weight, kv_weight, out_weight,
    gate_up_weight, down_weight, wide_adapters, kv_adapter, q_adapter, out_adapter,
    gate_up_adapter, down_adapter,
):
    rows, width = tokens.shape
    y_count, x_count, tensor_count = lax.axis_size("y"), lax.axis_size("x"), lax.axis_size("tensor")
    dp_count = 2 * x_count * y_count
    devices = dp_count * tensor_count
    group_rows = rows * tensor_count
    seq_length = 2 * group_rows
    shard_rows = q_weight.shape[0]
    q_cols, ff_cols = q_weight.shape[1], gate_up_weight.shape[2]
    pack_cols = 3 * ff_cols
    seqs = adapter_ids.shape[0]
    adapters = wide_adapters.shape[2] // RANK
    o_block = pack_cols // q_cols
    dp = lax.axis_index(DP)
    tensor = lax.axis_index("tensor")
    my_core = lax.axis_index("core")
    place = jnp.stack([lax.axis_index("y"), lax.axis_index("x"), my_core, tensor]).astype(jnp.int32)
    adapter = lax.dynamic_index_in_dim(adapter_ids, dp // 2, keepdims=False)
    column = adapter * RANK

    def sds(shape, dtype):
        return jax.ShapeDtypeStruct(shape, dtype)

    pack = jnp.concatenate([gate_up_weight[0], gate_up_weight[1], down_weight.T], axis=1)
    pack, q_weight, out_weight, wide_adapters = lax.optimization_barrier(
        (pack, q_weight, out_weight, wide_adapters)
    )
    weights = lax.all_gather(pack, ALL, axis=0, tiled=False)
    weights = weights.reshape(dp_count, tensor_count, shard_rows, pack_cols)

    def with_others(value, axis):
        count = lax.axis_size(axis)
        others = [
            lax.ppermute(value, axis, [((i + away) % count, i) for i in range(count)]) for away in range(1, count)
        ]
        return jnp.stack([value] + others)

    def from_other_core(value):
        return lax.ppermute(value, "core", [(0, 1), (1, 0)])

    pair_z = with_others(jnp.stack([q_weight, out_weight.T]), "tensor")
    q_own = with_others(with_others(pair_z[:, 0], "x"), "y")
    o_own = with_others(with_others(pair_z[:, 1], "y"), "x")
    q_other, o_other = from_other_core(q_own), from_other_core(o_own)

    wide = wide_adapters.reshape(7, shard_rows, adapters, RANK)
    wide = jnp.take(wide, adapter_ids, axis=2).transpose(2, 1, 0, 3)
    wide = wide.reshape(seqs, shard_rows, 7 * RANK)
    wide = jnp.pad(wide, ((0, 0), (0, 0), (0, LANES - 7 * RANK)))
    wide = jnp.repeat(wide, dp_count // seqs, axis=0)
    shared = jnp.broadcast_to(kv_weight[:, None], (2, dp_count, shard_rows, HD))
    wide = jnp.concatenate([wide, shared[0], shared[1]], axis=2)
    wide, _ = lax.optimization_barrier((wide, pair_z))
    a_all = lax.all_to_all(wide, DP, 0, 0, tiled=True).reshape(width, 3 * LANES)

    def take_rows(matrix):
        return lax.dynamic_slice_in_dim(matrix, column, RANK, matrix.ndim - 2)

    def take_cols(matrix):
        return lax.dynamic_slice_in_dim(matrix, column, RANK, matrix.ndim - 1)

    gu_rows = take_rows(gate_up_adapter)
    b_own = jnp.concatenate(
        [gu_rows[0], gu_rows[1], take_cols(down_adapter).T, take_cols(out_adapter).T, take_rows(q_adapter)],
        axis=1,
    )
    b_own, _ = lax.optimization_barrier((b_own, a_all))
    b_all = lax.all_gather(b_own, "tensor", axis=0, tiled=False)

    def in_slot(block, slot):
        pads = [(0, 0)] * block.ndim
        pads[-2] = (slot * RANK, LANES - (slot + 1) * RANK)
        return jnp.pad(block, pads)

    f1, f2, f3 = ff_cols, 2 * ff_cols, 3 * ff_cols
    b_pad = jnp.concatenate(
        [
            in_slot(b_all[:, :, :f1], SLOT_G),
            in_slot(b_all[:, :, f1:f2], SLOT_U),
            in_slot(b_all[:, :, f2:f3], SLOT_D),
            in_slot(b_all[:, :, f3 : f3 + q_cols], SLOT_O),
            in_slot(b_all[:, :, f3 + q_cols :], SLOT_Q),
        ],
        axis=2,
    )
    kv_rows = take_rows(kv_adapter)
    b_kv = jnp.stack([in_slot(kv_rows[0], SLOT_K), in_slot(kv_rows[1], SLOT_V)])

    start = dp * group_rows + tensor * rows
    positions = (start + jnp.arange(rows)) % seq_length
    half = HD // 2
    frequency = 10000.0 ** (-(jnp.arange(half).astype(F32) / half))
    angles = positions.astype(F32)[:, None] * frequency[None, :]
    cos, sin = jnp.cos(angles), jnp.sin(angles)
    cos = jnp.concatenate([cos, cos], axis=1)
    sin = jnp.concatenate([-sin, sin], axis=1)

    padded = jnp.concatenate([jnp.full((WINDOW,), -1, jnp.int32), segments])
    kseg = lax.dynamic_slice_in_dim(padded, start, WINDOW + rows, 0)
    qseg = kseg[WINDOW:].reshape(1, rows)
    kseg = kseg.reshape(WINDOW + rows, 1)
    span = WINDOW + rows

    gain_one, gain_two = norm_gains[0:1], norm_gains[1:2]

    def weight_spec(cols, block):
        return pl.BlockSpec((dp_count, 1, shard_rows, cols), lambda t: (0, t, 0, block))

    def adapter_spec(cols, block):
        return pl.BlockSpec((1, LANES, cols), lambda t: (t, 0, block))

    def token_cols(cols):
        return pl.BlockSpec((rows, cols), lambda t: (0, t))

    def by_step(*shape):
        return pl.BlockSpec((1,) + shape, lambda t: (t,) + (0,) * len(shape))

    heads_cols = tensor_count * q_cols
    o_spec, ob_spec = by_step(width, q_cols), adapter_spec(q_cols, o_block)
    q_spec, qb_spec = by_step(width, q_cols), adapter_spec(q_cols, o_block + 1)

    def lane_block(block):
        return pl.BlockSpec((width, LANES), lambda *_: (0, block))

    a_spec, wk_spec, wv_spec = lane_block(0), lane_block(1), lane_block(2)

    def wholes(*arrays):
        return [whole(v) for v in arrays]

    args = (place, tokens, gain_one, a_all, a_all, a_all, b_kv, cos, sin, b_pad, q_own, q_other)
    normed_one, rank_one, kv_own, queries, w_query = call(
        pre_kernel, "qkv", tensor_count, args,
        [scalars()] + wholes(tokens, gain_one) + [a_spec, wk_spec, wv_spec] + wholes(b_kv, cos, sin) + [qb_spec]
        + wholes(q_own, q_other),
        (
            sds((rows, width), BF), sds((rows, LANES), BF), sds((rows, 2 * HD), BF), sds((rows, heads_cols), BF),
            sds((tensor_count, width, q_cols), BF),
        ),
        (
            out_whole((rows, width)), out_whole((rows, LANES)), out_whole((rows, 2 * HD)), token_cols(q_cols),
            out_whole((tensor_count, width, q_cols)),
        ),
        [], 2 * rows * width * (heads_cols + 384), 2 * width * heads_cols,
    )

    parts = seq_length // rows
    reach = WINDOW // rows

    def moved(value, steps):
        return lax.ppermute(value, SEQ, [(c, c + steps) for c in range(parts) if 0 <= c + steps < parts])

    kv_window = jnp.concatenate([moved(kv_own, d) for d in range(reach, 0, -1)] + [kv_own])

    args = (kv_window, kseg, qseg, queries)
    q_heads = q_cols // HD
    p_spec = pl.BlockSpec((q_heads, span, rows), lambda t: (t, 0, 0))
    mixed, probs = call(
        attn_kernel, "attention", tensor_count, args,
        wholes(*args[:3]) + [token_cols(q_cols)],
        (sds((rows, heads_cols), BF), sds((tensor_count * q_heads, span, rows), BF)),
        (token_cols(q_cols), p_spec),
        [pltpu.VMEM((span, rows), F32), pltpu.VMEM((span, rows), F32), pltpu.VMEM((HD, span), BF)],
        4 * rows * heads_cols * span, 2 * rows * heads_cols * span // HD,
    )

    args = (place, tokens, gain_two, a_all, mixed, b_pad, o_own, o_other)
    residual, normed_two, rank_two, rank_out, w_out = call(
        out_kernel, "out_projection", tensor_count, args,
        [scalars()] + wholes(*args[1:3]) + [a_spec, token_cols(q_cols), ob_spec] + wholes(o_own, o_other),
        (
            sds((rows, width), F32), sds((rows, width), BF), sds((rows, LANES), BF), sds((rows, LANES), BF),
            sds((tensor_count, width, q_cols), BF),
        ),
        (
            out_whole((rows, width)), out_whole((rows, width)), out_whole((rows, LANES)), out_whole((rows, LANES)),
            out_whole((tensor_count, width, q_cols)),
        ),
        [pltpu.VMEM((rows, width), F32), pltpu.VMEM((rows, LANES), F32)],
        2 * rows * heads_cols * width, 2 * width * heads_cols,
    )

    args = (
        residual, normed_two, rank_two, cotangent, gain_two, mixed, rank_out, a_all,
        weights, weights, weights, b_pad, b_pad, b_pad,
    )
    block_output, grad_residual, grad_branch, wide_ffn, grad_ro, grad_bo, grad_bg, grad_bu, grad_bd = call(
        ffn_kernel, "feed_forward", tensor_count, args,
        wholes(*args[:7]) + [a_spec]
        + [weight_spec(ff_cols, j) for j in range(3)]
        + [adapter_spec(ff_cols, j) for j in range(3)],
        (
            sds((rows, width), BF), sds((rows, width), F32), sds((rows, width), BF), sds((LANES, width), F32),
            sds((rows, LANES), BF), sds((tensor_count, RANK, q_cols), BF),
        )
        + (sds((tensor_count, RANK, ff_cols), BF),) * 3,
        (
            out_whole((rows, width)), out_whole((rows, width)), out_whole((rows, width)), out_whole((LANES, width)),
            out_whole((rows, LANES)), out_whole((tensor_count, RANK, q_cols)),
        )
        + (by_step(RANK, ff_cols),) * 3,
        [
            pltpu.VMEM((rows, width), F32), pltpu.VMEM((rows, width), F32),
            pltpu.VMEM((rows, LANES), F32), pltpu.VMEM((rows, LANES), F32),
            pltpu.VMEM((LANES, rows), BF), pltpu.VMEM((rows, LANES), BF), pltpu.VMEM((LANES, rows), BF),
        ],
        12 * rows * width * tensor_count * ff_cols, 6 * width * tensor_count * ff_cols,
    )

    early_cols = f3 + q_cols
    early = jnp.concatenate([grad_bg, grad_bu, grad_bd, grad_bo], axis=2)
    early = early.reshape(tensor_count, RANK, 2, early_cols // 2).transpose(2, 0, 1, 3)
    early = lax.all_to_all(early.reshape(parts, RANK, early_cols // 2), SEQ, 0, 0, tiled=True)

    args = (
        place, kv_window, grad_branch, grad_ro, rank_one, cos, sin,
        queries, mixed, probs, w_out, b_pad, w_query, b_pad,
    )
    sent_rows = rows + 2 * RANK
    send, grad_one, grad_rank = call(
        attn_back_kernel, "attention_back", tensor_count, args,
        [scalars()] + wholes(*args[1:7])
        + [token_cols(q_cols), token_cols(q_cols), p_spec, o_spec, ob_spec, q_spec, qb_spec],
        (sds((parts, sent_rows, 2 * HD), BF), sds((rows, width), F32), sds((rows, LANES), F32)),
        (out_whole((parts, sent_rows, 2 * HD)), out_whole((rows, width)), out_whole((rows, LANES))),
        [
            pltpu.VMEM((span, rows), BF),
            pltpu.VMEM((span, HD), F32), pltpu.VMEM((span, HD), F32), pltpu.VMEM((HD, span), BF),
            pltpu.VMEM((LANES, rows), BF),
            pltpu.VMEM((rows, q_cols), BF), pltpu.VMEM((rows, q_cols), BF),
        ],
        2 * rows * heads_cols * (4 * span + 2 * width), 4 * width * heads_cols,
    )

    seq_terms = lax.all_to_all(send, SEQ, 0, 0, tiled=True)

    early, grad_one = lax.optimization_barrier((early, grad_one))
    early = jnp.sum(early.astype(F32), axis=0).astype(BF)
    early = jnp.broadcast_to(early[None], (seqs, RANK, early_cols // 2))
    early = lax.all_to_all(early, ("y", "x"), 0, 0, tiled=True)
    early_other = from_other_core(early)
    early_first = jnp.where(my_core == 0, early, early_other)
    early_second = jnp.where(my_core == 0, early_other, early)

    args = (normed_one, rank_one, b_kv, cos, sin, seq_terms, grad_rank, wide_ffn)
    wide_term, kv_term, grad_bq, grad_key, grad_value, grad_rank = call(
        shared_kernel, "shared_head", 1, args, wholes(*args),
        (
            sds((width, LANES), BF), sds((2, RANK, HD), BF), sds((RANK, q_cols), BF),
            sds((rows, HD), BF), sds((rows, HD), BF), sds((rows, LANES), BF),
        ),
        (
            out_whole((width, LANES)), out_whole((2, RANK, HD)), out_whole((RANK, q_cols)),
            out_whole((rows, HD)), out_whole((rows, HD)), out_whole((rows, LANES)),
        ),
        [], 2 * rows * width * 128, 4 * rows * width,
    )

    own_rows = width // devices
    kv_terms = jnp.tile(kv_term.transpose(1, 0, 2), (devices // RANK, 1, 1))
    owned = jnp.concatenate(
        [wide_term.reshape(devices, own_rows, LANES), kv_terms, jnp.zeros((devices, 2, LANES), BF)], axis=1
    )
    terms = lax.all_to_all(owned, ALL, 0, 0, tiled=True)
    terms = terms.reshape(seqs, parts, RANK, LANES)
    q_terms = lax.all_to_all(jnp.broadcast_to(grad_bq[None], (seqs, RANK, q_cols)), ("y", "x"), 0, 0, tiled=True)

    args = (
        tokens, gain_one, a_all, a_all, a_all, grad_key, grad_value, grad_rank, grad_one, grad_residual,
    )
    input_grad = call(
        input_kernel, "input_gradient", 1, args,
        wholes(*args[:2]) + [a_spec, wk_spec, wv_spec] + wholes(*args[5:]),
        sds((rows, width), F32), out_whole((rows, width)),
        [], 2 * rows * width * 384, 16 * rows * width,
    )

    gate_up_adapter_grad, down_adapter_grad, out_adapter_grad = pl.pallas_call(
        sum_hidden_kernel,
        name="sum_hidden",
        in_specs=[scalars()] + wholes(early_first, early_second),
        out_specs=(out_whole((2, LANES, ff_cols)), out_whole((ff_cols, LANES)), out_whole((q_cols, LANES))),
        out_shape=(sds((2, LANES, ff_cols), F32), sds((ff_cols, LANES), F32), sds((q_cols, LANES), F32)),
        scratch_shapes=[pltpu.VMEM((adapters, RANK, early_cols), F32)],
        compiler_params=pltpu.CompilerParams(vmem_limit_bytes=VMEM_LIMIT),
    )(adapter_ids, early_first, early_second)

    own_adapter = ((dp * tensor_count + tensor) // RANK).astype(jnp.int32).reshape(1)
    wide_grad, kv_adapter_grad, q_adapter_grad = pl.pallas_call(
        sum_wide_kernel,
        name="sum_wide",
        in_specs=[scalars(), scalars()] + wholes(terms, q_terms),
        out_specs=(out_whole((7, own_rows, LANES)), out_whole((2, 1, HD)), out_whole((LANES, q_cols))),
        out_shape=(sds((7, own_rows, LANES), F32), sds((2, 1, HD), F32), sds((LANES, q_cols), F32)),
        scratch_shapes=[pltpu.VMEM((adapters, RANK, LANES), F32), pltpu.VMEM((adapters, RANK, q_cols), F32)],
        compiler_params=pltpu.CompilerParams(vmem_limit_bytes=VMEM_LIMIT),
    )(adapter_ids, own_adapter, terms, q_terms)
    return (
        block_output, input_grad, wide_grad, kv_adapter_grad,
        q_adapter_grad, out_adapter_grad, gate_up_adapter_grad, down_adapter_grad,
    )


def solution(mesh):
    dp_count, tensor_count = mesh.shape["dp"], mesh.shape["tensor"]
    chips = dp_count // 2
    x_count = math.isqrt(chips)
    devices = mesh.devices.reshape(chips // x_count, x_count, 2, tensor_count)
    return jax.shard_map(
        on_device,
        mesh=Mesh(devices, ALL),
        in_specs=(
            P(ALL, None), P(ALL, None), P(), P(), P(), P(DP, "tensor"), P(None, DP, None),
            P("tensor", DP), P(None, DP, "tensor"), P("tensor", DP), P(None, DP, None), P(),
            P(None, "tensor"), P("tensor", None), P(None, None, "tensor"), P("tensor", None),
        ),
        out_specs=(
            P(ALL, None), P(ALL, None), P(None, ALL, None), P(None, ALL, None),
            P(None, "tensor"), P("tensor", None), P(None, None, "tensor"), P("tensor", None),
        ),
        check_vma=False,
    )
```

```python
import functools
import math

import jax
import jax.numpy as jnp
from jax import lax
from jax.experimental import pallas as pl
from jax.experimental.pallas import tpu as pltpu
from jax.sharding import Mesh, PartitionSpec as P

HD = 128
WINDOW = 1024
RANK = 16
LANES = 128
EPS = 1e-06
MASKED = -1e30
SCALE = HD ** (-0.5)
GELU_C = 0.7978845608028654
GELU_A = 0.044715
VMEM_LIMIT = 58 * 1024 * 1024
BF = jnp.bfloat16
F32 = jnp.float32
DP = ("y", "x", "core")
SEQ = ("core", "tensor")
ALL = ("y", "x", "core", "tensor")

SLOT_Q, SLOT_K, SLOT_V, SLOT_G, SLOT_U, SLOT_O, SLOT_D = range(7)


def rows_of(slot):
    return slice(slot * RANK, (slot + 1) * RANK)


def mm(a, b):
    return lax.dot_general(a, b, (((1,), (0,)), ((), ())), preferred_element_type=F32)


def mm_nt(a, b):
    return lax.dot_general(a, b, (((1,), (1,)), ((), ())), preferred_element_type=F32)


def rope(v, cos, sin):
    return v * cos + pltpu.roll(v, HD // 2, 1) * sin


def rope_back(g, cos, sin):
    return g * cos - pltpu.roll(g, HD // 2, 1) * sin


def flat(ref):
    block = ref[...]
    return block.reshape(block.shape[0] * block.shape[2], block.shape[3])


def rms(v, gain):
    return v * lax.rsqrt(jnp.mean(v * v, axis=-1, keepdims=True) + EPS) * gain


def rms_back(v, gain, grad):
    inv = lax.rsqrt(jnp.mean(v * v, axis=-1, keepdims=True) + EPS)
    scaled = grad * gain
    dot = jnp.mean(v * scaled, axis=-1, keepdims=True)
    return inv * scaled - v * (inv * inv * inv * dot)


def pre_kernel(
    x_ref, gain_ref, a_ref, wk_ref, wv_ref, bkv_ref, cos_ref, sin_ref, wq_ref, bq_ref,
    n1_ref, r1_ref, kv_ref, q_ref,
):
    @pl.when(pl.program_id(0) == 0)
    def _():
        n1 = rms(x_ref[...].astype(F32), gain_ref[...]).astype(BF)
        n1_ref[...] = n1
        r1 = mm(n1, a_ref[...]).astype(BF)
        r1_ref[...] = r1
        key = mm(n1, wk_ref[...]) + mm(r1, bkv_ref[0])
        kv_ref[:, :HD] = rope(key, cos_ref[...], sin_ref[...]).astype(BF)
        kv_ref[:, HD:] = (mm(n1, wv_ref[...]) + mm(r1, bkv_ref[1])).astype(BF)

    lin = mm(n1_ref[...], flat(wq_ref)) + mm(r1_ref[...], bq_ref[0])
    for h in range(lin.shape[1] // HD):
        part = slice(h * HD, (h + 1) * HD)
        q_ref[:, part] = rope(lin[:, part], cos_ref[...], sin_ref[...]).astype(BF)


def fill_bias(bias_ref, kseg_ref, qseg_ref):
    shape = bias_ref.shape
    key = lax.broadcasted_iota(jnp.int32, shape, 0)
    query = lax.broadcasted_iota(jnp.int32, shape, 1)
    allowed = (key >= query) & (key <= query + WINDOW) & (kseg_ref[...] == qseg_ref[...])
    bias_ref[...] = jnp.where(allowed, 0.0, MASKED)


def fill_window(kv_ref, place_ref, seq_ref):
    rows = seq_ref.shape[1]
    reach = kv_ref.shape[0] // rows - 1
    own = place_ref[2] * (seq_ref.shape[0] // 2) + place_ref[3]
    for w in range(reach + 1):
        kv_ref[w * rows : (w + 1) * rows] = seq_ref[jnp.maximum(own - reach + w, 0)]


def attn_kernel(place_ref, seq_ref, kseg_ref, qseg_ref, q_ref, mixed_ref, p_ref, bias_ref, s_ref, vt_ref, kv_ref):
    step = pl.program_id(0)
    rows = q_ref.shape[0]
    chunks = kv_ref.shape[0] // rows

    @pl.when(step == 0)
    def _():
        fill_window(kv_ref, place_ref, seq_ref)
        fill_bias(bias_ref, kseg_ref, qseg_ref)
        vt_ref[...] = kv_ref[:, HD:].astype(F32).T.astype(BF)

    for h in range(q_ref.shape[1] // HD):
        part = slice(h * HD, (h + 1) * HD)
        query = q_ref[:, part]
        top = jnp.full((1, rows), MASKED, F32)
        for c in range(chunks):
            span = slice(c * rows, (c + 1) * rows)
            s = mm_nt(kv_ref[span, :HD], query) * SCALE + bias_ref[span]
            s_ref[span] = s
            top = jnp.maximum(top, jnp.max(s, axis=0, keepdims=True))
        total = jnp.zeros((1, rows), F32)
        for c in range(chunks):
            span = slice(c * rows, (c + 1) * rows)
            p = jnp.exp(s_ref[span] - top)
            total = total + jnp.sum(p, axis=0, keepdims=True)
            s_ref[span] = p
        inv = 1.0 / total
        for c in range(chunks):
            span = slice(c * rows, (c + 1) * rows)
            p_ref[h, span] = (s_ref[span] * inv).astype(BF)
        mixed_ref[:, part] = mm(vt_ref[...], p_ref[h]).T.astype(BF)


def out_kernel(
    x_ref, gain_ref, a_ref, mixed_ref, wo_ref, bo_ref, res_ref, n2_ref, ro_ref, acc_ref, rank_ref,
):
    step = pl.program_id(0)

    @pl.when(step == 0)
    def _():
        acc_ref[...] = jnp.zeros_like(acc_ref)
        rank_ref[...] = jnp.zeros_like(rank_ref)

    mixed = mixed_ref[...]
    acc_ref[...] += mm_nt(mixed, flat(wo_ref))
    rank_ref[...] += mm_nt(mixed, bo_ref[0])

    @pl.when(step == pl.num_programs(0) - 1)
    def _():
        ro = rank_ref[...].astype(BF)
        ro_ref[...] = ro
        res = x_ref[...].astype(F32) + (acc_ref[...] + mm_nt(ro, a_ref[...]))
        res_ref[...] = res
        n2_ref[...] = rms(res, gain_ref[...]).astype(BF)


def ffn_kernel(count, a_ref, b_ref, w_ref, *rest):
    n2_refs, cot_refs, rest = rest[:count], rest[count : 2 * count], rest[2 * count :]
    g2_refs, ffn_refs, rest = rest[:count], rest[count : 2 * count], rest[2 * count :]
    wide_ref, gb_ref, n2_ref, cot_ref, wv_ref, sems = rest
    ff = wv_ref.shape[2]
    copies = [
        pltpu.make_async_copy(w_ref.at[:, pl.ds(j * ff, ff)], wv_ref.at[j], sems.at[j]) for j in range(3)
    ]
    for copy in copies:
        copy.start()
    rows = n2_refs[0].shape[0]
    for i in range(count):
        span = slice(i * rows, (i + 1) * rows)
        n2_ref[span] = n2_refs[i][...]
        cot_ref[span] = cot_refs[i][...]
    n2, cot = n2_ref[...], cot_ref[...]
    bg, bu, bd = (b_ref[:, j * ff : (j + 1) * ff] for j in range(3))
    r2 = mm(n2, a_ref[...])
    grd = mm(cot, a_ref[...])
    r2t, grdt = r2.T.astype(BF), grd.T.astype(BF)
    r2, grd = r2.astype(BF), grd.astype(BF)
    copies[0].wait()
    gate = mm(n2, wv_ref[0]) + mm(r2, bg)
    copies[1].wait()
    up = mm(n2, wv_ref[1]) + mm(r2, bu)
    copies[2].wait()
    grad_hidden = (mm(cot, wv_ref[2]) + mm(grd, bd)).astype(BF).astype(F32)
    square = gate * gate
    th = jnp.tanh(GELU_C * (gate + GELU_A * square * gate))
    half = 0.5 * (1.0 + th)
    act = gate * half
    slope = half + 0.5 * gate * (1.0 - th * th) * (GELU_C * (1.0 + 3.0 * GELU_A * square))
    hidden = (act * up).astype(BF)
    grad_gate = (grad_hidden * up * slope).astype(BF)
    grad_up = (grad_hidden * act).astype(BF)
    gr = mm_nt(grad_gate, bg) + mm_nt(grad_up, bu)
    rd = mm_nt(hidden, bd)
    g2 = mm_nt(grad_gate, wv_ref[0]) + mm_nt(grad_up, wv_ref[1]) + mm_nt(gr.astype(BF), a_ref[...])
    ffn = mm_nt(hidden, wv_ref[2]) + mm_nt(rd.astype(BF), a_ref[...])
    for i in range(count):
        span = slice(i * rows, (i + 1) * rows)
        g2_refs[i][...] = g2[span].astype(g2_refs[i].dtype)
        ffn_refs[i][...] = ffn[span].astype(ffn_refs[i].dtype)
    wide_ref[...] = mm(gr.T.astype(BF), n2) + mm(rd.T.astype(BF), cot)
    gb_ref[:, :ff] = mm(r2t[rows_of(SLOT_G)], grad_gate)
    gb_ref[:, ff : 2 * ff] = mm(r2t[rows_of(SLOT_U)], grad_up)
    gb_ref[:, 2 * ff :] = mm(grdt[rows_of(SLOT_D)], hidden)


def residual_kernel(
    res_ref, cot_ref, gain_ref, a_ref, mixed_ref, ro_ref, own_ref, *rest,
):
    others, (gres_ref, gb_ref, gro_ref, gbo_ref, wide_ref) = rest[:-5], rest[-5:]
    grad_two = own_ref[...]
    for other_ref in others:
        grad_two = grad_two + other_ref[...].astype(F32)
    grad_res = cot_ref[...].astype(F32) + rms_back(res_ref[...], gain_ref[...], grad_two)
    gres_ref[...] = grad_res
    grad_branch = grad_res.astype(BF)
    gb_ref[...] = grad_branch
    gro = mm(grad_branch, a_ref[...])
    gro_ref[...] = gro.astype(BF)
    grot = gro.T[rows_of(SLOT_O)].astype(BF)
    cols = gbo_ref.shape[2]
    for t in range(gbo_ref.shape[0]):
        gbo_ref[t] = mm(grot, mixed_ref[:, t * cols : (t + 1) * cols]).astype(BF)
    wide_ref[...] = mm(ro_ref[...].astype(F32).T.astype(BF), grad_branch)


def attn_back_kernel(
    place_ref, seq_ref, gb_ref, gro_ref, gbo_ref, r1_ref, cos_ref, sin_ref,
    q_ref, mixed_ref, p_ref, wo_ref, bo_ref, wq_ref, bq_ref,
    send_ref, g1_ref, gr_ref,
    ds_ref, dk_ref, dv_ref, kt_ref, r1t_ref, gq_ref, gm_ref, kv_ref,
):
    step = pl.program_id(0)
    rows = q_ref.shape[0]
    chunks = kv_ref.shape[0] // rows

    @pl.when(step == 0)
    def _():
        fill_window(kv_ref, place_ref, seq_ref)
        kt_ref[...] = kv_ref[:, :HD].astype(F32).T.astype(BF)
        r1t_ref[...] = r1_ref[...].astype(F32).T.astype(BF)
        send_ref[...] = jnp.zeros_like(send_ref)
        dk_ref[...] = jnp.zeros_like(dk_ref)
        dv_ref[...] = jnp.zeros_like(dv_ref)
        g1_ref[...] = jnp.zeros_like(g1_ref)
        gr_ref[...] = jnp.zeros_like(gr_ref)

    gm_ref[...] = (mm(gb_ref[...], flat(wo_ref)) + mm(gro_ref[...], bo_ref[0])).astype(BF)
    for h in range(q_ref.shape[1] // HD):
        part = slice(h * HD, (h + 1) * HD)
        query, grad = q_ref[:, part], gm_ref[:, part]
        delta = grad.astype(F32) * mixed_ref[:, part].astype(F32)
        delta = jnp.sum(delta.T, axis=0, keepdims=True)
        for c in range(chunks):
            span = slice(c * rows, (c + 1) * rows)
            p = p_ref[h, span]
            dp = mm_nt(kv_ref[span, HD:], grad)
            ds = (p.astype(F32) * (dp - delta)).astype(BF)
            ds_ref[span] = ds
            dk_ref[span] += mm(ds, query)
            dv_ref[span] += mm(p, grad)
        dq = mm(kt_ref[...], ds_ref[...]) * SCALE
        gq_ref[:, part] = rope_back(dq.T, cos_ref[...], sin_ref[...]).astype(BF)

    gq = gq_ref[...]
    grad_bq = mm(r1t_ref[rows_of(SLOT_Q)], gq).astype(BF)
    for core in range(2):
        target = core * pl.num_programs(0) + step
        for j, term in enumerate((grad_bq, gbo_ref[0])):
            first = rows + 2 * j * RANK
            send_ref[target, first : first + RANK] = term[:, : 2 * HD]
            send_ref[target, first + RANK : first + 2 * RANK, :HD] = term[:, 2 * HD :]
    gr_ref[...] += mm_nt(gq, bq_ref[0])
    g1_ref[...] += mm_nt(gq, flat(wq_ref))

    @pl.when(step == pl.num_programs(0) - 1)
    def _():
        own = place_ref[2] * pl.num_programs(0) + place_ref[3]
        for w in range(chunks):
            target = own - (chunks - 1) + w
            span = slice(w * rows, (w + 1) * rows)

            @pl.when(target >= 0)
            def _(target=target, span=span):
                send_ref[target, :rows, :HD] = (dk_ref[span] * SCALE).astype(BF)
                send_ref[target, :rows, HD:] = dv_ref[span].astype(BF)


def shared_kernel(
    n1_ref, r1_ref, bkv_ref, cos_ref, sin_ref, terms_ref, gr_ref, *rest,
):
    wides, (wide_ref, kvg_ref, gqo_ref, gk_ref, gv_ref, grt_ref) = rest[:-6], rest[-6:]
    rows = n1_ref.shape[0]
    total = terms_ref[0].astype(F32)
    for source in range(1, terms_ref.shape[0]):
        total = total + terms_ref[source].astype(F32)
    for j in range(2):
        first = rows + 2 * j * RANK
        gqo_ref[rows_of(j), : 2 * HD] = total[first : first + RANK].astype(BF)
        gqo_ref[rows_of(j), 2 * HD :] = total[first + RANK : first + 2 * RANK, :HD].astype(BF)
    gk = rope_back(total[:rows, :HD], cos_ref[...], sin_ref[...]).astype(BF)
    gv = total[:rows, HD:].astype(BF)
    gk_ref[...] = gk
    gv_ref[...] = gv
    gr = gr_ref[...] + mm_nt(gk, bkv_ref[0]) + mm_nt(gv, bkv_ref[1])
    grt_ref[...] = gr.astype(BF)
    wide = mm(gr.T.astype(BF), n1_ref[...])
    for part_ref in wides:
        wide = wide + part_ref[...]
    wide_ref[...] = wide.T.astype(BF)
    r1t = r1_ref[...].astype(F32).T.astype(BF)
    kvg_ref[0] = mm(r1t[rows_of(SLOT_K)], gk).astype(BF)
    kvg_ref[1] = mm(r1t[rows_of(SLOT_V)], gv).astype(BF)


def input_kernel(
    x_ref, gain_ref, a_ref, wk_ref, wv_ref, gk_ref, gv_ref, gr_ref, g1_ref, gres_ref, grad_ref,
):
    g1 = g1_ref[...] + mm_nt(gk_ref[...], wk_ref[...]) + mm_nt(gv_ref[...], wv_ref[...])
    g1 = g1 + mm_nt(gr_ref[...], a_ref[...])
    x = x_ref[...].astype(F32)
    grad_ref[...] = gres_ref[...] + rms_back(x, gain_ref[...], g1)


def sum_hidden_kernel(ids_ref, terms_ref, gu_ref, down_ref, acc_ref):
    acc_ref[...] = jnp.zeros_like(acc_ref)
    adapters, rank, _ = acc_ref.shape
    for s in range(terms_ref.shape[0] // 2):
        acc_ref[ids_ref[s]] += terms_ref[2 * s].astype(F32) + terms_ref[2 * s + 1].astype(F32)
    ff = gu_ref.shape[2]

    def taken(j):
        return acc_ref[:, :, j * ff : (j + 1) * ff].reshape(adapters * rank, ff)

    gu_ref[0] = taken(0)
    gu_ref[1] = taken(1)
    down_ref[...] = taken(2).T


def sum_wide_kernel(ids_ref, own_ref, terms_ref, heads_ref, wide_ref, kv_ref, q_ref, out_ref, acc_ref, acch_ref):
    acc_ref[...] = jnp.zeros_like(acc_ref)
    acch_ref[...] = jnp.zeros_like(acch_ref)
    seqs, parts = terms_ref.shape[:2]
    for s in range(seqs):
        term = terms_ref[s, 0].astype(F32)
        for part in range(1, parts):
            term = term + terms_ref[s, part].astype(F32)
        acc_ref[ids_ref[s]] += term
        acch_ref[ids_ref[s]] += heads_ref[s].astype(F32)
    adapters, rank, _ = acc_ref.shape
    q_ref[...] = acch_ref[:, :RANK].reshape(q_ref.shape)
    out_ref[...] = acch_ref[:, RANK:].reshape(q_ref.shape).T
    lane = lax.broadcasted_iota(jnp.int32, (rank, LANES), 1) // RANK
    slots, own_rows = wide_ref.shape[:2]
    for j in range(slots):
        total = jnp.zeros((rank, LANES), F32)
        for a in range(adapters):
            turned = pltpu.roll(acc_ref[a], ((a - j) * RANK) % LANES, 1)
            total = jnp.where(lane == a, turned, total)
        wide_ref[j] = total[:own_rows]
    mine = acc_ref[own_ref[0]]
    for j in range(2):
        kv_ref[j] = mine[own_rows + j : own_rows + j + 1]


def scalars():
    return pl.BlockSpec(memory_space=pltpu.SMEM)


def whole(array):
    rank = len(array.shape)
    return pl.BlockSpec(array.shape, lambda *_: (0,) * rank)


def out_whole(shape):
    rank = len(shape)
    return pl.BlockSpec(shape, lambda *_: (0,) * rank)


def call(kernel, name, steps, args, specs, outs, out_specs, scratch, flops, nbytes):
    return pl.pallas_call(
        kernel,
        name=name,
        grid=(steps,),
        in_specs=specs,
        out_specs=out_specs,
        out_shape=outs,
        scratch_shapes=scratch,
        compiler_params=pltpu.CompilerParams(
            dimension_semantics=("arbitrary",), vmem_limit_bytes=VMEM_LIMIT
        ),
        cost_estimate=pl.CostEstimate(flops=flops, bytes_accessed=nbytes, transcendentals=0),
    )(*args)


def on_device(
    tokens, cotangent, segments, adapter_ids, norm_gains, q_weight, kv_weight, out_weight,
    gate_up_weight, down_weight, wide_adapters, kv_adapter, q_adapter, out_adapter,
    gate_up_adapter, down_adapter,
):
    rows, width = tokens.shape
    y_count, x_count, tensor_count = lax.axis_size("y"), lax.axis_size("x"), lax.axis_size("tensor")
    dp_count = 2 * x_count * y_count
    devices = dp_count * tensor_count
    group_rows = rows * tensor_count
    seq_length = 2 * group_rows
    shard_rows = q_weight.shape[0]
    q_cols, ff_cols = q_weight.shape[1], gate_up_weight.shape[2]
    seqs = adapter_ids.shape[0]
    adapters = wide_adapters.shape[2] // RANK
    dp = lax.axis_index(DP)
    tensor = lax.axis_index("tensor")
    my_core = lax.axis_index("core")
    place = jnp.stack([lax.axis_index("y"), lax.axis_index("x"), my_core, tensor]).astype(jnp.int32)
    adapter = lax.dynamic_index_in_dim(adapter_ids, dp // 2, keepdims=False)
    column = adapter * RANK

    def sds(shape, dtype):
        return jax.ShapeDtypeStruct(shape, dtype)

    pack = jnp.concatenate([q_weight, out_weight.T], axis=1)
    pack, wide_adapters, cotangent = lax.optimization_barrier((pack, wide_adapters, cotangent))
    weights = lax.all_gather(pack, ALL, axis=0, tiled=False)
    weights = weights.reshape(dp_count, tensor_count, shard_rows, 2 * q_cols)
    pack_ff = jnp.concatenate([gate_up_weight[0], gate_up_weight[1], down_weight.T], axis=1)
    pack_ff, weights = lax.optimization_barrier((pack_ff, weights))
    weights_ff = lax.all_gather(pack_ff, DP, axis=0, tiled=True)

    def from_z(value, away):
        return lax.ppermute(value, "tensor", [((z + away) % tensor_count, z) for z in range(tensor_count)])

    cotangents = [cotangent] + [from_z(cotangent, d) for d in range(1, tensor_count)]

    wide = wide_adapters.reshape(7, shard_rows, adapters, RANK)
    wide = jnp.take(wide, adapter_ids, axis=2).transpose(2, 1, 0, 3)
    wide = wide.reshape(seqs, shard_rows, 7 * RANK)
    wide = jnp.pad(wide, ((0, 0), (0, 0), (0, LANES - 7 * RANK)))
    wide = jnp.repeat(wide, dp_count // seqs, axis=0)
    shared = jnp.broadcast_to(kv_weight[:, None], (2, dp_count, shard_rows, HD))
    wide = jnp.concatenate([wide, shared[0], shared[1]], axis=2)
    a_all = lax.all_to_all(wide, DP, 0, 0, tiled=True).reshape(width, 3 * LANES)

    def take_rows(matrix):
        return lax.dynamic_slice_in_dim(matrix, column, RANK, matrix.ndim - 2)

    def take_cols(matrix):
        return lax.dynamic_slice_in_dim(matrix, column, RANK, matrix.ndim - 1)

    def in_slot(block, slot):
        pads = [(0, 0)] * block.ndim
        pads[-2] = (slot * RANK, LANES - (slot + 1) * RANK)
        return jnp.pad(block, pads)

    gu_rows = take_rows(gate_up_adapter)
    b_ff = jnp.concatenate(
        [in_slot(gu_rows[0], SLOT_G), in_slot(gu_rows[1], SLOT_U), in_slot(take_cols(down_adapter).T, SLOT_D)], axis=1
    )
    b_own = jnp.concatenate([take_rows(q_adapter), take_cols(out_adapter).T], axis=1)
    b_own, _ = lax.optimization_barrier((b_own, a_all))
    b_all = lax.all_gather(b_own, "tensor", axis=0, tiled=False)
    b_pad = jnp.concatenate(
        [in_slot(b_all[:, :, :q_cols], SLOT_Q), in_slot(b_all[:, :, q_cols:], SLOT_O)], axis=2
    )
    kv_rows = take_rows(kv_adapter)
    b_kv = jnp.stack([in_slot(kv_rows[0], SLOT_K), in_slot(kv_rows[1], SLOT_V)])

    start = dp * group_rows + tensor * rows
    positions = (start + jnp.arange(rows)) % seq_length
    half = HD // 2
    frequency = 10000.0 ** (-(jnp.arange(half).astype(F32) / half))
    angles = positions.astype(F32)[:, None] * frequency[None, :]
    cos, sin = jnp.cos(angles), jnp.sin(angles)
    cos = jnp.concatenate([cos, cos], axis=1)
    sin = jnp.concatenate([-sin, sin], axis=1)

    padded = jnp.concatenate([jnp.full((WINDOW,), -1, jnp.int32), segments])
    kseg = lax.dynamic_slice_in_dim(padded, start, WINDOW + rows, 0)
    qseg = kseg[WINDOW:].reshape(1, rows)
    kseg = kseg.reshape(WINDOW + rows, 1)
    span = WINDOW + rows

    gain_one, gain_two = norm_gains[0:1], norm_gains[1:2]

    def weight_spec(cols, block):
        return pl.BlockSpec((dp_count, 1, shard_rows, cols), lambda t: (0, t, 0, block))

    def adapter_spec(cols, block):
        return pl.BlockSpec((1, LANES, cols), lambda t: (t, 0, block))

    def token_cols(cols):
        return pl.BlockSpec((rows, cols), lambda t: (0, t))

    def by_step(*shape):
        return pl.BlockSpec((1,) + shape, lambda t: (t,) + (0,) * len(shape))

    heads_cols = tensor_count * q_cols
    q_spec, qb_spec = weight_spec(q_cols, 0), adapter_spec(q_cols, 0)
    o_spec, ob_spec = weight_spec(q_cols, 1), adapter_spec(q_cols, 1)

    def lane_block(block):
        return pl.BlockSpec((width, LANES), lambda *_: (0, block))

    a_spec, wk_spec, wv_spec = lane_block(0), lane_block(1), lane_block(2)

    def wholes(*arrays):
        return [whole(v) for v in arrays]

    args = (tokens, gain_one, a_all, a_all, a_all, b_kv, cos, sin, weights, b_pad)
    normed_one, rank_one, kv_own, queries = call(
        pre_kernel, "qkv", tensor_count, args,
        wholes(tokens, gain_one) + [a_spec, wk_spec, wv_spec] + wholes(b_kv, cos, sin) + [q_spec, qb_spec],
        (sds((rows, width), BF), sds((rows, LANES), BF), sds((rows, 2 * HD), BF), sds((rows, heads_cols), BF)),
        (out_whole((rows, width)), out_whole((rows, LANES)), out_whole((rows, 2 * HD)), token_cols(q_cols)),
        [], 2 * rows * width * (heads_cols + 384), 2 * width * heads_cols,
    )

    parts = seq_length // rows
    kv_seq = lax.all_to_all(jnp.broadcast_to(kv_own[None], (parts, rows, 2 * HD)), SEQ, 0, 0, tiled=True)

    args = (place, kv_seq, kseg, qseg, queries)
    q_heads = q_cols // HD
    p_spec = pl.BlockSpec((q_heads, span, rows), lambda t: (t, 0, 0))
    mixed, probs = call(
        attn_kernel, "attention", tensor_count, args,
        [scalars()] + wholes(*args[1:4]) + [token_cols(q_cols)],
        (sds((rows, heads_cols), BF), sds((tensor_count * q_heads, span, rows), BF)),
        (token_cols(q_cols), p_spec),
        [
            pltpu.VMEM((span, rows), F32), pltpu.VMEM((span, rows), F32), pltpu.VMEM((HD, span), BF),
            pltpu.VMEM((span, 2 * HD), BF),
        ],
        4 * rows * heads_cols * span, 2 * rows * heads_cols * span // HD,
    )

    args = (tokens, gain_two, a_all, mixed, weights, b_pad)
    residual, normed_two, rank_out = call(
        out_kernel, "out_projection", tensor_count, args,
        wholes(*args[:2]) + [a_spec, token_cols(q_cols), o_spec, ob_spec],
        (sds((rows, width), F32), sds((rows, width), BF), sds((rows, LANES), BF)),
        (out_whole((rows, width)), out_whole((rows, width)), out_whole((rows, LANES))),
        [pltpu.VMEM((rows, width), F32), pltpu.VMEM((rows, LANES), F32)],
        2 * rows * heads_cols * width, 2 * width * heads_cols,
    )

    normed = [normed_two] + [from_z(normed_two, d) for d in range(1, tensor_count)]

    def feed_forward(aways):
        count = len(aways)
        args = (a_all, b_ff, weights_ff, *(normed[d] for d in aways), *(cotangents[d] for d in aways))
        kinds = [F32 if d == 0 else BF for d in aways] * 2
        outs = [sds((rows, width), kind) for kind in kinds] + [sds((LANES, width), F32), sds((RANK, 3 * ff_cols), F32)]
        out = call(
            functools.partial(ffn_kernel, count), "feed_forward", 1, args,
            [a_spec] + wholes(b_ff) + [pl.BlockSpec(memory_space=pl.ANY)] + wholes(*args[3:]),
            outs, [out_whole(v.shape) for v in outs],
            [
                pltpu.VMEM((count * rows, width), BF), pltpu.VMEM((count * rows, width), BF),
                pltpu.VMEM((3, width, ff_cols), BF), pltpu.SemaphoreType.DMA((3,)),
            ],
            12 * count * rows * width * ff_cols, 6 * width * ff_cols,
        )
        return out[:count], out[count : 2 * count], out[-2], out[-1]

    def back_to(value, away):
        return lax.ppermute(value, "tensor", [(z, (z + away) % tensor_count) for z in range(tensor_count)])

    near = [1, tensor_count - 1]
    groups = [near, [d for d in range(2, tensor_count - 1)], [0]]
    results = [(group, *feed_forward(group)) for group in groups]
    two_terms, ffn_parts, wide_parts, hidden_terms = {}, {}, [], 0.0
    for group, two, ffn, wide_part, hidden_term in results:
        for i, d in enumerate(group):
            two_terms[d] = two[i] if d == 0 else back_to(two[i], d)
            ffn_parts[d] = ffn[i]
        wide_parts.append(wide_part)
        hidden_terms = hidden_terms + hidden_term
    far = range(1, tensor_count)

    args = (residual, cotangent, gain_two, a_all, mixed, rank_out, *(two_terms[d] for d in range(tensor_count)))
    grad_residual, grad_branch, grad_ro, grad_bo, wide_out = call(
        residual_kernel, "residual_gradient", 1, args,
        wholes(*args[:3]) + [a_spec] + wholes(*args[4:]),
        (
            sds((rows, width), F32), sds((rows, width), BF), sds((rows, LANES), BF),
            sds((tensor_count, RANK, q_cols), BF), sds((LANES, width), F32),
        ),
        (
            out_whole((rows, width)), out_whole((rows, width)), out_whole((rows, LANES)),
            out_whole((tensor_count, RANK, q_cols)), out_whole((LANES, width)),
        ),
        [], 6 * rows * width * LANES, 20 * rows * width,
    )
    sent_ffn, _ = lax.optimization_barrier(([ffn_parts[d] for d in far], [two_terms[d] for d in far]))
    ffn_terms = [back_to(part, d) for part, d in zip(sent_ffn, far)]

    hidden_terms = lax.all_gather(hidden_terms.astype(BF), DP, axis=0, tiled=False)

    args = (
        place, kv_seq, grad_branch, grad_ro, grad_bo, rank_one, cos, sin,
        queries, mixed, probs, weights, b_pad, weights, b_pad,
    )
    sent_rows = rows + 4 * RANK
    send, grad_one, grad_rank = call(
        attn_back_kernel, "attention_back", tensor_count, args,
        [scalars()] + wholes(*args[1:4]) + [by_step(RANK, q_cols)] + wholes(*args[5:8])
        + [token_cols(q_cols), token_cols(q_cols), p_spec, o_spec, ob_spec, q_spec, qb_spec],
        (sds((parts, sent_rows, 2 * HD), BF), sds((rows, width), F32), sds((rows, LANES), F32)),
        (out_whole((parts, sent_rows, 2 * HD)), out_whole((rows, width)), out_whole((rows, LANES))),
        [
            pltpu.VMEM((span, rows), BF),
            pltpu.VMEM((span, HD), F32), pltpu.VMEM((span, HD), F32), pltpu.VMEM((HD, span), BF),
            pltpu.VMEM((LANES, rows), BF),
            pltpu.VMEM((rows, q_cols), BF), pltpu.VMEM((rows, q_cols), BF), pltpu.VMEM((span, 2 * HD), BF),
        ],
        2 * rows * heads_cols * (4 * span + 2 * width), 4 * width * heads_cols,
    )

    seq_terms = lax.all_to_all(send, SEQ, 0, 0, tiled=True)

    args = (normed_one, rank_one, b_kv, cos, sin, seq_terms, grad_rank, *wide_parts, wide_out)
    wide_term, kv_term, head_term, grad_key, grad_value, grad_rank = call(
        shared_kernel, "shared_head", 1, args, wholes(*args),
        (
            sds((width, LANES), BF), sds((2, RANK, HD), BF), sds((2 * RANK, q_cols), BF),
            sds((rows, HD), BF), sds((rows, HD), BF), sds((rows, LANES), BF),
        ),
        (
            out_whole((width, LANES)), out_whole((2, RANK, HD)), out_whole((2 * RANK, q_cols)),
            out_whole((rows, HD)), out_whole((rows, HD)), out_whole((rows, LANES)),
        ),
        [], 2 * rows * width * 128, 4 * rows * width,
    )

    own_rows = width // devices
    kv_terms = jnp.tile(kv_term.transpose(1, 0, 2), (devices // RANK, 1, 1))
    owned = jnp.concatenate(
        [wide_term.reshape(devices, own_rows, LANES), kv_terms, jnp.zeros((devices, 2, LANES), BF)], axis=1
    )
    terms = lax.all_to_all(owned, ALL, 0, 0, tiled=True)
    terms = terms.reshape(seqs, parts, RANK, LANES)
    head_terms = jnp.broadcast_to(head_term[None], (seqs, 2 * RANK, q_cols))
    head_terms = lax.all_to_all(head_terms, ("y", "x"), 0, 0, tiled=True)

    args = (
        tokens, gain_one, a_all, a_all, a_all, grad_key, grad_value, grad_rank, grad_one, grad_residual,
    )
    input_grad = call(
        input_kernel, "input_gradient", 1, args,
        wholes(*args[:2]) + [a_spec, wk_spec, wv_spec] + wholes(*args[5:]),
        sds((rows, width), F32), out_whole((rows, width)),
        [], 2 * rows * width * 384, 16 * rows * width,
    )

    ffn_out = ffn_parts[0]
    for term in ffn_terms:
        ffn_out = ffn_out + term.astype(F32)
    block_output = (residual + ffn_out).astype(BF)

    gate_up_adapter_grad, down_adapter_grad = pl.pallas_call(
        sum_hidden_kernel,
        name="sum_hidden",
        in_specs=[scalars()] + wholes(hidden_terms),
        out_specs=(out_whole((2, LANES, ff_cols)), out_whole((ff_cols, LANES))),
        out_shape=(sds((2, LANES, ff_cols), F32), sds((ff_cols, LANES), F32)),
        scratch_shapes=[pltpu.VMEM((adapters, RANK, 3 * ff_cols), F32)],
        compiler_params=pltpu.CompilerParams(vmem_limit_bytes=VMEM_LIMIT),
    )(adapter_ids, hidden_terms)

    own_adapter = ((dp * tensor_count + tensor) // RANK).astype(jnp.int32).reshape(1)
    wide_grad, kv_adapter_grad, q_adapter_grad, out_adapter_grad = pl.pallas_call(
        sum_wide_kernel,
        name="sum_wide",
        in_specs=[scalars(), scalars()] + wholes(terms, head_terms),
        out_specs=(
            out_whole((7, own_rows, LANES)), out_whole((2, 1, HD)), out_whole((LANES, q_cols)), out_whole((q_cols, LANES)),
        ),
        out_shape=(
            sds((7, own_rows, LANES), F32), sds((2, 1, HD), F32), sds((LANES, q_cols), F32), sds((q_cols, LANES), F32),
        ),
        scratch_shapes=[pltpu.VMEM((adapters, RANK, LANES), F32), pltpu.VMEM((adapters, 2 * RANK, q_cols), F32)],
        compiler_params=pltpu.CompilerParams(vmem_limit_bytes=VMEM_LIMIT),
    )(adapter_ids, own_adapter, terms, head_terms)
    return (
        block_output, input_grad, wide_grad, kv_adapter_grad,
        q_adapter_grad, out_adapter_grad, gate_up_adapter_grad, down_adapter_grad,
    )


def solution(mesh):
    dp_count, tensor_count = mesh.shape["dp"], mesh.shape["tensor"]
    chips = dp_count // 2
    x_count = math.isqrt(chips)
    devices = mesh.devices.reshape(chips // x_count, x_count, 2, tensor_count)
    return jax.shard_map(
        on_device,
        mesh=Mesh(devices, ALL),
        in_specs=(
            P(ALL, None), P(ALL, None), P(), P(), P(), P(DP, "tensor"), P(None, DP, None),
            P("tensor", DP), P(None, DP, "tensor"), P("tensor", DP), P(None, DP, None), P(),
            P(None, "tensor"), P("tensor", None), P(None, None, "tensor"), P("tensor", None),
        ),
        out_specs=(
            P(ALL, None), P(ALL, None), P(None, ALL, None), P(None, ALL, None),
            P(None, "tensor"), P("tensor", None), P(None, None, "tensor"), P("tensor", None),
        ),
        check_vma=False,
    )
```

```python
import functools
import math

import jax
import jax.numpy as jnp
from jax import lax
from jax.experimental import pallas as pl
from jax.experimental.pallas import tpu as pltpu
from jax.sharding import Mesh, PartitionSpec as P

HD = 128
WINDOW = 1024
RANK = 16
LANES = 128
EPS = 1e-06
MASKED = -1e30
SCALE = HD ** (-0.5)
GELU_C = 0.7978845608028654
GELU_A = 0.044715
VMEM_LIMIT = 58 * 1024 * 1024
BF = jnp.bfloat16
F32 = jnp.float32
DP = ("y", "x", "core")
SEQ = ("core", "tensor")
ALL = ("y", "x", "core", "tensor")

SLOT_Q, SLOT_K, SLOT_V, SLOT_G, SLOT_U, SLOT_O, SLOT_D = range(7)


def rows_of(slot):
    return slice(slot * RANK, (slot + 1) * RANK)


def mm(a, b):
    return lax.dot_general(a, b, (((1,), (0,)), ((), ())), preferred_element_type=F32)


def mm_nt(a, b):
    return lax.dot_general(a, b, (((1,), (1,)), ((), ())), preferred_element_type=F32)


def rope(v, cos, sin):
    return v * cos + pltpu.roll(v, HD // 2, 1) * sin


def rope_back(g, cos, sin):
    return g * cos - pltpu.roll(g, HD // 2, 1) * sin


def flat(ref):
    block = ref[...]
    return block.reshape(block.shape[0] * block.shape[2], block.shape[3])


def rms(v, gain):
    return v * lax.rsqrt(jnp.mean(v * v, axis=-1, keepdims=True) + EPS) * gain


def rms_back(v, gain, grad):
    inv = lax.rsqrt(jnp.mean(v * v, axis=-1, keepdims=True) + EPS)
    scaled = grad * gain
    dot = jnp.mean(v * scaled, axis=-1, keepdims=True)
    return inv * scaled - v * (inv * inv * inv * dot)


def pre_kernel(
    x_ref, gain_ref, a_ref, wk_ref, wv_ref, bkv_ref, cos_ref, sin_ref, wq_ref, bq_ref,
    n1_ref, r1_ref, kv_ref, q_ref,
):
    @pl.when(pl.program_id(0) == 0)
    def _():
        n1 = rms(x_ref[...].astype(F32), gain_ref[...]).astype(BF)
        n1_ref[...] = n1
        r1 = mm(n1, a_ref[...]).astype(BF)
        r1_ref[...] = r1
        key = mm(n1, wk_ref[...]) + mm(r1, bkv_ref[0])
        kv_ref[:, :HD] = rope(key, cos_ref[...], sin_ref[...]).astype(BF)
        kv_ref[:, HD:] = (mm(n1, wv_ref[...]) + mm(r1, bkv_ref[1])).astype(BF)

    lin = mm(n1_ref[...], flat(wq_ref)) + mm(r1_ref[...], bq_ref[0])
    for h in range(lin.shape[1] // HD):
        part = slice(h * HD, (h + 1) * HD)
        q_ref[:, part] = rope(lin[:, part], cos_ref[...], sin_ref[...]).astype(BF)


def fill_bias(bias_ref, kseg_ref, qseg_ref):
    shape = bias_ref.shape
    key = lax.broadcasted_iota(jnp.int32, shape, 0)
    query = lax.broadcasted_iota(jnp.int32, shape, 1)
    allowed = (key >= query) & (key <= query + WINDOW) & (kseg_ref[...] == qseg_ref[...])
    bias_ref[...] = jnp.where(allowed, 0.0, MASKED)


def fill_window(kv_ref, place_ref, seq_ref):
    rows = seq_ref.shape[1]
    reach = kv_ref.shape[0] // rows - 1
    own = place_ref[2] * (seq_ref.shape[0] // 2) + place_ref[3]
    for w in range(reach + 1):
        kv_ref[w * rows : (w + 1) * rows] = seq_ref[jnp.maximum(own - reach + w, 0)]


def attn_kernel(place_ref, seq_ref, kseg_ref, qseg_ref, q_ref, mixed_ref, p_ref, bias_ref, s_ref, vt_ref, kv_ref):
    step = pl.program_id(0)
    rows = q_ref.shape[0]
    chunks = kv_ref.shape[0] // rows

    @pl.when(step == 0)
    def _():
        fill_window(kv_ref, place_ref, seq_ref)
        fill_bias(bias_ref, kseg_ref, qseg_ref)
        vt_ref[...] = kv_ref[:, HD:].astype(F32).T.astype(BF)

    for h in range(q_ref.shape[1] // HD):
        part = slice(h * HD, (h + 1) * HD)
        query = q_ref[:, part]
        top = jnp.full((1, rows), MASKED, F32)
        for c in range(chunks):
            span = slice(c * rows, (c + 1) * rows)
            s = mm_nt(kv_ref[span, :HD], query) * SCALE + bias_ref[span]
            s_ref[span] = s
            top = jnp.maximum(top, jnp.max(s, axis=0, keepdims=True))
        total = jnp.zeros((1, rows), F32)
        for c in range(chunks):
            span = slice(c * rows, (c + 1) * rows)
            p = jnp.exp(s_ref[span] - top)
            total = total + jnp.sum(p, axis=0, keepdims=True)
            s_ref[span] = p
        inv = 1.0 / total
        for c in range(chunks):
            span = slice(c * rows, (c + 1) * rows)
            p_ref[h, span] = (s_ref[span] * inv).astype(BF)
        mixed_ref[:, part] = mm(vt_ref[...], p_ref[h]).T.astype(BF)


def out_kernel(
    x_ref, gain_ref, a_ref, mixed_ref, wo_ref, bo_ref, res_ref, n2_ref, ro_ref, acc_ref, rank_ref,
):
    step = pl.program_id(0)

    @pl.when(step == 0)
    def _():
        acc_ref[...] = jnp.zeros_like(acc_ref)
        rank_ref[...] = jnp.zeros_like(rank_ref)

    mixed = mixed_ref[...]
    acc_ref[...] += mm_nt(mixed, flat(wo_ref))
    rank_ref[...] += mm_nt(mixed, bo_ref[0])

    @pl.when(step == pl.num_programs(0) - 1)
    def _():
        ro = rank_ref[...].astype(BF)
        ro_ref[...] = ro
        res = x_ref[...].astype(F32) + (acc_ref[...] + mm_nt(ro, a_ref[...]))
        res_ref[...] = res
        n2_ref[...] = rms(res, gain_ref[...]).astype(BF)


def ffn_kernel(count, first, a_ref, b_ref, w_ref, *rest):
    n2_refs, cot_refs, rest = rest[:count], rest[count : 2 * count], rest[2 * count :]
    if not first:
        before_ref, rest = rest[0], rest[1:]
    g2_refs, ffn_refs, rest = rest[:count], rest[count : 2 * count], rest[2 * count :]
    gr_refs, rd_refs, rest = rest[:count], rest[count : 2 * count], rest[2 * count :]
    gb_ref, n2_ref, cot_ref, wv_ref, sems = rest
    ff = wv_ref.shape[2] - LANES
    copies = [
        pltpu.make_async_copy(w_ref.at[:, pl.ds(j * ff, ff)], wv_ref.at[j, :, pl.ds(0, ff)], sems.at[j])
        for j in range(3)
    ]
    for copy in copies:
        copy.start()
    wv_ref[0, :, ff:] = a_ref[...]
    wv_ref[2, :, ff:] = a_ref[...]
    rows = n2_refs[0].shape[0]
    for i in range(count):
        span = slice(i * rows, (i + 1) * rows)
        n2_ref[span] = n2_refs[i][...]
        cot_ref[span] = cot_refs[i][...]
    bg, bu, bd = (b_ref[:, j * ff : (j + 1) * ff] for j in range(3))
    copies[0].wait()
    lin = mm(n2_ref[...], wv_ref[0])
    r2t, r2 = lin[:, ff:].T.astype(BF), lin[:, ff:].astype(BF)
    gate = lin[:, :ff] + mm(r2, bg)
    copies[1].wait()
    up = mm(n2_ref[...], wv_ref[1, :, :ff]) + mm(r2, bu)
    copies[2].wait()
    lin = mm(cot_ref[...], wv_ref[2])
    grdt, grd = lin[:, ff:].T.astype(BF), lin[:, ff:].astype(BF)
    grad_hidden = (lin[:, :ff] + mm(grd, bd)).astype(BF).astype(F32)
    square = gate * gate
    th = jnp.tanh(GELU_C * (gate + GELU_A * square * gate))
    half = 0.5 * (1.0 + th)
    act = gate * half
    slope = half + 0.5 * gate * (1.0 - th * th) * (GELU_C * (1.0 + 3.0 * GELU_A * square))
    hidden = (act * up).astype(BF)
    grad_gate = (grad_hidden * up * slope).astype(BF)
    grad_up = (grad_hidden * act).astype(BF)
    gr = (mm_nt(grad_gate, bg) + mm_nt(grad_up, bu)).astype(BF)
    rd = mm_nt(hidden, bd).astype(BF)
    g2 = mm_nt(jnp.concatenate([grad_gate, gr], axis=1), wv_ref[0]) + mm_nt(grad_up, wv_ref[1, :, :ff])
    ffn = mm_nt(jnp.concatenate([hidden, rd], axis=1), wv_ref[2])
    for i in range(count):
        span = slice(i * rows, (i + 1) * rows)
        g2_refs[i][...] = g2[span].astype(g2_refs[i].dtype)
        ffn_refs[i][...] = ffn[span].astype(ffn_refs[i].dtype)
        gr_refs[i][...] = gr[span]
        rd_refs[i][...] = rd[span]
    terms = (
        mm(r2t[rows_of(SLOT_G)], grad_gate), mm(r2t[rows_of(SLOT_U)], grad_up), mm(grdt[rows_of(SLOT_D)], hidden)
    )
    for j, term in enumerate(terms):
        part = slice(j * ff, (j + 1) * ff)
        if not first:
            term = term + before_ref[:, part]
        gb_ref[:, part] = term.astype(gb_ref.dtype)


def wide_ffn_kernel(*refs):
    count = (len(refs) - 1) // 4
    total = None
    for left, right in zip(refs[: 2 * count], refs[2 * count : 4 * count]):
        term = mm(left[...].astype(F32).T.astype(BF), right[...])
        total = term if total is None else total + term
    refs[-1][...] = total


def residual_kernel(
    res_ref, cot_ref, gain_ref, a_ref, mixed_ref, ro_ref, own_ref, *rest,
):
    others, (gres_ref, gb_ref, gro_ref, gbo_ref, wide_ref) = rest[:-5], rest[-5:]
    grad_two = own_ref[...]
    for other_ref in others:
        grad_two = grad_two + other_ref[...].astype(F32)
    grad_res = cot_ref[...].astype(F32) + rms_back(res_ref[...], gain_ref[...], grad_two)
    gres_ref[...] = grad_res
    grad_branch = grad_res.astype(BF)
    gb_ref[...] = grad_branch
    gro = mm(grad_branch, a_ref[...])
    gro_ref[...] = gro.astype(BF)
    grot = gro.T[rows_of(SLOT_O)].astype(BF)
    cols = gbo_ref.shape[2]
    for t in range(gbo_ref.shape[0]):
        gbo_ref[t] = mm(grot, mixed_ref[:, t * cols : (t + 1) * cols]).astype(BF)
    wide_ref[...] = mm(ro_ref[...].astype(F32).T.astype(BF), grad_branch)


def attn_back_kernel(
    place_ref, seq_ref, gb_ref, gro_ref, gbo_ref, r1_ref, cos_ref, sin_ref,
    q_ref, mixed_ref, p_ref, wo_ref, bo_ref, wq_ref, bq_ref,
    send_ref, g1_ref, gr_ref,
    ds_ref, dk_ref, dv_ref, kt_ref, r1t_ref, gq_ref, gm_ref, kv_ref,
):
    step = pl.program_id(0)
    rows = q_ref.shape[0]
    chunks = kv_ref.shape[0] // rows

    @pl.when(step == 0)
    def _():
        fill_window(kv_ref, place_ref, seq_ref)
        kt_ref[...] = kv_ref[:, :HD].astype(F32).T.astype(BF)
        r1t_ref[...] = r1_ref[...].astype(F32).T.astype(BF)
        send_ref[...] = jnp.zeros_like(send_ref)
        dk_ref[...] = jnp.zeros_like(dk_ref)
        dv_ref[...] = jnp.zeros_like(dv_ref)
        g1_ref[...] = jnp.zeros_like(g1_ref)
        gr_ref[...] = jnp.zeros_like(gr_ref)

    gm_ref[...] = (mm(gb_ref[...], flat(wo_ref)) + mm(gro_ref[...], bo_ref[0])).astype(BF)
    for h in range(q_ref.shape[1] // HD):
        part = slice(h * HD, (h + 1) * HD)
        query, grad = q_ref[:, part], gm_ref[:, part]
        delta = grad.astype(F32) * mixed_ref[:, part].astype(F32)
        delta = jnp.sum(delta.T, axis=0, keepdims=True)
        for c in range(chunks):
            span = slice(c * rows, (c + 1) * rows)
            p = p_ref[h, span]
            dp = mm_nt(kv_ref[span, HD:], grad)
            ds = (p.astype(F32) * (dp - delta)).astype(BF)
            ds_ref[span] = ds
            dk_ref[span] += mm(ds, query)
            dv_ref[span] += mm(p, grad)
        dq = mm(kt_ref[...], ds_ref[...]) * SCALE
        gq_ref[:, part] = rope_back(dq.T, cos_ref[...], sin_ref[...]).astype(BF)

    gq = gq_ref[...]
    grad_bq = mm(r1t_ref[rows_of(SLOT_Q)], gq).astype(BF)
    for core in range(2):
        target = core * pl.num_programs(0) + step
        for j, term in enumerate((grad_bq, gbo_ref[0])):
            first = rows + 2 * j * RANK
            send_ref[target, first : first + RANK] = term[:, : 2 * HD]
            send_ref[target, first + RANK : first + 2 * RANK, :HD] = term[:, 2 * HD :]
    gr_ref[...] += mm_nt(gq, bq_ref[0])
    g1_ref[...] += mm_nt(gq, flat(wq_ref))

    @pl.when(step == pl.num_programs(0) - 1)
    def _():
        own = place_ref[2] * pl.num_programs(0) + place_ref[3]
        for w in range(chunks):
            target = own - (chunks - 1) + w
            span = slice(w * rows, (w + 1) * rows)

            @pl.when(target >= 0)
            def _(target=target, span=span):
                send_ref[target, :rows, :HD] = (dk_ref[span] * SCALE).astype(BF)
                send_ref[target, :rows, HD:] = dv_ref[span].astype(BF)


def shared_kernel(
    n1_ref, r1_ref, bkv_ref, cos_ref, sin_ref, terms_ref, gr_ref, *rest,
):
    wides, (wide_ref, kvg_ref, gqo_ref, gk_ref, gv_ref, grt_ref) = rest[:-6], rest[-6:]
    rows = n1_ref.shape[0]
    total = terms_ref[0].astype(F32)
    for source in range(1, terms_ref.shape[0]):
        total = total + terms_ref[source].astype(F32)
    for j in range(2):
        first = rows + 2 * j * RANK
        gqo_ref[rows_of(j), : 2 * HD] = total[first : first + RANK].astype(BF)
        gqo_ref[rows_of(j), 2 * HD :] = total[first + RANK : first + 2 * RANK, :HD].astype(BF)
    gk = rope_back(total[:rows, :HD], cos_ref[...], sin_ref[...]).astype(BF)
    gv = total[:rows, HD:].astype(BF)
    gk_ref[...] = gk
    gv_ref[...] = gv
    gr = gr_ref[...] + mm_nt(gk, bkv_ref[0]) + mm_nt(gv, bkv_ref[1])
    grt_ref[...] = gr.astype(BF)
    wide = mm(gr.T.astype(BF), n1_ref[...])
    for part_ref in wides:
        wide = wide + part_ref[...]
    wide_ref[...] = wide.T.astype(BF)
    r1t = r1_ref[...].astype(F32).T.astype(BF)
    kvg_ref[0] = mm(r1t[rows_of(SLOT_K)], gk).astype(BF)
    kvg_ref[1] = mm(r1t[rows_of(SLOT_V)], gv).astype(BF)


def input_kernel(
    x_ref, gain_ref, a_ref, wk_ref, wv_ref, gk_ref, gv_ref, gr_ref, g1_ref, gres_ref, grad_ref,
):
    g1 = g1_ref[...] + mm_nt(gk_ref[...], wk_ref[...]) + mm_nt(gv_ref[...], wv_ref[...])
    g1 = g1 + mm_nt(gr_ref[...], a_ref[...])
    x = x_ref[...].astype(F32)
    grad_ref[...] = gres_ref[...] + rms_back(x, gain_ref[...], g1)


def sum_hidden_kernel(ids_ref, terms_ref, gu_ref, down_ref, acc_ref):
    acc_ref[...] = jnp.zeros_like(acc_ref)
    adapters, rank, _ = acc_ref.shape
    for s in range(terms_ref.shape[0] // 2):
        acc_ref[ids_ref[s]] += terms_ref[2 * s].astype(F32) + terms_ref[2 * s + 1].astype(F32)
    ff = gu_ref.shape[2]

    def taken(j):
        return acc_ref[:, :, j * ff : (j + 1) * ff].reshape(adapters * rank, ff)

    gu_ref[0] = taken(0)
    gu_ref[1] = taken(1)
    down_ref[...] = taken(2).T


def sum_wide_kernel(ids_ref, own_ref, terms_ref, heads_ref, wide_ref, kv_ref, q_ref, out_ref, acc_ref, acch_ref):
    acc_ref[...] = jnp.zeros_like(acc_ref)
    acch_ref[...] = jnp.zeros_like(acch_ref)
    seqs, parts = terms_ref.shape[:2]
    for s in range(seqs):
        term = terms_ref[s, 0].astype(F32)
        for part in range(1, parts):
            term = term + terms_ref[s, part].astype(F32)
        acc_ref[ids_ref[s]] += term
        acch_ref[ids_ref[s]] += heads_ref[s].astype(F32)
    adapters, rank, _ = acc_ref.shape
    q_ref[...] = acch_ref[:, :RANK].reshape(q_ref.shape)
    out_ref[...] = acch_ref[:, RANK:].reshape(q_ref.shape).T
    lane = lax.broadcasted_iota(jnp.int32, (rank, LANES), 1) // RANK
    slots, own_rows = wide_ref.shape[:2]
    for j in range(slots):
        total = jnp.zeros((rank, LANES), F32)
        for a in range(adapters):
            turned = pltpu.roll(acc_ref[a], ((a - j) * RANK) % LANES, 1)
            total = jnp.where(lane == a, turned, total)
        wide_ref[j] = total[:own_rows]
    mine = acc_ref[own_ref[0]]
    for j in range(2):
        kv_ref[j] = mine[own_rows + j : own_rows + j + 1]


def scalars():
    return pl.BlockSpec(memory_space=pltpu.SMEM)


def whole(array):
    rank = len(array.shape)
    return pl.BlockSpec(array.shape, lambda *_: (0,) * rank)


def out_whole(shape):
    rank = len(shape)
    return pl.BlockSpec(shape, lambda *_: (0,) * rank)


def call(kernel, name, steps, args, specs, outs, out_specs, scratch, flops, nbytes):
    return pl.pallas_call(
        kernel,
        name=name,
        grid=(steps,),
        in_specs=specs,
        out_specs=out_specs,
        out_shape=outs,
        scratch_shapes=scratch,
        compiler_params=pltpu.CompilerParams(
            dimension_semantics=("arbitrary",), vmem_limit_bytes=VMEM_LIMIT
        ),
        cost_estimate=pl.CostEstimate(flops=flops, bytes_accessed=nbytes, transcendentals=0),
    )(*args)


def on_device(
    tokens, cotangent, segments, adapter_ids, norm_gains, q_weight, kv_weight, out_weight,
    gate_up_weight, down_weight, wide_adapters, kv_adapter, q_adapter, out_adapter,
    gate_up_adapter, down_adapter,
):
    rows, width = tokens.shape
    y_count, x_count, tensor_count = lax.axis_size("y"), lax.axis_size("x"), lax.axis_size("tensor")
    dp_count = 2 * x_count * y_count
    devices = dp_count * tensor_count
    group_rows = rows * tensor_count
    seq_length = 2 * group_rows
    shard_rows = q_weight.shape[0]
    q_cols, ff_cols = q_weight.shape[1], gate_up_weight.shape[2]
    seqs = adapter_ids.shape[0]
    adapters = wide_adapters.shape[2] // RANK
    dp = lax.axis_index(DP)
    tensor = lax.axis_index("tensor")
    my_core = lax.axis_index("core")
    place = jnp.stack([lax.axis_index("y"), lax.axis_index("x"), my_core, tensor]).astype(jnp.int32)
    adapter = lax.dynamic_index_in_dim(adapter_ids, dp // 2, keepdims=False)
    column = adapter * RANK

    def sds(shape, dtype):
        return jax.ShapeDtypeStruct(shape, dtype)

    pack = jnp.concatenate([q_weight, out_weight.T], axis=1)
    pack, wide_adapters, cotangent = lax.optimization_barrier((pack, wide_adapters, cotangent))
    weights = lax.all_gather(pack, ALL, axis=0, tiled=False)
    weights = weights.reshape(dp_count, tensor_count, shard_rows, 2 * q_cols)
    pack_ff = jnp.concatenate([gate_up_weight[0], gate_up_weight[1], down_weight.T], axis=1)

    def from_z(value, away):
        return lax.ppermute(value, "tensor", [((z + away) % tensor_count, z) for z in range(tensor_count)])

    cotangents = [cotangent] + [from_z(cotangent, d) for d in range(1, tensor_count)]

    wide = wide_adapters.reshape(7, shard_rows, adapters, RANK)
    wide = jnp.take(wide, adapter_ids, axis=2).transpose(2, 1, 0, 3)
    wide = wide.reshape(seqs, shard_rows, 7 * RANK)
    wide = jnp.pad(wide, ((0, 0), (0, 0), (0, LANES - 7 * RANK)))
    wide = jnp.repeat(wide, dp_count // seqs, axis=0)
    shared = jnp.broadcast_to(kv_weight[:, None], (2, dp_count, shard_rows, HD))
    wide = jnp.concatenate([wide, shared[0], shared[1]], axis=2)
    a_all = lax.all_to_all(wide, DP, 0, 0, tiled=True).reshape(width, 3 * LANES)

    def take_rows(matrix):
        return lax.dynamic_slice_in_dim(matrix, column, RANK, matrix.ndim - 2)

    def take_cols(matrix):
        return lax.dynamic_slice_in_dim(matrix, column, RANK, matrix.ndim - 1)

    def in_slot(block, slot):
        pads = [(0, 0)] * block.ndim
        pads[-2] = (slot * RANK, LANES - (slot + 1) * RANK)
        return jnp.pad(block, pads)

    gu_rows = take_rows(gate_up_adapter)
    b_ff = jnp.concatenate(
        [in_slot(gu_rows[0], SLOT_G), in_slot(gu_rows[1], SLOT_U), in_slot(take_cols(down_adapter).T, SLOT_D)], axis=1
    )
    b_own = jnp.concatenate([take_rows(q_adapter), take_cols(out_adapter).T], axis=1)
    b_own, _ = lax.optimization_barrier((b_own, a_all))
    b_all = lax.all_gather(b_own, "tensor", axis=0, tiled=False)
    pack_ff, weights, a_all, b_all, cotangents = lax.optimization_barrier(
        (pack_ff, weights, a_all, b_all, cotangents)
    )
    weights_ff = lax.all_gather(pack_ff, DP, axis=0, tiled=True)
    b_pad = jnp.concatenate(
        [in_slot(b_all[:, :, :q_cols], SLOT_Q), in_slot(b_all[:, :, q_cols:], SLOT_O)], axis=2
    )
    kv_rows = take_rows(kv_adapter)
    b_kv = jnp.stack([in_slot(kv_rows[0], SLOT_K), in_slot(kv_rows[1], SLOT_V)])

    start = dp * group_rows + tensor * rows
    positions = (start + jnp.arange(rows)) % seq_length
    half = HD // 2
    frequency = 10000.0 ** (-(jnp.arange(half).astype(F32) / half))
    angles = positions.astype(F32)[:, None] * frequency[None, :]
    cos, sin = jnp.cos(angles), jnp.sin(angles)
    cos = jnp.concatenate([cos, cos], axis=1)
    sin = jnp.concatenate([-sin, sin], axis=1)

    padded = jnp.concatenate([jnp.full((WINDOW,), -1, jnp.int32), segments])
    kseg = lax.dynamic_slice_in_dim(padded, start, WINDOW + rows, 0)
    qseg = kseg[WINDOW:].reshape(1, rows)
    kseg = kseg.reshape(WINDOW + rows, 1)
    span = WINDOW + rows

    gain_one, gain_two = norm_gains[0:1], norm_gains[1:2]

    def weight_spec(cols, block):
        return pl.BlockSpec((dp_count, 1, shard_rows, cols), lambda t: (0, t, 0, block))

    def adapter_spec(cols, block):
        return pl.BlockSpec((1, LANES, cols), lambda t: (t, 0, block))

    def token_cols(cols):
        return pl.BlockSpec((rows, cols), lambda t: (0, t))

    def by_step(*shape):
        return pl.BlockSpec((1,) + shape, lambda t: (t,) + (0,) * len(shape))

    heads_cols = tensor_count * q_cols
    q_spec, qb_spec = weight_spec(q_cols, 0), adapter_spec(q_cols, 0)
    o_spec, ob_spec = weight_spec(q_cols, 1), adapter_spec(q_cols, 1)

    def lane_block(block):
        return pl.BlockSpec((width, LANES), lambda *_: (0, block))

    a_spec, wk_spec, wv_spec = lane_block(0), lane_block(1), lane_block(2)

    def wholes(*arrays):
        return [whole(v) for v in arrays]

    args = (tokens, gain_one, a_all, a_all, a_all, b_kv, cos, sin, weights, b_pad)
    normed_one, rank_one, kv_own, queries = call(
        pre_kernel, "qkv", tensor_count, args,
        wholes(tokens, gain_one) + [a_spec, wk_spec, wv_spec] + wholes(b_kv, cos, sin) + [q_spec, qb_spec],
        (sds((rows, width), BF), sds((rows, LANES), BF), sds((rows, 2 * HD), BF), sds((rows, heads_cols), BF)),
        (out_whole((rows, width)), out_whole((rows, LANES)), out_whole((rows, 2 * HD)), token_cols(q_cols)),
        [], 2 * rows * width * (heads_cols + 384), 2 * width * heads_cols,
    )

    parts = seq_length // rows
    kv_seq = lax.all_to_all(jnp.broadcast_to(kv_own[None], (parts, rows, 2 * HD)), SEQ, 0, 0, tiled=True)

    args = (place, kv_seq, kseg, qseg, queries)
    q_heads = q_cols // HD
    p_spec = pl.BlockSpec((q_heads, span, rows), lambda t: (t, 0, 0))
    mixed, probs = call(
        attn_kernel, "attention", tensor_count, args,
        [scalars()] + wholes(*args[1:4]) + [token_cols(q_cols)],
        (sds((rows, heads_cols), BF), sds((tensor_count * q_heads, span, rows), BF)),
        (token_cols(q_cols), p_spec),
        [
            pltpu.VMEM((span, rows), F32), pltpu.VMEM((span, rows), F32), pltpu.VMEM((HD, span), BF),
            pltpu.VMEM((span, 2 * HD), BF),
        ],
        4 * rows * heads_cols * span, 2 * rows * heads_cols * span // HD,
    )

    args = (tokens, gain_two, a_all, mixed, weights, b_pad)
    residual, normed_two, rank_out = call(
        out_kernel, "out_projection", tensor_count, args,
        wholes(*args[:2]) + [a_spec, token_cols(q_cols), o_spec, ob_spec],
        (sds((rows, width), F32), sds((rows, width), BF), sds((rows, LANES), BF)),
        (out_whole((rows, width)), out_whole((rows, width)), out_whole((rows, LANES))),
        [pltpu.VMEM((rows, width), F32), pltpu.VMEM((rows, LANES), F32)],
        2 * rows * heads_cols * width, 2 * width * heads_cols,
    )

    normed = [normed_two] + [from_z(normed_two, d) for d in range(1, tensor_count)]

    def feed_forward(aways, before):
        count = len(aways)
        args = (a_all, b_ff, weights_ff, *(normed[d] for d in aways), *(cotangents[d] for d in aways), *before)
        kinds = [F32 if d == 0 else BF for d in aways] * 2
        outs = [sds((rows, width), kind) for kind in kinds] + [sds((rows, LANES), BF)] * (2 * count)
        outs.append(sds((RANK, 3 * ff_cols), BF if 0 in aways else F32))
        out = call(
            functools.partial(ffn_kernel, count, not before), "feed_forward", 1, args,
            [a_spec] + wholes(b_ff) + [pl.BlockSpec(memory_space=pl.ANY)] + wholes(*args[3:]),
            outs, [out_whole(v.shape) for v in outs],
            [
                pltpu.VMEM((count * rows, width), BF), pltpu.VMEM((count * rows, width), BF),
                pltpu.VMEM((3, width, ff_cols + LANES), BF), pltpu.SemaphoreType.DMA((3,)),
            ],
            12 * count * rows * width * ff_cols, 6 * width * ff_cols,
        )
        return [out[k * count : (k + 1) * count] for k in range(4)] + [out[-1]]

    def back_to(value, away):
        return lax.ppermute(value, "tensor", [(z, (z + away) % tensor_count) for z in range(tensor_count)])

    near = [1, tensor_count - 1]
    groups = [near, [d for d in range(2, tensor_count - 1)], [0]]
    two_terms, ffn_parts, rank_parts, wide_args, before = {}, {}, [], [], ()
    for group in groups:
        two, ffn, up_parts, down_parts, hidden_terms = feed_forward(group, before)
        before = (hidden_terms,)
        for i, d in enumerate(group):
            two_terms[d] = two[i] if d == 0 else back_to(two[i], d)
            ffn_parts[d] = ffn[i]
            rank_parts += [up_parts[i], down_parts[i]]
            wide_args += [normed[d], cotangents[d]]
    args = (*rank_parts, *wide_args)
    wide_ffn = call(
        wide_ffn_kernel, "wide_feed_forward", 1, args, wholes(*args), sds((LANES, width), F32),
        out_whole((LANES, width)), [], 4 * tensor_count * rows * width * LANES, 4 * tensor_count * rows * width,
    )
    far = range(1, tensor_count)

    args = (residual, cotangent, gain_two, a_all, mixed, rank_out, *(two_terms[d] for d in range(tensor_count)))
    grad_residual, grad_branch, grad_ro, grad_bo, wide_out = call(
        residual_kernel, "residual_gradient", 1, args,
        wholes(*args[:3]) + [a_spec] + wholes(*args[4:]),
        (
            sds((rows, width), F32), sds((rows, width), BF), sds((rows, LANES), BF),
            sds((tensor_count, RANK, q_cols), BF), sds((LANES, width), F32),
        ),
        (
            out_whole((rows, width)), out_whole((rows, width)), out_whole((rows, LANES)),
            out_whole((tensor_count, RANK, q_cols)), out_whole((LANES, width)),
        ),
        [], 6 * rows * width * LANES, 20 * rows * width,
    )
    sent_ffn, grad_branch = lax.optimization_barrier(([ffn_parts[d] for d in far], grad_branch))
    ffn_terms = [back_to(part, d) for part, d in zip(sent_ffn, far)]

    hidden_terms = lax.all_gather(hidden_terms, DP, axis=0, tiled=False)

    args = (
        place, kv_seq, grad_branch, grad_ro, grad_bo, rank_one, cos, sin,
        queries, mixed, probs, weights, b_pad, weights, b_pad,
    )
    sent_rows = rows + 4 * RANK
    send, grad_one, grad_rank = call(
        attn_back_kernel, "attention_back", tensor_count, args,
        [scalars()] + wholes(*args[1:4]) + [by_step(RANK, q_cols)] + wholes(*args[5:8])
        + [token_cols(q_cols), token_cols(q_cols), p_spec, o_spec, ob_spec, q_spec, qb_spec],
        (sds((parts, sent_rows, 2 * HD), BF), sds((rows, width), F32), sds((rows, LANES), F32)),
        (out_whole((parts, sent_rows, 2 * HD)), out_whole((rows, width)), out_whole((rows, LANES))),
        [
            pltpu.VMEM((span, rows), BF),
            pltpu.VMEM((span, HD), F32), pltpu.VMEM((span, HD), F32), pltpu.VMEM((HD, span), BF),
            pltpu.VMEM((LANES, rows), BF),
            pltpu.VMEM((rows, q_cols), BF), pltpu.VMEM((rows, q_cols), BF), pltpu.VMEM((span, 2 * HD), BF),
        ],
        2 * rows * heads_cols * (4 * span + 2 * width), 4 * width * heads_cols,
    )

    send, ffn_terms = lax.optimization_barrier((send, ffn_terms))
    seq_terms = lax.all_to_all(send, SEQ, 0, 0, tiled=True)

    args = (normed_one, rank_one, b_kv, cos, sin, seq_terms, grad_rank, wide_ffn, wide_out)
    wide_term, kv_term, head_term, grad_key, grad_value, grad_rank = call(
        shared_kernel, "shared_head", 1, args, wholes(*args),
        (
            sds((width, LANES), BF), sds((2, RANK, HD), BF), sds((2 * RANK, q_cols), BF),
            sds((rows, HD), BF), sds((rows, HD), BF), sds((rows, LANES), BF),
        ),
        (
            out_whole((width, LANES)), out_whole((2, RANK, HD)), out_whole((2 * RANK, q_cols)),
            out_whole((rows, HD)), out_whole((rows, HD)), out_whole((rows, LANES)),
        ),
        [], 2 * rows * width * 128, 4 * rows * width,
    )

    own_rows = width // devices
    kv_terms = jnp.tile(kv_term.transpose(1, 0, 2), (devices // RANK, 1, 1))
    owned = jnp.concatenate(
        [wide_term.reshape(devices, own_rows, LANES), kv_terms, jnp.zeros((devices, 2, LANES), BF)], axis=1
    )
    terms = lax.all_to_all(owned, ALL, 0, 0, tiled=True)
    terms = terms.reshape(seqs, parts, RANK, LANES)
    head_terms = jnp.broadcast_to(head_term[None], (seqs, 2 * RANK, q_cols))
    head_terms = lax.all_to_all(head_terms, ("y", "x"), 0, 0, tiled=True)

    args = (
        tokens, gain_one, a_all, a_all, a_all, grad_key, grad_value, grad_rank, grad_one, grad_residual,
    )
    input_grad = call(
        input_kernel, "input_gradient", 1, args,
        wholes(*args[:2]) + [a_spec, wk_spec, wv_spec] + wholes(*args[5:]),
        sds((rows, width), F32), out_whole((rows, width)),
        [], 2 * rows * width * 384, 16 * rows * width,
    )

    ffn_out = ffn_parts[0]
    for term in ffn_terms:
        ffn_out = ffn_out + term.astype(F32)
    block_output = (residual + ffn_out).astype(BF)

    gate_up_adapter_grad, down_adapter_grad = pl.pallas_call(
        sum_hidden_kernel,
        name="sum_hidden",
        in_specs=[scalars()] + wholes(hidden_terms),
        out_specs=(out_whole((2, LANES, ff_cols)), out_whole((ff_cols, LANES))),
        out_shape=(sds((2, LANES, ff_cols), F32), sds((ff_cols, LANES), F32)),
        scratch_shapes=[pltpu.VMEM((adapters, RANK, 3 * ff_cols), F32)],
        compiler_params=pltpu.CompilerParams(vmem_limit_bytes=VMEM_LIMIT),
    )(adapter_ids, hidden_terms)

    own_adapter = ((dp * tensor_count + tensor) // RANK).astype(jnp.int32).reshape(1)
    wide_grad, kv_adapter_grad, q_adapter_grad, out_adapter_grad = pl.pallas_call(
        sum_wide_kernel,
        name="sum_wide",
        in_specs=[scalars(), scalars()] + wholes(terms, head_terms),
        out_specs=(
            out_whole((7, own_rows, LANES)), out_whole((2, 1, HD)), out_whole((LANES, q_cols)), out_whole((q_cols, LANES)),
        ),
        out_shape=(
            sds((7, own_rows, LANES), F32), sds((2, 1, HD), F32), sds((LANES, q_cols), F32), sds((q_cols, LANES), F32),
        ),
        scratch_shapes=[pltpu.VMEM((adapters, RANK, LANES), F32), pltpu.VMEM((adapters, 2 * RANK, q_cols), F32)],
        compiler_params=pltpu.CompilerParams(vmem_limit_bytes=VMEM_LIMIT),
    )(adapter_ids, own_adapter, terms, head_terms)
    return (
        block_output, input_grad, wide_grad, kv_adapter_grad,
        q_adapter_grad, out_adapter_grad, gate_up_adapter_grad, down_adapter_grad,
    )


def solution(mesh):
    dp_count, tensor_count = mesh.shape["dp"], mesh.shape["tensor"]
    chips = dp_count // 2
    x_count = math.isqrt(chips)
    devices = mesh.devices.reshape(chips // x_count, x_count, 2, tensor_count)
    return jax.shard_map(
        on_device,
        mesh=Mesh(devices, ALL),
        in_specs=(
            P(ALL, None), P(ALL, None), P(), P(), P(), P(DP, "tensor"), P(None, DP, None),
            P("tensor", DP), P(None, DP, "tensor"), P("tensor", DP), P(None, DP, None), P(),
            P(None, "tensor"), P("tensor", None), P(None, None, "tensor"), P("tensor", None),
        ),
        out_specs=(
            P(ALL, None), P(ALL, None), P(None, ALL, None), P(None, ALL, None),
            P(None, "tensor"), P("tensor", None), P(None, None, "tensor"), P("tensor", None),
        ),
        check_vma=False,
    )
```

```python
import math

import jax
import jax.numpy as jnp
from jax import lax
from jax.experimental import pallas as pl
from jax.experimental.pallas import tpu as pltpu
from jax.sharding import Mesh, PartitionSpec as P

HD = 128
WINDOW = 1024
RANK = 16
LANES = 128
EPS = 1e-06
MASKED = -1e30
SCALE = HD ** (-0.5)
LOG2E = math.log2(math.e)
GELU_C = 0.7978845608028654
GELU_A = 0.044715
VMEM_LIMIT = 58 * 1024 * 1024
BF = jnp.bfloat16
F32 = jnp.float32
DP = ("y", "x", "core")
SEQ = ("core", "tensor")
ALL = ("y", "x", "core", "tensor")

SLOT_Q, SLOT_K, SLOT_V, SLOT_G, SLOT_U, SLOT_O, SLOT_D = range(7)


def rows_of(slot):
    return slice(slot * RANK, (slot + 1) * RANK)


def mm(a, b):
    return lax.dot_general(a, b, (((1,), (0,)), ((), ())), preferred_element_type=F32)


def mm_nt(a, b):
    return lax.dot_general(a, b, (((1,), (1,)), ((), ())), preferred_element_type=F32)


def turned(a):
    return a.astype(F32).T.astype(BF)


def rope(v, cos, sin):
    return v * cos + pltpu.roll(v, HD // 2, 1) * sin


def rope_back(g, cos, sin):
    return g * cos - pltpu.roll(g, HD // 2, 1) * sin


def flat(ref):
    block = ref[...]
    return block.reshape(block.shape[0] * block.shape[2], block.shape[3])


def rms(v, gain):
    return v * lax.rsqrt(jnp.mean(v * v, axis=-1, keepdims=True) + EPS) * gain


def rms_back(v, gain, grad):
    inv = lax.rsqrt(jnp.mean(v * v, axis=-1, keepdims=True) + EPS)
    scaled = grad * gain
    dot = jnp.mean(v * scaled, axis=-1, keepdims=True)
    return inv * scaled - v * (inv * inv * inv * dot)


def shared_kernel(x_ref, gain_ref, a_ref, wk_ref, wv_ref, bkv_ref, cos_ref, sin_ref, n1_ref, r1_ref, kv_ref):
    n1 = rms(x_ref[...].astype(F32), gain_ref[...]).astype(BF)
    n1_ref[...] = n1
    r1 = mm(n1, a_ref[...]).astype(BF)
    r1_ref[...] = r1
    key = mm(n1, wk_ref[...]) + mm(r1, bkv_ref[0])
    kv_ref[:, :HD] = rope(key, cos_ref[...], sin_ref[...]).astype(BF)
    kv_ref[:, HD:] = (mm(n1, wv_ref[...]) + mm(r1, bkv_ref[1])).astype(BF)


def fill_window(kv_ref, place_ref, seq_ref):
    rows = seq_ref.shape[1]
    reach = kv_ref.shape[0] // rows - 1
    own = place_ref[0] * (seq_ref.shape[0] // 2) + place_ref[1]
    for w in range(reach + 1):
        kv_ref[w * rows : (w + 1) * rows] = seq_ref[jnp.maximum(own - reach + w, 0)]


def attn_kernel(
    place_ref, seq_ref, kseg_ref, qseg_ref, n1_ref, r1_ref, cos_ref, sin_ref, x_ref, gain_ref, a_ref,
    wq_ref, bq_ref, wo_ref, bo_ref,
    q_ref, mixed_ref, p_ref, inv_ref, res_ref, n2_ref, r2_ref, ro_ref,
    bias_ref, s_ref, vt_ref, kv_ref, acc_ref, rank_ref,
):
    step = pl.program_id(0)
    rows = q_ref.shape[0]
    chunks = kv_ref.shape[0] // rows

    @pl.when(step == 0)
    def _():
        fill_window(kv_ref, place_ref, seq_ref)
        key = lax.broadcasted_iota(jnp.int32, bias_ref.shape, 0)
        query = lax.broadcasted_iota(jnp.int32, bias_ref.shape, 1)
        allowed = (key >= query) & (key <= query + WINDOW) & (kseg_ref[...] == qseg_ref[...])
        bias_ref[...] = jnp.where(allowed, 0.0, MASKED)
        vt_ref[...] = turned(kv_ref[:, HD:])
        acc_ref[...] = jnp.zeros_like(acc_ref)
        rank_ref[...] = jnp.zeros_like(rank_ref)

    lin = mm(n1_ref[...], flat(wq_ref)) + mm(r1_ref[...], bq_ref[0])
    for h in range(q_ref.shape[1] // HD):
        part = slice(h * HD, (h + 1) * HD)
        query = (rope(lin[:, part], cos_ref[...], sin_ref[...]) * (SCALE * LOG2E)).astype(BF)
        q_ref[:, part] = query
        top = jnp.full((1, rows), MASKED, F32)
        for c in range(chunks):
            span = slice(c * rows, (c + 1) * rows)
            s = mm_nt(kv_ref[span, :HD], query) + bias_ref[span]
            s_ref[span] = s
            top = jnp.maximum(top, jnp.max(s, axis=0, keepdims=True))
        total = jnp.zeros((1, rows), F32)
        for c in range(chunks):
            span = slice(c * rows, (c + 1) * rows)
            p = jnp.exp2(s_ref[span] - top)
            total = total + jnp.sum(p, axis=0, keepdims=True)
            p_ref[h, span] = p.astype(BF)
        inv = 1.0 / total
        inv_ref[0, h : h + 1] = inv
        mixed_ref[:, part] = (mm(vt_ref[...], p_ref[h]) * inv).T.astype(BF)

    mixed = mixed_ref[...]
    acc_ref[...] += mm_nt(mixed, flat(wo_ref))
    rank_ref[...] += mm_nt(mixed, bo_ref[0])

    @pl.when(step == pl.num_programs(0) - 1)
    def _():
        ro = rank_ref[...].astype(BF)
        ro_ref[...] = ro
        res = x_ref[...].astype(F32) + (acc_ref[...] + mm_nt(ro, a_ref[...]))
        res_ref[...] = res
        n2 = rms(res, gain_ref[...]).astype(BF)
        n2_ref[...] = n2
        r2_ref[...] = mm(n2, a_ref[...]).astype(BF)


def ffn_kernel(
    res_ref, n2_ref, r2_ref, cot_ref, gain_ref, mixed_ref, ro_ref, a_ref, b_ref, w_ref,
    out_ref, gres_ref, gb_ref, wide_ref, gro_ref, gbo_ref, gbh_ref,
    ffn_ref, g2_ref, rd_ref, gr_ref, r2t_ref, grd_ref, grdt_ref, wv_ref, sems,
):
    step = pl.program_id(0)
    last = pl.num_programs(0) - 1
    ff = b_ref.shape[2] // 3
    slot = lax.rem(step, 2)

    def copies(at, to):
        spans = (pl.ds(2 * ff, ff), pl.ds(0, 2 * ff))
        return [
            pltpu.make_async_copy(w_ref.at[:, at, :, cols], wv_ref.at[to, :, :, cols], sems.at[to, j])
            for j, cols in enumerate(spans)
        ]

    @pl.when(step == 0)
    def _():
        for copy in copies(0, 0):
            copy.start()
        ffn_ref[...] = jnp.zeros_like(ffn_ref)
        g2_ref[...] = jnp.zeros_like(g2_ref)
        rd_ref[...] = jnp.zeros_like(rd_ref)
        gr_ref[...] = jnp.zeros_like(gr_ref)
        r2t_ref[...] = turned(r2_ref[...])
        grd = mm(cot_ref[...], a_ref[...]).astype(BF)
        grd_ref[...] = grd
        grdt_ref[...] = turned(grd)

    @pl.when(step < last)
    def _():
        for copy in copies(step + 1, 1 - slot):
            copy.start()

    n2, r2, cot = n2_ref[...], r2_ref[...], cot_ref[...]
    b_gu, b_d = b_ref[0, :, : 2 * ff], b_ref[0, :, 2 * ff :]
    down, gate_up = copies(step, slot)
    rows_of_weight = wv_ref.shape[1] * wv_ref.shape[2]
    down.wait()
    w_d = wv_ref[slot, :, :, 2 * ff :].reshape(rows_of_weight, ff)
    grad_hidden = (mm(cot, w_d) + mm(grd_ref[...], b_d)).astype(BF).astype(F32)
    gate_up.wait()
    w_gu = wv_ref[slot, :, :, : 2 * ff].reshape(rows_of_weight, 2 * ff)
    lin = mm(n2, w_gu) + mm(r2, b_gu)
    gate, up = lin[:, :ff], lin[:, ff:]
    square = gate * gate
    th = jnp.tanh(GELU_C * (gate + GELU_A * square * gate))
    half = 0.5 * (1.0 + th)
    act = gate * half
    slope = half + 0.5 * gate * (1.0 - th * th) * (GELU_C * (1.0 + 3.0 * GELU_A * square))
    hidden = (act * up).astype(BF)
    grad_gate = (grad_hidden * up * slope).astype(BF)
    grad_up = (grad_hidden * act).astype(BF)
    grads = jnp.concatenate([grad_gate, grad_up], axis=1)
    ffn_ref[...] += mm_nt(hidden, w_d)
    rd_ref[...] += mm_nt(hidden, b_d)
    g2_ref[...] += mm_nt(grads, w_gu)
    gr_ref[...] += mm_nt(grads, b_gu)
    gbh_ref[0, :, :ff] = mm(r2t_ref[rows_of(SLOT_G)], grad_gate).astype(BF)
    gbh_ref[0, :, ff : 2 * ff] = mm(r2t_ref[rows_of(SLOT_U)], grad_up).astype(BF)
    gbh_ref[0, :, 2 * ff :] = mm(grdt_ref[rows_of(SLOT_D)], hidden).astype(BF)

    @pl.when(step == last)
    def _():
        rd = rd_ref[...].astype(BF)
        gr = gr_ref[...].astype(BF)
        res = res_ref[...]
        out_ref[...] = (res + (ffn_ref[...] + mm_nt(rd, a_ref[...]))).astype(BF)
        grad_two = g2_ref[...] + mm_nt(gr, a_ref[...])
        grad_res = cot_ref[...].astype(F32) + rms_back(res, gain_ref[...], grad_two)
        gres_ref[...] = grad_res
        grad_branch = grad_res.astype(BF)
        gb_ref[...] = grad_branch
        gro = mm(grad_branch, a_ref[...])
        gro_ref[...] = gro.astype(BF)
        grot = gro.T[rows_of(SLOT_O)].astype(BF)
        cols = gbo_ref.shape[2]
        for t in range(gbo_ref.shape[0]):
            gbo_ref[t] = mm(grot, mixed_ref[:, t * cols : (t + 1) * cols]).astype(BF)
        wide = mm(gr_ref[...].T.astype(BF), n2) + mm(rd_ref[...].T.astype(BF), cot)
        wide_ref[...] = wide + mm(turned(ro_ref[...]), grad_branch)


def attn_back_kernel(
    place_ref, seq_ref, gb_ref, gro_ref, r1_ref, cos_ref, sin_ref, cosw_ref, sinw_ref, a_ref, bkv_ref, widef_ref,
    n1a_ref, n1b_ref, n1c_ref, n1d_ref, n1e_ref,
    q_ref, mixed_ref, p_ref, inv_ref, wo_ref, bo_ref, wq_ref, bq_ref,
    dkv_ref, g1_ref, gr_ref, gbq_ref, wide_ref, kvg_ref,
    ds_ref, dk_ref, dv_ref, kt_ref, r1t_ref, gq_ref, gm_ref, kv_ref,
):
    step = pl.program_id(0)
    rows = q_ref.shape[0]
    chunks = kv_ref.shape[0] // rows

    @pl.when(step == 0)
    def _():
        fill_window(kv_ref, place_ref, seq_ref)
        kt_ref[...] = turned(kv_ref[:, :HD])
        r1t_ref[...] = turned(r1_ref[...])
        dk_ref[...] = jnp.zeros_like(dk_ref)
        dv_ref[...] = jnp.zeros_like(dv_ref)
        g1_ref[...] = jnp.zeros_like(g1_ref)
        gr_ref[...] = jnp.zeros_like(gr_ref)

    gm_ref[...] = (mm(gb_ref[...], flat(wo_ref)) + mm(gro_ref[...], bo_ref[0])).astype(BF)
    for h in range(q_ref.shape[1] // HD):
        part = slice(h * HD, (h + 1) * HD)
        query, grad = q_ref[:, part], gm_ref[:, part]
        delta = grad.astype(F32) * mixed_ref[:, part].astype(F32)
        delta = jnp.sum(delta.T, axis=0, keepdims=True)
        inv = inv_ref[0, h : h + 1]
        for c in range(chunks):
            span = slice(c * rows, (c + 1) * rows)
            p = p_ref[h, span].astype(F32) * inv
            dp = mm_nt(kv_ref[span, HD:], grad)
            ds = (p * (dp - delta)).astype(BF)
            ds_ref[span] = ds
            dk_ref[span] += mm(ds, query)
            dv_ref[span] += mm(p.astype(BF), grad)
        dq = mm(kt_ref[...], ds_ref[...]) * SCALE
        gq_ref[:, part] = rope_back(dq.T, cos_ref[...], sin_ref[...]).astype(BF)

    gq = gq_ref[...]
    gbq_ref[0] = mm(r1t_ref[rows_of(SLOT_Q)], gq).astype(BF)
    gr_ref[...] += mm_nt(gq, bq_ref[0])
    g1_ref[...] += mm_nt(gq, flat(wq_ref))

    @pl.when(step == pl.num_programs(0) - 1)
    def _():
        wide = widef_ref[...]
        kvg = [jnp.zeros((RANK, HD), F32), jnp.zeros((RANK, HD), F32)]
        n1_refs = (n1a_ref, n1b_ref, n1c_ref, n1d_ref, n1e_ref)
        for w, n1w_ref in enumerate(n1_refs):
            span = slice(w * rows, (w + 1) * rows)
            grad_key = dk_ref[span] * (1.0 / LOG2E)
            gv = dv_ref[span].astype(BF)
            dkv_ref[span, :HD] = grad_key.astype(BF)
            dkv_ref[span, HD:] = gv
            gk = rope_back(grad_key, cosw_ref[span], sinw_ref[span]).astype(BF)
            gr = mm_nt(gk, bkv_ref[0]) + mm_nt(gv, bkv_ref[1])
            if w == chunks - 1:
                gr = gr + gr_ref[...]
                r1t = r1t_ref[...]
            else:
                r1t = mm(n1w_ref[...], a_ref[...]).T.astype(BF)
            wide = wide + mm(gr.T.astype(BF), n1w_ref[...])
            kvg[0] = kvg[0] + mm(r1t[rows_of(SLOT_K)], gk)
            kvg[1] = kvg[1] + mm(r1t[rows_of(SLOT_V)], gv)
        wide_ref[...] = wide.T.astype(BF)
        kvg_ref[0] = kvg[0].astype(BF)
        kvg_ref[1] = kvg[1].astype(BF)


def input_kernel(
    x_ref, gain_ref, a_ref, wk_ref, wv_ref, bkv_ref, cos_ref, sin_ref,
    own_ref, back1_ref, back2_ref, back3_ref, back4_ref, gr_ref, g1_ref, gres_ref, grad_ref,
):
    gkv = own_ref[...].astype(F32)
    for back_ref in (back1_ref, back2_ref, back3_ref, back4_ref):
        gkv = gkv + back_ref[...].astype(F32)
    gk = rope_back(gkv[:, :HD], cos_ref[...], sin_ref[...]).astype(BF)
    gv = gkv[:, HD:].astype(BF)
    gr = gr_ref[...] + mm_nt(gk, bkv_ref[0]) + mm_nt(gv, bkv_ref[1])
    g1 = g1_ref[...] + mm_nt(gk, wk_ref[...]) + mm_nt(gv, wv_ref[...])
    g1 = g1 + mm_nt(gr.astype(BF), a_ref[...])
    x = x_ref[...].astype(F32)
    grad_ref[...] = gres_ref[...] + rms_back(x, gain_ref[...], g1)


def sum_hidden_kernel(ids_ref, terms_ref, gu_ref, down_ref, out_ref, acc_ref):
    acc_ref[...] = jnp.zeros_like(acc_ref)
    for s in range(terms_ref.shape[0] // 2):
        acc_ref[ids_ref[s]] += terms_ref[2 * s].astype(F32) + terms_ref[2 * s + 1].astype(F32)
    adapters, rank, cols = acc_ref.shape
    ff = gu_ref.shape[2]

    def taken(first, last):
        return acc_ref[:, :, first:last].reshape(adapters * rank, last - first)

    gu_ref[0] = taken(0, ff)
    gu_ref[1] = taken(ff, 2 * ff)
    down_ref[...] = taken(2 * ff, 3 * ff).T
    out_ref[...] = taken(3 * ff, cols).T


def sum_wide_kernel(ids_ref, own_ref, terms_ref, wide_ref, kv_ref, q_ref, acc_ref):
    acc_ref[...] = jnp.zeros_like(acc_ref)
    seqs, parts = terms_ref.shape[:2]
    for s in range(seqs):
        term = terms_ref[s, 0].astype(F32)
        for part in range(1, parts):
            term = term + terms_ref[s, part].astype(F32)
        acc_ref[ids_ref[s]] += term
    adapters, rank, _ = acc_ref.shape
    q_ref[...] = acc_ref[:, :, LANES:].reshape(q_ref.shape)
    lane = lax.broadcasted_iota(jnp.int32, (rank, LANES), 1) // RANK
    slots, own_rows = wide_ref.shape[:2]
    for j in range(slots):
        total = jnp.zeros((rank, LANES), F32)
        for a in range(adapters):
            moved = pltpu.roll(acc_ref[a, :, :LANES], ((a - j) * RANK) % LANES, 1)
            total = jnp.where(lane == a, moved, total)
        wide_ref[j] = total[:own_rows]
    mine = acc_ref[own_ref[0], :, :LANES]
    for j in range(2):
        kv_ref[j] = mine[own_rows + j : own_rows + j + 1]


def sds(shape, dtype):
    return jax.ShapeDtypeStruct(shape, dtype)


def scalars():
    return pl.BlockSpec(memory_space=pltpu.SMEM)


def whole(array):
    rank = len(array.shape)
    return pl.BlockSpec(array.shape, lambda *_: (0,) * rank)


def wholes(*arrays):
    return [whole(v) for v in arrays]


def by_step(*shape):
    return pl.BlockSpec((1,) + shape, lambda t: (t,) + (0,) * len(shape))


def call(kernel, name, steps, args, specs, outs, scratch, flops, nbytes):
    shapes = [shape for shape, _ in outs]
    return pl.pallas_call(
        kernel,
        name=name,
        grid=(steps,),
        in_specs=specs,
        out_specs=[whole(shape) if spec is None else spec for shape, spec in outs],
        out_shape=shapes,
        scratch_shapes=scratch,
        compiler_params=pltpu.CompilerParams(
            dimension_semantics=("arbitrary",), vmem_limit_bytes=VMEM_LIMIT
        ),
        cost_estimate=pl.CostEstimate(flops=flops, bytes_accessed=nbytes, transcendentals=0),
    )(*args)


def rope_tables(positions):
    half = HD // 2
    frequency = 10000.0 ** (-(jnp.arange(half).astype(F32) / half))
    angles = positions.astype(F32)[:, None] * frequency[None, :]
    cos, sin = jnp.cos(angles), jnp.sin(angles)
    return jnp.concatenate([cos, cos], axis=1), jnp.concatenate([-sin, sin], axis=1)


def on_device(
    tokens, cotangent, segments, adapter_ids, norm_gains, q_weight, kv_weight, out_weight,
    gate_up_weight, down_weight, wide_adapters, kv_adapter, q_adapter, out_adapter,
    gate_up_adapter, down_adapter,
):
    rows, width = tokens.shape
    tensor_count = lax.axis_size("tensor")
    dp_count = lax.axis_size("y") * lax.axis_size("x") * 2
    devices = dp_count * tensor_count
    group_rows = rows * tensor_count
    seq_length = 2 * group_rows
    shard_rows = q_weight.shape[0]
    q_cols, ff_cols = q_weight.shape[1], gate_up_weight.shape[2]
    heads_cols = tensor_count * q_cols
    seqs = adapter_ids.shape[0]
    adapters = wide_adapters.shape[2] // RANK
    dp = lax.axis_index(DP)
    tensor = lax.axis_index("tensor")
    place = jnp.stack([lax.axis_index("core"), tensor]).astype(jnp.int32)
    adapter = lax.dynamic_index_in_dim(adapter_ids, dp // 2, keepdims=False)
    column = adapter * RANK
    f3 = 3 * ff_cols

    pack = jnp.concatenate(
        [gate_up_weight[0], gate_up_weight[1], down_weight.T, q_weight, out_weight.T], axis=1
    )
    pack, wide_adapters = lax.optimization_barrier((pack, wide_adapters))
    weights = lax.all_gather(pack, ALL, axis=0, tiled=False)
    weights = weights.reshape(dp_count, tensor_count, shard_rows, f3 + 2 * q_cols)

    wide = wide_adapters.reshape(7, shard_rows, adapters, RANK)
    wide = jnp.take(wide, adapter_ids, axis=2).transpose(2, 1, 0, 3)
    wide = wide.reshape(seqs, shard_rows, 7 * RANK)
    wide = jnp.pad(wide, ((0, 0), (0, 0), (0, LANES - 7 * RANK)))
    wide = jnp.repeat(wide, dp_count // seqs, axis=0)
    shared = jnp.broadcast_to(kv_weight[:, None], (2, dp_count, shard_rows, HD))
    wide = jnp.concatenate([wide, shared[0], shared[1]], axis=2)
    a_all = lax.all_to_all(wide, DP, 0, 0, tiled=True).reshape(width, 3 * LANES)

    def take_rows(matrix):
        return lax.dynamic_slice_in_dim(matrix, column, RANK, matrix.ndim - 2)

    def take_cols(matrix):
        return lax.dynamic_slice_in_dim(matrix, column, RANK, matrix.ndim - 1)

    def in_slot(block, slot):
        pads = [(0, 0)] * block.ndim
        pads[-2] = (slot * RANK, LANES - (slot + 1) * RANK)
        return jnp.pad(block, pads)

    gu_rows = take_rows(gate_up_adapter)
    b_own = jnp.concatenate(
        [gu_rows[0], gu_rows[1], take_cols(down_adapter).T, take_rows(q_adapter), take_cols(out_adapter).T], axis=1
    )
    b_all = lax.all_gather(b_own, "tensor", axis=0, tiled=False)
    edges = [0, ff_cols, 2 * ff_cols, f3, f3 + q_cols, f3 + 2 * q_cols]
    b_pad = jnp.concatenate(
        [
            in_slot(b_all[:, :, first:last], slot)
            for first, last, slot in zip(edges, edges[1:], (SLOT_G, SLOT_U, SLOT_D, SLOT_Q, SLOT_O))
        ],
        axis=2,
    )
    kv_rows = take_rows(kv_adapter)
    b_kv = jnp.stack([in_slot(kv_rows[0], SLOT_K), in_slot(kv_rows[1], SLOT_V)])

    start = dp * group_rows + tensor * rows
    span = WINDOW + rows
    cos_window, sin_window = rope_tables((start - WINDOW + jnp.arange(span)) % seq_length)
    cos, sin = cos_window[WINDOW:], sin_window[WINDOW:]
    padded = jnp.concatenate([jnp.full((WINDOW,), -1, jnp.int32), segments])
    kseg = lax.dynamic_slice_in_dim(padded, start, span, 0)
    qseg = kseg[WINDOW:].reshape(1, rows)
    kseg = kseg.reshape(span, 1)

    gain_one, gain_two = norm_gains[0:1], norm_gains[1:2]
    q_block = f3 // q_cols

    def weight_spec(block):
        return pl.BlockSpec((dp_count, 1, shard_rows, q_cols), lambda t: (0, t, 0, block))

    def adapter_spec(block):
        return pl.BlockSpec((1, LANES, q_cols), lambda t: (t, 0, block))

    def lane_block(block):
        return pl.BlockSpec((width, LANES), lambda *_: (0, block))

    head_specs = [weight_spec(q_block), adapter_spec(q_block), weight_spec(q_block + 1), adapter_spec(q_block + 1)]
    q_spec, qb_spec, o_spec, ob_spec = head_specs
    a_spec, wk_spec, wv_spec = lane_block(0), lane_block(1), lane_block(2)
    token_cols = pl.BlockSpec((rows, q_cols), lambda t: (0, t))
    tok_bf, tok_f32, rank_bf = sds((rows, width), BF), sds((rows, width), F32), sds((rows, LANES), BF)

    args = (tokens, gain_one, a_all, a_all, a_all, b_kv, cos, sin)
    normed_one, rank_one, kv_own = call(
        shared_kernel, "keys_values", 1, args,
        wholes(*args[:2]) + [a_spec, wk_spec, wv_spec] + wholes(*args[5:]),
        [(tok_bf, None), (rank_bf, None), (sds((rows, 2 * HD), BF), None)],
        [], 2 * rows * width * 384, 6 * rows * width,
    )
    parts = seq_length // rows
    reach = WINDOW // rows
    kv_seq = lax.all_to_all(jnp.broadcast_to(kv_own[None], (parts, rows, 2 * HD)), SEQ, 0, 0, tiled=True)

    def moved(value, steps):
        return lax.ppermute(value, SEQ, [(c, c + steps) for c in range(parts) if 0 <= c + steps < parts])

    args = (
        place, kv_seq, kseg, qseg, normed_one, rank_one, cos, sin, tokens, gain_two, a_all,
        weights, b_pad, weights, b_pad,
    )
    heads = q_cols // HD
    p_spec = pl.BlockSpec((heads, span, rows), lambda t: (t, 0, 0))
    queries, mixed, probs, norms, residual, normed_two, rank_two, rank_out = call(
        attn_kernel, "attention", tensor_count, args,
        [scalars()] + wholes(*args[1:10]) + [a_spec] + head_specs,
        [
            (sds((rows, heads_cols), BF), token_cols), (sds((rows, heads_cols), BF), token_cols),
            (sds((tensor_count * heads, span, rows), BF), p_spec), (sds((tensor_count, 8, rows), F32), by_step(8, rows)),
            (tok_f32, None), (tok_bf, None), (rank_bf, None), (rank_bf, None),
        ],
        [
            pltpu.VMEM((span, rows), F32), pltpu.VMEM((span, rows), F32), pltpu.VMEM((HD, span), BF),
            pltpu.VMEM((span, 2 * HD), BF), pltpu.VMEM((rows, width), F32), pltpu.VMEM((rows, LANES), F32),
        ],
        4 * rows * heads_cols * (span + width), 4 * width * heads_cols,
    )

    sent_one, normed_two = lax.optimization_barrier((normed_one, normed_two))
    window_one = [moved(sent_one, d) for d in range(reach, 0, -1)]

    args = (
        residual, normed_two, rank_two, cotangent, gain_two, mixed, rank_out, a_all, b_pad, weights,
    )
    block_output, grad_residual, grad_branch, wide_ffn, grad_ro, grad_bo, grad_bh = call(
        ffn_kernel, "feed_forward", tensor_count, args,
        wholes(*args[:7]) + [a_spec, by_step(LANES, f3), pl.BlockSpec(memory_space=pl.ANY)],
        [
            (tok_bf, None), (tok_f32, None), (tok_bf, None), (sds((LANES, width), F32), None), (rank_bf, None),
            (sds((tensor_count, RANK, q_cols), BF), None), (sds((tensor_count, RANK, f3), BF), by_step(RANK, f3)),
        ],
        [
            pltpu.VMEM((rows, width), F32), pltpu.VMEM((rows, width), F32),
            pltpu.VMEM((rows, LANES), F32), pltpu.VMEM((rows, LANES), F32),
            pltpu.VMEM((LANES, rows), BF), pltpu.VMEM((rows, LANES), BF), pltpu.VMEM((LANES, rows), BF),
            pltpu.VMEM((2, dp_count, shard_rows, f3), BF), pltpu.SemaphoreType.DMA((2, 2)),
        ],
        12 * rows * width * tensor_count * ff_cols, 6 * width * tensor_count * ff_cols,
    )
    early = jnp.concatenate([grad_bh, grad_bo], axis=2)
    early = lax.psum_scatter(early, "tensor", scatter_dimension=0, tiled=True).reshape(RANK, -1)

    args = (
        place, kv_seq, grad_branch, grad_ro, rank_one, cos, sin, cos_window, sin_window, a_all, b_kv, wide_ffn,
        *window_one, normed_one, queries, mixed, probs, norms, weights, b_pad, weights, b_pad,
    )
    dkv, grad_one, grad_rank, grad_bq, wide_term, kv_term = call(
        attn_back_kernel, "attention_back", tensor_count, args,
        [scalars()] + wholes(*args[1:9]) + [a_spec] + wholes(*args[10:17])
        + [token_cols, token_cols, p_spec, by_step(8, rows), o_spec, ob_spec, q_spec, qb_spec],
        [
            (sds((span, 2 * HD), BF), None), (tok_f32, None), (sds((rows, LANES), F32), None),
            (sds((tensor_count, RANK, q_cols), BF), by_step(RANK, q_cols)),
            (sds((width, LANES), BF), None), (sds((2, RANK, HD), BF), None),
        ],
        [
            pltpu.VMEM((span, rows), BF),
            pltpu.VMEM((span, HD), F32), pltpu.VMEM((span, HD), F32), pltpu.VMEM((HD, span), BF),
            pltpu.VMEM((LANES, rows), BF),
            pltpu.VMEM((rows, q_cols), BF), pltpu.VMEM((rows, q_cols), BF), pltpu.VMEM((span, 2 * HD), BF),
        ],
        2 * rows * heads_cols * (4 * span + 2 * width), 4 * width * heads_cols,
    )

    own_rows = width // devices
    kv_terms = jnp.tile(kv_term.transpose(1, 0, 2), (devices // RANK, 1, 1))
    owned = jnp.concatenate(
        [wide_term.reshape(devices, own_rows, LANES), kv_terms, jnp.zeros((devices, 2, LANES), BF)], axis=1
    )
    every = jnp.broadcast_to(grad_bq[None], (dp_count, tensor_count, RANK, q_cols)).reshape(devices, RANK, q_cols)
    terms = lax.all_to_all(jnp.concatenate([owned, every], axis=2), ALL, 0, 0, tiled=True)
    terms = terms.reshape(seqs, parts, RANK, LANES + q_cols)

    backs = [moved(dkv[(reach - d) * rows : (reach - d + 1) * rows], -d) for d in range(1, reach + 1)]
    args = (
        tokens, gain_one, a_all, a_all, a_all, b_kv, cos, sin, dkv, *backs, grad_rank, grad_one, grad_residual,
    )
    (input_grad,) = call(
        input_kernel, "input_gradient", 1, args,
        wholes(*args[:2]) + [a_spec, wk_spec, wv_spec] + wholes(*args[5:8])
        + [pl.BlockSpec((rows, 2 * HD), lambda *_: (reach, 0))] + wholes(*args[9:]),
        [(tok_f32, None)], [], 2 * rows * width * 384, 16 * rows * width,
    )

    early, grad_one = lax.optimization_barrier((early, grad_one))
    early = lax.all_gather(early, DP, axis=0, tiled=False)
    gate_up_adapter_grad, down_adapter_grad, out_adapter_grad = call(
        sum_hidden_kernel, "sum_hidden", 1, (adapter_ids, early),
        [scalars()] + wholes(early),
        [(sds((2, LANES, ff_cols), F32), None), (sds((ff_cols, LANES), F32), None), (sds((q_cols, LANES), F32), None)],
        [pltpu.VMEM((adapters, RANK, f3 + q_cols), F32)], 0, 4 * LANES * f3,
    )
    own_adapter = ((dp * tensor_count + tensor) // RANK).astype(jnp.int32).reshape(1)
    wide_grad, kv_adapter_grad, q_adapter_grad = call(
        sum_wide_kernel, "sum_wide", 1, (adapter_ids, own_adapter, terms),
        [scalars(), scalars()] + wholes(terms),
        [(sds((7, own_rows, LANES), F32), None), (sds((2, 1, HD), F32), None), (sds((LANES, q_cols), F32), None)],
        [pltpu.VMEM((adapters, RANK, LANES + q_cols), F32)], 0, 4 * LANES * f3,
    )
    return (
        block_output, input_grad, wide_grad, kv_adapter_grad,
        q_adapter_grad, out_adapter_grad, gate_up_adapter_grad, down_adapter_grad,
    )


def solution(mesh):
    dp_count, tensor_count = mesh.shape["dp"], mesh.shape["tensor"]
    chips = dp_count // 2
    x_count = math.isqrt(chips)
    devices = mesh.devices.reshape(chips // x_count, x_count, 2, tensor_count)
    return jax.shard_map(
        on_device,
        mesh=Mesh(devices, ALL),
        in_specs=(
            P(ALL, None), P(ALL, None), P(), P(), P(), P(DP, "tensor"), P(None, DP, None),
            P("tensor", DP), P(None, DP, "tensor"), P("tensor", DP), P(None, DP, None), P(),
            P(None, "tensor"), P("tensor", None), P(None, None, "tensor"), P("tensor", None),
        ),
        out_specs=(
            P(ALL, None), P(ALL, None), P(None, ALL, None), P(None, ALL, None),
            P(None, "tensor"), P("tensor", None), P(None, None, "tensor"), P("tensor", None),
        ),
        check_vma=False,
    )
```

```python
import functools
import math

import jax
import jax.numpy as jnp
from jax import lax
from jax.experimental import pallas as pl
from jax.experimental.pallas import tpu as pltpu
from jax.sharding import Mesh, PartitionSpec as P

HD = 128
WINDOW = 1024
RANK = 16
LANES = 128
EPS = 1e-06
MASKED = -1e30
SCALE = HD ** (-0.5)
LOG2E = math.log2(math.e)
GELU_C = 0.7978845608028654
GELU_A = 0.044715
VMEM_LIMIT = 58 * 1024 * 1024
BF = jnp.bfloat16
F32 = jnp.float32
DP = ("y", "x", "core")
SEQ = ("core", "tensor")
PLANES = ("y", "x", "tensor")
ALL = ("y", "x", "core", "tensor")

SLOT_Q, SLOT_K, SLOT_V, SLOT_G, SLOT_U, SLOT_O, SLOT_D = range(7)


def rows_of(slot):
    return slice(slot * RANK, (slot + 1) * RANK)


def mm(a, b):
    return lax.dot_general(a, b, (((1,), (0,)), ((), ())), preferred_element_type=F32)


def mm_nt(a, b):
    return lax.dot_general(a, b, (((1,), (1,)), ((), ())), preferred_element_type=F32)


def turned(a):
    return a.astype(F32).T.astype(BF)


def rope(v, cos, sin):
    return v * cos + pltpu.roll(v, HD // 2, 1) * sin


def rope_back(g, cos, sin):
    return g * cos - pltpu.roll(g, HD // 2, 1) * sin


def flat(ref):
    block = ref[...]
    return block.reshape(block.shape[0] * block.shape[2], block.shape[3])


def rms(v, gain):
    return v * lax.rsqrt(jnp.mean(v * v, axis=-1, keepdims=True) + EPS) * gain


def rms_back(v, gain, grad):
    inv = lax.rsqrt(jnp.mean(v * v, axis=-1, keepdims=True) + EPS)
    scaled = grad * gain
    dot = jnp.mean(v * scaled, axis=-1, keepdims=True)
    return inv * scaled - v * (inv * inv * inv * dot)


def shared_kernel(x_ref, gain_ref, a_ref, wk_ref, wv_ref, bkv_ref, cos_ref, sin_ref, n1_ref, r1_ref, kv_ref):
    n1 = rms(x_ref[...].astype(F32), gain_ref[...]).astype(BF)
    n1_ref[...] = n1
    r1 = mm(n1, a_ref[...]).astype(BF)
    r1_ref[...] = r1
    key = mm(n1, wk_ref[...]) + mm(r1, bkv_ref[0])
    kv_ref[:, :HD] = rope(key, cos_ref[...], sin_ref[...]).astype(BF)
    kv_ref[:, HD:] = (mm(n1, wv_ref[...]) + mm(r1, bkv_ref[1])).astype(BF)


def attn_kernel(
    kv_ref, kseg_ref, qseg_ref, n1_ref, r1_ref, cos_ref, sin_ref, x_ref, gain_ref, a_ref,
    wq_ref, bq_ref, wo_ref, bo_ref,
    q_ref, mixed_ref, p_ref, inv_ref, res_ref, n2_ref, r2_ref, ro_ref,
    bias_ref, s_ref, vt_ref, acc_ref, rank_ref, qs_ref,
):
    step = pl.program_id(0)
    rows = q_ref.shape[0]
    chunks = kv_ref.shape[0] // rows

    @pl.when(step == 0)
    def _():
        key = lax.broadcasted_iota(jnp.int32, bias_ref.shape, 0)
        query = lax.broadcasted_iota(jnp.int32, bias_ref.shape, 1)
        allowed = (key >= query) & (key <= query + WINDOW) & (kseg_ref[...] == qseg_ref[...])
        bias_ref[...] = jnp.where(allowed, 0.0, MASKED)
        vt_ref[...] = turned(kv_ref[:, HD:])
        acc_ref[...] = jnp.zeros_like(acc_ref)
        rank_ref[...] = jnp.zeros_like(rank_ref)

    lin = mm(n1_ref[...], flat(wq_ref)) + mm(r1_ref[...], bq_ref[0])
    heads = q_ref.shape[1] // HD
    for h in range(heads):
        part = slice(h * HD, (h + 1) * HD)
        query = (rope(lin[:, part], cos_ref[...], sin_ref[...]) * (SCALE * LOG2E)).astype(BF)
        q_ref[:, part] = query
        qs_ref[h * rows : (h + 1) * rows] = query
    queries = qs_ref[...]
    top = jnp.full((1, heads * rows), MASKED, F32)
    for c in range(chunks):
        span = slice(c * rows, (c + 1) * rows)
        s = mm_nt(kv_ref[span, :HD], queries)
        bias = bias_ref[span]
        s = jnp.concatenate([s[:, h * rows : (h + 1) * rows] + bias for h in range(heads)], axis=1)
        s_ref[span] = s
        top = jnp.maximum(top, jnp.max(s, axis=0, keepdims=True))
    total = jnp.zeros((1, heads * rows), F32)
    for c in range(chunks):
        span = slice(c * rows, (c + 1) * rows)
        p = jnp.exp2(s_ref[span] - top)
        total = total + jnp.sum(p, axis=0, keepdims=True)
        p_ref[0, span] = p.astype(BF)
    inv = 1.0 / total
    inv_ref[0, 0:1] = inv
    out = mm(vt_ref[...], p_ref[0]) * inv
    for h in range(heads):
        mixed_ref[:, h * HD : (h + 1) * HD] = out[:, h * rows : (h + 1) * rows].T.astype(BF)

    mixed = mixed_ref[...]
    acc_ref[...] += mm_nt(mixed, flat(wo_ref))
    rank_ref[...] += mm_nt(mixed, bo_ref[0])

    @pl.when(step == pl.num_programs(0) - 1)
    def _():
        ro = rank_ref[...].astype(BF)
        ro_ref[...] = ro
        res = x_ref[...].astype(F32) + (acc_ref[...] + mm_nt(ro, a_ref[...]))
        res_ref[...] = res
        n2 = rms(res, gain_ref[...]).astype(BF)
        n2_ref[...] = n2
        r2_ref[...] = mm(n2, a_ref[...]).astype(BF)


def ffn_kernel(
    res_ref, n2_ref, r2_ref, cot_ref, gain_ref, mixed_ref, ro_ref, a_ref, b_ref, w_ref,
    out_ref, gres_ref, gb_ref, wide_ref, gro_ref, gbo_ref, gbh_ref,
    ffn_ref, g2_ref, rd_ref, gr_ref, r2t_ref, grd_ref, grdt_ref, wv_ref, sems,
):
    step = pl.program_id(0)
    steps = pl.num_programs(0)
    tensor_count = w_ref.shape[1]
    ff = b_ref.shape[2] // 3
    part = ff // tensor_count
    slot = lax.rem(step, 2)

    def copies(at, to):
        moves = []
        for kind in (2, 0, 1):
            for t in range(tensor_count):
                source = pl.multiple_of((kind * steps + at) * part, LANES)
                target = (kind * tensor_count + t) * part
                moves.append(
                    pltpu.make_async_copy(
                        w_ref.at[:, t, :, pl.ds(source, part)],
                        wv_ref.at[to, :, :, pl.ds(target, part)],
                        sems.at[to, len(moves)],
                    )
                )
        return moves

    @pl.when(step == 0)
    def _():
        for copy in copies(0, 0):
            copy.start()
        ffn_ref[...] = jnp.zeros_like(ffn_ref)
        g2_ref[...] = jnp.zeros_like(g2_ref)
        rd_ref[...] = jnp.zeros_like(rd_ref)
        gr_ref[...] = jnp.zeros_like(gr_ref)
        r2t_ref[...] = turned(r2_ref[...])
        grd = mm(cot_ref[...], a_ref[...]).astype(BF)
        grd_ref[...] = grd
        grdt_ref[...] = turned(grd)

    @pl.when(step < steps - 1)
    def _():
        for copy in copies(step + 1, 1 - slot):
            copy.start()

    n2, r2, cot = n2_ref[...], r2_ref[...], cot_ref[...]
    b_gu, b_d = b_ref[0, :, : 2 * ff], b_ref[0, :, 2 * ff :]
    arrivals = copies(step, slot)
    rows_of_weight = wv_ref.shape[1] * wv_ref.shape[2]
    for copy in arrivals[:tensor_count]:
        copy.wait()
    w_d = wv_ref[slot, :, :, 2 * ff :].reshape(rows_of_weight, ff)
    grad_hidden = (mm(cot, w_d) + mm(grd_ref[...], b_d)).astype(BF).astype(F32)
    for copy in arrivals[tensor_count:]:
        copy.wait()
    w_gu = wv_ref[slot, :, :, : 2 * ff].reshape(rows_of_weight, 2 * ff)
    lin = mm(n2, w_gu) + mm(r2, b_gu)
    gate, up = lin[:, :ff], lin[:, ff:]
    square = gate * gate
    th = jnp.tanh(GELU_C * (gate + GELU_A * square * gate))
    half = 0.5 * (1.0 + th)
    act = gate * half
    slope = half + 0.5 * gate * (1.0 - th * th) * (GELU_C * (1.0 + 3.0 * GELU_A * square))
    hidden = (act * up).astype(BF)
    grad_gate = (grad_hidden * up * slope).astype(BF)
    grad_up = (grad_hidden * act).astype(BF)
    grads = jnp.concatenate([grad_gate, grad_up], axis=1)
    ffn_ref[...] += mm_nt(hidden, w_d)
    rd_ref[...] += mm_nt(hidden, b_d)
    g2_ref[...] += mm_nt(grads, w_gu)
    gr_ref[...] += mm_nt(grads, b_gu)
    terms = (
        mm(r2t_ref[rows_of(SLOT_G)], grad_gate), mm(r2t_ref[rows_of(SLOT_U)], grad_up),
        mm(grdt_ref[rows_of(SLOT_D)], hidden),
    )
    for kind, term in enumerate(terms):
        target = pl.multiple_of((kind * steps + step) * part, LANES)
        for t in range(tensor_count):
            gbh_ref[t, :, pl.ds(target, part)] = term[:, t * part : (t + 1) * part].astype(BF)

    @pl.when(step == steps - 1)
    def _():
        rd = rd_ref[...].astype(BF)
        gr = gr_ref[...].astype(BF)
        res = res_ref[...]
        out_ref[...] = (res + (ffn_ref[...] + mm_nt(rd, a_ref[...]))).astype(BF)
        grad_two = g2_ref[...] + mm_nt(gr, a_ref[...])
        grad_res = cot_ref[...].astype(F32) + rms_back(res, gain_ref[...], grad_two)
        gres_ref[...] = grad_res
        grad_branch = grad_res.astype(BF)
        gb_ref[...] = grad_branch
        gro = mm(grad_branch, a_ref[...])
        gro_ref[...] = gro.astype(BF)
        grot = gro.T[rows_of(SLOT_O)].astype(BF)
        cols = gbo_ref.shape[2]
        for t in range(gbo_ref.shape[0]):
            gbo_ref[t] = mm(grot, mixed_ref[:, t * cols : (t + 1) * cols]).astype(BF)
        wide = mm(gr_ref[...].T.astype(BF), n2) + mm(rd_ref[...].T.astype(BF), cot)
        wide_ref[...] = wide + mm(turned(ro_ref[...]), grad_branch)


def attn_back_kernel(
    kv_ref, gb_ref, gro_ref, r1_ref, cos_ref, sin_ref,
    q_ref, mixed_ref, p_ref, inv_ref, wo_ref, bo_ref, wq_ref, bq_ref,
    dkv_ref, g1_ref, gr_ref, gbq_ref,
    ds_ref, dk_ref, dv_ref, kt_ref, r1t_ref, gq_ref, gm_ref, qs_ref, gs_ref,
):
    step = pl.program_id(0)
    rows = q_ref.shape[0]
    chunks = kv_ref.shape[0] // rows

    @pl.when(step == 0)
    def _():
        kt_ref[...] = turned(kv_ref[:, :HD])
        r1t_ref[...] = turned(r1_ref[...])
        dk_ref[...] = jnp.zeros_like(dk_ref)
        dv_ref[...] = jnp.zeros_like(dv_ref)
        g1_ref[...] = jnp.zeros_like(g1_ref)
        gr_ref[...] = jnp.zeros_like(gr_ref)

    gm_ref[...] = (mm(gb_ref[...], flat(wo_ref)) + mm(gro_ref[...], bo_ref[0])).astype(BF)
    heads = q_ref.shape[1] // HD
    deltas = []
    for h in range(heads):
        part, span = slice(h * HD, (h + 1) * HD), slice(h * rows, (h + 1) * rows)
        grad = gm_ref[:, part]
        qs_ref[span] = q_ref[:, part]
        gs_ref[span] = grad
        delta = grad.astype(F32) * mixed_ref[:, part].astype(F32)
        deltas.append(jnp.sum(delta.T, axis=0, keepdims=True))
    delta, inv = jnp.concatenate(deltas, axis=1), inv_ref[0, 0:1]
    queries, grads = qs_ref[...], gs_ref[...]
    for c in range(chunks):
        span = slice(c * rows, (c + 1) * rows)
        p = p_ref[0, span].astype(F32) * inv
        dp = mm_nt(kv_ref[span, HD:], grads)
        ds = (p * (dp - delta)).astype(BF)
        ds_ref[span] = ds
        dk_ref[span] += mm(ds, queries)
        dv_ref[span] += mm(p.astype(BF), grads)
    dq = mm(kt_ref[...], ds_ref[...]) * SCALE
    for h in range(heads):
        part, span = slice(h * HD, (h + 1) * HD), slice(h * rows, (h + 1) * rows)
        gq_ref[:, part] = rope_back(dq[:, span].T, cos_ref[...], sin_ref[...]).astype(BF)

    gq = gq_ref[...]
    gbq_ref[0] = mm(r1t_ref[rows_of(SLOT_Q)], gq).astype(BF)
    gr_ref[...] += mm_nt(gq, bq_ref[0])
    g1_ref[...] += mm_nt(gq, flat(wq_ref))

    @pl.when(step == pl.num_programs(0) - 1)
    def _():
        dkv_ref[:, :HD] = (dk_ref[...] * (1.0 / LOG2E)).astype(BF)
        dkv_ref[:, HD:] = dv_ref[...].astype(BF)


def shared_back_kernel(
    chips, core_ref, n1_ref, r1_ref, bkv_ref, cos_ref, sin_ref, own_ref, back1_ref, back2_ref, back3_ref, back4_ref,
    gr_ref, widef_ref,
    mine_ref, theirs_ref, gk_ref, gv_ref, grt_ref,
):
    gkv = own_ref[...].astype(F32)
    for back_ref in (back1_ref, back2_ref, back3_ref, back4_ref):
        gkv = gkv + back_ref[...].astype(F32)
    gk = rope_back(gkv[:, :HD], cos_ref[...], sin_ref[...]).astype(BF)
    gv = gkv[:, HD:].astype(BF)
    gk_ref[...] = gk
    gv_ref[...] = gv
    gr = gr_ref[...] + mm_nt(gk, bkv_ref[0]) + mm_nt(gv, bkv_ref[1])
    grt_ref[...] = gr.astype(BF)
    wide = (mm(gr.T.astype(BF), n1_ref[...]) + widef_ref[...]).T.astype(BF)
    share = mine_ref.shape[0] - 2 * RANK
    wide = wide.reshape(chips, 2, share // chips, LANES)
    first = core_ref[0] == 0
    mine_ref[:share] = jnp.where(first, wide[:, 0], wide[:, 1]).reshape(share, LANES)
    theirs_ref[:share] = jnp.where(first, wide[:, 1], wide[:, 0]).reshape(share, LANES)
    r1t = turned(r1_ref[...])
    for j, (slot, grad) in enumerate(((SLOT_K, gk), (SLOT_V, gv))):
        term = mm(r1t[rows_of(slot)], grad).astype(BF)
        rows = slice(share + j * RANK, share + (j + 1) * RANK)
        mine_ref[rows] = term
        theirs_ref[rows] = term


def input_kernel(
    x_ref, gain_ref, a_ref, wk_ref, wv_ref, gk_ref, gv_ref, gr_ref, g1_ref, gres_ref, grad_ref,
):
    g1 = g1_ref[...] + mm_nt(gk_ref[...], wk_ref[...]) + mm_nt(gv_ref[...], wv_ref[...])
    g1 = g1 + mm_nt(gr_ref[...], a_ref[...])
    x = x_ref[...].astype(F32)
    grad_ref[...] = gres_ref[...] + rms_back(x, gain_ref[...], g1)


def sum_hidden_kernel(ids_ref, terms_ref, gu_ref, down_ref, out_ref, acc_ref):
    acc_ref[...] = jnp.zeros_like(acc_ref)
    for s in range(terms_ref.shape[0] // 2):
        acc_ref[ids_ref[s]] += terms_ref[2 * s].astype(F32) + terms_ref[2 * s + 1].astype(F32)
    adapters, rank, cols = acc_ref.shape
    ff = gu_ref.shape[2]

    def taken(first, last):
        return acc_ref[:, :, first:last].reshape(adapters * rank, last - first)

    gu_ref[0] = taken(0, ff)
    gu_ref[1] = taken(ff, 2 * ff)
    down_ref[...] = taken(2 * ff, 3 * ff).T
    out_ref[...] = taken(3 * ff, cols).T


def sum_wide_kernel(ids_ref, own_ref, terms_ref, wide_ref, kv_ref, q_ref, acc_ref):
    acc_ref[...] = jnp.zeros_like(acc_ref)
    seqs, parts = terms_ref.shape[:2]
    for s in range(seqs):
        term = terms_ref[s, 0].astype(F32)
        for part in range(1, parts):
            term = term + terms_ref[s, part].astype(F32)
        acc_ref[ids_ref[s]] += term
    adapters, rank, _ = acc_ref.shape
    q_ref[...] = acc_ref[:, :, LANES:].reshape(q_ref.shape)
    lane = lax.broadcasted_iota(jnp.int32, (rank, LANES), 1) // RANK
    slots, own_rows = wide_ref.shape[:2]
    for j in range(slots):
        total = jnp.zeros((rank, LANES), F32)
        for a in range(adapters):
            moved = pltpu.roll(acc_ref[a, :, :LANES], ((a - j) * RANK) % LANES, 1)
            total = jnp.where(lane == a, moved, total)
        wide_ref[j] = total[:own_rows]
    mine = acc_ref[own_ref[0], :, :LANES]
    for j in range(2):
        kv_ref[j] = mine[own_rows + j : own_rows + j + 1]


def sds(shape, dtype):
    return jax.ShapeDtypeStruct(shape, dtype)


def scalars():
    return pl.BlockSpec(memory_space=pltpu.SMEM)


def whole(array):
    rank = len(array.shape)
    return pl.BlockSpec(array.shape, lambda *_: (0,) * rank)


def wholes(*arrays):
    return [whole(v) for v in arrays]


def by_step(*shape):
    return pl.BlockSpec((1,) + shape, lambda t: (t,) + (0,) * len(shape))


def call(kernel, name, steps, args, specs, outs, scratch, flops, nbytes):
    shapes = [shape for shape, _ in outs]
    return pl.pallas_call(
        kernel,
        name=name,
        grid=(steps,),
        in_specs=specs,
        out_specs=[whole(shape) if spec is None else spec for shape, spec in outs],
        out_shape=shapes,
        scratch_shapes=scratch,
        compiler_params=pltpu.CompilerParams(
            dimension_semantics=("arbitrary",), vmem_limit_bytes=VMEM_LIMIT
        ),
        cost_estimate=pl.CostEstimate(flops=flops, bytes_accessed=nbytes, transcendentals=0),
    )(*args)


def rope_tables(positions):
    half = HD // 2
    frequency = 10000.0 ** (-(jnp.arange(half).astype(F32) / half))
    angles = positions.astype(F32)[:, None] * frequency[None, :]
    cos, sin = jnp.cos(angles), jnp.sin(angles)
    return jnp.concatenate([cos, cos], axis=1), jnp.concatenate([-sin, sin], axis=1)


def on_device(
    tokens, cotangent, segments, adapter_ids, norm_gains, q_weight, kv_weight, out_weight,
    gate_up_weight, down_weight, wide_adapters, kv_adapter, q_adapter, out_adapter,
    gate_up_adapter, down_adapter,
):
    rows, width = tokens.shape
    tensor_count = lax.axis_size("tensor")
    dp_count = lax.axis_size("y") * lax.axis_size("x") * 2
    devices = dp_count * tensor_count
    group_rows = rows * tensor_count
    seq_length = 2 * group_rows
    shard_rows = q_weight.shape[0]
    q_cols, ff_cols = q_weight.shape[1], gate_up_weight.shape[2]
    heads_cols = tensor_count * q_cols
    seqs = adapter_ids.shape[0]
    adapters = wide_adapters.shape[2] // RANK
    dp = lax.axis_index(DP)
    tensor = lax.axis_index("tensor")
    my_core = lax.axis_index("core")
    adapter = lax.dynamic_index_in_dim(adapter_ids, dp // 2, keepdims=False)
    column = adapter * RANK
    f3 = 3 * ff_cols

    pack = jnp.concatenate(
        [gate_up_weight[0], gate_up_weight[1], down_weight.T, q_weight, out_weight.T], axis=1
    )
    pack, wide_adapters = lax.optimization_barrier((pack, wide_adapters))
    weights = lax.all_gather(pack, ALL, axis=0, tiled=False)
    weights = weights.reshape(dp_count, tensor_count, shard_rows, f3 + 2 * q_cols)

    wide = wide_adapters.reshape(7, shard_rows, adapters, RANK)
    wide = jnp.take(wide, adapter_ids, axis=2).transpose(2, 1, 0, 3)
    wide = wide.reshape(seqs, shard_rows, 7 * RANK)
    wide = jnp.pad(wide, ((0, 0), (0, 0), (0, LANES - 7 * RANK)))
    wide = jnp.repeat(wide, dp_count // seqs, axis=0)
    shared = jnp.broadcast_to(kv_weight[:, None], (2, dp_count, shard_rows, HD))
    wide = jnp.concatenate([wide, shared[0], shared[1]], axis=2)
    a_all = lax.all_to_all(wide, DP, 0, 0, tiled=True).reshape(width, 3 * LANES)

    def take_rows(matrix):
        return lax.dynamic_slice_in_dim(matrix, column, RANK, matrix.ndim - 2)

    def take_cols(matrix):
        return lax.dynamic_slice_in_dim(matrix, column, RANK, matrix.ndim - 1)

    def in_slot(block, slot):
        pads = [(0, 0)] * block.ndim
        pads[-2] = (slot * RANK, LANES - (slot + 1) * RANK)
        return jnp.pad(block, pads)

    gu_rows = take_rows(gate_up_adapter)
    b_own = jnp.concatenate(
        [gu_rows[0], gu_rows[1], take_cols(down_adapter).T, take_rows(q_adapter), take_cols(out_adapter).T], axis=1
    )
    kv_rows = take_rows(kv_adapter)
    b_kv = jnp.stack([in_slot(kv_rows[0], SLOT_K), in_slot(kv_rows[1], SLOT_V)])

    start = dp * group_rows + tensor * rows
    span = WINDOW + rows
    cos_window, sin_window = rope_tables((start - WINDOW + jnp.arange(span)) % seq_length)
    cos, sin = cos_window[WINDOW:], sin_window[WINDOW:]
    padded = jnp.concatenate([jnp.full((WINDOW,), -1, jnp.int32), segments])
    kseg = lax.dynamic_slice_in_dim(padded, start, span, 0)
    qseg = kseg[WINDOW:].reshape(1, rows)
    kseg = kseg.reshape(span, 1)

    gain_one, gain_two = norm_gains[0:1], norm_gains[1:2]
    q_block = f3 // q_cols

    def weight_spec(block):
        return pl.BlockSpec((dp_count, 1, shard_rows, q_cols), lambda t: (0, t, 0, block))

    def adapter_spec(block):
        return pl.BlockSpec((1, LANES, q_cols), lambda t: (t, 0, block))

    def lane_block(block):
        return pl.BlockSpec((width, LANES), lambda *_: (0, block))

    head_specs = [weight_spec(q_block), adapter_spec(0), weight_spec(q_block + 1), adapter_spec(1)]
    q_spec, qb_spec, o_spec, ob_spec = head_specs
    a_spec, wk_spec, wv_spec = lane_block(0), lane_block(1), lane_block(2)
    token_cols = pl.BlockSpec((rows, q_cols), lambda t: (0, t))
    tok_bf, tok_f32, rank_bf = sds((rows, width), BF), sds((rows, width), F32), sds((rows, LANES), BF)

    args = (tokens, gain_one, a_all, a_all, a_all, b_kv, cos, sin)
    normed_one, rank_one, kv_own = call(
        shared_kernel, "keys_values", 1, args,
        wholes(*args[:2]) + [a_spec, wk_spec, wv_spec] + wholes(*args[5:]),
        [(tok_bf, None), (rank_bf, None), (sds((rows, 2 * HD), BF), None)],
        [], 2 * rows * width * 384, 6 * rows * width,
    )
    parts = seq_length // rows
    reach = WINDOW // rows

    def moved(value, steps):
        return lax.ppermute(value, SEQ, [(c, c + steps) for c in range(parts) if 0 <= c + steps < parts])

    def from_other_core(value):
        return lax.ppermute(value, "core", [(0, 1), (1, 0)])

    kv_window = jnp.concatenate([moved(kv_own, d) for d in range(reach, 0, -1)] + [kv_own])

    b_own, kv_window = lax.optimization_barrier((b_own, kv_window))
    b_all = lax.all_gather(b_own, "tensor", axis=0, tiled=False)
    b_heads = jnp.concatenate(
        [in_slot(b_all[:, :, f3 : f3 + q_cols], SLOT_Q), in_slot(b_all[:, :, f3 + q_cols :], SLOT_O)], axis=2
    )
    steps = 3
    part_cols = ff_cols // steps
    b_hidden = b_all[:, :, :f3].reshape(tensor_count, RANK, 3, steps, part_cols).transpose(3, 2, 1, 0, 4)
    b_hidden = b_hidden.reshape(steps, 3, RANK, tensor_count * part_cols)
    b_hidden = jnp.concatenate(
        [in_slot(b_hidden[:, kind], slot) for kind, slot in enumerate((SLOT_G, SLOT_U, SLOT_D))], axis=2
    )

    args = (
        kv_window, kseg, qseg, normed_one, rank_one, cos, sin, tokens, gain_two, a_all,
        weights, b_heads, weights, b_heads,
    )
    heads = q_cols // HD
    p_spec, norm_spec = by_step(span, heads * rows), by_step(8, heads * rows)
    queries, mixed, probs, norms, residual, normed_two, rank_two, rank_out = call(
        attn_kernel, "attention", tensor_count, args,
        wholes(*args[:9]) + [a_spec] + head_specs,
        [
            (sds((rows, heads_cols), BF), token_cols), (sds((rows, heads_cols), BF), token_cols),
            (sds((tensor_count, span, heads * rows), BF), p_spec),
            (sds((tensor_count, 8, heads * rows), F32), norm_spec),
            (tok_f32, None), (tok_bf, None), (rank_bf, None), (rank_bf, None),
        ],
        [
            pltpu.VMEM((span, rows), F32), pltpu.VMEM((span, heads * rows), F32), pltpu.VMEM((HD, span), BF),
            pltpu.VMEM((rows, width), F32), pltpu.VMEM((rows, LANES), F32), pltpu.VMEM((heads * rows, HD), BF),
        ],
        4 * rows * heads_cols * (span + width), 4 * width * heads_cols,
    )

    args = (
        residual, normed_two, rank_two, cotangent, gain_two, mixed, rank_out, a_all, b_hidden, weights,
    )
    block_output, grad_residual, grad_branch, wide_ffn, grad_ro, grad_bo, grad_bh = call(
        ffn_kernel, "feed_forward", steps, args,
        wholes(*args[:7]) + [a_spec, by_step(LANES, 3 * tensor_count * part_cols), pl.BlockSpec(memory_space=pl.ANY)],
        [
            (tok_bf, None), (tok_f32, None), (tok_bf, None), (sds((LANES, width), F32), None), (rank_bf, None),
            (sds((tensor_count, RANK, q_cols), BF), None), (sds((tensor_count, RANK, f3), BF), None),
        ],
        [
            pltpu.VMEM((rows, width), F32), pltpu.VMEM((rows, width), F32),
            pltpu.VMEM((rows, LANES), F32), pltpu.VMEM((rows, LANES), F32),
            pltpu.VMEM((LANES, rows), BF), pltpu.VMEM((rows, LANES), BF), pltpu.VMEM((LANES, rows), BF),
            pltpu.VMEM((2, dp_count, shard_rows, 3 * tensor_count * part_cols), BF),
            pltpu.SemaphoreType.DMA((2, 3 * tensor_count)),
        ],
        12 * rows * width * tensor_count * ff_cols, 6 * width * tensor_count * ff_cols,
    )
    early = jnp.concatenate([grad_bh, grad_bo], axis=2)
    early = lax.psum_scatter(early, "tensor", scatter_dimension=0, tiled=True).reshape(RANK, -1)

    args = (
        kv_window, grad_branch, grad_ro, rank_one, cos, sin, queries, mixed, probs, norms,
        weights, b_heads, weights, b_heads,
    )
    dkv, grad_one, grad_rank, grad_bq = call(
        attn_back_kernel, "attention_back", tensor_count, args,
        wholes(*args[:6]) + [token_cols, token_cols, p_spec, norm_spec, o_spec, ob_spec, q_spec, qb_spec],
        [
            (sds((span, 2 * HD), BF), None), (tok_f32, None), (sds((rows, LANES), F32), None),
            (sds((tensor_count, RANK, q_cols), BF), by_step(RANK, q_cols)),
        ],
        [
            pltpu.VMEM((span, heads * rows), BF),
            pltpu.VMEM((span, HD), F32), pltpu.VMEM((span, HD), F32), pltpu.VMEM((HD, span), BF),
            pltpu.VMEM((LANES, rows), BF), pltpu.VMEM((rows, q_cols), BF), pltpu.VMEM((rows, q_cols), BF),
            pltpu.VMEM((heads * rows, HD), BF), pltpu.VMEM((heads * rows, HD), BF),
        ],
        2 * rows * heads_cols * (4 * span + 2 * width), 4 * width * heads_cols,
    )

    backs = [moved(dkv[(reach - d) * rows : (reach - d + 1) * rows], -d) for d in range(1, reach + 1)]
    grad_bq = (grad_bq.astype(F32) + from_other_core(grad_bq).astype(F32)).astype(BF)
    chips = dp_count // 2
    share = width // 2 + 2 * RANK
    args = (
        my_core.astype(jnp.int32).reshape(1), normed_one, rank_one, b_kv, cos, sin, dkv, *backs, grad_rank, wide_ffn,
    )
    mine, theirs, grad_key, grad_value, grad_rank = call(
        functools.partial(shared_back_kernel, chips), "shared_back", 1, args,
        [scalars()] + wholes(*args[1:6]) + [pl.BlockSpec((rows, 2 * HD), lambda *_: (reach, 0))] + wholes(*args[7:]),
        [
            (sds((share, LANES), BF), None), (sds((share, LANES), BF), None),
            (sds((rows, HD), BF), None), (sds((rows, HD), BF), None), (rank_bf, None),
        ],
        [], 4 * rows * width * LANES, 6 * rows * width,
    )
    mine = (mine.astype(F32) + from_other_core(theirs).astype(F32)).astype(BF)

    own_rows = width // devices
    planes = chips * tensor_count
    kv_terms = mine[width // 2 :].reshape(2, RANK // (2 * tensor_count), 2, tensor_count, HD)
    kv_terms = lax.dynamic_index_in_dim(kv_terms, my_core, 2, keepdims=False).transpose(1, 2, 0, 3)
    kv_terms = jnp.tile(kv_terms.reshape(-1, 2, HD), (planes // (RANK // 2), 1, 1))
    owned = jnp.concatenate(
        [mine[: width // 2].reshape(planes, own_rows, LANES), kv_terms, jnp.zeros((planes, 2, LANES), BF)], axis=1
    )
    every = jnp.broadcast_to(grad_bq[None], (chips, tensor_count, RANK, q_cols)).reshape(planes, RANK, q_cols)
    terms = lax.all_to_all(jnp.concatenate([owned, every], axis=2), PLANES, 0, 0, tiled=True)
    terms = terms.reshape(seqs, tensor_count, RANK, LANES + q_cols)

    args = (
        tokens, gain_one, a_all, a_all, a_all, grad_key, grad_value, grad_rank, grad_one, grad_residual,
    )
    (input_grad,) = call(
        input_kernel, "input_gradient", 1, args,
        wholes(*args[:2]) + [a_spec, wk_spec, wv_spec] + wholes(*args[5:]),
        [(tok_f32, None)], [], 2 * rows * width * 384, 16 * rows * width,
    )

    early, grad_one = lax.optimization_barrier((early, grad_one))
    early = lax.all_gather(early, DP, axis=0, tiled=False)
    gate_up_adapter_grad, down_adapter_grad, out_adapter_grad = call(
        sum_hidden_kernel, "sum_hidden", 1, (adapter_ids, early),
        [scalars()] + wholes(early),
        [(sds((2, LANES, ff_cols), F32), None), (sds((ff_cols, LANES), F32), None), (sds((q_cols, LANES), F32), None)],
        [pltpu.VMEM((adapters, RANK, f3 + q_cols), F32)], 0, 4 * LANES * f3,
    )
    own_adapter = ((dp * tensor_count + tensor) // RANK).astype(jnp.int32).reshape(1)
    wide_grad, kv_adapter_grad, q_adapter_grad = call(
        sum_wide_kernel, "sum_wide", 1, (adapter_ids, own_adapter, terms),
        [scalars(), scalars()] + wholes(terms),
        [(sds((7, own_rows, LANES), F32), None), (sds((2, 1, HD), F32), None), (sds((LANES, q_cols), F32), None)],
        [pltpu.VMEM((adapters, RANK, LANES + q_cols), F32)], 0, 4 * LANES * f3,
    )
    return (
        block_output, input_grad, wide_grad, kv_adapter_grad,
        q_adapter_grad, out_adapter_grad, gate_up_adapter_grad, down_adapter_grad,
    )


def solution(mesh):
    dp_count, tensor_count = mesh.shape["dp"], mesh.shape["tensor"]
    chips = dp_count // 2
    x_count = math.isqrt(chips)
    devices = mesh.devices.reshape(chips // x_count, x_count, 2, tensor_count)
    return jax.shard_map(
        on_device,
        mesh=Mesh(devices, ALL),
        in_specs=(
            P(ALL, None), P(ALL, None), P(), P(), P(), P(DP, "tensor"), P(None, DP, None),
            P("tensor", DP), P(None, DP, "tensor"), P("tensor", DP), P(None, DP, None), P(),
            P(None, "tensor"), P("tensor", None), P(None, None, "tensor"), P("tensor", None),
        ),
        out_specs=(
            P(ALL, None), P(ALL, None), P(None, ALL, None), P(None, ALL, None),
            P(None, "tensor"), P("tensor", None), P(None, None, "tensor"), P("tensor", None),
        ),
        check_vma=False,
    )
```

```python
import functools
import math

import jax
import jax.numpy as jnp
from jax import lax
from jax.experimental import pallas as pl
from jax.experimental.pallas import tpu as pltpu
from jax.sharding import Mesh, PartitionSpec as P

HD = 128
WINDOW = 1024
RANK = 16
LANES = 128
EPS = 1e-06
MASKED = -1e30
SCALE = HD ** (-0.5)
LOG2E = math.log2(math.e)
GELU_C = 0.7978845608028654
GELU_A = 0.044715
VMEM_LIMIT = 58 * 1024 * 1024
BF = jnp.bfloat16
F32 = jnp.float32
DP = ("y", "x", "core")
SEQ = ("core", "tensor")
PLANES = ("y", "x", "tensor")
ALL = ("y", "x", "core", "tensor")

SLOT_Q, SLOT_K, SLOT_V, SLOT_G, SLOT_U, SLOT_O, SLOT_D = range(7)


def rows_of(slot):
    return slice(slot * RANK, (slot + 1) * RANK)


def mm(a, b):
    return lax.dot_general(a, b, (((1,), (0,)), ((), ())), preferred_element_type=F32)


def mm_nt(a, b):
    return lax.dot_general(a, b, (((1,), (1,)), ((), ())), preferred_element_type=F32)


def turned(a):
    return a.astype(F32).T.astype(BF)


def rope(v, cos, sin):
    return v * cos + pltpu.roll(v, HD // 2, 1) * sin


def rope_back(g, cos, sin):
    return g * cos - pltpu.roll(g, HD // 2, 1) * sin


def flat(ref):
    block = ref[...]
    return block.reshape(block.shape[0] * block.shape[2], block.shape[3])


def rms(v, gain):
    return v * lax.rsqrt(jnp.mean(v * v, axis=-1, keepdims=True) + EPS) * gain


def rms_back(v, gain, grad):
    inv = lax.rsqrt(jnp.mean(v * v, axis=-1, keepdims=True) + EPS)
    scaled = grad * gain
    dot = jnp.mean(v * scaled, axis=-1, keepdims=True)
    return inv * scaled - v * (inv * inv * inv * dot)


def shared_kernel(x_ref, gain_ref, a_ref, wk_ref, wv_ref, bkv_ref, cos_ref, sin_ref, n1_ref, r1_ref, kv_ref):
    n1 = rms(x_ref[...].astype(F32), gain_ref[...]).astype(BF)
    n1_ref[...] = n1
    r1 = mm(n1, a_ref[...]).astype(BF)
    r1_ref[...] = r1
    key = mm(n1, wk_ref[...]) + mm(r1, bkv_ref[0])
    kv_ref[:, :HD] = rope(key, cos_ref[...], sin_ref[...]).astype(BF)
    kv_ref[:, HD:] = (mm(n1, wv_ref[...]) + mm(r1, bkv_ref[1])).astype(BF)


def attn_kernel(
    kv_ref, kseg_ref, qseg_ref, n1_ref, r1_ref, cos_ref, sin_ref, x_ref, gain_ref, a_ref,
    wq_ref, bq_ref, wo_ref, bo_ref,
    q_ref, mixed_ref, p_ref, inv_ref, res_ref, n2_ref, r2_ref, ro_ref,
    bias_ref, s_ref, vt_ref, acc_ref, rank_ref, qs_ref,
):
    step = pl.program_id(0)
    rows = q_ref.shape[0]
    chunks = kv_ref.shape[0] // rows

    @pl.when(step == 0)
    def _():
        key = lax.broadcasted_iota(jnp.int32, bias_ref.shape, 0)
        query = lax.broadcasted_iota(jnp.int32, bias_ref.shape, 1)
        allowed = (key >= query) & (key <= query + WINDOW) & (kseg_ref[...] == qseg_ref[...])
        bias_ref[...] = jnp.where(allowed, 0.0, MASKED)
        vt_ref[...] = turned(kv_ref[:, HD:])
        acc_ref[...] = jnp.zeros_like(acc_ref)
        rank_ref[...] = jnp.zeros_like(rank_ref)

    lin = mm(n1_ref[...], flat(wq_ref)) + mm(r1_ref[...], bq_ref[0])
    heads = q_ref.shape[1] // HD
    for h in range(heads):
        part = slice(h * HD, (h + 1) * HD)
        query = (rope(lin[:, part], cos_ref[...], sin_ref[...]) * (SCALE * LOG2E)).astype(BF)
        q_ref[:, part] = query
        qs_ref[h * rows : (h + 1) * rows] = query
    queries = qs_ref[...]
    top = jnp.full((1, heads * rows), MASKED, F32)
    for c in range(chunks):
        span = slice(c * rows, (c + 1) * rows)
        s = mm_nt(kv_ref[span, :HD], queries)
        bias = bias_ref[span]
        s = jnp.concatenate([s[:, h * rows : (h + 1) * rows] + bias for h in range(heads)], axis=1)
        s_ref[span] = s
        top = jnp.maximum(top, jnp.max(s, axis=0, keepdims=True))
    total = jnp.zeros((1, heads * rows), F32)
    for c in range(chunks):
        span = slice(c * rows, (c + 1) * rows)
        p = jnp.exp2(s_ref[span] - top)
        total = total + jnp.sum(p, axis=0, keepdims=True)
        p_ref[0, span] = p.astype(BF)
    inv = 1.0 / total
    inv_ref[0, 0:1] = inv
    out = mm(vt_ref[...], p_ref[0]) * inv
    for h in range(heads):
        mixed_ref[:, h * HD : (h + 1) * HD] = out[:, h * rows : (h + 1) * rows].T.astype(BF)

    mixed = mixed_ref[...]
    acc_ref[...] += mm_nt(mixed, flat(wo_ref))
    rank_ref[...] += mm_nt(mixed, bo_ref[0])

    @pl.when(step == pl.num_programs(0) - 1)
    def _():
        ro = rank_ref[...].astype(BF)
        ro_ref[...] = ro
        res = x_ref[...].astype(F32) + (acc_ref[...] + mm_nt(ro, a_ref[...]))
        res_ref[...] = res
        n2 = rms(res, gain_ref[...]).astype(BF)
        n2_ref[...] = n2
        r2_ref[...] = mm(n2, a_ref[...]).astype(BF)


def ffn_kernel(
    res_ref, n2_ref, r2_ref, cot_ref, gain_ref, mixed_ref, ro_ref, a_ref, b_ref, w_ref,
    out_ref, gres_ref, gb_ref, wide_ref, gro_ref, gbo_ref, gbh_ref,
    ffn_ref, g2_ref, rd_ref, gr_ref, r2t_ref, grd_ref, grdt_ref, wv_ref, sems,
):
    step = pl.program_id(0)
    steps = pl.num_programs(0)
    tensor_count = w_ref.shape[1]
    ff = b_ref.shape[2] // 3
    part = ff // tensor_count
    slot = lax.rem(step, 2)

    def copies(at, to):
        moves = []
        for kind in (2, 0, 1):
            for t in range(tensor_count):
                source = pl.multiple_of((kind * steps + at) * part, LANES)
                target = (kind * tensor_count + t) * part
                moves.append(
                    pltpu.make_async_copy(
                        w_ref.at[:, t, :, pl.ds(source, part)],
                        wv_ref.at[to, :, :, pl.ds(target, part)],
                        sems.at[to, len(moves)],
                    )
                )
        return moves

    @pl.when(step == 0)
    def _():
        for copy in copies(0, 0):
            copy.start()
        ffn_ref[...] = jnp.zeros_like(ffn_ref)
        g2_ref[...] = jnp.zeros_like(g2_ref)
        rd_ref[...] = jnp.zeros_like(rd_ref)
        gr_ref[...] = jnp.zeros_like(gr_ref)
        r2t_ref[...] = turned(r2_ref[...])
        grd = mm(cot_ref[...], a_ref[...]).astype(BF)
        grd_ref[...] = grd
        grdt_ref[...] = turned(grd)

    @pl.when(step < steps - 1)
    def _():
        for copy in copies(step + 1, 1 - slot):
            copy.start()

    n2, r2, cot = n2_ref[...], r2_ref[...], cot_ref[...]
    b_gu, b_d = b_ref[0, :, : 2 * ff], b_ref[0, :, 2 * ff :]
    arrivals = copies(step, slot)
    rows_of_weight = wv_ref.shape[1] * wv_ref.shape[2]
    for copy in arrivals[:tensor_count]:
        copy.wait()
    w_d = wv_ref[slot, :, :, 2 * ff :].reshape(rows_of_weight, ff)
    grad_hidden = (mm(cot, w_d) + mm(grd_ref[...], b_d)).astype(BF).astype(F32)
    for copy in arrivals[tensor_count:]:
        copy.wait()
    w_gu = wv_ref[slot, :, :, : 2 * ff].reshape(rows_of_weight, 2 * ff)
    lin = mm(n2, w_gu) + mm(r2, b_gu)
    gate, up = lin[:, :ff], lin[:, ff:]
    square = gate * gate
    th = jnp.tanh(GELU_C * (gate + GELU_A * square * gate))
    half = 0.5 * (1.0 + th)
    act = gate * half
    slope = half + 0.5 * gate * (1.0 - th * th) * (GELU_C * (1.0 + 3.0 * GELU_A * square))
    hidden = (act * up).astype(BF)
    grad_gate = (grad_hidden * up * slope).astype(BF)
    grad_up = (grad_hidden * act).astype(BF)
    grads = jnp.concatenate([grad_gate, grad_up], axis=1)
    ffn_ref[...] += mm_nt(hidden, w_d)
    rd_ref[...] += mm_nt(hidden, b_d)
    g2_ref[...] += mm_nt(grads, w_gu)
    gr_ref[...] += mm_nt(grads, b_gu)
    terms = (
        mm(r2t_ref[rows_of(SLOT_G)], grad_gate), mm(r2t_ref[rows_of(SLOT_U)], grad_up),
        mm(grdt_ref[rows_of(SLOT_D)], hidden),
    )
    for kind, term in enumerate(terms):
        target = pl.multiple_of((kind * steps + step) * part, LANES)
        for t in range(tensor_count):
            gbh_ref[t, :, pl.ds(target, part)] = term[:, t * part : (t + 1) * part].astype(BF)

    @pl.when(step == steps - 1)
    def _():
        rd = rd_ref[...].astype(BF)
        gr = gr_ref[...].astype(BF)
        res = res_ref[...]
        out_ref[...] = (res + (ffn_ref[...] + mm_nt(rd, a_ref[...]))).astype(BF)
        grad_two = g2_ref[...] + mm_nt(gr, a_ref[...])
        grad_res = cot_ref[...].astype(F32) + rms_back(res, gain_ref[...], grad_two)
        gres_ref[...] = grad_res
        grad_branch = grad_res.astype(BF)
        gb_ref[...] = grad_branch
        gro = mm(grad_branch, a_ref[...])
        gro_ref[...] = gro.astype(BF)
        grot = gro.T[rows_of(SLOT_O)].astype(BF)
        cols = gbo_ref.shape[2]
        for t in range(gbo_ref.shape[0]):
            gbo_ref[t] = mm(grot, mixed_ref[:, t * cols : (t + 1) * cols]).astype(BF)
        wide = mm(gr_ref[...].T.astype(BF), n2) + mm(rd_ref[...].T.astype(BF), cot)
        wide_ref[...] = wide + mm(turned(ro_ref[...]), grad_branch)


def attn_back_kernel(
    kv_ref, gb_ref, gro_ref, r1_ref, cos_ref, sin_ref,
    q_ref, mixed_ref, p_ref, inv_ref, wo_ref, bo_ref, wq_ref, bq_ref,
    dkva_ref, dkvb_ref, dkvc_ref, dkvd_ref, dkve_ref, g1_ref, gr_ref, gbq_ref,
    ds_ref, dk_ref, dv_ref, kt_ref, r1t_ref, gq_ref, gm_ref, qs_ref, gs_ref,
):
    step = pl.program_id(0)
    rows = q_ref.shape[0]
    chunks = kv_ref.shape[0] // rows

    @pl.when(step == 0)
    def _():
        kt_ref[...] = turned(kv_ref[:, :HD])
        r1t_ref[...] = turned(r1_ref[...])
        dk_ref[...] = jnp.zeros_like(dk_ref)
        dv_ref[...] = jnp.zeros_like(dv_ref)
        g1_ref[...] = jnp.zeros_like(g1_ref)
        gr_ref[...] = jnp.zeros_like(gr_ref)

    gm_ref[...] = (mm(gb_ref[...], flat(wo_ref)) + mm(gro_ref[...], bo_ref[0])).astype(BF)
    heads = q_ref.shape[1] // HD
    deltas = []
    for h in range(heads):
        part, span = slice(h * HD, (h + 1) * HD), slice(h * rows, (h + 1) * rows)
        grad = gm_ref[:, part]
        qs_ref[span] = q_ref[:, part]
        gs_ref[span] = grad
        delta = grad.astype(F32) * mixed_ref[:, part].astype(F32)
        deltas.append(jnp.sum(delta.T, axis=0, keepdims=True))
    delta, inv = jnp.concatenate(deltas, axis=1), inv_ref[0, 0:1]
    queries, grads = qs_ref[...], gs_ref[...]
    for c in range(chunks):
        span = slice(c * rows, (c + 1) * rows)
        p = p_ref[0, span].astype(F32) * inv
        dp = mm_nt(kv_ref[span, HD:], grads)
        ds = (p * (dp - delta)).astype(BF)
        ds_ref[span] = ds
        dk_ref[span] += mm(ds, queries)
        dv_ref[span] += mm(p.astype(BF), grads)
    dq = mm(kt_ref[...], ds_ref[...]) * SCALE
    for h in range(heads):
        part, span = slice(h * HD, (h + 1) * HD), slice(h * rows, (h + 1) * rows)
        gq_ref[:, part] = rope_back(dq[:, span].T, cos_ref[...], sin_ref[...]).astype(BF)

    gq = gq_ref[...]
    gbq_ref[0] = mm(r1t_ref[rows_of(SLOT_Q)], gq).astype(BF)
    gr_ref[...] += mm_nt(gq, bq_ref[0])
    g1_ref[...] += mm_nt(gq, flat(wq_ref))

    @pl.when(step == pl.num_programs(0) - 1)
    def _():
        for c, dkv_ref in enumerate((dkva_ref, dkvb_ref, dkvc_ref, dkvd_ref, dkve_ref)):
            span = slice(c * rows, (c + 1) * rows)
            dkv_ref[:, :HD] = (dk_ref[span] * (1.0 / LOG2E)).astype(BF)
            dkv_ref[:, HD:] = dv_ref[span].astype(BF)


def shared_back_kernel(
    chips, core_ref, n1_ref, r1_ref, bkv_ref, cos_ref, sin_ref, own_ref, back1_ref, back2_ref, back3_ref, back4_ref,
    gr_ref, widef_ref,
    mine_ref, theirs_ref, gk_ref, gv_ref, grt_ref,
):
    gkv = own_ref[...].astype(F32)
    for back_ref in (back1_ref, back2_ref, back3_ref, back4_ref):
        gkv = gkv + back_ref[...].astype(F32)
    gk = rope_back(gkv[:, :HD], cos_ref[...], sin_ref[...]).astype(BF)
    gv = gkv[:, HD:].astype(BF)
    gk_ref[...] = gk
    gv_ref[...] = gv
    gr = gr_ref[...] + mm_nt(gk, bkv_ref[0]) + mm_nt(gv, bkv_ref[1])
    grt_ref[...] = gr.astype(BF)
    wide = (mm(gr.T.astype(BF), n1_ref[...]) + widef_ref[...]).T.astype(BF)
    share = mine_ref.shape[0] - 2 * RANK
    wide = wide.reshape(chips, 2, share // chips, LANES)
    first = core_ref[0] == 0
    mine_ref[:share] = jnp.where(first, wide[:, 0], wide[:, 1]).reshape(share, LANES)
    theirs_ref[:share] = jnp.where(first, wide[:, 1], wide[:, 0]).reshape(share, LANES)
    r1t = turned(r1_ref[...])
    for j, (slot, grad) in enumerate(((SLOT_K, gk), (SLOT_V, gv))):
        term = mm(r1t[rows_of(slot)], grad).astype(BF)
        rows = slice(share + j * RANK, share + (j + 1) * RANK)
        mine_ref[rows] = term
        theirs_ref[rows] = term


def payload_kernel(core_ref, mine_ref, other_ref, q_ref, q_other_ref, out_ref):
    first = core_ref[0] == 0
    total = mine_ref[...].astype(F32) + other_ref[...].astype(F32)
    tensor_count = q_ref.shape[0]
    count = out_ref.shape[0]
    own_rows = (total.shape[0] - 2 * RANK) // count
    queries = [(q_ref[t].astype(F32) + q_other_ref[t].astype(F32)).astype(BF) for t in range(tensor_count)]
    blank = jnp.zeros((RANK - own_rows - 2, LANES), F32)
    for n in range(count):
        pieces = [total[n * own_rows : (n + 1) * own_rows]]
        row = (2 * (n // tensor_count) * tensor_count + n % tensor_count) % RANK
        for j in range(2):
            at = count * own_rows + j * RANK + row
            low, high = total[at : at + 1], total[at + tensor_count : at + tensor_count + 1]
            pieces.append(jnp.where(first, low, high))
        out_ref[n, :, :LANES] = jnp.concatenate(pieces + [blank], axis=0).astype(BF)
        out_ref[n, :, LANES:] = queries[n % tensor_count]


def input_kernel(
    x_ref, gain_ref, a_ref, wk_ref, wv_ref, gk_ref, gv_ref, gr_ref, g1_ref, gres_ref, grad_ref,
):
    g1 = g1_ref[...] + mm_nt(gk_ref[...], wk_ref[...]) + mm_nt(gv_ref[...], wv_ref[...])
    g1 = g1 + mm_nt(gr_ref[...], a_ref[...])
    x = x_ref[...].astype(F32)
    grad_ref[...] = gres_ref[...] + rms_back(x, gain_ref[...], g1)


def sum_hidden_kernel(ids_ref, core_ref, own_ref, other_ref, gu_ref, down_ref, out_ref, acc_ref):
    acc_ref[...] = jnp.zeros_like(acc_ref)
    adapters, rank, cols = acc_ref.shape
    for core, terms_ref in ((core_ref[0], own_ref), (1 - core_ref[0], other_ref)):
        part = pl.ds(pl.multiple_of(core * (cols // 2), LANES), cols // 2)
        for s in range(terms_ref.shape[0]):
            acc_ref[ids_ref[s], :, part] += terms_ref[s].astype(F32)
    ff = gu_ref.shape[2]

    def taken(first, last):
        return acc_ref[:, :, first:last].reshape(adapters * rank, last - first)

    gu_ref[0] = taken(0, ff)
    gu_ref[1] = taken(ff, 2 * ff)
    down_ref[...] = taken(2 * ff, 3 * ff).T
    out_ref[...] = taken(3 * ff, cols).T


def sum_wide_kernel(ids_ref, own_ref, terms_ref, wide_ref, kv_ref, q_ref, acc_ref):
    acc_ref[...] = jnp.zeros_like(acc_ref)
    seqs, parts = terms_ref.shape[:2]
    for s in range(seqs):
        term = terms_ref[s, 0].astype(F32)
        for part in range(1, parts):
            term = term + terms_ref[s, part].astype(F32)
        acc_ref[ids_ref[s]] += term
    adapters, rank, _ = acc_ref.shape
    q_ref[...] = acc_ref[:, :, LANES:].reshape(q_ref.shape)
    lane = lax.broadcasted_iota(jnp.int32, (rank, LANES), 1) // RANK
    own_rows, slots = wide_ref.shape[:2]
    for j in range(slots):
        total = jnp.zeros((rank, LANES), F32)
        for a in range(adapters):
            moved = pltpu.roll(acc_ref[a, :, :LANES], ((a - j) * RANK) % LANES, 1)
            total = jnp.where(lane == a, moved, total)
        wide_ref[:, j] = total[:own_rows]
    mine = acc_ref[own_ref[0], :, :LANES]
    for j in range(2):
        kv_ref[j] = mine[own_rows + j : own_rows + j + 1]


def sds(shape, dtype):
    return jax.ShapeDtypeStruct(shape, dtype)


def scalars():
    return pl.BlockSpec(memory_space=pltpu.SMEM)


def whole(array):
    rank = len(array.shape)
    return pl.BlockSpec(array.shape, lambda *_: (0,) * rank)


def wholes(*arrays):
    return [whole(v) for v in arrays]


def by_step(*shape):
    return pl.BlockSpec((1,) + shape, lambda t: (t,) + (0,) * len(shape))


def call(kernel, name, steps, args, specs, outs, scratch, flops, nbytes):
    shapes = [shape for shape, _ in outs]
    return pl.pallas_call(
        kernel,
        name=name,
        grid=(steps,),
        in_specs=specs,
        out_specs=[whole(shape) if spec is None else spec for shape, spec in outs],
        out_shape=shapes,
        scratch_shapes=scratch,
        compiler_params=pltpu.CompilerParams(
            dimension_semantics=("arbitrary",), vmem_limit_bytes=VMEM_LIMIT
        ),
        cost_estimate=pl.CostEstimate(flops=flops, bytes_accessed=nbytes, transcendentals=0),
    )(*args)


def rope_tables(positions):
    half = HD // 2
    frequency = 10000.0 ** (-(jnp.arange(half).astype(F32) / half))
    angles = positions.astype(F32)[:, None] * frequency[None, :]
    cos, sin = jnp.cos(angles), jnp.sin(angles)
    return jnp.concatenate([cos, cos], axis=1), jnp.concatenate([-sin, sin], axis=1)


def on_device(
    tokens, cotangent, segments, adapter_ids, norm_gains, q_weight, kv_weight, out_weight,
    gate_up_weight, down_weight, wide_adapters, kv_adapter, q_adapter, out_adapter,
    gate_up_adapter, down_adapter,
):
    rows, width = tokens.shape
    tensor_count = lax.axis_size("tensor")
    dp_count = lax.axis_size("y") * lax.axis_size("x") * 2
    devices = dp_count * tensor_count
    group_rows = rows * tensor_count
    seq_length = 2 * group_rows
    shard_rows = q_weight.shape[0]
    q_cols, ff_cols = q_weight.shape[1], gate_up_weight.shape[2]
    heads_cols = tensor_count * q_cols
    seqs = adapter_ids.shape[0]
    adapters = wide_adapters.shape[2] // RANK
    dp = lax.axis_index(DP)
    tensor = lax.axis_index("tensor")
    my_core = lax.axis_index("core")
    adapter = lax.dynamic_index_in_dim(adapter_ids, dp // 2, keepdims=False)
    column = adapter * RANK
    f3 = 3 * ff_cols

    pack = jnp.concatenate(
        [gate_up_weight[0], gate_up_weight[1], down_weight.T, q_weight, out_weight.T], axis=1
    )
    pack, wide_adapters = lax.optimization_barrier((pack, wide_adapters))
    weights = lax.all_gather(pack, ALL, axis=0, tiled=False)
    weights = weights.reshape(dp_count, tensor_count, shard_rows, f3 + 2 * q_cols)

    wide = wide_adapters.reshape(7, shard_rows, adapters, RANK)
    wide = jnp.take(wide, adapter_ids, axis=2).transpose(2, 1, 0, 3)
    wide = wide.reshape(seqs, shard_rows, 7 * RANK)
    wide = jnp.pad(wide, ((0, 0), (0, 0), (0, LANES - 7 * RANK)))
    shared = jnp.broadcast_to(kv_weight[:, None], (2, seqs, shard_rows, HD))
    wide = jnp.concatenate([wide, shared[0], shared[1]], axis=2)

    def from_other_core(value):
        return lax.ppermute(value, "core", [(0, 1), (1, 0)])

    a_own = lax.all_to_all(wide, ("y", "x"), 0, 0, tiled=True)
    a_other = from_other_core(a_own)
    a_all = jnp.where(my_core == 0, jnp.stack([a_own, a_other], 1), jnp.stack([a_other, a_own], 1))
    a_all = a_all.reshape(width, 3 * LANES)

    def take_rows(matrix):
        return lax.dynamic_slice_in_dim(matrix, column, RANK, matrix.ndim - 2)

    def take_cols(matrix):
        return lax.dynamic_slice_in_dim(matrix, column, RANK, matrix.ndim - 1)

    def in_slot(block, slot):
        pads = [(0, 0)] * block.ndim
        pads[-2] = (slot * RANK, LANES - (slot + 1) * RANK)
        return jnp.pad(block, pads)

    gu_rows = take_rows(gate_up_adapter)
    b_own = jnp.concatenate(
        [gu_rows[0], gu_rows[1], take_cols(down_adapter).T, take_rows(q_adapter), take_cols(out_adapter).T], axis=1
    )
    kv_rows = take_rows(kv_adapter)
    b_kv = jnp.stack([in_slot(kv_rows[0], SLOT_K), in_slot(kv_rows[1], SLOT_V)])

    start = dp * group_rows + tensor * rows
    span = WINDOW + rows
    cos_window, sin_window = rope_tables((start - WINDOW + jnp.arange(span)) % seq_length)
    cos, sin = cos_window[WINDOW:], sin_window[WINDOW:]
    padded = jnp.concatenate([jnp.full((WINDOW,), -1, jnp.int32), segments])
    kseg = lax.dynamic_slice_in_dim(padded, start, span, 0)
    qseg = kseg[WINDOW:].reshape(1, rows)
    kseg = kseg.reshape(span, 1)

    gain_one, gain_two = norm_gains[0:1], norm_gains[1:2]
    q_block = f3 // q_cols

    def weight_spec(block):
        return pl.BlockSpec((dp_count, 1, shard_rows, q_cols), lambda t: (0, t, 0, block))

    def adapter_spec(block):
        return pl.BlockSpec((1, LANES, q_cols), lambda t: (t, 0, block))

    def lane_block(block):
        return pl.BlockSpec((width, LANES), lambda *_: (0, block))

    head_specs = [weight_spec(q_block), adapter_spec(0), weight_spec(q_block + 1), adapter_spec(1)]
    q_spec, qb_spec, o_spec, ob_spec = head_specs
    a_spec, wk_spec, wv_spec = lane_block(0), lane_block(1), lane_block(2)
    token_cols = pl.BlockSpec((rows, q_cols), lambda t: (0, t))
    tok_bf, tok_f32, rank_bf = sds((rows, width), BF), sds((rows, width), F32), sds((rows, LANES), BF)

    args = (tokens, gain_one, a_all, a_all, a_all, b_kv, cos, sin)
    normed_one, rank_one, kv_own = call(
        shared_kernel, "keys_values", 1, args,
        wholes(*args[:2]) + [a_spec, wk_spec, wv_spec] + wholes(*args[5:]),
        [(tok_bf, None), (rank_bf, None), (sds((rows, 2 * HD), BF), None)],
        [], 2 * rows * width * 384, 6 * rows * width,
    )
    parts = seq_length // rows
    reach = WINDOW // rows

    def moved(value, steps):
        return lax.ppermute(value, SEQ, [(c, c + steps) for c in range(parts) if 0 <= c + steps < parts])

    kv_window = jnp.concatenate([moved(kv_own, d) for d in range(reach, 0, -1)] + [kv_own])

    b_own, kv_window = lax.optimization_barrier((b_own, kv_window))
    b_all = lax.all_gather(b_own, "tensor", axis=0, tiled=False)
    b_heads = jnp.concatenate(
        [in_slot(b_all[:, :, f3 : f3 + q_cols], SLOT_Q), in_slot(b_all[:, :, f3 + q_cols :], SLOT_O)], axis=2
    )
    steps = 3
    part_cols = ff_cols // steps
    b_hidden = b_all[:, :, :f3].reshape(tensor_count, RANK, 3, steps, part_cols).transpose(3, 2, 1, 0, 4)
    b_hidden = b_hidden.reshape(steps, 3, RANK, tensor_count * part_cols)
    b_hidden = jnp.concatenate(
        [in_slot(b_hidden[:, kind], slot) for kind, slot in enumerate((SLOT_G, SLOT_U, SLOT_D))], axis=2
    )

    args = (
        kv_window, kseg, qseg, normed_one, rank_one, cos, sin, tokens, gain_two, a_all,
        weights, b_heads, weights, b_heads,
    )
    heads = q_cols // HD
    p_spec, norm_spec = by_step(span, heads * rows), by_step(8, heads * rows)
    queries, mixed, probs, norms, residual, normed_two, rank_two, rank_out = call(
        attn_kernel, "attention", tensor_count, args,
        wholes(*args[:9]) + [a_spec] + head_specs,
        [
            (sds((rows, heads_cols), BF), token_cols), (sds((rows, heads_cols), BF), token_cols),
            (sds((tensor_count, span, heads * rows), BF), p_spec),
            (sds((tensor_count, 8, heads * rows), F32), norm_spec),
            (tok_f32, None), (tok_bf, None), (rank_bf, None), (rank_bf, None),
        ],
        [
            pltpu.VMEM((span, rows), F32), pltpu.VMEM((span, heads * rows), F32), pltpu.VMEM((HD, span), BF),
            pltpu.VMEM((rows, width), F32), pltpu.VMEM((rows, LANES), F32), pltpu.VMEM((heads * rows, HD), BF),
        ],
        4 * rows * heads_cols * (span + width), 4 * width * heads_cols,
    )

    args = (
        residual, normed_two, rank_two, cotangent, gain_two, mixed, rank_out, a_all, b_hidden, weights,
    )
    block_output, grad_residual, grad_branch, wide_ffn, grad_ro, grad_bo, grad_bh = call(
        ffn_kernel, "feed_forward", steps, args,
        wholes(*args[:7]) + [a_spec, by_step(LANES, 3 * tensor_count * part_cols), pl.BlockSpec(memory_space=pl.ANY)],
        [
            (tok_bf, None), (tok_f32, None), (tok_bf, None), (sds((LANES, width), F32), None), (rank_bf, None),
            (sds((tensor_count, RANK, q_cols), BF), None), (sds((tensor_count, RANK, f3), BF), None),
        ],
        [
            pltpu.VMEM((rows, width), F32), pltpu.VMEM((rows, width), F32),
            pltpu.VMEM((rows, LANES), F32), pltpu.VMEM((rows, LANES), F32),
            pltpu.VMEM((LANES, rows), BF), pltpu.VMEM((rows, LANES), BF), pltpu.VMEM((LANES, rows), BF),
            pltpu.VMEM((2, dp_count, shard_rows, 3 * tensor_count * part_cols), BF),
            pltpu.SemaphoreType.DMA((2, 3 * tensor_count)),
        ],
        12 * rows * width * tensor_count * ff_cols, 6 * width * tensor_count * ff_cols,
    )
    early = jnp.concatenate([grad_bh, grad_bo], axis=2)
    early = lax.psum_scatter(early, "tensor", scatter_dimension=0, tiled=True).reshape(RANK, -1)

    args = (
        kv_window, grad_branch, grad_ro, rank_one, cos, sin, queries, mixed, probs, norms,
        weights, b_heads, weights, b_heads,
    )
    *dkv, grad_one, grad_rank, grad_bq = call(
        attn_back_kernel, "attention_back", tensor_count, args,
        wholes(*args[:6]) + [token_cols, token_cols, p_spec, norm_spec, o_spec, ob_spec, q_spec, qb_spec],
        [
            *[(sds((rows, 2 * HD), BF), None)] * (reach + 1), (tok_f32, None), (sds((rows, LANES), F32), None),
            (sds((tensor_count, RANK, q_cols), BF), by_step(RANK, q_cols)),
        ],
        [
            pltpu.VMEM((span, heads * rows), BF),
            pltpu.VMEM((span, HD), F32), pltpu.VMEM((span, HD), F32), pltpu.VMEM((HD, span), BF),
            pltpu.VMEM((LANES, rows), BF), pltpu.VMEM((rows, q_cols), BF), pltpu.VMEM((rows, q_cols), BF),
            pltpu.VMEM((heads * rows, HD), BF), pltpu.VMEM((heads * rows, HD), BF),
        ],
        2 * rows * heads_cols * (4 * span + 2 * width), 4 * width * heads_cols,
    )

    half_cols = (f3 + q_cols) // 2
    early, grad_one = lax.optimization_barrier((early, grad_one))
    early_mine = lax.dynamic_slice_in_dim(early, my_core * half_cols, half_cols, 1)
    early_theirs = lax.dynamic_slice_in_dim(early, (1 - my_core) * half_cols, half_cols, 1)
    early = (early_mine.astype(F32) + from_other_core(early_theirs).astype(F32)).astype(BF)
    early = lax.all_to_all(jnp.broadcast_to(early[None], (seqs, RANK, half_cols)), ("y", "x"), 0, 0, tiled=True)

    backs = [moved(dkv[reach - d], -d) for d in range(1, reach + 1)]
    chips = dp_count // 2
    share = width // 2 + 2 * RANK
    args = (
        my_core.astype(jnp.int32).reshape(1), normed_one, rank_one, b_kv, cos, sin, dkv[reach], *backs, grad_rank, wide_ffn,
    )
    mine, theirs, grad_key, grad_value, grad_rank = call(
        functools.partial(shared_back_kernel, chips), "shared_back", 1, args,
        [scalars()] + wholes(*args[1:]),
        [
            (sds((share, LANES), BF), None), (sds((share, LANES), BF), None),
            (sds((rows, HD), BF), None), (sds((rows, HD), BF), None), (rank_bf, None),
        ],
        [], 4 * rows * width * LANES, 6 * rows * width,
    )
    own_rows = width // devices
    planes = chips * tensor_count
    theirs, early = lax.optimization_barrier((theirs, early))
    other, grad_bq_other = from_other_core(theirs), from_other_core(grad_bq)
    args = (my_core.astype(jnp.int32).reshape(1), mine, other, grad_bq, grad_bq_other)
    (payload,) = call(
        payload_kernel, "payload", 1, args, [scalars()] + wholes(*args[1:]),
        [(sds((planes, RANK, LANES + q_cols), BF), None)], [], 0, 2 * planes * RANK * (LANES + q_cols),
    )
    payload, grad_key = lax.optimization_barrier((payload, grad_key))
    terms = lax.all_to_all(payload, PLANES, 0, 0, tiled=True)
    terms = terms.reshape(seqs, tensor_count, RANK, LANES + q_cols)

    args = (
        tokens, gain_one, a_all, a_all, a_all, grad_key, grad_value, grad_rank, grad_one, grad_residual,
    )
    (input_grad,) = call(
        input_kernel, "input_gradient", 1, args,
        wholes(*args[:2]) + [a_spec, wk_spec, wv_spec] + wholes(*args[5:]),
        [(tok_f32, None)], [], 2 * rows * width * 384, 16 * rows * width,
    )

    early_other = from_other_core(early)
    args = (adapter_ids, my_core.astype(jnp.int32).reshape(1), early, early_other)
    gate_up_adapter_grad, down_adapter_grad, out_adapter_grad = call(
        sum_hidden_kernel, "sum_hidden", 1, args, [scalars(), scalars()] + wholes(*args[2:]),
        [(sds((2, LANES, ff_cols), F32), None), (sds((ff_cols, LANES), F32), None), (sds((q_cols, LANES), F32), None)],
        [pltpu.VMEM((adapters, RANK, f3 + q_cols), F32)], 0, 4 * LANES * f3,
    )
    own_adapter = ((dp * tensor_count + tensor) // RANK).astype(jnp.int32).reshape(1)
    wide_grad, kv_adapter_grad, q_adapter_grad = call(
        sum_wide_kernel, "sum_wide", 1, (adapter_ids, own_adapter, terms),
        [scalars(), scalars()] + wholes(terms),
        [(sds((own_rows, 7, LANES), F32), None), (sds((2, 1, HD), F32), None), (sds((LANES, q_cols), F32), None)],
        [pltpu.VMEM((adapters, RANK, LANES + q_cols), F32)], 0, 4 * LANES * f3,
    )
    return (
        block_output, input_grad, wide_grad.transpose(1, 0, 2), kv_adapter_grad,
        q_adapter_grad, out_adapter_grad, gate_up_adapter_grad, down_adapter_grad,
    )


def solution(mesh):
    dp_count, tensor_count = mesh.shape["dp"], mesh.shape["tensor"]
    chips = dp_count // 2
    x_count = math.isqrt(chips)
    devices = mesh.devices.reshape(chips // x_count, x_count, 2, tensor_count)
    return jax.shard_map(
        on_device,
        mesh=Mesh(devices, ALL),
        in_specs=(
            P(ALL, None), P(ALL, None), P(), P(), P(), P(DP, "tensor"), P(None, DP, None),
            P("tensor", DP), P(None, DP, "tensor"), P("tensor", DP), P(None, DP, None), P(),
            P(None, "tensor"), P("tensor", None), P(None, None, "tensor"), P("tensor", None),
        ),
        out_specs=(
            P(ALL, None), P(ALL, None), P(None, ALL, None), P(None, ALL, None),
            P(None, "tensor"), P("tensor", None), P(None, None, "tensor"), P("tensor", None),
        ),
        check_vma=False,
    )
```

```python
import functools
import math

import jax
import jax.numpy as jnp
from jax import lax
from jax.experimental import pallas as pl
from jax.experimental.pallas import tpu as pltpu
from jax.sharding import Mesh, PartitionSpec as P

HD = 128
WINDOW = 1024
RANK = 16
LANES = 128
EPS = 1e-06
MASKED = -1e30
SCALE = HD ** (-0.5)
LOG2E = math.log2(math.e)
GELU_C = 0.7978845608028654
GELU_A = 0.044715
VMEM_LIMIT = 58 * 1024 * 1024
BF = jnp.bfloat16
F32 = jnp.float32
DP = ("y", "x", "core")
SEQ = ("core", "tensor")
PLANES = ("y", "x", "tensor")
ALL = ("y", "x", "core", "tensor")

SLOT_Q, SLOT_K, SLOT_V, SLOT_G, SLOT_U, SLOT_O, SLOT_D = range(7)


def rows_of(slot):
    return slice(slot * RANK, (slot + 1) * RANK)


def mm(a, b):
    return lax.dot_general(a, b, (((1,), (0,)), ((), ())), preferred_element_type=F32)


def mm_nt(a, b):
    return lax.dot_general(a, b, (((1,), (1,)), ((), ())), preferred_element_type=F32)


def turned(a):
    return a.astype(F32).T.astype(BF)


def rope(v, cos, sin):
    return v * cos + pltpu.roll(v, HD // 2, 1) * sin


def rope_back(g, cos, sin):
    return g * cos - pltpu.roll(g, HD // 2, 1) * sin


def flat(ref):
    block = ref[...]
    return block.reshape(block.shape[0] * block.shape[2], block.shape[3])


def rms(v, gain):
    return v * lax.rsqrt(jnp.mean(v * v, axis=-1, keepdims=True) + EPS) * gain


def rms_back(v, gain, grad):
    inv = lax.rsqrt(jnp.mean(v * v, axis=-1, keepdims=True) + EPS)
    scaled = grad * gain
    dot = jnp.mean(v * scaled, axis=-1, keepdims=True)
    return inv * scaled - v * (inv * inv * inv * dot)


def shared_kernel(x_ref, gain_ref, a_ref, wk_ref, wv_ref, bkv_ref, cos_ref, sin_ref, n1_ref, r1_ref, kv_ref):
    n1 = rms(x_ref[...].astype(F32), gain_ref[...]).astype(BF)
    n1_ref[...] = n1
    r1 = mm(n1, a_ref[...]).astype(BF)
    r1_ref[...] = r1
    key = mm(n1, wk_ref[...]) + mm(r1, bkv_ref[0])
    kv_ref[:, :HD] = rope(key, cos_ref[...], sin_ref[...]).astype(BF)
    kv_ref[:, HD:] = (mm(n1, wv_ref[...]) + mm(r1, bkv_ref[1])).astype(BF)


def forward_kernel(
    kv_ref, kseg_ref, qseg_ref, n1_ref, r1_ref, cos_ref, sin_ref, x_ref, cot_ref, gain_ref, a_ref,
    wq_ref, bq_ref, wo_ref, bo_ref, b_ref, w_ref,
    q_ref, mixed_ref, p_ref, inv_ref, out_ref, gres_ref, gb_ref, wide_ref, gro_ref, early_ref,
    bias_ref, s_ref, vt_ref, ffn_ref, g2_ref, ro_ref, rd_ref, gr_ref, qs_ref,
    all_mixed_ref, res_ref, n2_ref, r2_ref, r2t_ref, grd_ref, grdt_ref, wv_ref, sems,
):
    step = pl.program_id(0)
    slots, tensor_count = wv_ref.shape[0], w_ref.shape[1]
    steps = pl.num_programs(0) - tensor_count
    rows = q_ref.shape[0]
    chunks = kv_ref.shape[0] // rows
    ff = b_ref.shape[2] // 3
    part_cols = ff // tensor_count

    def copies(at, to):
        moves = []
        for kind in (2, 0, 1):
            for t in range(tensor_count):
                source = pl.multiple_of((kind * steps + at) * part_cols, LANES)
                target = (kind * tensor_count + t) * part_cols
                moves.append(
                    pltpu.make_async_copy(
                        w_ref.at[:, t, :, pl.ds(source, part_cols)],
                        wv_ref.at[to, :, :, pl.ds(target, part_cols)],
                        sems.at[to, len(moves)],
                    )
                )
        return moves

    @pl.when(step == 0)
    def _():
        key = lax.broadcasted_iota(jnp.int32, bias_ref.shape, 0)
        query = lax.broadcasted_iota(jnp.int32, bias_ref.shape, 1)
        allowed = (key >= query) & (key <= query + WINDOW) & (kseg_ref[...] == qseg_ref[...])
        bias_ref[...] = jnp.where(allowed, 0.0, MASKED)
        vt_ref[...] = turned(kv_ref[:, HD:])
        ffn_ref[...] = jnp.zeros_like(ffn_ref)
        ro_ref[...] = jnp.zeros_like(ro_ref)

    @pl.when((step >= 1) & (step < 1 + slots))
    def _():
        for copy in copies(step - 1, step - 1):
            copy.start()

    @pl.when(step < tensor_count)
    def _():
        lin = mm(n1_ref[...], flat(wq_ref)) + mm(r1_ref[...], bq_ref[0])
        heads = q_ref.shape[1] // HD
        for h in range(heads):
            part = slice(h * HD, (h + 1) * HD)
            query = (rope(lin[:, part], cos_ref[...], sin_ref[...]) * (SCALE * LOG2E)).astype(BF)
            q_ref[:, part] = query
            qs_ref[h * rows : (h + 1) * rows] = query
        queries = qs_ref[...]
        top = jnp.full((1, heads * rows), MASKED, F32)
        for c in range(chunks):
            span = slice(c * rows, (c + 1) * rows)
            s = mm_nt(kv_ref[span, :HD], queries)
            bias = bias_ref[span]
            s = jnp.concatenate([s[:, h * rows : (h + 1) * rows] + bias for h in range(heads)], axis=1)
            s_ref[span] = s
            top = jnp.maximum(top, jnp.max(s, axis=0, keepdims=True))
        total = jnp.zeros((1, heads * rows), F32)
        for c in range(chunks):
            span = slice(c * rows, (c + 1) * rows)
            p = jnp.exp2(s_ref[span] - top)
            total = total + jnp.sum(p, axis=0, keepdims=True)
            p_ref[0, span] = p.astype(BF)
        inv = 1.0 / total
        inv_ref[0, 0:1] = inv
        out = mm(vt_ref[...], p_ref[0]) * inv
        for h in range(heads):
            mixed_ref[:, h * HD : (h + 1) * HD] = out[:, h * rows : (h + 1) * rows].T.astype(BF)
        mixed = mixed_ref[...]
        all_mixed_ref[step] = mixed
        ffn_ref[...] += mm_nt(mixed, flat(wo_ref))
        ro_ref[...] += mm_nt(mixed, bo_ref[0])

    @pl.when(step == tensor_count - 1)
    def _():
        res = x_ref[...].astype(F32) + (ffn_ref[...] + mm_nt(ro_ref[...].astype(BF), a_ref[...]))
        res_ref[...] = res
        n2 = rms(res, gain_ref[...]).astype(BF)
        n2_ref[...] = n2
        r2 = mm(n2, a_ref[...]).astype(BF)
        r2_ref[...] = r2
        r2t_ref[...] = turned(r2)
        grd = mm(cot_ref[...], a_ref[...]).astype(BF)
        grd_ref[...] = grd
        grdt_ref[...] = turned(grd)
        ffn_ref[...] = jnp.zeros_like(ffn_ref)
        g2_ref[...] = jnp.zeros_like(g2_ref)
        rd_ref[...] = jnp.zeros_like(rd_ref)
        gr_ref[...] = jnp.zeros_like(gr_ref)

    @pl.when(step >= tensor_count)
    def _():
        at = step - tensor_count
        slot = lax.rem(at, slots)

        @pl.when((at >= 1) & (at + slots - 1 < steps))
        def _():
            for copy in copies(at + slots - 1, lax.rem(at + slots - 1, slots)):
                copy.start()

        n2, r2, cot = n2_ref[...], r2_ref[...], cot_ref[...]
        b_gu, b_d = b_ref[0, :, : 2 * ff], b_ref[0, :, 2 * ff :]
        arrivals = copies(at, slot)
        weight_rows = wv_ref.shape[1] * wv_ref.shape[2]
        for copy in arrivals[:tensor_count]:
            copy.wait()
        w_d = wv_ref[slot, :, :, 2 * ff :].reshape(weight_rows, ff)
        grad_hidden = (mm(cot, w_d) + mm(grd_ref[...], b_d)).astype(BF).astype(F32)
        for copy in arrivals[tensor_count:]:
            copy.wait()
        w_gu = wv_ref[slot, :, :, : 2 * ff].reshape(weight_rows, 2 * ff)
        lin = mm(n2, w_gu) + mm(r2, b_gu)
        gate, up = lin[:, :ff], lin[:, ff:]
        square = gate * gate
        th = jnp.tanh(GELU_C * (gate + GELU_A * square * gate))
        half = 0.5 * (1.0 + th)
        act = gate * half
        slope = half + 0.5 * gate * (1.0 - th * th) * (GELU_C * (1.0 + 3.0 * GELU_A * square))
        hidden = (act * up).astype(BF)
        grad_gate = (grad_hidden * up * slope).astype(BF)
        grad_up = (grad_hidden * act).astype(BF)
        grads = jnp.concatenate([grad_gate, grad_up], axis=1)
        ffn_ref[...] += mm_nt(hidden, w_d)
        rd_ref[...] += mm_nt(hidden, b_d)
        g2_ref[...] += mm_nt(grads, w_gu)
        gr_ref[...] += mm_nt(grads, b_gu)
        terms = (
            mm(r2t_ref[rows_of(SLOT_G)], grad_gate), mm(r2t_ref[rows_of(SLOT_U)], grad_up),
            mm(grdt_ref[rows_of(SLOT_D)], hidden),
        )
        for kind, term in enumerate(terms):
            target = pl.multiple_of((kind * steps + at) * part_cols, LANES)
            for t in range(tensor_count):
                early_ref[t, :, pl.ds(target, part_cols)] = term[:, t * part_cols : (t + 1) * part_cols].astype(BF)

    @pl.when(step == tensor_count + steps - 1)
    def _():
        res, n2, cot = res_ref[...], n2_ref[...], cot_ref[...]
        out_ref[...] = (res + (ffn_ref[...] + mm_nt(rd_ref[...].astype(BF), a_ref[...]))).astype(BF)
        grad_two = g2_ref[...] + mm_nt(gr_ref[...].astype(BF), a_ref[...])
        grad_res = cot.astype(F32) + rms_back(res, gain_ref[...], grad_two)
        gres_ref[...] = grad_res
        grad_branch = grad_res.astype(BF)
        gb_ref[...] = grad_branch
        gro = mm(grad_branch, a_ref[...])
        gro_ref[...] = gro.astype(BF)
        grot = gro.T[rows_of(SLOT_O)].astype(BF)
        first = 3 * steps * part_cols
        for t in range(tensor_count):
            early_ref[t, :, first:] = mm(grot, all_mixed_ref[t]).astype(BF)
        wide = mm(gr_ref[...].T.astype(BF), n2) + mm(rd_ref[...].T.astype(BF), cot)
        wide_ref[...] = wide + mm(ro_ref[...].T.astype(BF), grad_branch)


def attn_back_kernel(
    kv_ref, gb_ref, gro_ref, r1_ref, cos_ref, sin_ref,
    q_ref, mixed_ref, p_ref, inv_ref, wo_ref, bo_ref, wq_ref, bq_ref,
    dkva_ref, dkvb_ref, dkvc_ref, dkvd_ref, dkve_ref, g1_ref, gr_ref, gbq_ref,
    ds_ref, dk_ref, dv_ref, kt_ref, r1t_ref, gq_ref, gm_ref, qs_ref, gs_ref,
):
    step = pl.program_id(0)
    rows = q_ref.shape[0]
    chunks = kv_ref.shape[0] // rows

    @pl.when(step == 0)
    def _():
        kt_ref[...] = turned(kv_ref[:, :HD])
        r1t_ref[...] = turned(r1_ref[...])
        dk_ref[...] = jnp.zeros_like(dk_ref)
        dv_ref[...] = jnp.zeros_like(dv_ref)
        g1_ref[...] = jnp.zeros_like(g1_ref)
        gr_ref[...] = jnp.zeros_like(gr_ref)

    gm_ref[...] = (mm(gb_ref[...], flat(wo_ref)) + mm(gro_ref[...], bo_ref[0])).astype(BF)
    heads = q_ref.shape[1] // HD
    deltas = []
    for h in range(heads):
        part, span = slice(h * HD, (h + 1) * HD), slice(h * rows, (h + 1) * rows)
        grad = gm_ref[:, part]
        qs_ref[span] = q_ref[:, part]
        gs_ref[span] = grad
        delta = grad.astype(F32) * mixed_ref[:, part].astype(F32)
        deltas.append(jnp.sum(delta.T, axis=0, keepdims=True))
    delta, inv = jnp.concatenate(deltas, axis=1), inv_ref[0, 0:1]
    queries, grads = qs_ref[...], gs_ref[...]
    for c in range(chunks):
        span = slice(c * rows, (c + 1) * rows)
        p = p_ref[0, span].astype(F32) * inv
        dp = mm_nt(kv_ref[span, HD:], grads)
        ds = (p * (dp - delta)).astype(BF)
        ds_ref[span] = ds
        dk_ref[span] += mm(ds, queries)
        dv_ref[span] += mm(p.astype(BF), grads)
    dq = mm(kt_ref[...], ds_ref[...]) * SCALE
    for h in range(heads):
        part, span = slice(h * HD, (h + 1) * HD), slice(h * rows, (h + 1) * rows)
        gq_ref[:, part] = rope_back(dq[:, span].T, cos_ref[...], sin_ref[...]).astype(BF)

    gq = gq_ref[...]
    gbq_ref[0] = mm(r1t_ref[rows_of(SLOT_Q)], gq).astype(BF)
    gr_ref[...] += mm_nt(gq, bq_ref[0])
    g1_ref[...] += mm_nt(gq, flat(wq_ref))

    @pl.when(step == pl.num_programs(0) - 1)
    def _():
        for c, dkv_ref in enumerate((dkva_ref, dkvb_ref, dkvc_ref, dkvd_ref, dkve_ref)):
            span = slice(c * rows, (c + 1) * rows)
            dkv_ref[:, :HD] = (dk_ref[span] * (1.0 / LOG2E)).astype(BF)
            dkv_ref[:, HD:] = dv_ref[span].astype(BF)


def shared_back_kernel(
    chips, core_ref, n1_ref, r1_ref, bkv_ref, cos_ref, sin_ref, own_ref, back1_ref, back2_ref, back3_ref, back4_ref,
    gr_ref, widef_ref,
    mine_ref, theirs_ref, gk_ref, gv_ref, grt_ref,
):
    gkv = own_ref[...].astype(F32)
    for back_ref in (back1_ref, back2_ref, back3_ref, back4_ref):
        gkv = gkv + back_ref[...].astype(F32)
    gk = rope_back(gkv[:, :HD], cos_ref[...], sin_ref[...]).astype(BF)
    gv = gkv[:, HD:].astype(BF)
    gk_ref[...] = gk
    gv_ref[...] = gv
    gr = gr_ref[...] + mm_nt(gk, bkv_ref[0]) + mm_nt(gv, bkv_ref[1])
    grt_ref[...] = gr.astype(BF)
    wide = (mm(gr.T.astype(BF), n1_ref[...]) + widef_ref[...]).T.astype(BF)
    share = mine_ref.shape[0] - 2 * RANK
    wide = wide.reshape(chips, 2, share // chips, LANES)
    first = core_ref[0] == 0
    mine_ref[:share] = jnp.where(first, wide[:, 0], wide[:, 1]).reshape(share, LANES)
    theirs_ref[:share] = jnp.where(first, wide[:, 1], wide[:, 0]).reshape(share, LANES)
    r1t = turned(r1_ref[...])
    for j, (slot, grad) in enumerate(((SLOT_K, gk), (SLOT_V, gv))):
        term = mm(r1t[rows_of(slot)], grad).astype(BF)
        rows = slice(share + j * RANK, share + (j + 1) * RANK)
        mine_ref[rows] = term
        theirs_ref[rows] = term


def payload_kernel(core_ref, mine_ref, other_ref, q_ref, q_other_ref, out_ref):
    first = core_ref[0] == 0
    total = mine_ref[...].astype(F32) + other_ref[...].astype(F32)
    tensor_count = q_ref.shape[0]
    count = out_ref.shape[0]
    own_rows = (total.shape[0] - 2 * RANK) // count
    queries = [(q_ref[t].astype(F32) + q_other_ref[t].astype(F32)).astype(BF) for t in range(tensor_count)]
    blank = jnp.zeros((RANK - own_rows - 2, LANES), F32)
    for n in range(count):
        pieces = [total[n * own_rows : (n + 1) * own_rows]]
        row = (2 * (n // tensor_count) * tensor_count + n % tensor_count) % RANK
        for j in range(2):
            at = count * own_rows + j * RANK + row
            low, high = total[at : at + 1], total[at + tensor_count : at + tensor_count + 1]
            pieces.append(jnp.where(first, low, high))
        out_ref[n, :, :LANES] = jnp.concatenate(pieces + [blank], axis=0).astype(BF)
        out_ref[n, :, LANES:] = queries[n % tensor_count]


def input_kernel(
    x_ref, gain_ref, a_ref, wk_ref, wv_ref, gk_ref, gv_ref, gr_ref, g1_ref, gres_ref, grad_ref,
):
    g1 = g1_ref[...] + mm_nt(gk_ref[...], wk_ref[...]) + mm_nt(gv_ref[...], wv_ref[...])
    g1 = g1 + mm_nt(gr_ref[...], a_ref[...])
    x = x_ref[...].astype(F32)
    grad_ref[...] = gres_ref[...] + rms_back(x, gain_ref[...], g1)


def sum_hidden_kernel(ids_ref, terms_ref, gu_ref, down_ref, out_ref, acc_ref):
    acc_ref[...] = jnp.zeros_like(acc_ref)
    for s in range(terms_ref.shape[0] // 2):
        acc_ref[ids_ref[s]] += terms_ref[2 * s].astype(F32) + terms_ref[2 * s + 1].astype(F32)
    adapters, rank, cols = acc_ref.shape
    ff = gu_ref.shape[2]

    def taken(first, last):
        return acc_ref[:, :, first:last].reshape(adapters * rank, last - first)

    gu_ref[0] = taken(0, ff)
    gu_ref[1] = taken(ff, 2 * ff)
    down_ref[...] = taken(2 * ff, 3 * ff).T
    out_ref[...] = taken(3 * ff, cols).T


def sum_wide_kernel(ids_ref, own_ref, terms_ref, wide_ref, kv_ref, q_ref, acc_ref):
    acc_ref[...] = jnp.zeros_like(acc_ref)
    seqs, parts = terms_ref.shape[:2]
    for s in range(seqs):
        term = terms_ref[s, 0].astype(F32)
        for part in range(1, parts):
            term = term + terms_ref[s, part].astype(F32)
        acc_ref[ids_ref[s]] += term
    adapters, rank, _ = acc_ref.shape
    q_ref[...] = acc_ref[:, :, LANES:].reshape(q_ref.shape)
    lane = lax.broadcasted_iota(jnp.int32, (rank, LANES), 1) // RANK
    own_rows, slots = wide_ref.shape[:2]
    for j in range(slots):
        total = jnp.zeros((rank, LANES), F32)
        for a in range(adapters):
            moved = pltpu.roll(acc_ref[a, :, :LANES], ((a - j) * RANK) % LANES, 1)
            total = jnp.where(lane == a, moved, total)
        wide_ref[:, j] = total[:own_rows]
    mine = acc_ref[own_ref[0], :, :LANES]
    for j in range(2):
        kv_ref[j] = mine[own_rows + j : own_rows + j + 1]


def sds(shape, dtype):
    return jax.ShapeDtypeStruct(shape, dtype)


def scalars():
    return pl.BlockSpec(memory_space=pltpu.SMEM)


def whole(array):
    rank = len(array.shape)
    return pl.BlockSpec(array.shape, lambda *_: (0,) * rank)


def wholes(*arrays):
    return [whole(v) for v in arrays]


def by_step(*shape):
    return pl.BlockSpec((1,) + shape, lambda t: (t,) + (0,) * len(shape))


def call(kernel, name, steps, args, specs, outs, scratch, flops, nbytes):
    shapes = [shape for shape, _ in outs]
    return pl.pallas_call(
        kernel,
        name=name,
        grid=(steps,),
        in_specs=specs,
        out_specs=[whole(shape) if spec is None else spec for shape, spec in outs],
        out_shape=shapes,
        scratch_shapes=scratch,
        compiler_params=pltpu.CompilerParams(
            dimension_semantics=("arbitrary",), vmem_limit_bytes=VMEM_LIMIT
        ),
        cost_estimate=pl.CostEstimate(flops=flops, bytes_accessed=nbytes, transcendentals=0),
    )(*args)


def rope_tables(positions):
    half = HD // 2
    frequency = 10000.0 ** (-(jnp.arange(half).astype(F32) / half))
    angles = positions.astype(F32)[:, None] * frequency[None, :]
    cos, sin = jnp.cos(angles), jnp.sin(angles)
    return jnp.concatenate([cos, cos], axis=1), jnp.concatenate([-sin, sin], axis=1)


def on_device(
    tokens, cotangent, segments, adapter_ids, norm_gains, q_weight, kv_weight, out_weight,
    gate_up_weight, down_weight, wide_adapters, kv_adapter, q_adapter, out_adapter,
    gate_up_adapter, down_adapter,
):
    rows, width = tokens.shape
    tensor_count = lax.axis_size("tensor")
    dp_count = lax.axis_size("y") * lax.axis_size("x") * 2
    devices = dp_count * tensor_count
    group_rows = rows * tensor_count
    seq_length = 2 * group_rows
    shard_rows = q_weight.shape[0]
    q_cols, ff_cols = q_weight.shape[1], gate_up_weight.shape[2]
    heads_cols = tensor_count * q_cols
    seqs = adapter_ids.shape[0]
    adapters = wide_adapters.shape[2] // RANK
    dp = lax.axis_index(DP)
    tensor = lax.axis_index("tensor")
    my_core = lax.axis_index("core")
    adapter = lax.dynamic_index_in_dim(adapter_ids, dp // 2, keepdims=False)
    column = adapter * RANK
    f3 = 3 * ff_cols

    pack = jnp.concatenate(
        [gate_up_weight[0], gate_up_weight[1], down_weight.T, q_weight, out_weight.T], axis=1
    )
    pack, wide_adapters = lax.optimization_barrier((pack, wide_adapters))
    weights = lax.all_gather(pack, ALL, axis=0, tiled=False)
    weights = weights.reshape(dp_count, tensor_count, shard_rows, f3 + 2 * q_cols)

    wide = wide_adapters.reshape(7, shard_rows, adapters, RANK)
    wide = jnp.take(wide, adapter_ids, axis=2).transpose(2, 1, 0, 3)
    wide = wide.reshape(seqs, shard_rows, 7 * RANK)
    wide = jnp.pad(wide, ((0, 0), (0, 0), (0, LANES - 7 * RANK)))
    shared = jnp.broadcast_to(kv_weight[:, None], (2, seqs, shard_rows, HD))
    wide = jnp.concatenate([wide, shared[0], shared[1]], axis=2)

    def from_other_core(value):
        return lax.ppermute(value, "core", [(0, 1), (1, 0)])

    a_own = lax.all_to_all(wide, ("y", "x"), 0, 0, tiled=True)
    a_other = from_other_core(a_own)
    a_all = jnp.where(my_core == 0, jnp.stack([a_own, a_other], 1), jnp.stack([a_other, a_own], 1))
    a_all = a_all.reshape(width, 3 * LANES)

    def take_rows(matrix):
        return lax.dynamic_slice_in_dim(matrix, column, RANK, matrix.ndim - 2)

    def take_cols(matrix):
        return lax.dynamic_slice_in_dim(matrix, column, RANK, matrix.ndim - 1)

    def in_slot(block, slot):
        pads = [(0, 0)] * block.ndim
        pads[-2] = (slot * RANK, LANES - (slot + 1) * RANK)
        return jnp.pad(block, pads)

    gu_rows = take_rows(gate_up_adapter)
    b_own = jnp.concatenate(
        [gu_rows[0], gu_rows[1], take_cols(down_adapter).T, take_rows(q_adapter), take_cols(out_adapter).T], axis=1
    )
    kv_rows = take_rows(kv_adapter)
    b_kv = jnp.stack([in_slot(kv_rows[0], SLOT_K), in_slot(kv_rows[1], SLOT_V)])

    start = dp * group_rows + tensor * rows
    span = WINDOW + rows
    cos_window, sin_window = rope_tables((start - WINDOW + jnp.arange(span)) % seq_length)
    cos, sin = cos_window[WINDOW:], sin_window[WINDOW:]
    padded = jnp.concatenate([jnp.full((WINDOW,), -1, jnp.int32), segments])
    kseg = lax.dynamic_slice_in_dim(padded, start, span, 0)
    qseg = kseg[WINDOW:].reshape(1, rows)
    kseg = kseg.reshape(span, 1)

    gain_one, gain_two = norm_gains[0:1], norm_gains[1:2]
    q_block = f3 // q_cols

    def weight_spec(block):
        return pl.BlockSpec((dp_count, 1, shard_rows, q_cols), lambda t: (0, t, 0, block))

    def adapter_spec(block):
        return pl.BlockSpec((1, LANES, q_cols), lambda t: (t, 0, block))

    def lane_block(block):
        return pl.BlockSpec((width, LANES), lambda *_: (0, block))

    head_specs = [weight_spec(q_block), adapter_spec(0), weight_spec(q_block + 1), adapter_spec(1)]
    q_spec, qb_spec, o_spec, ob_spec = head_specs
    a_spec, wk_spec, wv_spec = lane_block(0), lane_block(1), lane_block(2)
    token_cols = pl.BlockSpec((rows, q_cols), lambda t: (0, t))
    tok_bf, tok_f32, rank_bf = sds((rows, width), BF), sds((rows, width), F32), sds((rows, LANES), BF)

    args = (tokens, gain_one, a_all, a_all, a_all, b_kv, cos, sin)
    normed_one, rank_one, kv_own = call(
        shared_kernel, "keys_values", 1, args,
        wholes(*args[:2]) + [a_spec, wk_spec, wv_spec] + wholes(*args[5:]),
        [(tok_bf, None), (rank_bf, None), (sds((rows, 2 * HD), BF), None)],
        [], 2 * rows * width * 384, 6 * rows * width,
    )
    parts = seq_length // rows
    reach = WINDOW // rows

    def moved(value, steps):
        return lax.ppermute(value, SEQ, [(c, c + steps) for c in range(parts) if 0 <= c + steps < parts])

    kv_window = jnp.concatenate([moved(kv_own, d) for d in range(reach, 0, -1)] + [kv_own])

    b_own, kv_window = lax.optimization_barrier((b_own, kv_window))
    b_all = lax.all_gather(b_own, "tensor", axis=0, tiled=False)
    b_heads = jnp.concatenate(
        [in_slot(b_all[:, :, f3 : f3 + q_cols], SLOT_Q), in_slot(b_all[:, :, f3 + q_cols :], SLOT_O)], axis=2
    )
    steps, slots = ff_cols // LANES, 2
    part_cols = ff_cols // steps
    b_hidden = b_all[:, :, :f3].reshape(tensor_count, RANK, 3, steps, part_cols).transpose(3, 2, 1, 0, 4)
    b_hidden = b_hidden.reshape(steps, 3, RANK, tensor_count * part_cols)
    b_hidden = jnp.concatenate(
        [in_slot(b_hidden[:, kind], slot) for kind, slot in enumerate((SLOT_G, SLOT_U, SLOT_D))], axis=2
    )

    heads = q_cols // HD
    first, last = tensor_count, tensor_count - 1

    def until_last(spec):
        return pl.BlockSpec(spec.block_shape, lambda t: spec.index_map(jnp.minimum(t, last)))

    p_spec, norm_spec = by_step(span, heads * rows), by_step(8, heads * rows)
    hidden_spec = pl.BlockSpec(
        (1, LANES, 3 * tensor_count * part_cols), lambda t: (jnp.maximum(t - first, 0), 0, 0)
    )
    args = (
        kv_window, kseg, qseg, normed_one, rank_one, cos, sin, tokens, cotangent, gain_two, a_all,
        weights, b_heads, weights, b_heads, b_hidden, weights,
    )
    (
        queries, mixed, probs, norms, block_output, grad_residual, grad_branch, wide_ffn, grad_ro, early
    ) = call(
        forward_kernel, "forward", tensor_count + steps, args,
        wholes(*args[:10]) + [a_spec] + [until_last(spec) for spec in head_specs]
        + [hidden_spec, pl.BlockSpec(memory_space=pl.ANY)],
        [
            (sds((rows, heads_cols), BF), until_last(token_cols)), (sds((rows, heads_cols), BF), until_last(token_cols)),
            (sds((tensor_count, span, heads * rows), BF), until_last(p_spec)),
            (sds((tensor_count, 8, heads * rows), F32), until_last(norm_spec)),
            (tok_bf, None), (tok_f32, None), (tok_bf, None), (sds((LANES, width), F32), None), (rank_bf, None),
            (sds((tensor_count, RANK, f3 + q_cols), BF), None),
        ],
        [
            pltpu.VMEM((span, rows), F32), pltpu.VMEM((span, heads * rows), F32), pltpu.VMEM((HD, span), BF),
            pltpu.VMEM((rows, width), F32), pltpu.VMEM((rows, width), F32), pltpu.VMEM((rows, LANES), F32),
            pltpu.VMEM((rows, LANES), F32), pltpu.VMEM((rows, LANES), F32), pltpu.VMEM((heads * rows, HD), BF),
            pltpu.VMEM((tensor_count, rows, q_cols), BF), pltpu.VMEM((rows, width), F32), pltpu.VMEM((rows, width), BF),
            pltpu.VMEM((rows, LANES), BF), pltpu.VMEM((LANES, rows), BF),
            pltpu.VMEM((rows, LANES), BF), pltpu.VMEM((LANES, rows), BF),
            pltpu.VMEM((slots, dp_count, shard_rows, 3 * tensor_count * part_cols), BF),
            pltpu.SemaphoreType.DMA((slots, 3 * tensor_count)),
        ],
        4 * rows * heads_cols * (span + width) + 12 * rows * width * tensor_count * ff_cols,
        4 * width * heads_cols + 6 * width * tensor_count * ff_cols,
    )
    early = lax.psum_scatter(early, "tensor", scatter_dimension=0, tiled=True).reshape(RANK, -1)

    args = (
        kv_window, grad_branch, grad_ro, rank_one, cos, sin, queries, mixed, probs, norms,
        weights, b_heads, weights, b_heads,
    )
    *dkv, grad_one, grad_rank, grad_bq = call(
        attn_back_kernel, "attention_back", tensor_count, args,
        wholes(*args[:6]) + [token_cols, token_cols, p_spec, norm_spec, o_spec, ob_spec, q_spec, qb_spec],
        [
            *[(sds((rows, 2 * HD), BF), None)] * (reach + 1), (tok_f32, None), (sds((rows, LANES), F32), None),
            (sds((tensor_count, RANK, q_cols), BF), by_step(RANK, q_cols)),
        ],
        [
            pltpu.VMEM((span, heads * rows), BF),
            pltpu.VMEM((span, HD), F32), pltpu.VMEM((span, HD), F32), pltpu.VMEM((HD, span), BF),
            pltpu.VMEM((LANES, rows), BF), pltpu.VMEM((rows, q_cols), BF), pltpu.VMEM((rows, q_cols), BF),
            pltpu.VMEM((heads * rows, HD), BF), pltpu.VMEM((heads * rows, HD), BF),
        ],
        2 * rows * heads_cols * (4 * span + 2 * width), 4 * width * heads_cols,
    )

    early, grad_one = lax.optimization_barrier((early, grad_one))
    early = lax.all_gather(early, DP, axis=0, tiled=False)

    backs = [moved(dkv[reach - d], -d) for d in range(1, reach + 1)]
    chips = dp_count // 2
    share = width // 2 + 2 * RANK
    args = (
        my_core.astype(jnp.int32).reshape(1), normed_one, rank_one, b_kv, cos, sin, dkv[reach], *backs, grad_rank, wide_ffn,
    )
    mine, theirs, grad_key, grad_value, grad_rank = call(
        functools.partial(shared_back_kernel, chips), "shared_back", 1, args,
        [scalars()] + wholes(*args[1:]),
        [
            (sds((share, LANES), BF), None), (sds((share, LANES), BF), None),
            (sds((rows, HD), BF), None), (sds((rows, HD), BF), None), (rank_bf, None),
        ],
        [], 4 * rows * width * LANES, 6 * rows * width,
    )
    own_rows = width // devices
    planes = chips * tensor_count
    other, grad_bq_other = from_other_core(theirs), from_other_core(grad_bq)
    args = (my_core.astype(jnp.int32).reshape(1), mine, other, grad_bq, grad_bq_other)
    (payload,) = call(
        payload_kernel, "payload", 1, args, [scalars()] + wholes(*args[1:]),
        [(sds((planes, RANK, LANES + q_cols), BF), None)], [], 0, 2 * planes * RANK * (LANES + q_cols),
    )
    payload, grad_key = lax.optimization_barrier((payload, grad_key))
    terms = lax.all_to_all(payload, PLANES, 0, 0, tiled=True)
    terms = terms.reshape(seqs, tensor_count, RANK, LANES + q_cols)

    args = (
        tokens, gain_one, a_all, a_all, a_all, grad_key, grad_value, grad_rank, grad_one, grad_residual,
    )
    (input_grad,) = call(
        input_kernel, "input_gradient", 1, args,
        wholes(*args[:2]) + [a_spec, wk_spec, wv_spec] + wholes(*args[5:]),
        [(tok_f32, None)], [], 2 * rows * width * 384, 16 * rows * width,
    )

    gate_up_adapter_grad, down_adapter_grad, out_adapter_grad = call(
        sum_hidden_kernel, "sum_hidden", 1, (adapter_ids, early), [scalars()] + wholes(early),
        [(sds((2, LANES, ff_cols), F32), None), (sds((ff_cols, LANES), F32), None), (sds((q_cols, LANES), F32), None)],
        [pltpu.VMEM((adapters, RANK, f3 + q_cols), F32)], 0, 4 * LANES * f3,
    )
    own_adapter = ((dp * tensor_count + tensor) // RANK).astype(jnp.int32).reshape(1)
    wide_grad, kv_adapter_grad, q_adapter_grad = call(
        sum_wide_kernel, "sum_wide", 1, (adapter_ids, own_adapter, terms),
        [scalars(), scalars()] + wholes(terms),
        [(sds((own_rows, 7, LANES), F32), None), (sds((2, 1, HD), F32), None), (sds((LANES, q_cols), F32), None)],
        [pltpu.VMEM((adapters, RANK, LANES + q_cols), F32)], 0, 4 * LANES * f3,
    )
    return (
        block_output, input_grad, wide_grad.transpose(1, 0, 2), kv_adapter_grad,
        q_adapter_grad, out_adapter_grad, gate_up_adapter_grad, down_adapter_grad,
    )


def solution(mesh):
    dp_count, tensor_count = mesh.shape["dp"], mesh.shape["tensor"]
    chips = dp_count // 2
    x_count = math.isqrt(chips)
    devices = mesh.devices.reshape(chips // x_count, x_count, 2, tensor_count)
    return jax.shard_map(
        on_device,
        mesh=Mesh(devices, ALL),
        in_specs=(
            P(ALL, None), P(ALL, None), P(), P(), P(), P(DP, "tensor"), P(None, DP, None),
            P("tensor", DP), P(None, DP, "tensor"), P("tensor", DP), P(None, DP, None), P(),
            P(None, "tensor"), P("tensor", None), P(None, None, "tensor"), P("tensor", None),
        ),
        out_specs=(
            P(ALL, None), P(ALL, None), P(None, ALL, None), P(None, ALL, None),
            P(None, "tensor"), P("tensor", None), P(None, None, "tensor"), P("tensor", None),
        ),
        check_vma=False,
    )
```

```python
import functools
import math

import jax
import jax.numpy as jnp
from jax import lax
from jax.experimental import pallas as pl
from jax.experimental.pallas import tpu as pltpu
from jax.sharding import Mesh, PartitionSpec as P

HD = 128
WINDOW = 1024
RANK = 16
LANES = 128
EPS = 1e-06
MASKED = -1e30
SCALE = HD ** (-0.5)
LOG2E = math.log2(math.e)
GELU_C = 0.7978845608028654
GELU_A = 0.044715
VMEM_LIMIT = 58 * 1024 * 1024
BF = jnp.bfloat16
F32 = jnp.float32
DP = ("y", "x", "core")
SEQ = ("core", "tensor")
PLANES = ("y", "x", "tensor")
ALL = ("y", "x", "core", "tensor")

SLOT_Q, SLOT_K, SLOT_V, SLOT_G, SLOT_U, SLOT_O, SLOT_D = range(7)


def rows_of(slot):
    return slice(slot * RANK, (slot + 1) * RANK)


def mm(a, b):
    return lax.dot_general(a, b, (((1,), (0,)), ((), ())), preferred_element_type=F32)


def mm_nt(a, b):
    return lax.dot_general(a, b, (((1,), (1,)), ((), ())), preferred_element_type=F32)


def turned(a):
    return a.astype(F32).T.astype(BF)


def rope(v, cos, sin):
    return v * cos + pltpu.roll(v, HD // 2, 1) * sin


def rope_back(g, cos, sin):
    return g * cos - pltpu.roll(g, HD // 2, 1) * sin


def flat(ref):
    block = ref[...]
    return block.reshape(block.shape[0] * block.shape[2], block.shape[3])


def rms(v, gain):
    return v * lax.rsqrt(jnp.mean(v * v, axis=-1, keepdims=True) + EPS) * gain


def rms_back(v, gain, grad):
    inv = lax.rsqrt(jnp.mean(v * v, axis=-1, keepdims=True) + EPS)
    scaled = grad * gain
    dot = jnp.mean(v * scaled, axis=-1, keepdims=True)
    return inv * scaled - v * (inv * inv * inv * dot)


def pack_kernel(gu_ref, down_ref, q_ref, o_ref, out_ref):
    ff, cols = gu_ref.shape[2], q_ref.shape[1]
    out_ref[:, :ff] = gu_ref[0]
    out_ref[:, ff : 2 * ff] = gu_ref[1]
    out_ref[:, 2 * ff : 3 * ff] = down_ref[...]
    out_ref[:, 3 * ff : 3 * ff + cols] = q_ref[...]
    out_ref[:, 3 * ff + cols :] = o_ref[...]


def shared_kernel(x_ref, gain_ref, a_ref, wk_ref, wv_ref, bkv_ref, cos_ref, sin_ref, n1_ref, r1_ref, kv_ref):
    n1 = rms(x_ref[...].astype(F32), gain_ref[...]).astype(BF)
    n1_ref[...] = n1
    r1 = mm(n1, a_ref[...]).astype(BF)
    r1_ref[...] = r1
    key = mm(n1, wk_ref[...]) + mm(r1, bkv_ref[0])
    kv_ref[:, :HD] = rope(key, cos_ref[...], sin_ref[...]).astype(BF)
    kv_ref[:, HD:] = (mm(n1, wv_ref[...]) + mm(r1, bkv_ref[1])).astype(BF)


def forward_kernel(
    kv_ref, kseg_ref, qseg_ref, n1_ref, r1_ref, cos_ref, sin_ref, x_ref, cot_ref, gain_ref, a_ref,
    wq_ref, bq_ref, wo_ref, bo_ref, b_ref, w_ref,
    q_ref, mixed_ref, p_ref, inv_ref, out_ref, gres_ref, gb_ref, wide_ref, gro_ref, early_ref,
    bias_ref, s_ref, vt_ref, ffn_ref, g2_ref, ro_ref, rd_ref, gr_ref, qs_ref,
    all_mixed_ref, res_ref, n2_ref, r2_ref, r2t_ref, grd_ref, grdt_ref, wv_ref, sems,
):
    step = pl.program_id(0)
    slots, tensor_count = wv_ref.shape[0], w_ref.shape[1]
    steps = pl.num_programs(0) - tensor_count
    rows = q_ref.shape[0]
    chunks = kv_ref.shape[0] // rows
    ff = b_ref.shape[2] // 3
    part_cols = ff // tensor_count

    def copies(at, to):
        moves = []
        for kind in (2, 0, 1):
            for t in range(tensor_count):
                source = pl.multiple_of((kind * steps + at) * part_cols, LANES)
                target = (kind * tensor_count + t) * part_cols
                moves.append(
                    pltpu.make_async_copy(
                        w_ref.at[:, t, :, pl.ds(source, part_cols)],
                        wv_ref.at[to, :, :, pl.ds(target, part_cols)],
                        sems.at[to, len(moves)],
                    )
                )
        return moves

    @pl.when(step == 0)
    def _():
        key = lax.broadcasted_iota(jnp.int32, bias_ref.shape, 0)
        query = lax.broadcasted_iota(jnp.int32, bias_ref.shape, 1)
        allowed = (key >= query) & (key <= query + WINDOW) & (kseg_ref[...] == qseg_ref[...])
        bias_ref[...] = jnp.where(allowed, 0.0, MASKED)
        vt_ref[...] = turned(kv_ref[:, HD:])
        ffn_ref[...] = jnp.zeros_like(ffn_ref)
        ro_ref[...] = jnp.zeros_like(ro_ref)

    @pl.when((step >= 1) & (step < 1 + slots))
    def _():
        for copy in copies(step - 1, step - 1):
            copy.start()

    @pl.when(step < tensor_count)
    def _():
        lin = mm(n1_ref[...], flat(wq_ref)) + mm(r1_ref[...], bq_ref[0])
        heads = q_ref.shape[1] // HD
        for h in range(heads):
            part = slice(h * HD, (h + 1) * HD)
            query = (rope(lin[:, part], cos_ref[...], sin_ref[...]) * (SCALE * LOG2E)).astype(BF)
            q_ref[:, part] = query
            qs_ref[h * rows : (h + 1) * rows] = query
        queries = qs_ref[...]
        top = jnp.full((1, heads * rows), MASKED, F32)
        for c in range(chunks):
            span = slice(c * rows, (c + 1) * rows)
            s = mm_nt(kv_ref[span, :HD], queries)
            bias = bias_ref[span]
            s = jnp.concatenate([s[:, h * rows : (h + 1) * rows] + bias for h in range(heads)], axis=1)
            s_ref[span] = s
            top = jnp.maximum(top, jnp.max(s, axis=0, keepdims=True))
        total = jnp.zeros((1, heads * rows), F32)
        for c in range(chunks):
            span = slice(c * rows, (c + 1) * rows)
            p = jnp.exp2(s_ref[span] - top)
            total = total + jnp.sum(p, axis=0, keepdims=True)
            p_ref[0, span] = p.astype(BF)
        inv = 1.0 / total
        inv_ref[0, 0:1] = inv
        out = mm(vt_ref[...], p_ref[0]) * inv
        for h in range(heads):
            mixed_ref[:, h * HD : (h + 1) * HD] = out[:, h * rows : (h + 1) * rows].T.astype(BF)
        mixed = mixed_ref[...]
        all_mixed_ref[step] = mixed
        ffn_ref[...] += mm_nt(mixed, flat(wo_ref))
        ro_ref[...] += mm_nt(mixed, bo_ref[0])

    @pl.when(step == tensor_count - 1)
    def _():
        res = x_ref[...].astype(F32) + (ffn_ref[...] + mm_nt(ro_ref[...].astype(BF), a_ref[...]))
        res_ref[...] = res
        n2 = rms(res, gain_ref[...]).astype(BF)
        n2_ref[...] = n2
        r2 = mm(n2, a_ref[...]).astype(BF)
        r2_ref[...] = r2
        r2t_ref[...] = turned(r2)
        grd = mm(cot_ref[...], a_ref[...]).astype(BF)
        grd_ref[...] = grd
        grdt_ref[...] = turned(grd)
        ffn_ref[...] = jnp.zeros_like(ffn_ref)
        g2_ref[...] = jnp.zeros_like(g2_ref)
        rd_ref[...] = jnp.zeros_like(rd_ref)
        gr_ref[...] = jnp.zeros_like(gr_ref)

    @pl.when(step >= tensor_count)
    def _():
        at = step - tensor_count
        slot = lax.rem(at, slots)

        @pl.when((at >= 1) & (at + slots - 1 < steps))
        def _():
            for copy in copies(at + slots - 1, lax.rem(at + slots - 1, slots)):
                copy.start()

        n2, r2, cot = n2_ref[...], r2_ref[...], cot_ref[...]
        b_gu, b_d = b_ref[0, :, : 2 * ff], b_ref[0, :, 2 * ff :]
        arrivals = copies(at, slot)
        weight_rows = wv_ref.shape[1] * wv_ref.shape[2]
        for copy in arrivals[:tensor_count]:
            copy.wait()
        w_d = wv_ref[slot, :, :, 2 * ff :].reshape(weight_rows, ff)
        grad_hidden = (mm(cot, w_d) + mm(grd_ref[...], b_d)).astype(BF).astype(F32)
        for copy in arrivals[tensor_count:]:
            copy.wait()
        w_gu = wv_ref[slot, :, :, : 2 * ff].reshape(weight_rows, 2 * ff)
        lin = mm(n2, w_gu) + mm(r2, b_gu)
        gate, up = lin[:, :ff], lin[:, ff:]
        square = gate * gate
        th = jnp.tanh(GELU_C * (gate + GELU_A * square * gate))
        half = 0.5 * (1.0 + th)
        act = gate * half
        slope = half + 0.5 * gate * (1.0 - th * th) * (GELU_C * (1.0 + 3.0 * GELU_A * square))
        hidden = (act * up).astype(BF)
        grad_gate = (grad_hidden * up * slope).astype(BF)
        grad_up = (grad_hidden * act).astype(BF)
        grads = jnp.concatenate([grad_gate, grad_up], axis=1)
        ffn_ref[...] += mm_nt(hidden, w_d)
        rd_ref[...] += mm_nt(hidden, b_d)
        g2_ref[...] += mm_nt(grads, w_gu)
        gr_ref[...] += mm_nt(grads, b_gu)
        terms = (
            mm(r2t_ref[rows_of(SLOT_G)], grad_gate), mm(r2t_ref[rows_of(SLOT_U)], grad_up),
            mm(grdt_ref[rows_of(SLOT_D)], hidden),
        )
        for kind, term in enumerate(terms):
            target = pl.multiple_of((kind * steps + at) * part_cols, LANES)
            for t in range(tensor_count):
                early_ref[t, :, pl.ds(target, part_cols)] = term[:, t * part_cols : (t + 1) * part_cols].astype(BF)

    @pl.when(step == tensor_count + steps - 1)
    def _():
        res, n2, cot = res_ref[...], n2_ref[...], cot_ref[...]
        out_ref[...] = (res + (ffn_ref[...] + mm_nt(rd_ref[...].astype(BF), a_ref[...]))).astype(BF)
        grad_two = g2_ref[...] + mm_nt(gr_ref[...].astype(BF), a_ref[...])
        grad_res = cot.astype(F32) + rms_back(res, gain_ref[...], grad_two)
        gres_ref[...] = grad_res
        grad_branch = grad_res.astype(BF)
        gb_ref[...] = grad_branch
        gro = mm(grad_branch, a_ref[...])
        gro_ref[...] = gro.astype(BF)
        grot = gro.T[rows_of(SLOT_O)].astype(BF)
        first = 3 * steps * part_cols
        for t in range(tensor_count):
            early_ref[t, :, first:] = mm(grot, all_mixed_ref[t]).astype(BF)
        wide = mm(gr_ref[...].T.astype(BF), n2) + mm(rd_ref[...].T.astype(BF), cot)
        wide_ref[...] = wide + mm(ro_ref[...].T.astype(BF), grad_branch)


def attn_back_kernel(
    tensor_ref, kv_ref, gb_ref, gro_ref, r1_ref, cos_ref, sin_ref,
    q_ref, mixed_ref, p_ref, inv_ref, wo_ref, bo_ref, wq_ref, bq_ref,
    dkva_ref, dkvb_ref, dkvc_ref, dkvd_ref, dkve_ref, q0_ref, g1_ref, gr_ref,
    ds_ref, dk_ref, dv_ref, kt_ref, r1t_ref, gq_ref, gm_ref, qs_ref, gs_ref,
):
    step = pl.program_id(0)
    rows = q_ref.shape[0]
    chunks = kv_ref.shape[0] // rows

    @pl.when(step == 0)
    def _():
        kt_ref[...] = turned(kv_ref[:, :HD])
        r1t_ref[...] = turned(r1_ref[...])
        dk_ref[...] = jnp.zeros_like(dk_ref)
        dv_ref[...] = jnp.zeros_like(dv_ref)
        g1_ref[...] = jnp.zeros_like(g1_ref)
        gr_ref[...] = jnp.zeros_like(gr_ref)

    gm_ref[...] = (mm(gb_ref[...], flat(wo_ref)) + mm(gro_ref[...], bo_ref[0])).astype(BF)
    heads = q_ref.shape[1] // HD
    deltas = []
    for h in range(heads):
        part, span = slice(h * HD, (h + 1) * HD), slice(h * rows, (h + 1) * rows)
        grad = gm_ref[:, part]
        qs_ref[span] = q_ref[:, part]
        gs_ref[span] = grad
        delta = grad.astype(F32) * mixed_ref[:, part].astype(F32)
        deltas.append(jnp.sum(delta.T, axis=0, keepdims=True))
    delta, inv = jnp.concatenate(deltas, axis=1), inv_ref[0, 0:1]
    queries, grads = qs_ref[...], gs_ref[...]
    for c in range(chunks):
        span = slice(c * rows, (c + 1) * rows)
        p = p_ref[0, span].astype(F32) * inv
        dp = mm_nt(kv_ref[span, HD:], grads)
        ds = (p * (dp - delta)).astype(BF)
        ds_ref[span] = ds
        dk_ref[span] += mm(ds, queries)
        dv_ref[span] += mm(p.astype(BF), grads)
    dq = mm(kt_ref[...], ds_ref[...]) * SCALE
    for h in range(heads):
        part, span = slice(h * HD, (h + 1) * HD), slice(h * rows, (h + 1) * rows)
        gq_ref[:, part] = rope_back(dq[:, span].T, cos_ref[...], sin_ref[...]).astype(BF)

    gq = gq_ref[...]
    grad_bq = mm(r1t_ref[rows_of(SLOT_Q)], gq).astype(BF)
    away = lax.rem(tensor_ref[0] + pl.num_programs(0) - step, pl.num_programs(0))

    @pl.when(away == 0)
    def _():
        q0_ref[...] = grad_bq

    for d, dkv_ref in ((1, dkvd_ref), (2, dkvc_ref), (3, dkvb_ref)):

        @pl.when(away == d)
        def _(dkv_ref=dkv_ref):
            dkv_ref[rows : rows + RANK] = grad_bq[:, : 2 * HD]
            dkv_ref[rows + RANK :, :HD] = grad_bq[:, 2 * HD :]
            dkv_ref[rows + RANK :, HD:] = jnp.zeros((RANK, HD), BF)

    gr_ref[...] += mm_nt(gq, bq_ref[0])
    g1_ref[...] += mm_nt(gq, flat(wq_ref))

    @pl.when(step == pl.num_programs(0) - 1)
    def _():
        for c, dkv_ref in enumerate((dkva_ref, dkvb_ref, dkvc_ref, dkvd_ref, dkve_ref)):
            span = slice(c * rows, (c + 1) * rows)
            dkv_ref[:rows, :HD] = (dk_ref[span] * (1.0 / LOG2E)).astype(BF)
            dkv_ref[:rows, HD:] = dv_ref[span].astype(BF)


def shared_back_kernel(
    chips, core_ref, n1_ref, r1_ref, bkv_ref, cos_ref, sin_ref, own_ref, back1_ref, back2_ref, back3_ref, back4_ref,
    q0_ref, gr_ref, widef_ref,
    mine_ref, theirs_ref, gk_ref, gv_ref, grt_ref,
):
    rows = own_ref.shape[0]
    gkv = own_ref[...].astype(F32)
    for back_ref in (back1_ref, back2_ref, back3_ref, back4_ref):
        gkv = gkv + back_ref[:rows].astype(F32)
    queries = [q0_ref[:, j * LANES : (j + 1) * LANES].astype(F32) for j in range(3)]
    for back_ref in (back1_ref, back2_ref, back3_ref):
        queries[0] = queries[0] + back_ref[rows : rows + RANK, :HD].astype(F32)
        queries[1] = queries[1] + back_ref[rows : rows + RANK, HD:].astype(F32)
        queries[2] = queries[2] + back_ref[rows + RANK :, :HD].astype(F32)
    gk = rope_back(gkv[:, :HD], cos_ref[...], sin_ref[...]).astype(BF)
    gv = gkv[:, HD:].astype(BF)
    gk_ref[...] = gk
    gv_ref[...] = gv
    gr = gr_ref[...] + mm_nt(gk, bkv_ref[0]) + mm_nt(gv, bkv_ref[1])
    grt_ref[...] = gr.astype(BF)
    wide = (mm(gr.T.astype(BF), n1_ref[...]) + widef_ref[...]).T.astype(BF)
    share = mine_ref.shape[0] - 5 * RANK
    wide = wide.reshape(chips, 2, share // chips, LANES)
    first = core_ref[0] == 0
    mine_ref[:share] = jnp.where(first, wide[:, 0], wide[:, 1]).reshape(share, LANES)
    theirs_ref[:share] = jnp.where(first, wide[:, 1], wide[:, 0]).reshape(share, LANES)
    r1t = turned(r1_ref[...])
    for j, (slot, grad) in enumerate(((SLOT_K, gk), (SLOT_V, gv))):
        term = mm(r1t[rows_of(slot)], grad).astype(BF)
        part = slice(share + j * RANK, share + (j + 1) * RANK)
        mine_ref[part] = term
        theirs_ref[part] = term
    for j, term in enumerate(queries):
        part = slice(share + (2 + j) * RANK, share + (3 + j) * RANK)
        mine_ref[part] = term.astype(BF)
        theirs_ref[part] = term.astype(BF)


def payload_kernel(core_ref, mine_ref, other_ref, out_ref, q_ref):
    first = core_ref[0] == 0
    total = mine_ref[...].astype(F32) + other_ref[...].astype(F32)
    count = out_ref.shape[0]
    own_rows = (total.shape[0] - 5 * RANK) // count
    queries = total[total.shape[0] - 3 * RANK :].astype(BF)
    for n in range(q_ref.shape[0]):
        for j in range(3):
            q_ref[n, :, j * LANES : (j + 1) * LANES] = queries[j * RANK : (j + 1) * RANK]
    tensor_count = RANK // 4
    blank = jnp.zeros((RANK - own_rows - 2, LANES), F32)
    for n in range(count):
        pieces = [total[n * own_rows : (n + 1) * own_rows]]
        row = (2 * (n // tensor_count) * tensor_count + n % tensor_count) % RANK
        for j in range(2):
            at = count * own_rows + j * RANK + row
            low, high = total[at : at + 1], total[at + tensor_count : at + tensor_count + 1]
            pieces.append(jnp.where(first, low, high))
        out_ref[n] = jnp.concatenate(pieces + [blank], axis=0).astype(BF)


def input_kernel(
    x_ref, gain_ref, a_ref, wk_ref, wv_ref, gk_ref, gv_ref, gr_ref, g1_ref, gres_ref, grad_ref,
):
    g1 = g1_ref[...] + mm_nt(gk_ref[...], wk_ref[...]) + mm_nt(gv_ref[...], wv_ref[...])
    g1 = g1 + mm_nt(gr_ref[...], a_ref[...])
    x = x_ref[...].astype(F32)
    grad_ref[...] = gres_ref[...] + rms_back(x, gain_ref[...], g1)


def sum_hidden_kernel(ids_ref, terms_ref, gu_ref, down_ref, out_ref, acc_ref):
    acc_ref[...] = jnp.zeros_like(acc_ref)
    for s in range(terms_ref.shape[0] // 2):
        acc_ref[ids_ref[s]] += terms_ref[2 * s].astype(F32) + terms_ref[2 * s + 1].astype(F32)
    adapters, rank, _ = acc_ref.shape
    ff, heads = gu_ref.shape[2], out_ref.shape[0]

    def taken(first, count):
        return acc_ref[:, :, first : first + count].reshape(adapters * rank, count)

    gu_ref[0] = taken(0, ff)
    gu_ref[1] = taken(ff, ff)
    down_ref[...] = taken(2 * ff, ff).T
    out_ref[...] = taken(3 * ff, heads).T


def sum_wide_kernel(ids_ref, own_ref, terms_ref, *rest):
    q_refs, (wide_ref, kv_ref, q_ref, acc_ref, accq_ref) = rest[:-5], rest[-5:]
    acc_ref[...] = jnp.zeros_like(acc_ref)
    accq_ref[...] = jnp.zeros_like(accq_ref)
    y_count, x_count = len(q_refs), q_refs[0].shape[0]
    for away_y, terms in enumerate(q_refs):
        y = lax.rem(own_ref[1] + away_y, y_count)
        for away_x in range(x_count):
            x = lax.rem(own_ref[2] + away_x, x_count)
            accq_ref[ids_ref[y * x_count + x]] += terms[away_x].astype(F32)
    q_ref[...] = accq_ref[...].reshape(q_ref.shape)
    seqs, parts = terms_ref.shape[:2]
    for s in range(seqs):
        term = terms_ref[s, 0].astype(F32)
        for part in range(1, parts):
            term = term + terms_ref[s, part].astype(F32)
        acc_ref[ids_ref[s]] += term
    adapters, rank, _ = acc_ref.shape
    lane = lax.broadcasted_iota(jnp.int32, (rank, LANES), 1) // RANK
    own_rows, slots = wide_ref.shape[:2]
    for j in range(slots):
        total = jnp.zeros((rank, LANES), F32)
        for a in range(adapters):
            moved = pltpu.roll(acc_ref[a], ((a - j) * RANK) % LANES, 1)
            total = jnp.where(lane == a, moved, total)
        wide_ref[:, j] = total[:own_rows]
    mine = acc_ref[own_ref[0]]
    for j in range(2):
        kv_ref[j] = mine[own_rows + j : own_rows + j + 1]


def sds(shape, dtype):
    return jax.ShapeDtypeStruct(shape, dtype)


def scalars():
    return pl.BlockSpec(memory_space=pltpu.SMEM)


def whole(array):
    rank = len(array.shape)
    return pl.BlockSpec(array.shape, lambda *_: (0,) * rank)


def wholes(*arrays):
    return [whole(v) for v in arrays]


def by_step(*shape):
    return pl.BlockSpec((1,) + shape, lambda t: (t,) + (0,) * len(shape))


def call(kernel, name, steps, args, specs, outs, scratch, flops, nbytes):
    shapes = [shape for shape, _ in outs]
    return pl.pallas_call(
        kernel,
        name=name,
        grid=(steps,),
        in_specs=specs,
        out_specs=[whole(shape) if spec is None else spec for shape, spec in outs],
        out_shape=shapes,
        scratch_shapes=scratch,
        compiler_params=pltpu.CompilerParams(
            dimension_semantics=("arbitrary",), vmem_limit_bytes=VMEM_LIMIT
        ),
        cost_estimate=pl.CostEstimate(flops=flops, bytes_accessed=nbytes, transcendentals=0),
    )(*args)


def rope_tables(positions):
    half = HD // 2
    frequency = 10000.0 ** (-(jnp.arange(half).astype(F32) / half))
    angles = positions.astype(F32)[:, None] * frequency[None, :]
    cos, sin = jnp.cos(angles), jnp.sin(angles)
    return jnp.concatenate([cos, cos], axis=1), jnp.concatenate([-sin, sin], axis=1)


def on_device(
    tokens, cotangent, segments, adapter_ids, norm_gains, q_weight, kv_weight, out_weight,
    gate_up_weight, down_weight, wide_adapters, kv_adapter, q_adapter, out_adapter,
    gate_up_adapter, down_adapter,
):
    rows, width = tokens.shape
    tensor_count = lax.axis_size("tensor")
    dp_count = lax.axis_size("y") * lax.axis_size("x") * 2
    devices = dp_count * tensor_count
    group_rows = rows * tensor_count
    seq_length = 2 * group_rows
    shard_rows = q_weight.shape[0]
    q_cols, ff_cols = q_weight.shape[1], gate_up_weight.shape[2]
    heads_cols = tensor_count * q_cols
    seqs = adapter_ids.shape[0]
    adapters = wide_adapters.shape[2] // RANK
    dp = lax.axis_index(DP)
    tensor = lax.axis_index("tensor")
    my_core = lax.axis_index("core")
    adapter = lax.dynamic_index_in_dim(adapter_ids, dp // 2, keepdims=False)
    column = adapter * RANK
    f3 = 3 * ff_cols

    args = (gate_up_weight, down_weight.T, q_weight, out_weight.T)
    (pack,) = call(
        pack_kernel, "pack", 1, args, wholes(*args), [(sds((shard_rows, f3 + 2 * q_cols), BF), None)], [],
        0, 4 * shard_rows * (f3 + 2 * q_cols),
    )
    pack, wide_adapters = lax.optimization_barrier((pack, wide_adapters))
    weights = lax.all_gather(pack, ALL, axis=0, tiled=False)
    weights = weights.reshape(dp_count, tensor_count, shard_rows, f3 + 2 * q_cols)

    wide = wide_adapters.reshape(7, shard_rows, adapters, RANK)
    wide = jnp.take(wide, adapter_ids, axis=2).transpose(2, 1, 0, 3)
    wide = wide.reshape(seqs, shard_rows, 7 * RANK)
    wide = jnp.pad(wide, ((0, 0), (0, 0), (0, LANES - 7 * RANK)))
    shared = jnp.broadcast_to(kv_weight[:, None], (2, seqs, shard_rows, HD))
    wide = jnp.concatenate([wide, shared[0], shared[1]], axis=2)

    def from_other_core(value):
        return lax.ppermute(value, "core", [(0, 1), (1, 0)])

    a_own = lax.all_to_all(wide, ("y", "x"), 0, 0, tiled=True)
    a_other = from_other_core(a_own)
    a_all = jnp.where(my_core == 0, jnp.stack([a_own, a_other], 1), jnp.stack([a_other, a_own], 1))
    a_all = a_all.reshape(width, 3 * LANES)

    def take_rows(matrix):
        return lax.dynamic_slice_in_dim(matrix, column, RANK, matrix.ndim - 2)

    def take_cols(matrix):
        return lax.dynamic_slice_in_dim(matrix, column, RANK, matrix.ndim - 1)

    def in_slot(block, slot):
        pads = [(0, 0)] * block.ndim
        pads[-2] = (slot * RANK, LANES - (slot + 1) * RANK)
        return jnp.pad(block, pads)

    gu_rows = take_rows(gate_up_adapter)
    b_own = jnp.concatenate(
        [gu_rows[0], gu_rows[1], take_cols(down_adapter).T, take_rows(q_adapter), take_cols(out_adapter).T], axis=1
    )
    b_parts = [b_own] + [
        lax.ppermute(b_own, "tensor", [((z + d) % tensor_count, z) for z in range(tensor_count)])
        for d in range(1, tensor_count)
    ]
    kv_rows = take_rows(kv_adapter)
    b_kv = jnp.stack([in_slot(kv_rows[0], SLOT_K), in_slot(kv_rows[1], SLOT_V)])

    start = dp * group_rows + tensor * rows
    span = WINDOW + rows
    cos_window, sin_window = rope_tables((start - WINDOW + jnp.arange(span)) % seq_length)
    cos, sin = cos_window[WINDOW:], sin_window[WINDOW:]
    padded = jnp.concatenate([jnp.full((WINDOW,), -1, jnp.int32), segments])
    kseg = lax.dynamic_slice_in_dim(padded, start, span, 0)
    qseg = kseg[WINDOW:].reshape(1, rows)
    kseg = kseg.reshape(span, 1)

    gain_one, gain_two = norm_gains[0:1], norm_gains[1:2]
    q_block = f3 // q_cols

    def weight_spec(block):
        return pl.BlockSpec((dp_count, 1, shard_rows, q_cols), lambda t: (0, t, 0, block))

    def adapter_spec(block):
        return pl.BlockSpec((1, LANES, q_cols), lambda t: (t, 0, block))

    def lane_block(block):
        return pl.BlockSpec((width, LANES), lambda *_: (0, block))

    head_specs = [weight_spec(q_block), adapter_spec(0), weight_spec(q_block + 1), adapter_spec(1)]
    q_spec, qb_spec, o_spec, ob_spec = head_specs
    a_spec, wk_spec, wv_spec = lane_block(0), lane_block(1), lane_block(2)
    token_cols = pl.BlockSpec((rows, q_cols), lambda t: (0, t))
    tok_bf, tok_f32, rank_bf = sds((rows, width), BF), sds((rows, width), F32), sds((rows, LANES), BF)

    args = (tokens, gain_one, a_all, a_all, a_all, b_kv, cos, sin)
    normed_one, rank_one, kv_own = call(
        shared_kernel, "keys_values", 1, args,
        wholes(*args[:2]) + [a_spec, wk_spec, wv_spec] + wholes(*args[5:]),
        [(tok_bf, None), (rank_bf, None), (sds((rows, 2 * HD), BF), None)],
        [], 2 * rows * width * 384, 6 * rows * width,
    )
    parts = seq_length // rows
    reach = WINDOW // rows

    def moved(value, steps):
        return lax.ppermute(value, SEQ, [(c, c + steps) for c in range(parts) if 0 <= c + steps < parts])

    kv_window = jnp.concatenate([moved(kv_own, d) for d in range(reach, 0, -1)] + [kv_own])

    b_all = jnp.roll(jnp.stack(b_parts), tensor, axis=0)
    b_heads = jnp.concatenate(
        [in_slot(b_all[:, :, f3 : f3 + q_cols], SLOT_Q), in_slot(b_all[:, :, f3 + q_cols :], SLOT_O)], axis=2
    )
    steps, slots = ff_cols // LANES, 2
    part_cols = ff_cols // steps
    b_hidden = b_all[:, :, :f3].reshape(tensor_count, RANK, 3, steps, part_cols).transpose(3, 2, 1, 0, 4)
    b_hidden = b_hidden.reshape(steps, 3, RANK, tensor_count * part_cols)
    b_hidden = jnp.concatenate(
        [in_slot(b_hidden[:, kind], slot) for kind, slot in enumerate((SLOT_G, SLOT_U, SLOT_D))], axis=2
    )

    heads = q_cols // HD
    first, last = tensor_count, tensor_count - 1

    def until_last(spec):
        return pl.BlockSpec(spec.block_shape, lambda t: spec.index_map(jnp.minimum(t, last)))

    p_spec, norm_spec = by_step(span, heads * rows), by_step(8, heads * rows)
    hidden_spec = pl.BlockSpec(
        (1, LANES, 3 * tensor_count * part_cols), lambda t: (jnp.maximum(t - first, 0), 0, 0)
    )
    args = (
        kv_window, kseg, qseg, normed_one, rank_one, cos, sin, tokens, cotangent, gain_two, a_all,
        weights, b_heads, weights, b_heads, b_hidden, weights,
    )
    (
        queries, mixed, probs, norms, block_output, grad_residual, grad_branch, wide_ffn, grad_ro, early
    ) = call(
        forward_kernel, "forward", tensor_count + steps, args,
        wholes(*args[:10]) + [a_spec] + [until_last(spec) for spec in head_specs]
        + [hidden_spec, pl.BlockSpec(memory_space=pl.ANY)],
        [
            (sds((rows, heads_cols), BF), until_last(token_cols)), (sds((rows, heads_cols), BF), until_last(token_cols)),
            (sds((tensor_count, span, heads * rows), BF), until_last(p_spec)),
            (sds((tensor_count, 8, heads * rows), F32), until_last(norm_spec)),
            (tok_bf, None), (tok_f32, None), (tok_bf, None), (sds((LANES, width), F32), None), (rank_bf, None),
            (sds((tensor_count, RANK, f3 + q_cols), BF), None),
        ],
        [
            pltpu.VMEM((span, rows), F32), pltpu.VMEM((span, heads * rows), F32), pltpu.VMEM((HD, span), BF),
            pltpu.VMEM((rows, width), F32), pltpu.VMEM((rows, width), F32), pltpu.VMEM((rows, LANES), F32),
            pltpu.VMEM((rows, LANES), F32), pltpu.VMEM((rows, LANES), F32), pltpu.VMEM((heads * rows, HD), BF),
            pltpu.VMEM((tensor_count, rows, q_cols), BF), pltpu.VMEM((rows, width), F32), pltpu.VMEM((rows, width), BF),
            pltpu.VMEM((rows, LANES), BF), pltpu.VMEM((LANES, rows), BF),
            pltpu.VMEM((rows, LANES), BF), pltpu.VMEM((LANES, rows), BF),
            pltpu.VMEM((slots, dp_count, shard_rows, 3 * tensor_count * part_cols), BF),
            pltpu.SemaphoreType.DMA((slots, 3 * tensor_count)),
        ],
        4 * rows * heads_cols * (span + width) + 12 * rows * width * tensor_count * ff_cols,
        4 * width * heads_cols + 6 * width * tensor_count * ff_cols,
    )
    early = lax.psum_scatter(early, "tensor", scatter_dimension=0, tiled=True).reshape(RANK, -1)

    args = (
        tensor.astype(jnp.int32).reshape(1), kv_window, grad_branch, grad_ro, rank_one, cos, sin,
        queries, mixed, probs, norms, weights, b_heads, weights, b_heads,
    )
    *dkv, q_own, grad_one, grad_rank = call(
        attn_back_kernel, "attention_back", tensor_count, args,
        [scalars()] + wholes(*args[1:7]) + [token_cols, token_cols, p_spec, norm_spec, o_spec, ob_spec, q_spec, qb_spec],
        [
            *[(sds((rows + (2 * RANK if 0 < w < reach else 0), 2 * HD), BF), None) for w in range(reach + 1)],
            (sds((RANK, q_cols), BF), None), (tok_f32, None), (sds((rows, LANES), F32), None),
        ],
        [
            pltpu.VMEM((span, heads * rows), BF),
            pltpu.VMEM((span, HD), F32), pltpu.VMEM((span, HD), F32), pltpu.VMEM((HD, span), BF),
            pltpu.VMEM((LANES, rows), BF), pltpu.VMEM((rows, q_cols), BF), pltpu.VMEM((rows, q_cols), BF),
            pltpu.VMEM((heads * rows, HD), BF), pltpu.VMEM((heads * rows, HD), BF),
        ],
        2 * rows * heads_cols * (4 * span + 2 * width), 4 * width * heads_cols,
    )

    early, grad_one = lax.optimization_barrier((early, grad_one))
    early = lax.all_gather(early, DP, axis=0, tiled=False)

    def around(value, steps):
        return lax.ppermute(value, SEQ, [(c, (c - steps) % parts) for c in range(parts)])

    backs = [around(dkv[reach - d], d) for d in range(1, reach)] + [moved(dkv[0], -reach)]
    core = my_core.astype(jnp.int32).reshape(1)
    chips = dp_count // 2
    share = width // 2 + 5 * RANK
    args = (
        core, normed_one, rank_one, b_kv, cos, sin, dkv[reach], *backs, q_own, grad_rank, wide_ffn,
    )
    mine, theirs, grad_key, grad_value, grad_rank = call(
        functools.partial(shared_back_kernel, chips), "shared_back", 1, args,
        [scalars()] + wholes(*args[1:]),
        [
            (sds((share, LANES), BF), None), (sds((share, LANES), BF), None),
            (sds((rows, HD), BF), None), (sds((rows, HD), BF), None), (rank_bf, None),
        ],
        [], 4 * rows * width * LANES, 6 * rows * width,
    )
    own_rows = width // devices
    planes = chips * tensor_count
    args = (core, mine, from_other_core(theirs))
    payload, q_terms = call(
        payload_kernel, "payload", 1, args, [scalars()] + wholes(*args[1:]),
        [(sds((planes, RANK, LANES), BF), None), (sds((1, RANK, q_cols), BF), None)], [],
        0, 2 * planes * RANK * LANES,
    )
    payload, grad_key = lax.optimization_barrier((payload, grad_key))
    terms = lax.all_to_all(payload, PLANES, 0, 0, tiled=True)

    def with_others(value, axis):
        count = lax.axis_size(axis)
        return [value] + [
            lax.ppermute(value, axis, [((i + d) % count, i) for i in range(count)]) for d in range(1, count)
        ]

    q_terms = with_others(jnp.concatenate(with_others(q_terms, "x")), "y")
    terms = terms.reshape(seqs, tensor_count, RANK, LANES)

    args = (
        tokens, gain_one, a_all, a_all, a_all, grad_key, grad_value, grad_rank, grad_one, grad_residual,
    )
    (input_grad,) = call(
        input_kernel, "input_gradient", 1, args,
        wholes(*args[:2]) + [a_spec, wk_spec, wv_spec] + wholes(*args[5:]),
        [(tok_f32, None)], [], 2 * rows * width * 384, 16 * rows * width,
    )

    terms, input_grad = lax.optimization_barrier((terms, input_grad))
    own = jnp.stack([(dp * tensor_count + tensor) // RANK, lax.axis_index("y"), lax.axis_index("x")]).astype(jnp.int32)
    wide_grad, kv_adapter_grad, q_adapter_grad = call(
        sum_wide_kernel, "sum_wide", 1, (adapter_ids, own, terms, *q_terms),
        [scalars(), scalars()] + wholes(terms, *q_terms),
        [(sds((own_rows, 7, LANES), F32), None), (sds((2, 1, HD), F32), None), (sds((LANES, q_cols), F32), None)],
        [pltpu.VMEM((adapters, RANK, LANES), F32), pltpu.VMEM((adapters, RANK, q_cols), F32)], 0, 4 * LANES * f3,
    )
    gate_up_adapter_grad, down_adapter_grad, out_adapter_grad = call(
        sum_hidden_kernel, "sum_hidden", 1, (adapter_ids, early), [scalars()] + wholes(early),
        [(sds((2, LANES, ff_cols), F32), None), (sds((ff_cols, LANES), F32), None), (sds((q_cols, LANES), F32), None)],
        [pltpu.VMEM((adapters, RANK, f3 + q_cols), F32)], 0, 4 * LANES * f3,
    )
    return (
        block_output, input_grad, wide_grad.transpose(1, 0, 2), kv_adapter_grad,
        q_adapter_grad, out_adapter_grad, gate_up_adapter_grad, down_adapter_grad,
    )


def solution(mesh):
    dp_count, tensor_count = mesh.shape["dp"], mesh.shape["tensor"]
    chips = dp_count // 2
    x_count = math.isqrt(chips)
    devices = mesh.devices.reshape(chips // x_count, x_count, 2, tensor_count)
    return jax.shard_map(
        on_device,
        mesh=Mesh(devices, ALL),
        in_specs=(
            P(ALL, None), P(ALL, None), P(), P(), P(), P(DP, "tensor"), P(None, DP, None),
            P("tensor", DP), P(None, DP, "tensor"), P("tensor", DP), P(None, DP, None), P(),
            P(None, "tensor"), P("tensor", None), P(None, None, "tensor"), P("tensor", None),
        ),
        out_specs=(
            P(ALL, None), P(ALL, None), P(None, ALL, None), P(None, ALL, None),
            P(None, "tensor"), P("tensor", None), P(None, None, "tensor"), P("tensor", None),
        ),
        check_vma=False,
    )
```

```python
import functools
import math

import jax
import jax.numpy as jnp
from jax import lax
from jax.experimental import pallas as pl
from jax.experimental.pallas import tpu as pltpu
from jax.sharding import Mesh, PartitionSpec as P

HD = 128
WINDOW = 1024
RANK = 16
LANES = 128
EPS = 1e-06
MASKED = -1e30
SCALE = HD ** (-0.5)
LOG2E = math.log2(math.e)
GELU_C = 0.7978845608028654
GELU_A = 0.044715
VMEM_LIMIT = 58 * 1024 * 1024
BF = jnp.bfloat16
F32 = jnp.float32
DP = ("y", "x", "core")
SEQ = ("core", "tensor")
PLANES = ("y", "x", "tensor")
ALL = ("y", "x", "core", "tensor")

SLOT_Q, SLOT_K, SLOT_V, SLOT_G, SLOT_U, SLOT_O, SLOT_D = range(7)


def rows_of(slot):
    return slice(slot * RANK, (slot + 1) * RANK)


def mm(a, b):
    return lax.dot_general(a, b, (((1,), (0,)), ((), ())), preferred_element_type=F32)


def mm_nt(a, b):
    return lax.dot_general(a, b, (((1,), (1,)), ((), ())), preferred_element_type=F32)


def turned(a):
    return a.astype(F32).T.astype(BF)


def rope(v, cos, sin):
    return v * cos + pltpu.roll(v, HD // 2, 1) * sin


def rope_back(g, cos, sin):
    return g * cos - pltpu.roll(g, HD // 2, 1) * sin


def flat(ref):
    block = ref[...]
    return block.reshape(block.shape[0] * block.shape[2], block.shape[3])


def rms(v, gain):
    return v * lax.rsqrt(jnp.mean(v * v, axis=-1, keepdims=True) + EPS) * gain


def rms_back(v, gain, grad):
    inv = lax.rsqrt(jnp.mean(v * v, axis=-1, keepdims=True) + EPS)
    scaled = grad * gain
    dot = jnp.mean(v * scaled, axis=-1, keepdims=True)
    return inv * scaled - v * (inv * inv * inv * dot)


def pack_kernel(gu_ref, down_ref, q_ref, o_ref, out_ref):
    ff, cols = gu_ref.shape[2], q_ref.shape[1]
    out_ref[:, :ff] = gu_ref[0]
    out_ref[:, ff : 2 * ff] = gu_ref[1]
    out_ref[:, 2 * ff : 3 * ff] = down_ref[...]
    out_ref[:, 3 * ff : 3 * ff + cols] = q_ref[...]
    out_ref[:, 3 * ff + cols :] = o_ref[...]


def shared_kernel(x_ref, gain_ref, a_ref, wk_ref, wv_ref, bkv_ref, cos_ref, sin_ref, n1_ref, r1_ref, kv_ref):
    n1 = rms(x_ref[...].astype(F32), gain_ref[...]).astype(BF)
    n1_ref[...] = n1
    r1 = mm(n1, a_ref[...]).astype(BF)
    r1_ref[...] = r1
    key = mm(n1, wk_ref[...]) + mm(r1, bkv_ref[0])
    kv_ref[:, :HD] = rope(key, cos_ref[...], sin_ref[...]).astype(BF)
    kv_ref[:, HD:] = (mm(n1, wv_ref[...]) + mm(r1, bkv_ref[1])).astype(BF)


def forward_kernel(
    kv_ref, kseg_ref, qseg_ref, n1_ref, r1_ref, cos_ref, sin_ref, gain_ref, a_ref,
    wq_ref, bq_ref, wo_ref, bo_ref, x_hbm, cot_hbm, b_hbm, w_ref,
    q_ref, mixed_ref, p_ref, inv_ref, out_ref, gres_ref, gb_ref, wide_ref, gro_ref, early_ref,
    bias_ref, s_ref, vt_ref, ffn_ref, g2_ref, ro_ref, rd_ref, gr_ref, qs_ref,
    all_mixed_ref, res_ref, n2_ref, r2_ref, r2t_ref, grd_ref, grdt_ref, wv_ref, x_ref, cot_ref, b_ref, sems, late_sems,
):
    step = pl.program_id(0)
    slots, tensor_count = wv_ref.shape[0], w_ref.shape[1]
    steps = b_ref.shape[0]
    rows = q_ref.shape[0]
    chunks = kv_ref.shape[0] // rows
    ff = b_ref.shape[2] // 3
    part_cols = ff // tensor_count

    def copies(at, to):
        moves = []
        for kind in (2, 0, 1):
            for t in range(tensor_count):
                source = pl.multiple_of((kind * steps + at) * part_cols, LANES)
                target = (kind * tensor_count + t) * part_cols
                moves.append(
                    pltpu.make_async_copy(
                        w_ref.at[:, t, :, pl.ds(source, part_cols)],
                        wv_ref.at[to, :, :, pl.ds(target, part_cols)],
                        sems.at[to, len(moves)],
                    )
                )
        return moves

    late = [
        pltpu.make_async_copy(source, target, late_sems.at[j])
        for j, (source, target) in enumerate(((x_hbm, x_ref), (cot_hbm, cot_ref), (b_hbm, b_ref)))
    ]

    @pl.when(step == 0)
    def _():
        for copy in late:
            copy.start()
        key = lax.broadcasted_iota(jnp.int32, bias_ref.shape, 0)
        query = lax.broadcasted_iota(jnp.int32, bias_ref.shape, 1)
        allowed = (key >= query) & (key <= query + WINDOW) & (kseg_ref[...] == qseg_ref[...])
        bias_ref[...] = jnp.where(allowed, 0.0, MASKED)
        vt_ref[...] = turned(kv_ref[:, HD:])
        ffn_ref[...] = jnp.zeros_like(ffn_ref)
        ro_ref[...] = jnp.zeros_like(ro_ref)

    @pl.when((step >= 1) & (step < 1 + slots))
    def _():
        for copy in copies(step - 1, step - 1):
            copy.start()

    @pl.when(step < tensor_count)
    def _():
        lin = mm(n1_ref[...], flat(wq_ref)) + mm(r1_ref[...], bq_ref[0])
        heads = q_ref.shape[1] // HD
        for h in range(heads):
            part = slice(h * HD, (h + 1) * HD)
            query = (rope(lin[:, part], cos_ref[...], sin_ref[...]) * (SCALE * LOG2E)).astype(BF)
            q_ref[:, part] = query
            qs_ref[h * rows : (h + 1) * rows] = query
        queries = qs_ref[...]
        top = jnp.full((1, heads * rows), MASKED, F32)
        for c in range(chunks):
            span = slice(c * rows, (c + 1) * rows)
            s = mm_nt(kv_ref[span, :HD], queries)
            bias = bias_ref[span]
            s = jnp.concatenate([s[:, h * rows : (h + 1) * rows] + bias for h in range(heads)], axis=1)
            s_ref[span] = s
            top = jnp.maximum(top, jnp.max(s, axis=0, keepdims=True))
        total = jnp.zeros((1, heads * rows), F32)
        for c in range(chunks):
            span = slice(c * rows, (c + 1) * rows)
            p = jnp.exp2(s_ref[span] - top)
            total = total + jnp.sum(p, axis=0, keepdims=True)
            p_ref[0, span] = p.astype(BF)
        inv = 1.0 / total
        inv_ref[0, 0:1] = inv
        out = mm(vt_ref[...], p_ref[0]) * inv
        for h in range(heads):
            mixed_ref[:, h * HD : (h + 1) * HD] = out[:, h * rows : (h + 1) * rows].T.astype(BF)
        mixed = mixed_ref[...]
        all_mixed_ref[step] = mixed
        ffn_ref[...] += mm_nt(mixed, flat(wo_ref))
        ro_ref[...] += mm_nt(mixed, bo_ref[0])

    @pl.when(step == tensor_count - 1)
    def _():
        for copy in late:
            copy.wait()
        res = x_ref[...].astype(F32) + (ffn_ref[...] + mm_nt(ro_ref[...].astype(BF), a_ref[...]))
        res_ref[...] = res
        n2 = rms(res, gain_ref[...]).astype(BF)
        n2_ref[...] = n2
        r2 = mm(n2, a_ref[...]).astype(BF)
        r2_ref[...] = r2
        r2t_ref[...] = turned(r2)
        grd = mm(cot_ref[...], a_ref[...]).astype(BF)
        grd_ref[...] = grd
        grdt_ref[...] = turned(grd)
        ffn_ref[...] = jnp.zeros_like(ffn_ref)
        g2_ref[...] = jnp.zeros_like(g2_ref)
        rd_ref[...] = jnp.zeros_like(rd_ref)
        gr_ref[...] = jnp.zeros_like(gr_ref)

    def feed_forward(at, carry):
        slot = lax.rem(at, slots)

        @pl.when((at >= 1) & (at + slots - 1 < steps))
        def _():
            for copy in copies(at + slots - 1, lax.rem(at + slots - 1, slots)):
                copy.start()

        n2, r2, cot = n2_ref[...], r2_ref[...], cot_ref[...]
        b_gu, b_d = b_ref[at, :, : 2 * ff], b_ref[at, :, 2 * ff :]
        arrivals = copies(at, slot)
        weight_rows = wv_ref.shape[1] * wv_ref.shape[2]
        for copy in arrivals[:tensor_count]:
            copy.wait()
        w_d = wv_ref[slot, :, :, 2 * ff :].reshape(weight_rows, ff)
        grad_hidden = (mm(cot, w_d) + mm(grd_ref[...], b_d)).astype(BF).astype(F32)
        for copy in arrivals[tensor_count:]:
            copy.wait()
        w_gu = wv_ref[slot, :, :, : 2 * ff].reshape(weight_rows, 2 * ff)
        lin = mm(n2, w_gu) + mm(r2, b_gu)
        gate, up = lin[:, :ff], lin[:, ff:]
        square = gate * gate
        th = jnp.tanh(GELU_C * (gate + GELU_A * square * gate))
        half = 0.5 * (1.0 + th)
        act = gate * half
        slope = half + 0.5 * gate * (1.0 - th * th) * (GELU_C * (1.0 + 3.0 * GELU_A * square))
        hidden = (act * up).astype(BF)
        grad_gate = (grad_hidden * up * slope).astype(BF)
        grad_up = (grad_hidden * act).astype(BF)
        grads = jnp.concatenate([grad_gate, grad_up], axis=1)
        ffn_ref[...] += mm_nt(hidden, w_d)
        rd_ref[...] += mm_nt(hidden, b_d)
        g2_ref[...] += mm_nt(grads, w_gu)
        gr_ref[...] += mm_nt(grads, b_gu)
        terms = (
            mm(r2t_ref[rows_of(SLOT_G)], grad_gate), mm(r2t_ref[rows_of(SLOT_U)], grad_up),
            mm(grdt_ref[rows_of(SLOT_D)], hidden),
        )
        for kind, term in enumerate(terms):
            target = pl.multiple_of((kind * steps + at) * part_cols, LANES)
            for t in range(tensor_count):
                early_ref[t, :, pl.ds(target, part_cols)] = term[:, t * part_cols : (t + 1) * part_cols].astype(BF)
        return carry

    @pl.when(step == tensor_count)
    def _():
        lax.fori_loop(0, steps, feed_forward, 0)
        res, n2, cot = res_ref[...], n2_ref[...], cot_ref[...]
        out_ref[...] = (res + (ffn_ref[...] + mm_nt(rd_ref[...].astype(BF), a_ref[...]))).astype(BF)
        grad_two = g2_ref[...] + mm_nt(gr_ref[...].astype(BF), a_ref[...])
        grad_res = cot.astype(F32) + rms_back(res, gain_ref[...], grad_two)
        gres_ref[...] = grad_res
        grad_branch = grad_res.astype(BF)
        gb_ref[...] = grad_branch
        gro = mm(grad_branch, a_ref[...])
        gro_ref[...] = gro.astype(BF)
        grot = gro.T[rows_of(SLOT_O)].astype(BF)
        first = 3 * steps * part_cols
        for t in range(tensor_count):
            early_ref[t, :, first:] = mm(grot, all_mixed_ref[t]).astype(BF)
        wide = mm(gr_ref[...].T.astype(BF), n2) + mm(rd_ref[...].T.astype(BF), cot)
        wide_ref[...] = wide + mm(ro_ref[...].T.astype(BF), grad_branch)


def attn_back_kernel(
    tensor_ref, kv_ref, gb_ref, gro_ref, r1_ref, cos_ref, sin_ref,
    q_ref, mixed_ref, p_ref, inv_ref, wo_ref, bo_ref, wq_ref, bq_ref,
    dkva_ref, dkvb_ref, dkvc_ref, dkvd_ref, dkve_ref, q0_ref, g1_ref, gr_ref,
    ds_ref, dk_ref, dv_ref, kt_ref, r1t_ref, gq_ref, gm_ref, qs_ref, gs_ref,
):
    step = pl.program_id(0)
    rows = q_ref.shape[0]
    chunks = kv_ref.shape[0] // rows

    @pl.when(step == 0)
    def _():
        kt_ref[...] = turned(kv_ref[:, :HD])
        r1t_ref[...] = turned(r1_ref[...])
        dk_ref[...] = jnp.zeros_like(dk_ref)
        dv_ref[...] = jnp.zeros_like(dv_ref)
        g1_ref[...] = jnp.zeros_like(g1_ref)
        gr_ref[...] = jnp.zeros_like(gr_ref)

    gm_ref[...] = (mm(gb_ref[...], flat(wo_ref)) + mm(gro_ref[...], bo_ref[0])).astype(BF)
    heads = q_ref.shape[1] // HD
    deltas = []
    for h in range(heads):
        part, span = slice(h * HD, (h + 1) * HD), slice(h * rows, (h + 1) * rows)
        grad = gm_ref[:, part]
        qs_ref[span] = q_ref[:, part]
        gs_ref[span] = grad
        delta = grad.astype(F32) * mixed_ref[:, part].astype(F32)
        deltas.append(jnp.sum(delta.T, axis=0, keepdims=True))
    delta, inv = jnp.concatenate(deltas, axis=1), inv_ref[0, 0:1]
    queries, grads = qs_ref[...], gs_ref[...]
    for c in range(chunks):
        span = slice(c * rows, (c + 1) * rows)
        p = p_ref[0, span].astype(F32) * inv
        dp = mm_nt(kv_ref[span, HD:], grads)
        ds = (p * (dp - delta)).astype(BF)
        ds_ref[span] = ds
        dk_ref[span] += mm(ds, queries)
        dv_ref[span] += mm(p.astype(BF), grads)
    dq = mm(kt_ref[...], ds_ref[...]) * SCALE
    for h in range(heads):
        part, span = slice(h * HD, (h + 1) * HD), slice(h * rows, (h + 1) * rows)
        gq_ref[:, part] = rope_back(dq[:, span].T, cos_ref[...], sin_ref[...]).astype(BF)

    gq = gq_ref[...]
    grad_bq = mm(r1t_ref[rows_of(SLOT_Q)], gq).astype(BF)
    away = lax.rem(tensor_ref[0] + pl.num_programs(0) - step, pl.num_programs(0))

    @pl.when(away == 0)
    def _():
        q0_ref[...] = grad_bq

    for d, dkv_ref in ((1, dkvd_ref), (2, dkvc_ref), (3, dkvb_ref)):

        @pl.when(away == d)
        def _(dkv_ref=dkv_ref):
            dkv_ref[rows : rows + RANK] = grad_bq[:, : 2 * HD]
            dkv_ref[rows + RANK :, :HD] = grad_bq[:, 2 * HD :]
            dkv_ref[rows + RANK :, HD:] = jnp.zeros((RANK, HD), BF)

    gr_ref[...] += mm_nt(gq, bq_ref[0])
    g1_ref[...] += mm_nt(gq, flat(wq_ref))

    @pl.when(step == pl.num_programs(0) - 1)
    def _():
        for c, dkv_ref in enumerate((dkva_ref, dkvb_ref, dkvc_ref, dkvd_ref, dkve_ref)):
            span = slice(c * rows, (c + 1) * rows)
            dkv_ref[:rows, :HD] = (dk_ref[span] * (1.0 / LOG2E)).astype(BF)
            dkv_ref[:rows, HD:] = dv_ref[span].astype(BF)


def shared_back_kernel(
    chips, core_ref, n1_ref, r1_ref, bkv_ref, cos_ref, sin_ref, own_ref, back1_ref, back2_ref, back3_ref, back4_ref,
    q0_ref, gr_ref, widef_ref,
    mine_ref, theirs_ref, gk_ref, gv_ref, grt_ref,
):
    rows = own_ref.shape[0]
    gkv = own_ref[...].astype(F32)
    for back_ref in (back1_ref, back2_ref, back3_ref, back4_ref):
        gkv = gkv + back_ref[:rows].astype(F32)
    queries = [q0_ref[:, j * LANES : (j + 1) * LANES].astype(F32) for j in range(3)]
    for back_ref in (back1_ref, back2_ref, back3_ref):
        queries[0] = queries[0] + back_ref[rows : rows + RANK, :HD].astype(F32)
        queries[1] = queries[1] + back_ref[rows : rows + RANK, HD:].astype(F32)
        queries[2] = queries[2] + back_ref[rows + RANK :, :HD].astype(F32)
    gk = rope_back(gkv[:, :HD], cos_ref[...], sin_ref[...]).astype(BF)
    gv = gkv[:, HD:].astype(BF)
    gk_ref[...] = gk
    gv_ref[...] = gv
    gr = gr_ref[...] + mm_nt(gk, bkv_ref[0]) + mm_nt(gv, bkv_ref[1])
    grt_ref[...] = gr.astype(BF)
    wide = (mm(gr.T.astype(BF), n1_ref[...]) + widef_ref[...]).T.astype(BF)
    share = mine_ref.shape[0] - 5 * RANK
    wide = wide.reshape(chips, 2, share // chips, LANES)
    first = core_ref[0] == 0
    mine_ref[:share] = jnp.where(first, wide[:, 0], wide[:, 1]).reshape(share, LANES)
    theirs_ref[:share] = jnp.where(first, wide[:, 1], wide[:, 0]).reshape(share, LANES)
    r1t = turned(r1_ref[...])
    for j, (slot, grad) in enumerate(((SLOT_K, gk), (SLOT_V, gv))):
        term = mm(r1t[rows_of(slot)], grad).astype(BF)
        part = slice(share + j * RANK, share + (j + 1) * RANK)
        mine_ref[part] = term
        theirs_ref[part] = term
    for j, term in enumerate(queries):
        part = slice(share + (2 + j) * RANK, share + (3 + j) * RANK)
        mine_ref[part] = term.astype(BF)
        theirs_ref[part] = term.astype(BF)


def payload_kernel(core_ref, mine_ref, other_ref, out_ref, q_ref):
    first = core_ref[0] == 0
    total = mine_ref[...].astype(F32) + other_ref[...].astype(F32)
    count = out_ref.shape[0]
    own_rows = (total.shape[0] - 5 * RANK) // count
    queries = total[total.shape[0] - 3 * RANK :].astype(BF)
    for n in range(q_ref.shape[0]):
        for j in range(3):
            q_ref[n, :, j * LANES : (j + 1) * LANES] = queries[j * RANK : (j + 1) * RANK]
    tensor_count = RANK // 4
    blank = jnp.zeros((RANK - own_rows - 2, LANES), F32)
    for n in range(count):
        pieces = [total[n * own_rows : (n + 1) * own_rows]]
        row = (2 * (n // tensor_count) * tensor_count + n % tensor_count) % RANK
        for j in range(2):
            at = count * own_rows + j * RANK + row
            low, high = total[at : at + 1], total[at + tensor_count : at + tensor_count + 1]
            pieces.append(jnp.where(first, low, high))
        out_ref[n] = jnp.concatenate(pieces + [blank], axis=0).astype(BF)


def input_kernel(
    x_ref, gain_ref, a_ref, wk_ref, wv_ref, gk_ref, gv_ref, gr_ref, g1_ref, gres_ref, grad_ref,
):
    g1 = g1_ref[...] + mm_nt(gk_ref[...], wk_ref[...]) + mm_nt(gv_ref[...], wv_ref[...])
    g1 = g1 + mm_nt(gr_ref[...], a_ref[...])
    x = x_ref[...].astype(F32)
    grad_ref[...] = gres_ref[...] + rms_back(x, gain_ref[...], g1)


def sum_hidden_kernel(ids_ref, terms_hbm, gu_ref, down_ref, out_ref, acc_ref, terms_ref, sems):
    share = terms_ref.shape[0] // sems.shape[0]
    copies = []
    for j in range(sems.shape[0]):
        part = pl.ds(j * share, share)
        copies.append(pltpu.make_async_copy(terms_hbm.at[part], terms_ref.at[part], sems.at[j]))
        copies[j].start()
    acc_ref[...] = jnp.zeros_like(acc_ref)
    for s in range(terms_ref.shape[0] // 2):
        if 2 * s % share == 0:
            copies[2 * s // share].wait()
        acc_ref[ids_ref[s]] += terms_ref[2 * s].astype(F32) + terms_ref[2 * s + 1].astype(F32)
    adapters, rank, _ = acc_ref.shape
    ff, heads = gu_ref.shape[2], out_ref.shape[0]

    def taken(first, count):
        return acc_ref[:, :, first : first + count].reshape(adapters * rank, count)

    gu_ref[0] = taken(0, ff)
    gu_ref[1] = taken(ff, ff)
    down_ref[...] = taken(2 * ff, ff).T
    out_ref[...] = taken(3 * ff, heads).T


def sum_wide_kernel(ids_ref, own_ref, terms_ref, *rest):
    q_refs, (wide_ref, kv_ref, q_ref, acc_ref, accq_ref) = rest[:-5], rest[-5:]
    acc_ref[...] = jnp.zeros_like(acc_ref)
    accq_ref[...] = jnp.zeros_like(accq_ref)
    y_count, x_count = len(q_refs), q_refs[0].shape[0]
    for away_y, terms in enumerate(q_refs):
        y = lax.rem(own_ref[1] + away_y, y_count)
        for away_x in range(x_count):
            x = lax.rem(own_ref[2] + away_x, x_count)
            accq_ref[ids_ref[y * x_count + x]] += terms[away_x].astype(F32)
    q_ref[...] = accq_ref[...].reshape(q_ref.shape)
    seqs, parts = terms_ref.shape[:2]
    for s in range(seqs):
        term = terms_ref[s, 0].astype(F32)
        for part in range(1, parts):
            term = term + terms_ref[s, part].astype(F32)
        acc_ref[ids_ref[s]] += term
    adapters, rank, _ = acc_ref.shape
    lane = lax.broadcasted_iota(jnp.int32, (rank, LANES), 1) // RANK
    own_rows, slots = wide_ref.shape[:2]
    for j in range(slots):
        total = jnp.zeros((rank, LANES), F32)
        for a in range(adapters):
            moved = pltpu.roll(acc_ref[a], ((a - j) * RANK) % LANES, 1)
            total = jnp.where(lane == a, moved, total)
        wide_ref[:, j] = total[:own_rows]
    mine = acc_ref[own_ref[0]]
    for j in range(2):
        kv_ref[j] = mine[own_rows + j : own_rows + j + 1]


def sds(shape, dtype):
    return jax.ShapeDtypeStruct(shape, dtype)


def scalars():
    return pl.BlockSpec(memory_space=pltpu.SMEM)


def whole(array):
    rank = len(array.shape)
    return pl.BlockSpec(array.shape, lambda *_: (0,) * rank)


def wholes(*arrays):
    return [whole(v) for v in arrays]


def by_step(*shape):
    return pl.BlockSpec((1,) + shape, lambda t: (t,) + (0,) * len(shape))


def call(kernel, name, steps, args, specs, outs, scratch, flops, nbytes):
    shapes = [shape for shape, _ in outs]
    return pl.pallas_call(
        kernel,
        name=name,
        grid=(steps,),
        in_specs=specs,
        out_specs=[whole(shape) if spec is None else spec for shape, spec in outs],
        out_shape=shapes,
        scratch_shapes=scratch,
        compiler_params=pltpu.CompilerParams(
            dimension_semantics=("arbitrary",), vmem_limit_bytes=VMEM_LIMIT
        ),
        cost_estimate=pl.CostEstimate(flops=flops, bytes_accessed=nbytes, transcendentals=0),
    )(*args)


def rope_tables(positions):
    half = HD // 2
    frequency = 10000.0 ** (-(jnp.arange(half).astype(F32) / half))
    angles = positions.astype(F32)[:, None] * frequency[None, :]
    cos, sin = jnp.cos(angles), jnp.sin(angles)
    return jnp.concatenate([cos, cos], axis=1), jnp.concatenate([-sin, sin], axis=1)


def on_device(
    tokens, cotangent, segments, adapter_ids, norm_gains, q_weight, kv_weight, out_weight,
    gate_up_weight, down_weight, wide_adapters, kv_adapter, q_adapter, out_adapter,
    gate_up_adapter, down_adapter,
):
    rows, width = tokens.shape
    tensor_count = lax.axis_size("tensor")
    dp_count = lax.axis_size("y") * lax.axis_size("x") * 2
    devices = dp_count * tensor_count
    group_rows = rows * tensor_count
    seq_length = 2 * group_rows
    shard_rows = q_weight.shape[0]
    q_cols, ff_cols = q_weight.shape[1], gate_up_weight.shape[2]
    heads_cols = tensor_count * q_cols
    seqs = adapter_ids.shape[0]
    adapters = wide_adapters.shape[2] // RANK
    dp = lax.axis_index(DP)
    tensor = lax.axis_index("tensor")
    my_core = lax.axis_index("core")
    adapter = lax.dynamic_index_in_dim(adapter_ids, dp // 2, keepdims=False)
    column = adapter * RANK
    f3 = 3 * ff_cols

    args = (gate_up_weight, down_weight.T, q_weight, out_weight.T)
    (pack,) = call(
        pack_kernel, "pack", 1, args, wholes(*args), [(sds((shard_rows, f3 + 2 * q_cols), BF), None)], [],
        0, 4 * shard_rows * (f3 + 2 * q_cols),
    )
    pack, wide_adapters = lax.optimization_barrier((pack, wide_adapters))
    weights = lax.all_gather(pack, ALL, axis=0, tiled=False)
    weights = weights.reshape(dp_count, tensor_count, shard_rows, f3 + 2 * q_cols)

    wide = wide_adapters.reshape(7, shard_rows, adapters, RANK)
    wide = jnp.take(wide, adapter_ids, axis=2).transpose(2, 1, 0, 3)
    wide = wide.reshape(seqs, shard_rows, 7 * RANK)
    wide = jnp.pad(wide, ((0, 0), (0, 0), (0, LANES - 7 * RANK)))
    shared = jnp.broadcast_to(kv_weight[:, None], (2, seqs, shard_rows, HD))
    wide = jnp.concatenate([wide, shared[0], shared[1]], axis=2)

    def from_other_core(value):
        return lax.ppermute(value, "core", [(0, 1), (1, 0)])

    a_own = lax.all_to_all(wide, ("y", "x"), 0, 0, tiled=True)
    a_other = from_other_core(a_own)
    a_all = jnp.where(my_core == 0, jnp.stack([a_own, a_other], 1), jnp.stack([a_other, a_own], 1))
    a_all = a_all.reshape(width, 3 * LANES)

    def take_rows(matrix):
        return lax.dynamic_slice_in_dim(matrix, column, RANK, matrix.ndim - 2)

    def take_cols(matrix):
        return lax.dynamic_slice_in_dim(matrix, column, RANK, matrix.ndim - 1)

    def in_slot(block, slot):
        pads = [(0, 0)] * block.ndim
        pads[-2] = (slot * RANK, LANES - (slot + 1) * RANK)
        return jnp.pad(block, pads)

    gu_rows = take_rows(gate_up_adapter)
    b_own = jnp.concatenate(
        [gu_rows[0], gu_rows[1], take_cols(down_adapter).T, take_rows(q_adapter), take_cols(out_adapter).T], axis=1
    )
    b_parts = [b_own] + [
        lax.ppermute(b_own, "tensor", [((z + d) % tensor_count, z) for z in range(tensor_count)])
        for d in range(1, tensor_count)
    ]
    kv_rows = take_rows(kv_adapter)
    b_kv = jnp.stack([in_slot(kv_rows[0], SLOT_K), in_slot(kv_rows[1], SLOT_V)])

    start = dp * group_rows + tensor * rows
    span = WINDOW + rows
    cos_window, sin_window = rope_tables((start - WINDOW + jnp.arange(span)) % seq_length)
    cos, sin = cos_window[WINDOW:], sin_window[WINDOW:]
    padded = jnp.concatenate([jnp.full((WINDOW,), -1, jnp.int32), segments])
    kseg = lax.dynamic_slice_in_dim(padded, start, span, 0)
    qseg = kseg[WINDOW:].reshape(1, rows)
    kseg = kseg.reshape(span, 1)

    gain_one, gain_two = norm_gains[0:1], norm_gains[1:2]
    q_block = f3 // q_cols

    def weight_spec(block):
        return pl.BlockSpec((dp_count, 1, shard_rows, q_cols), lambda t: (0, t, 0, block))

    def adapter_spec(block):
        return pl.BlockSpec((1, LANES, q_cols), lambda t: (t, 0, block))

    def lane_block(block):
        return pl.BlockSpec((width, LANES), lambda *_: (0, block))

    head_specs = [weight_spec(q_block), adapter_spec(0), weight_spec(q_block + 1), adapter_spec(1)]
    q_spec, qb_spec, o_spec, ob_spec = head_specs
    a_spec, wk_spec, wv_spec = lane_block(0), lane_block(1), lane_block(2)
    token_cols = pl.BlockSpec((rows, q_cols), lambda t: (0, t))
    tok_bf, tok_f32, rank_bf = sds((rows, width), BF), sds((rows, width), F32), sds((rows, LANES), BF)

    args = (tokens, gain_one, a_all, a_all, a_all, b_kv, cos, sin)
    normed_one, rank_one, kv_own = call(
        shared_kernel, "keys_values", 1, args,
        wholes(*args[:2]) + [a_spec, wk_spec, wv_spec] + wholes(*args[5:]),
        [(tok_bf, None), (rank_bf, None), (sds((rows, 2 * HD), BF), None)],
        [], 2 * rows * width * 384, 6 * rows * width,
    )
    parts = seq_length // rows
    reach = WINDOW // rows

    def moved(value, steps):
        return lax.ppermute(value, SEQ, [(c, c + steps) for c in range(parts) if 0 <= c + steps < parts])

    kv_window = jnp.concatenate([moved(kv_own, d) for d in range(reach, 0, -1)] + [kv_own])

    b_all = jnp.roll(jnp.stack(b_parts), tensor, axis=0)
    b_heads = jnp.concatenate(
        [in_slot(b_all[:, :, f3 : f3 + q_cols], SLOT_Q), in_slot(b_all[:, :, f3 + q_cols :], SLOT_O)], axis=2
    )
    steps, slots = ff_cols // LANES, 2
    part_cols = ff_cols // steps
    b_hidden = b_all[:, :, :f3].reshape(tensor_count, RANK, 3, steps, part_cols).transpose(3, 2, 1, 0, 4)
    b_hidden = b_hidden.reshape(steps, 3, RANK, tensor_count * part_cols)
    b_hidden = jnp.concatenate(
        [in_slot(b_hidden[:, kind], slot) for kind, slot in enumerate((SLOT_G, SLOT_U, SLOT_D))], axis=2
    )

    heads = q_cols // HD
    last = tensor_count - 1

    def until_last(spec):
        return pl.BlockSpec(spec.block_shape, lambda t: spec.index_map(jnp.minimum(t, last)))

    p_spec, norm_spec = by_step(span, heads * rows), by_step(8, heads * rows)
    args = (
        kv_window, kseg, qseg, normed_one, rank_one, cos, sin, gain_two, a_all,
        weights, b_heads, weights, b_heads, tokens, cotangent, b_hidden, weights,
    )
    (
        queries, mixed, probs, norms, block_output, grad_residual, grad_branch, wide_ffn, grad_ro, early
    ) = call(
        forward_kernel, "forward", tensor_count + 1, args,
        wholes(*args[:8]) + [a_spec] + [until_last(spec) for spec in head_specs]
        + [pl.BlockSpec(memory_space=pl.ANY)] * 4,
        [
            (sds((rows, heads_cols), BF), until_last(token_cols)), (sds((rows, heads_cols), BF), until_last(token_cols)),
            (sds((tensor_count, span, heads * rows), BF), until_last(p_spec)),
            (sds((tensor_count, 8, heads * rows), F32), until_last(norm_spec)),
            (tok_bf, None), (tok_f32, None), (tok_bf, None), (sds((LANES, width), F32), None), (rank_bf, None),
            (sds((tensor_count, RANK, f3 + q_cols), BF), None),
        ],
        [
            pltpu.VMEM((span, rows), F32), pltpu.VMEM((span, heads * rows), F32), pltpu.VMEM((HD, span), BF),
            pltpu.VMEM((rows, width), F32), pltpu.VMEM((rows, width), F32), pltpu.VMEM((rows, LANES), F32),
            pltpu.VMEM((rows, LANES), F32), pltpu.VMEM((rows, LANES), F32), pltpu.VMEM((heads * rows, HD), BF),
            pltpu.VMEM((tensor_count, rows, q_cols), BF), pltpu.VMEM((rows, width), F32), pltpu.VMEM((rows, width), BF),
            pltpu.VMEM((rows, LANES), BF), pltpu.VMEM((LANES, rows), BF),
            pltpu.VMEM((rows, LANES), BF), pltpu.VMEM((LANES, rows), BF),
            pltpu.VMEM((slots, dp_count, shard_rows, 3 * tensor_count * part_cols), BF),
            pltpu.VMEM((rows, width), BF), pltpu.VMEM((rows, width), BF), pltpu.VMEM(b_hidden.shape, BF),
            pltpu.SemaphoreType.DMA((slots, 3 * tensor_count)), pltpu.SemaphoreType.DMA((3,)),
        ],
        4 * rows * heads_cols * (span + width) + 12 * rows * width * tensor_count * ff_cols,
        4 * width * heads_cols + 6 * width * tensor_count * ff_cols,
    )
    early = lax.psum_scatter(early, "tensor", scatter_dimension=0, tiled=True).reshape(RANK, -1)

    args = (
        tensor.astype(jnp.int32).reshape(1), kv_window, grad_branch, grad_ro, rank_one, cos, sin,
        queries, mixed, probs, norms, weights, b_heads, weights, b_heads,
    )
    *dkv, q_own, grad_one, grad_rank = call(
        attn_back_kernel, "attention_back", tensor_count, args,
        [scalars()] + wholes(*args[1:7]) + [token_cols, token_cols, p_spec, norm_spec, o_spec, ob_spec, q_spec, qb_spec],
        [
            *[(sds((rows + (2 * RANK if 0 < w < reach else 0), 2 * HD), BF), None) for w in range(reach + 1)],
            (sds((RANK, q_cols), BF), None), (tok_f32, None), (sds((rows, LANES), F32), None),
        ],
        [
            pltpu.VMEM((span, heads * rows), BF),
            pltpu.VMEM((span, HD), F32), pltpu.VMEM((span, HD), F32), pltpu.VMEM((HD, span), BF),
            pltpu.VMEM((LANES, rows), BF), pltpu.VMEM((rows, q_cols), BF), pltpu.VMEM((rows, q_cols), BF),
            pltpu.VMEM((heads * rows, HD), BF), pltpu.VMEM((heads * rows, HD), BF),
        ],
        2 * rows * heads_cols * (4 * span + 2 * width), 4 * width * heads_cols,
    )

    early, grad_one = lax.optimization_barrier((early, grad_one))
    early = lax.all_gather(early, DP, axis=0, tiled=False)

    def around(value, steps):
        return lax.ppermute(value, SEQ, [(c, (c - steps) % parts) for c in range(parts)])

    backs = [around(dkv[reach - d], d) for d in range(1, reach)] + [moved(dkv[0], -reach)]
    core = my_core.astype(jnp.int32).reshape(1)
    chips = dp_count // 2
    share = width // 2 + 5 * RANK
    args = (
        core, normed_one, rank_one, b_kv, cos, sin, dkv[reach], *backs, q_own, grad_rank, wide_ffn,
    )
    mine, theirs, grad_key, grad_value, grad_rank = call(
        functools.partial(shared_back_kernel, chips), "shared_back", 1, args,
        [scalars()] + wholes(*args[1:]),
        [
            (sds((share, LANES), BF), None), (sds((share, LANES), BF), None),
            (sds((rows, HD), BF), None), (sds((rows, HD), BF), None), (rank_bf, None),
        ],
        [], 4 * rows * width * LANES, 6 * rows * width,
    )
    own_rows = width // devices
    planes = chips * tensor_count
    args = (core, mine, from_other_core(theirs))
    payload, q_terms = call(
        payload_kernel, "payload", 1, args, [scalars()] + wholes(*args[1:]),
        [(sds((planes, RANK, LANES), BF), None), (sds((1, RANK, q_cols), BF), None)], [],
        0, 2 * planes * RANK * LANES,
    )
    payload, grad_key = lax.optimization_barrier((payload, grad_key))
    terms = lax.all_to_all(payload, PLANES, 0, 0, tiled=True)

    def with_others(value, axis):
        count = lax.axis_size(axis)
        return [value] + [
            lax.ppermute(value, axis, [((i + d) % count, i) for i in range(count)]) for d in range(1, count)
        ]

    q_terms = with_others(jnp.concatenate(with_others(q_terms, "x")), "y")
    terms = terms.reshape(seqs, tensor_count, RANK, LANES)

    args = (
        tokens, gain_one, a_all, a_all, a_all, grad_key, grad_value, grad_rank, grad_one, grad_residual,
    )
    (input_grad,) = call(
        input_kernel, "input_gradient", 1, args,
        wholes(*args[:2]) + [a_spec, wk_spec, wv_spec] + wholes(*args[5:]),
        [(tok_f32, None)], [], 2 * rows * width * 384, 16 * rows * width,
    )

    terms, input_grad = lax.optimization_barrier((terms, input_grad))
    own = jnp.stack([(dp * tensor_count + tensor) // RANK, lax.axis_index("y"), lax.axis_index("x")]).astype(jnp.int32)
    wide_grad, kv_adapter_grad, q_adapter_grad = call(
        sum_wide_kernel, "sum_wide", 1, (adapter_ids, own, terms, *q_terms),
        [scalars(), scalars()] + wholes(terms, *q_terms),
        [(sds((own_rows, 7, LANES), F32), None), (sds((2, 1, HD), F32), None), (sds((LANES, q_cols), F32), None)],
        [pltpu.VMEM((adapters, RANK, LANES), F32), pltpu.VMEM((adapters, RANK, q_cols), F32)], 0, 4 * LANES * f3,
    )
    gate_up_adapter_grad, down_adapter_grad, out_adapter_grad = call(
        sum_hidden_kernel, "sum_hidden", 1, (adapter_ids, early),
        [scalars(), pl.BlockSpec(memory_space=pl.ANY)],
        [(sds((2, LANES, ff_cols), F32), None), (sds((ff_cols, LANES), F32), None), (sds((q_cols, LANES), F32), None)],
        [
            pltpu.VMEM((adapters, RANK, f3 + q_cols), F32), pltpu.VMEM(early.shape, BF), pltpu.SemaphoreType.DMA((8,)),
        ],
        0, 4 * LANES * f3,
    )
    return (
        block_output, input_grad, wide_grad.transpose(1, 0, 2), kv_adapter_grad,
        q_adapter_grad, out_adapter_grad, gate_up_adapter_grad, down_adapter_grad,
    )


def solution(mesh):
    dp_count, tensor_count = mesh.shape["dp"], mesh.shape["tensor"]
    chips = dp_count // 2
    x_count = math.isqrt(chips)
    devices = mesh.devices.reshape(chips // x_count, x_count, 2, tensor_count)
    return jax.shard_map(
        on_device,
        mesh=Mesh(devices, ALL),
        in_specs=(
            P(ALL, None), P(ALL, None), P(), P(), P(), P(DP, "tensor"), P(None, DP, None),
            P("tensor", DP), P(None, DP, "tensor"), P("tensor", DP), P(None, DP, None), P(),
            P(None, "tensor"), P("tensor", None), P(None, None, "tensor"), P("tensor", None),
        ),
        out_specs=(
            P(ALL, None), P(ALL, None), P(None, ALL, None), P(None, ALL, None),
            P(None, "tensor"), P("tensor", None), P(None, None, "tensor"), P("tensor", None),
        ),
        check_vma=False,
    )
```

```python
import functools
import math

import jax
import jax.numpy as jnp
from jax import lax
from jax.experimental import pallas as pl
from jax.experimental.pallas import tpu as pltpu
from jax.sharding import Mesh, PartitionSpec as P

HD = 128
WINDOW = 1024
RANK = 16
LANES = 128
EPS = 1e-06
MASKED = -1e30
SCALE = HD ** (-0.5)
LOG2E = math.log2(math.e)
GELU_C = 0.7978845608028654
GELU_A = 0.044715
VMEM_LIMIT = 58 * 1024 * 1024
BF = jnp.bfloat16
F32 = jnp.float32
DP = ("y", "x", "core")
SEQ = ("core", "tensor")
PLANES = ("y", "x", "tensor")
ALL = ("y", "x", "core", "tensor")

SLOT_Q, SLOT_K, SLOT_V, SLOT_G, SLOT_U, SLOT_O, SLOT_D = range(7)


def rows_of(slot):
    return slice(slot * RANK, (slot + 1) * RANK)


def mm(a, b):
    return lax.dot_general(a, b, (((1,), (0,)), ((), ())), preferred_element_type=F32)


def mm_nt(a, b):
    return lax.dot_general(a, b, (((1,), (1,)), ((), ())), preferred_element_type=F32)


def turned(a):
    return a.astype(F32).T.astype(BF)


def rope(v, cos, sin):
    return v * cos + pltpu.roll(v, HD // 2, 1) * sin


def rope_back(g, cos, sin):
    return g * cos - pltpu.roll(g, HD // 2, 1) * sin


def flat(ref):
    block = ref[...]
    return block.reshape(block.shape[0] * block.shape[2], block.shape[3])


def rms(v, gain):
    return v * lax.rsqrt(jnp.mean(v * v, axis=-1, keepdims=True) + EPS) * gain


def rms_back(v, gain, grad):
    inv = lax.rsqrt(jnp.mean(v * v, axis=-1, keepdims=True) + EPS)
    scaled = grad * gain
    dot = jnp.mean(v * scaled, axis=-1, keepdims=True)
    return inv * scaled - v * (inv * inv * inv * dot)


def pack_kernel(gu_ref, down_ref, q_ref, o_ref, out_ref):
    ff, cols = gu_ref.shape[2], q_ref.shape[1]
    out_ref[:, :ff] = gu_ref[0]
    out_ref[:, ff : 2 * ff] = gu_ref[1]
    out_ref[:, 2 * ff : 3 * ff] = down_ref[...]
    out_ref[:, 3 * ff : 3 * ff + cols] = q_ref[...]
    out_ref[:, 3 * ff + cols :] = o_ref[...]


def shared_kernel(x_ref, gain_ref, a_ref, wk_ref, wv_ref, bkv_ref, cos_ref, sin_ref, n1_ref, r1_ref, kv_ref):
    n1 = rms(x_ref[...].astype(F32), gain_ref[...]).astype(BF)
    n1_ref[...] = n1
    r1 = mm(n1, a_ref[...]).astype(BF)
    r1_ref[...] = r1
    key = mm(n1, wk_ref[...]) + mm(r1, bkv_ref[0])
    kv_ref[:, :HD] = rope(key, cos_ref[...], sin_ref[...]).astype(BF)
    kv_ref[:, HD:] = (mm(n1, wv_ref[...]) + mm(r1, bkv_ref[1])).astype(BF)


def forward_kernel(
    kv_ref, kseg_ref, qseg_ref, n1_ref, r1_ref, cos_ref, sin_ref, gain_ref, a_ref,
    wq_ref, bq_ref, wo_ref, bo_ref, x_hbm, cot_hbm, b_hbm, w_ref,
    q_ref, mixed_ref, p_ref, inv_ref, out_ref, gres_ref, gb_ref, wide_ref, gro_ref, early_ref,
    bias_ref, s_ref, vt_ref, ffn_ref, g2_ref, ro_ref, rd_ref, gr_ref, qs_ref,
    all_mixed_ref, res_ref, n2_ref, r2_ref, r2t_ref, grd_ref, grdt_ref, wv_ref, x_ref, cot_ref, b_ref, sems, late_sems,
):
    step = pl.program_id(0)
    slots, tensor_count = wv_ref.shape[0], w_ref.shape[1]
    steps = b_ref.shape[0]
    rows = q_ref.shape[0]
    chunks = kv_ref.shape[0] // rows
    ff = b_ref.shape[2] // 3
    part_cols = ff // tensor_count

    def copies(at, to):
        moves = []
        for kind in (2, 0, 1):
            for t in range(tensor_count):
                source = pl.multiple_of((kind * steps + at) * part_cols, LANES)
                target = (kind * tensor_count + t) * part_cols
                moves.append(
                    pltpu.make_async_copy(
                        w_ref.at[:, t, :, pl.ds(source, part_cols)],
                        wv_ref.at[to, :, :, pl.ds(target, part_cols)],
                        sems.at[to, len(moves)],
                    )
                )
        return moves

    late = [
        pltpu.make_async_copy(source, target, late_sems.at[j])
        for j, (source, target) in enumerate(((x_hbm, x_ref), (cot_hbm, cot_ref), (b_hbm, b_ref)))
    ]

    @pl.when(step == 0)
    def _():
        for copy in late:
            copy.start()
        key = lax.broadcasted_iota(jnp.int32, bias_ref.shape, 0)
        query = lax.broadcasted_iota(jnp.int32, bias_ref.shape, 1)
        allowed = (key >= query) & (key <= query + WINDOW) & (kseg_ref[...] == qseg_ref[...])
        bias_ref[...] = jnp.where(allowed, 0.0, MASKED)
        vt_ref[...] = turned(kv_ref[:, HD:])
        ffn_ref[...] = jnp.zeros_like(ffn_ref)
        ro_ref[...] = jnp.zeros_like(ro_ref)

    @pl.when((step >= 1) & (step < 1 + slots))
    def _():
        for copy in copies(step - 1, step - 1):
            copy.start()

    @pl.when(step < tensor_count)
    def _():
        lin = mm(n1_ref[...], flat(wq_ref)) + mm(r1_ref[...], bq_ref[0])
        heads = q_ref.shape[1] // HD
        for h in range(heads):
            part = slice(h * HD, (h + 1) * HD)
            query = (rope(lin[:, part], cos_ref[...], sin_ref[...]) * (SCALE * LOG2E)).astype(BF)
            q_ref[:, part] = query
            qs_ref[h * rows : (h + 1) * rows] = query
        queries = qs_ref[...]
        top = jnp.full((1, heads * rows), MASKED, F32)
        for c in range(chunks):
            span = slice(c * rows, (c + 1) * rows)
            s = mm_nt(kv_ref[span, :HD], queries)
            bias = bias_ref[span]
            s = jnp.concatenate([s[:, h * rows : (h + 1) * rows] + bias for h in range(heads)], axis=1)
            s_ref[span] = s
            top = jnp.maximum(top, jnp.max(s, axis=0, keepdims=True))
        total = jnp.zeros((1, heads * rows), F32)
        for c in range(chunks):
            span = slice(c * rows, (c + 1) * rows)
            p = jnp.exp2(s_ref[span] - top)
            total = total + jnp.sum(p, axis=0, keepdims=True)
            p_ref[0, span] = p.astype(BF)
        inv = 1.0 / total
        inv_ref[0, 0:1] = inv
        out = mm(vt_ref[...], p_ref[0]) * inv
        for h in range(heads):
            mixed_ref[:, h * HD : (h + 1) * HD] = out[:, h * rows : (h + 1) * rows].T.astype(BF)
        mixed = mixed_ref[...]
        all_mixed_ref[step] = mixed
        ffn_ref[...] += mm_nt(mixed, flat(wo_ref))
        ro_ref[...] += mm_nt(mixed, bo_ref[0])

    @pl.when(step == tensor_count - 1)
    def _():
        for copy in late:
            copy.wait()
        res = x_ref[...].astype(F32) + (ffn_ref[...] + mm_nt(ro_ref[...].astype(BF), a_ref[...]))
        res_ref[...] = res
        n2 = rms(res, gain_ref[...]).astype(BF)
        n2_ref[...] = n2
        r2 = mm(n2, a_ref[...]).astype(BF)
        r2_ref[...] = r2
        r2t_ref[...] = turned(r2)
        grd = mm(cot_ref[...], a_ref[...]).astype(BF)
        grd_ref[...] = grd
        grdt_ref[...] = turned(grd)
        ffn_ref[...] = jnp.zeros_like(ffn_ref)
        g2_ref[...] = jnp.zeros_like(g2_ref)
        rd_ref[...] = jnp.zeros_like(rd_ref)
        gr_ref[...] = jnp.zeros_like(gr_ref)

    def feed_forward(at, carry):
        slot = lax.rem(at, slots)

        @pl.when((at >= 1) & (at + slots - 1 < steps))
        def _():
            for copy in copies(at + slots - 1, lax.rem(at + slots - 1, slots)):
                copy.start()

        n2, r2, cot = n2_ref[...], r2_ref[...], cot_ref[...]
        b_gu, b_d = b_ref[at, :, : 2 * ff], b_ref[at, :, 2 * ff :]
        arrivals = copies(at, slot)
        weight_rows = wv_ref.shape[1] * wv_ref.shape[2]
        for copy in arrivals[:tensor_count]:
            copy.wait()
        w_d = wv_ref[slot, :, :, 2 * ff :].reshape(weight_rows, ff)
        grad_hidden = (mm(cot, w_d) + mm(grd_ref[...], b_d)).astype(BF).astype(F32)
        for copy in arrivals[tensor_count:]:
            copy.wait()
        w_gu = wv_ref[slot, :, :, : 2 * ff].reshape(weight_rows, 2 * ff)
        lin = mm(n2, w_gu) + mm(r2, b_gu)
        gate, up = lin[:, :ff], lin[:, ff:]
        square = gate * gate
        th = jnp.tanh(GELU_C * (gate + GELU_A * square * gate))
        half = 0.5 * (1.0 + th)
        act = gate * half
        slope = half + 0.5 * gate * (1.0 - th * th) * (GELU_C * (1.0 + 3.0 * GELU_A * square))
        hidden = (act * up).astype(BF)
        grad_gate = (grad_hidden * up * slope).astype(BF)
        grad_up = (grad_hidden * act).astype(BF)
        grads = jnp.concatenate([grad_gate, grad_up], axis=1)
        ffn_ref[...] += mm_nt(hidden, w_d)
        rd_ref[...] += mm_nt(hidden, b_d)
        g2_ref[...] += mm_nt(grads, w_gu)
        gr_ref[...] += mm_nt(grads, b_gu)
        terms = (
            mm(r2t_ref[rows_of(SLOT_G)], grad_gate), mm(r2t_ref[rows_of(SLOT_U)], grad_up),
            mm(grdt_ref[rows_of(SLOT_D)], hidden),
        )
        for kind, term in enumerate(terms):
            target = pl.multiple_of((kind * steps + at) * part_cols, LANES)
            for t in range(tensor_count):
                early_ref[t, :, pl.ds(target, part_cols)] = term[:, t * part_cols : (t + 1) * part_cols].astype(BF)
        return carry

    @pl.when(step == tensor_count)
    def _():
        lax.fori_loop(0, steps, feed_forward, 0)
        res, n2, cot = res_ref[...], n2_ref[...], cot_ref[...]
        out_ref[...] = (res + (ffn_ref[...] + mm_nt(rd_ref[...].astype(BF), a_ref[...]))).astype(BF)
        grad_two = g2_ref[...] + mm_nt(gr_ref[...].astype(BF), a_ref[...])
        grad_res = cot.astype(F32) + rms_back(res, gain_ref[...], grad_two)
        gres_ref[...] = grad_res
        grad_branch = grad_res.astype(BF)
        gb_ref[...] = grad_branch
        gro = mm(grad_branch, a_ref[...])
        gro_ref[...] = gro.astype(BF)
        grot = gro.T[rows_of(SLOT_O)].astype(BF)
        first = 3 * steps * part_cols
        for t in range(tensor_count):
            early_ref[t, :, first:] = mm(grot, all_mixed_ref[t]).astype(BF)
        wide = mm(gr_ref[...].T.astype(BF), n2) + mm(rd_ref[...].T.astype(BF), cot)
        wide_ref[...] = wide + mm(ro_ref[...].T.astype(BF), grad_branch)


def attn_back_kernel(
    tensor_ref, kv_ref, gb_ref, gro_ref, r1_ref, cos_ref, sin_ref,
    q_ref, mixed_ref, p_ref, inv_ref, wo_ref, bo_ref, wq_ref, bq_ref,
    dkva_ref, dkvb_ref, dkvc_ref, dkvd_ref, dkve_ref, q0_ref, g1_ref, gr_ref,
    ds_ref, dk_ref, dv_ref, kt_ref, r1t_ref, gq_ref, gm_ref, qs_ref, gs_ref,
):
    step = pl.program_id(0)
    rows = q_ref.shape[0]
    chunks = kv_ref.shape[0] // rows

    @pl.when(step == 0)
    def _():
        kt_ref[...] = turned(kv_ref[:, :HD])
        r1t_ref[...] = turned(r1_ref[...])
        dk_ref[...] = jnp.zeros_like(dk_ref)
        dv_ref[...] = jnp.zeros_like(dv_ref)
        g1_ref[...] = jnp.zeros_like(g1_ref)
        gr_ref[...] = jnp.zeros_like(gr_ref)

    gm_ref[...] = (mm(gb_ref[...], flat(wo_ref)) + mm(gro_ref[...], bo_ref[0])).astype(BF)
    heads = q_ref.shape[1] // HD
    deltas = []
    for h in range(heads):
        part, span = slice(h * HD, (h + 1) * HD), slice(h * rows, (h + 1) * rows)
        grad = gm_ref[:, part]
        qs_ref[span] = q_ref[:, part]
        gs_ref[span] = grad
        delta = grad.astype(F32) * mixed_ref[:, part].astype(F32)
        deltas.append(jnp.sum(delta.T, axis=0, keepdims=True))
    delta, inv = jnp.concatenate(deltas, axis=1), inv_ref[0, 0:1]
    queries, grads = qs_ref[...], gs_ref[...]
    for c in range(chunks):
        span = slice(c * rows, (c + 1) * rows)
        p = p_ref[0, span].astype(F32) * inv
        dp = mm_nt(kv_ref[span, HD:], grads)
        ds = (p * (dp - delta)).astype(BF)
        ds_ref[span] = ds
        dk_ref[span] += mm(ds, queries)
        dv_ref[span] += mm(p.astype(BF), grads)
    dq = mm(kt_ref[...], ds_ref[...]) * SCALE
    for h in range(heads):
        part, span = slice(h * HD, (h + 1) * HD), slice(h * rows, (h + 1) * rows)
        gq_ref[:, part] = rope_back(dq[:, span].T, cos_ref[...], sin_ref[...]).astype(BF)

    gq = gq_ref[...]
    grad_bq = mm(r1t_ref[rows_of(SLOT_Q)], gq).astype(BF)
    away = lax.rem(tensor_ref[0] + pl.num_programs(0) - step, pl.num_programs(0))

    @pl.when(away == 0)
    def _():
        q0_ref[...] = grad_bq

    for d, dkv_ref in ((1, dkvd_ref), (2, dkvc_ref), (3, dkvb_ref)):

        @pl.when(away == d)
        def _(dkv_ref=dkv_ref):
            dkv_ref[rows : rows + RANK] = grad_bq[:, : 2 * HD]
            dkv_ref[rows + RANK :, :HD] = grad_bq[:, 2 * HD :]
            dkv_ref[rows + RANK :, HD:] = jnp.zeros((RANK, HD), BF)

    gr_ref[...] += mm_nt(gq, bq_ref[0])
    g1_ref[...] += mm_nt(gq, flat(wq_ref))

    @pl.when(step == pl.num_programs(0) - 1)
    def _():
        for c, dkv_ref in enumerate((dkva_ref, dkvb_ref, dkvc_ref, dkvd_ref, dkve_ref)):
            span = slice(c * rows, (c + 1) * rows)
            dkv_ref[:rows, :HD] = (dk_ref[span] * (1.0 / LOG2E)).astype(BF)
            dkv_ref[:rows, HD:] = dv_ref[span].astype(BF)


def shared_back_kernel(
    chips, core_ref, n1_ref, r1_ref, bkv_ref, cos_ref, sin_ref, own_ref, back1_ref, back2_ref, back3_ref, back4_ref,
    q0_ref, gr_ref, widef_ref,
    mine_ref, theirs_ref, gk_ref, gv_ref, grt_ref,
):
    rows = own_ref.shape[0]
    gkv = own_ref[...].astype(F32)
    for back_ref in (back1_ref, back2_ref, back3_ref, back4_ref):
        gkv = gkv + back_ref[:rows].astype(F32)
    queries = [q0_ref[:, j * LANES : (j + 1) * LANES].astype(F32) for j in range(3)]
    for back_ref in (back1_ref, back2_ref, back3_ref):
        queries[0] = queries[0] + back_ref[rows : rows + RANK, :HD].astype(F32)
        queries[1] = queries[1] + back_ref[rows : rows + RANK, HD:].astype(F32)
        queries[2] = queries[2] + back_ref[rows + RANK :, :HD].astype(F32)
    gk = rope_back(gkv[:, :HD], cos_ref[...], sin_ref[...]).astype(BF)
    gv = gkv[:, HD:].astype(BF)
    gk_ref[...] = gk
    gv_ref[...] = gv
    gr = gr_ref[...] + mm_nt(gk, bkv_ref[0]) + mm_nt(gv, bkv_ref[1])
    grt_ref[...] = gr.astype(BF)
    wide = (mm(gr.T.astype(BF), n1_ref[...]) + widef_ref[...]).T.astype(BF)
    share = mine_ref.shape[0] - 5 * RANK
    wide = wide.reshape(chips, 2, share // chips, LANES)
    first = core_ref[0] == 0
    mine_ref[:share] = jnp.where(first, wide[:, 0], wide[:, 1]).reshape(share, LANES)
    theirs_ref[:share] = jnp.where(first, wide[:, 1], wide[:, 0]).reshape(share, LANES)
    r1t = turned(r1_ref[...])
    for j, (slot, grad) in enumerate(((SLOT_K, gk), (SLOT_V, gv))):
        term = mm(r1t[rows_of(slot)], grad).astype(BF)
        part = slice(share + j * RANK, share + (j + 1) * RANK)
        mine_ref[part] = term
        theirs_ref[part] = term
    for j, term in enumerate(queries):
        part = slice(share + (2 + j) * RANK, share + (3 + j) * RANK)
        mine_ref[part] = term.astype(BF)
        theirs_ref[part] = term.astype(BF)


def payload_kernel(core_ref, mine_ref, other_ref, out_ref, q_ref):
    first = core_ref[0] == 0
    total = mine_ref[...].astype(F32) + other_ref[...].astype(F32)
    count = out_ref.shape[0]
    own_rows = (total.shape[0] - 5 * RANK) // count
    queries = total[total.shape[0] - 3 * RANK :].astype(BF)
    for n in range(q_ref.shape[0]):
        for j in range(3):
            q_ref[n, :, j * LANES : (j + 1) * LANES] = queries[j * RANK : (j + 1) * RANK]
    tensor_count = RANK // 4
    blank = jnp.zeros((RANK - own_rows - 2, LANES), F32)
    for n in range(count):
        pieces = [total[n * own_rows : (n + 1) * own_rows]]
        row = (2 * (n // tensor_count) * tensor_count + n % tensor_count) % RANK
        for j in range(2):
            at = count * own_rows + j * RANK + row
            low, high = total[at : at + 1], total[at + tensor_count : at + tensor_count + 1]
            pieces.append(jnp.where(first, low, high))
        out_ref[n] = jnp.concatenate(pieces + [blank], axis=0).astype(BF)


def input_kernel(
    x_ref, gain_ref, a_ref, wk_ref, wv_ref, gk_ref, gv_ref, gr_ref, g1_ref, gres_ref, grad_ref,
):
    g1 = g1_ref[...] + mm_nt(gk_ref[...], wk_ref[...]) + mm_nt(gv_ref[...], wv_ref[...])
    g1 = g1 + mm_nt(gr_ref[...], a_ref[...])
    x = x_ref[...].astype(F32)
    grad_ref[...] = gres_ref[...] + rms_back(x, gain_ref[...], g1)


def sum_hidden_kernel(
    ids_ref, terms_hbm, gu_hbm, down_hbm, out_hbm, terms_ref, acc_ref, gu_ref, down_ref, out_ref, sems, out_sems,
):
    adapters, rank, cols = acc_ref.shape
    ff = gu_ref.shape[2]
    groups = (slice(2 * ff, cols), slice(0, ff), slice(ff, 2 * ff))
    arrivals = []
    for j, group in enumerate(groups):
        part = pl.ds(group.start, group.stop - group.start)
        arrivals.append(pltpu.make_async_copy(terms_hbm.at[:, :, part], terms_ref.at[:, :, part], sems.at[j]))
        arrivals[j].start()
    acc_ref[...] = jnp.zeros_like(acc_ref)

    def added(group):
        for s in range(terms_ref.shape[0] // 2):
            pair = terms_ref[2 * s, :, group].astype(F32) + terms_ref[2 * s + 1, :, group].astype(F32)
            acc_ref[ids_ref[s], :, group] += pair

    sent = [
        pltpu.make_async_copy(down_ref, down_hbm, out_sems.at[0]),
        pltpu.make_async_copy(out_ref, out_hbm, out_sems.at[1]),
        pltpu.make_async_copy(gu_ref.at[0], gu_hbm.at[0], out_sems.at[2]),
        pltpu.make_async_copy(gu_ref.at[1], gu_hbm.at[1], out_sems.at[3]),
    ]
    arrivals[0].wait()
    added(groups[0])
    down_ref[...] = acc_ref[:, :, 2 * ff : 3 * ff].reshape(adapters * rank, ff).T
    sent[0].start()
    out_ref[...] = acc_ref[:, :, 3 * ff :].reshape(adapters * rank, cols - 3 * ff).T
    sent[1].start()
    for j in range(2):
        arrivals[1 + j].wait()
        added(groups[1 + j])
        gu_ref[j] = acc_ref[:, :, groups[1 + j]].reshape(adapters * rank, ff)
        sent[2 + j].start()
    for copy in sent:
        copy.wait()


def sum_wide_kernel(ids_ref, own_ref, terms_ref, *rest):
    q_refs, (wide_ref, kv_ref, q_ref, acc_ref, accq_ref) = rest[:-5], rest[-5:]
    acc_ref[...] = jnp.zeros_like(acc_ref)
    accq_ref[...] = jnp.zeros_like(accq_ref)
    y_count, x_count = len(q_refs), q_refs[0].shape[0]
    for away_y, terms in enumerate(q_refs):
        y = lax.rem(own_ref[1] + away_y, y_count)
        for away_x in range(x_count):
            x = lax.rem(own_ref[2] + away_x, x_count)
            accq_ref[ids_ref[y * x_count + x]] += terms[away_x].astype(F32)
    q_ref[...] = accq_ref[...].reshape(q_ref.shape)
    seqs, parts = terms_ref.shape[:2]
    for s in range(seqs):
        term = terms_ref[s, 0].astype(F32)
        for part in range(1, parts):
            term = term + terms_ref[s, part].astype(F32)
        acc_ref[ids_ref[s]] += term
    adapters, rank, _ = acc_ref.shape
    lane = lax.broadcasted_iota(jnp.int32, (rank, LANES), 1) // RANK
    own_rows, slots = wide_ref.shape[:2]
    for j in range(slots):
        total = jnp.zeros((rank, LANES), F32)
        for a in range(adapters):
            moved = pltpu.roll(acc_ref[a], ((a - j) * RANK) % LANES, 1)
            total = jnp.where(lane == a, moved, total)
        wide_ref[:, j] = total[:own_rows]
    mine = acc_ref[own_ref[0]]
    for j in range(2):
        kv_ref[j] = mine[own_rows + j : own_rows + j + 1]


def sds(shape, dtype):
    return jax.ShapeDtypeStruct(shape, dtype)


def scalars():
    return pl.BlockSpec(memory_space=pltpu.SMEM)


def whole(array):
    rank = len(array.shape)
    return pl.BlockSpec(array.shape, lambda *_: (0,) * rank)


def wholes(*arrays):
    return [whole(v) for v in arrays]


def by_step(*shape):
    return pl.BlockSpec((1,) + shape, lambda t: (t,) + (0,) * len(shape))


def call(kernel, name, steps, args, specs, outs, scratch, flops, nbytes):
    shapes = [shape for shape, _ in outs]
    return pl.pallas_call(
        kernel,
        name=name,
        grid=(steps,),
        in_specs=specs,
        out_specs=[whole(shape) if spec is None else spec for shape, spec in outs],
        out_shape=shapes,
        scratch_shapes=scratch,
        compiler_params=pltpu.CompilerParams(
            dimension_semantics=("arbitrary",), vmem_limit_bytes=VMEM_LIMIT
        ),
        cost_estimate=pl.CostEstimate(flops=flops, bytes_accessed=nbytes, transcendentals=0),
    )(*args)


def rope_tables(positions):
    half = HD // 2
    frequency = 10000.0 ** (-(jnp.arange(half).astype(F32) / half))
    angles = positions.astype(F32)[:, None] * frequency[None, :]
    cos, sin = jnp.cos(angles), jnp.sin(angles)
    return jnp.concatenate([cos, cos], axis=1), jnp.concatenate([-sin, sin], axis=1)


def on_device(
    tokens, cotangent, segments, adapter_ids, norm_gains, q_weight, kv_weight, out_weight,
    gate_up_weight, down_weight, wide_adapters, kv_adapter, q_adapter, out_adapter,
    gate_up_adapter, down_adapter,
):
    rows, width = tokens.shape
    tensor_count = lax.axis_size("tensor")
    dp_count = lax.axis_size("y") * lax.axis_size("x") * 2
    devices = dp_count * tensor_count
    group_rows = rows * tensor_count
    seq_length = 2 * group_rows
    shard_rows = q_weight.shape[0]
    q_cols, ff_cols = q_weight.shape[1], gate_up_weight.shape[2]
    heads_cols = tensor_count * q_cols
    seqs = adapter_ids.shape[0]
    adapters = wide_adapters.shape[2] // RANK
    dp = lax.axis_index(DP)
    tensor = lax.axis_index("tensor")
    my_core = lax.axis_index("core")
    adapter = lax.dynamic_index_in_dim(adapter_ids, dp // 2, keepdims=False)
    column = adapter * RANK
    f3 = 3 * ff_cols

    args = (gate_up_weight, down_weight.T, q_weight, out_weight.T)
    (pack,) = call(
        pack_kernel, "pack", 1, args, wholes(*args), [(sds((shard_rows, f3 + 2 * q_cols), BF), None)], [],
        0, 4 * shard_rows * (f3 + 2 * q_cols),
    )
    pack, wide_adapters = lax.optimization_barrier((pack, wide_adapters))
    weights = lax.all_gather(pack, ALL, axis=0, tiled=False)
    weights = weights.reshape(dp_count, tensor_count, shard_rows, f3 + 2 * q_cols)

    wide = wide_adapters.reshape(7, shard_rows, adapters, RANK)
    wide = jnp.take(wide, adapter_ids, axis=2).transpose(2, 1, 0, 3)
    wide = wide.reshape(seqs, shard_rows, 7 * RANK)
    wide = jnp.pad(wide, ((0, 0), (0, 0), (0, LANES - 7 * RANK)))
    shared = jnp.broadcast_to(kv_weight[:, None], (2, seqs, shard_rows, HD))
    wide = jnp.concatenate([wide, shared[0], shared[1]], axis=2)

    def from_other_core(value):
        return lax.ppermute(value, "core", [(0, 1), (1, 0)])

    a_own = lax.all_to_all(wide, ("y", "x"), 0, 0, tiled=True)
    a_other = from_other_core(a_own)
    a_all = jnp.where(my_core == 0, jnp.stack([a_own, a_other], 1), jnp.stack([a_other, a_own], 1))
    a_all = a_all.reshape(width, 3 * LANES)

    def take_rows(matrix):
        return lax.dynamic_slice_in_dim(matrix, column, RANK, matrix.ndim - 2)

    def take_cols(matrix):
        return lax.dynamic_slice_in_dim(matrix, column, RANK, matrix.ndim - 1)

    def in_slot(block, slot):
        pads = [(0, 0)] * block.ndim
        pads[-2] = (slot * RANK, LANES - (slot + 1) * RANK)
        return jnp.pad(block, pads)

    gu_rows = take_rows(gate_up_adapter)
    b_own = jnp.concatenate(
        [gu_rows[0], gu_rows[1], take_cols(down_adapter).T, take_rows(q_adapter), take_cols(out_adapter).T], axis=1
    )
    kv_rows = take_rows(kv_adapter)
    b_kv = jnp.stack([in_slot(kv_rows[0], SLOT_K), in_slot(kv_rows[1], SLOT_V)])

    start = dp * group_rows + tensor * rows
    span = WINDOW + rows
    cos_window, sin_window = rope_tables((start - WINDOW + jnp.arange(span)) % seq_length)
    cos, sin = cos_window[WINDOW:], sin_window[WINDOW:]
    padded = jnp.concatenate([jnp.full((WINDOW,), -1, jnp.int32), segments])
    kseg = lax.dynamic_slice_in_dim(padded, start, span, 0)
    qseg = kseg[WINDOW:].reshape(1, rows)
    kseg = kseg.reshape(span, 1)

    gain_one, gain_two = norm_gains[0:1], norm_gains[1:2]
    q_block = f3 // q_cols

    def weight_spec(block):
        return pl.BlockSpec((dp_count, 1, shard_rows, q_cols), lambda t: (0, t, 0, block))

    def adapter_spec(block):
        return pl.BlockSpec((1, LANES, q_cols), lambda t: (t, 0, block))

    def lane_block(block):
        return pl.BlockSpec((width, LANES), lambda *_: (0, block))

    head_specs = [weight_spec(q_block), adapter_spec(0), weight_spec(q_block + 1), adapter_spec(1)]
    q_spec, qb_spec, o_spec, ob_spec = head_specs
    a_spec, wk_spec, wv_spec = lane_block(0), lane_block(1), lane_block(2)
    token_cols = pl.BlockSpec((rows, q_cols), lambda t: (0, t))
    tok_bf, tok_f32, rank_bf = sds((rows, width), BF), sds((rows, width), F32), sds((rows, LANES), BF)

    args = (tokens, gain_one, a_all, a_all, a_all, b_kv, cos, sin)
    normed_one, rank_one, kv_own = call(
        shared_kernel, "keys_values", 1, args,
        wholes(*args[:2]) + [a_spec, wk_spec, wv_spec] + wholes(*args[5:]),
        [(tok_bf, None), (rank_bf, None), (sds((rows, 2 * HD), BF), None)],
        [], 2 * rows * width * 384, 6 * rows * width,
    )
    parts = seq_length // rows
    reach = WINDOW // rows

    def moved(value, steps):
        return lax.ppermute(value, SEQ, [(c, c + steps) for c in range(parts) if 0 <= c + steps < parts])

    kv_window = jnp.concatenate([moved(kv_own, d) for d in range(reach, 0, -1)] + [kv_own])

    b_own, kv_own = lax.optimization_barrier((b_own, kv_own))
    b_parts = [b_own] + [
        lax.ppermute(b_own, "tensor", [((z + d) % tensor_count, z) for z in range(tensor_count)])
        for d in range(1, tensor_count)
    ]
    b_all = jnp.roll(jnp.stack(b_parts), tensor, axis=0)
    b_heads = jnp.concatenate(
        [in_slot(b_all[:, :, f3 : f3 + q_cols], SLOT_Q), in_slot(b_all[:, :, f3 + q_cols :], SLOT_O)], axis=2
    )
    steps, slots = ff_cols // LANES, 2
    part_cols = ff_cols // steps
    b_hidden = b_all[:, :, :f3].reshape(tensor_count, RANK, 3, steps, part_cols).transpose(3, 2, 1, 0, 4)
    b_hidden = b_hidden.reshape(steps, 3, RANK, tensor_count * part_cols)
    b_hidden = jnp.concatenate(
        [in_slot(b_hidden[:, kind], slot) for kind, slot in enumerate((SLOT_G, SLOT_U, SLOT_D))], axis=2
    )

    heads = q_cols // HD
    last = tensor_count - 1

    def until_last(spec):
        return pl.BlockSpec(spec.block_shape, lambda t: spec.index_map(jnp.minimum(t, last)))

    p_spec, norm_spec = by_step(span, heads * rows), by_step(8, heads * rows)
    args = (
        kv_window, kseg, qseg, normed_one, rank_one, cos, sin, gain_two, a_all,
        weights, b_heads, weights, b_heads, tokens, cotangent, b_hidden, weights,
    )
    (
        queries, mixed, probs, norms, block_output, grad_residual, grad_branch, wide_ffn, grad_ro, early
    ) = call(
        forward_kernel, "forward", tensor_count + 1, args,
        wholes(*args[:8]) + [a_spec] + [until_last(spec) for spec in head_specs]
        + [pl.BlockSpec(memory_space=pl.ANY)] * 4,
        [
            (sds((rows, heads_cols), BF), until_last(token_cols)), (sds((rows, heads_cols), BF), until_last(token_cols)),
            (sds((tensor_count, span, heads * rows), BF), until_last(p_spec)),
            (sds((tensor_count, 8, heads * rows), F32), until_last(norm_spec)),
            (tok_bf, None), (tok_f32, None), (tok_bf, None), (sds((LANES, width), F32), None), (rank_bf, None),
            (sds((tensor_count, RANK, f3 + q_cols), BF), None),
        ],
        [
            pltpu.VMEM((span, rows), F32), pltpu.VMEM((span, heads * rows), F32), pltpu.VMEM((HD, span), BF),
            pltpu.VMEM((rows, width), F32), pltpu.VMEM((rows, width), F32), pltpu.VMEM((rows, LANES), F32),
            pltpu.VMEM((rows, LANES), F32), pltpu.VMEM((rows, LANES), F32), pltpu.VMEM((heads * rows, HD), BF),
            pltpu.VMEM((tensor_count, rows, q_cols), BF), pltpu.VMEM((rows, width), F32), pltpu.VMEM((rows, width), BF),
            pltpu.VMEM((rows, LANES), BF), pltpu.VMEM((LANES, rows), BF),
            pltpu.VMEM((rows, LANES), BF), pltpu.VMEM((LANES, rows), BF),
            pltpu.VMEM((slots, dp_count, shard_rows, 3 * tensor_count * part_cols), BF),
            pltpu.VMEM((rows, width), BF), pltpu.VMEM((rows, width), BF), pltpu.VMEM(b_hidden.shape, BF),
            pltpu.SemaphoreType.DMA((slots, 3 * tensor_count)), pltpu.SemaphoreType.DMA((3,)),
        ],
        4 * rows * heads_cols * (span + width) + 12 * rows * width * tensor_count * ff_cols,
        4 * width * heads_cols + 6 * width * tensor_count * ff_cols,
    )
    early = lax.psum_scatter(early, "tensor", scatter_dimension=0, tiled=True).reshape(RANK, -1)

    args = (
        tensor.astype(jnp.int32).reshape(1), kv_window, grad_branch, grad_ro, rank_one, cos, sin,
        queries, mixed, probs, norms, weights, b_heads, weights, b_heads,
    )
    *dkv, q_own, grad_one, grad_rank = call(
        attn_back_kernel, "attention_back", tensor_count, args,
        [scalars()] + wholes(*args[1:7]) + [token_cols, token_cols, p_spec, norm_spec, o_spec, ob_spec, q_spec, qb_spec],
        [
            *[(sds((rows + (2 * RANK if 0 < w < reach else 0), 2 * HD), BF), None) for w in range(reach + 1)],
            (sds((RANK, q_cols), BF), None), (tok_f32, None), (sds((rows, LANES), F32), None),
        ],
        [
            pltpu.VMEM((span, heads * rows), BF),
            pltpu.VMEM((span, HD), F32), pltpu.VMEM((span, HD), F32), pltpu.VMEM((HD, span), BF),
            pltpu.VMEM((LANES, rows), BF), pltpu.VMEM((rows, q_cols), BF), pltpu.VMEM((rows, q_cols), BF),
            pltpu.VMEM((heads * rows, HD), BF), pltpu.VMEM((heads * rows, HD), BF),
        ],
        2 * rows * heads_cols * (4 * span + 2 * width), 4 * width * heads_cols,
    )

    early, grad_one = lax.optimization_barrier((early, grad_one))
    early = lax.all_gather(early, DP, axis=0, tiled=False)

    def around(value, steps):
        return lax.ppermute(value, SEQ, [(c, (c - steps) % parts) for c in range(parts)])

    backs = [around(dkv[reach - d], d) for d in range(1, reach)] + [moved(dkv[0], -reach)]
    core = my_core.astype(jnp.int32).reshape(1)
    chips = dp_count // 2
    share = width // 2 + 5 * RANK
    args = (
        core, normed_one, rank_one, b_kv, cos, sin, dkv[reach], *backs, q_own, grad_rank, wide_ffn,
    )
    mine, theirs, grad_key, grad_value, grad_rank = call(
        functools.partial(shared_back_kernel, chips), "shared_back", 1, args,
        [scalars()] + wholes(*args[1:]),
        [
            (sds((share, LANES), BF), None), (sds((share, LANES), BF), None),
            (sds((rows, HD), BF), None), (sds((rows, HD), BF), None), (rank_bf, None),
        ],
        [], 4 * rows * width * LANES, 6 * rows * width,
    )
    own_rows = width // devices
    planes = chips * tensor_count
    args = (core, mine, from_other_core(theirs))
    payload, q_terms = call(
        payload_kernel, "payload", 1, args, [scalars()] + wholes(*args[1:]),
        [(sds((planes, RANK, LANES), BF), None), (sds((1, RANK, q_cols), BF), None)], [],
        0, 2 * planes * RANK * LANES,
    )
    payload, grad_key = lax.optimization_barrier((payload, grad_key))
    terms = lax.all_to_all(payload, PLANES, 0, 0, tiled=True)

    def with_others(value, axis):
        count = lax.axis_size(axis)
        return [value] + [
            lax.ppermute(value, axis, [((i + d) % count, i) for i in range(count)]) for d in range(1, count)
        ]

    q_terms = with_others(jnp.concatenate(with_others(q_terms, "x")), "y")
    terms = terms.reshape(seqs, tensor_count, RANK, LANES)

    args = (
        tokens, gain_one, a_all, a_all, a_all, grad_key, grad_value, grad_rank, grad_one, grad_residual,
    )
    (input_grad,) = call(
        input_kernel, "input_gradient", 1, args,
        wholes(*args[:2]) + [a_spec, wk_spec, wv_spec] + wholes(*args[5:]),
        [(tok_f32, None)], [], 2 * rows * width * 384, 16 * rows * width,
    )

    terms, input_grad = lax.optimization_barrier((terms, input_grad))
    own = jnp.stack([(dp * tensor_count + tensor) // RANK, lax.axis_index("y"), lax.axis_index("x")]).astype(jnp.int32)
    wide_grad, kv_adapter_grad, q_adapter_grad = call(
        sum_wide_kernel, "sum_wide", 1, (adapter_ids, own, terms, *q_terms),
        [scalars(), scalars()] + wholes(terms, *q_terms),
        [(sds((own_rows, 7, LANES), F32), None), (sds((2, 1, HD), F32), None), (sds((LANES, q_cols), F32), None)],
        [pltpu.VMEM((adapters, RANK, LANES), F32), pltpu.VMEM((adapters, RANK, q_cols), F32)], 0, 4 * LANES * f3,
    )
    shapes = [(2, LANES, ff_cols), (ff_cols, LANES), (q_cols, LANES)]
    gate_up_adapter_grad, down_adapter_grad, out_adapter_grad = call(
        sum_hidden_kernel, "sum_hidden", 1, (adapter_ids, early),
        [scalars(), pl.BlockSpec(memory_space=pl.ANY)],
        [(sds(shape, F32), pl.BlockSpec(memory_space=pl.ANY)) for shape in shapes],
        [pltpu.VMEM(early.shape, BF), pltpu.VMEM((adapters, RANK, f3 + q_cols), F32)]
        + [pltpu.VMEM(shape, F32) for shape in shapes]
        + [pltpu.SemaphoreType.DMA((3,)), pltpu.SemaphoreType.DMA((4,))],
        0, 4 * LANES * f3,
    )
    return (
        block_output, input_grad, wide_grad.transpose(1, 0, 2), kv_adapter_grad,
        q_adapter_grad, out_adapter_grad, gate_up_adapter_grad, down_adapter_grad,
    )


def solution(mesh):
    dp_count, tensor_count = mesh.shape["dp"], mesh.shape["tensor"]
    chips = dp_count // 2
    x_count = math.isqrt(chips)
    devices = mesh.devices.reshape(chips // x_count, x_count, 2, tensor_count)
    return jax.shard_map(
        on_device,
        mesh=Mesh(devices, ALL),
        in_specs=(
            P(ALL, None), P(ALL, None), P(), P(), P(), P(DP, "tensor"), P(None, DP, None),
            P("tensor", DP), P(None, DP, "tensor"), P("tensor", DP), P(None, DP, None), P(),
            P(None, "tensor"), P("tensor", None), P(None, None, "tensor"), P("tensor", None),
        ),
        out_specs=(
            P(ALL, None), P(ALL, None), P(None, ALL, None), P(None, ALL, None),
            P(None, "tensor"), P("tensor", None), P(None, None, "tensor"), P("tensor", None),
        ),
        check_vma=False,
    )
```

```python
import functools
import math

import jax
import jax.numpy as jnp
from jax import lax
from jax.experimental import pallas as pl
from jax.experimental.pallas import tpu as pltpu
from jax.sharding import Mesh, PartitionSpec as P

HD = 128
WINDOW = 1024
RANK = 16
LANES = 128
EPS = 1e-06
MASKED = -1e30
SCALE = HD ** (-0.5)
LOG2E = math.log2(math.e)
GELU_C = 0.7978845608028654
GELU_A = 0.044715
VMEM_LIMIT = 58 * 1024 * 1024
BF = jnp.bfloat16
F32 = jnp.float32
DP = ("y", "x", "core")
SEQ = ("core", "tensor")
PLANES = ("y", "x", "tensor")
ALL = ("y", "x", "core", "tensor")

SLOT_Q, SLOT_K, SLOT_V, SLOT_G, SLOT_U, SLOT_O, SLOT_D = range(7)


def rows_of(slot):
    return slice(slot * RANK, (slot + 1) * RANK)


def mm(a, b):
    return lax.dot_general(a, b, (((1,), (0,)), ((), ())), preferred_element_type=F32)


def mm_nt(a, b):
    return lax.dot_general(a, b, (((1,), (1,)), ((), ())), preferred_element_type=F32)


def turned(a):
    return a.astype(F32).T.astype(BF)


def rope(v, cos, sin):
    return v * cos + pltpu.roll(v, HD // 2, 1) * sin


def rope_back(g, cos, sin):
    return g * cos - pltpu.roll(g, HD // 2, 1) * sin


def flat(ref):
    block = ref[...]
    return block.reshape(block.shape[0] * block.shape[2], block.shape[3])


def rms(v, gain):
    return v * lax.rsqrt(jnp.mean(v * v, axis=-1, keepdims=True) + EPS) * gain


def rms_back(v, gain, grad):
    inv = lax.rsqrt(jnp.mean(v * v, axis=-1, keepdims=True) + EPS)
    scaled = grad * gain
    dot = jnp.mean(v * scaled, axis=-1, keepdims=True)
    return inv * scaled - v * (inv * inv * inv * dot)


def pack_kernel(gu_ref, down_ref, q_ref, o_ref, out_ref):
    ff, cols = gu_ref.shape[2], q_ref.shape[1]
    out_ref[:, :ff] = gu_ref[0]
    out_ref[:, ff : 2 * ff] = gu_ref[1]
    out_ref[:, 2 * ff : 3 * ff] = down_ref[...]
    out_ref[:, 3 * ff : 3 * ff + cols] = q_ref[...]
    out_ref[:, 3 * ff + cols :] = o_ref[...]


def shared_kernel(x_ref, gain_ref, a_ref, wk_ref, wv_ref, bkv_ref, cos_ref, sin_ref, n1_ref, r1_ref, kv_ref):
    n1 = rms(x_ref[...].astype(F32), gain_ref[...]).astype(BF)
    n1_ref[...] = n1
    r1 = mm(n1, a_ref[...]).astype(BF)
    r1_ref[...] = r1
    key = mm(n1, wk_ref[...]) + mm(r1, bkv_ref[0])
    kv_ref[:, :HD] = rope(key, cos_ref[...], sin_ref[...]).astype(BF)
    kv_ref[:, HD:] = (mm(n1, wv_ref[...]) + mm(r1, bkv_ref[1])).astype(BF)


def forward_kernel(
    kv_ref, kseg_ref, qseg_ref, n1_ref, r1_ref, cos_ref, sin_ref, gain_ref, a_ref,
    wq_ref, bq_ref, wo_ref, bo_ref, x_hbm, cot_hbm, b_hbm, w_ref,
    q_ref, mixed_ref, p_ref, inv_ref, out_ref, gres_ref, gb_ref, n2_ref, ranks_ref, gro_ref, early_ref,
    bias_ref, s_ref, vt_ref, ffn_ref, g2_ref, ro_ref, rd_ref, gr_ref, qs_ref,
    all_mixed_ref, res_ref, r2_ref, r2t_ref, grd_ref, grdt_ref, wv_ref, x_ref, cot_ref, b_ref, sems, late_sems,
):
    step = pl.program_id(0)
    slots, tensor_count = wv_ref.shape[0], w_ref.shape[1]
    steps = b_ref.shape[0]
    rows = q_ref.shape[0]
    chunks = kv_ref.shape[0] // rows
    ff = b_ref.shape[2] // 3
    part_cols = ff // tensor_count

    def copies(at, to):
        moves = []
        for kind in (2, 0, 1):
            for t in range(tensor_count):
                source = pl.multiple_of((kind * steps + at) * part_cols, LANES)
                target = (kind * tensor_count + t) * part_cols
                moves.append(
                    pltpu.make_async_copy(
                        w_ref.at[:, t, :, pl.ds(source, part_cols)],
                        wv_ref.at[to, :, :, pl.ds(target, part_cols)],
                        sems.at[to, len(moves)],
                    )
                )
        return moves

    late = [
        pltpu.make_async_copy(source, target, late_sems.at[j])
        for j, (source, target) in enumerate(((x_hbm, x_ref), (cot_hbm, cot_ref), (b_hbm, b_ref)))
    ]

    @pl.when(step == 0)
    def _():
        for copy in late:
            copy.start()
        key = lax.broadcasted_iota(jnp.int32, bias_ref.shape, 0)
        query = lax.broadcasted_iota(jnp.int32, bias_ref.shape, 1)
        allowed = (key >= query) & (key <= query + WINDOW) & (kseg_ref[...] == qseg_ref[...])
        bias_ref[...] = jnp.where(allowed, 0.0, MASKED)
        vt_ref[...] = turned(kv_ref[:, HD:])
        ffn_ref[...] = jnp.zeros_like(ffn_ref)
        ro_ref[...] = jnp.zeros_like(ro_ref)

    @pl.when((step >= 1) & (step < 1 + slots))
    def _():
        for copy in copies(step - 1, step - 1):
            copy.start()

    @pl.when(step < tensor_count)
    def _():
        lin = mm(n1_ref[...], flat(wq_ref)) + mm(r1_ref[...], bq_ref[0])
        heads = q_ref.shape[1] // HD
        for h in range(heads):
            part = slice(h * HD, (h + 1) * HD)
            query = (rope(lin[:, part], cos_ref[...], sin_ref[...]) * (SCALE * LOG2E)).astype(BF)
            q_ref[:, part] = query
            qs_ref[h * rows : (h + 1) * rows] = query
        queries = qs_ref[...]
        top = jnp.full((1, heads * rows), MASKED, F32)
        for c in range(chunks):
            span = slice(c * rows, (c + 1) * rows)
            s = mm_nt(kv_ref[span, :HD], queries)
            bias = bias_ref[span]
            s = jnp.concatenate([s[:, h * rows : (h + 1) * rows] + bias for h in range(heads)], axis=1)
            s_ref[span] = s
            top = jnp.maximum(top, jnp.max(s, axis=0, keepdims=True))
        total = jnp.zeros((1, heads * rows), F32)
        for c in range(chunks):
            span = slice(c * rows, (c + 1) * rows)
            p = jnp.exp2(s_ref[span] - top)
            total = total + jnp.sum(p, axis=0, keepdims=True)
            p_ref[0, span] = p.astype(BF)
        inv = 1.0 / total
        inv_ref[0, 0:1] = inv
        out = mm(vt_ref[...], p_ref[0]) * inv
        for h in range(heads):
            mixed_ref[:, h * HD : (h + 1) * HD] = out[:, h * rows : (h + 1) * rows].T.astype(BF)
        mixed = mixed_ref[...]
        all_mixed_ref[step] = mixed
        ffn_ref[...] += mm_nt(mixed, flat(wo_ref))
        ro_ref[...] += mm_nt(mixed, bo_ref[0])

    @pl.when(step == tensor_count - 1)
    def _():
        for copy in late:
            copy.wait()
        res = x_ref[...].astype(F32) + (ffn_ref[...] + mm_nt(ro_ref[...].astype(BF), a_ref[...]))
        res_ref[...] = res
        n2 = rms(res, gain_ref[...]).astype(BF)
        n2_ref[...] = n2
        r2 = mm(n2, a_ref[...]).astype(BF)
        r2_ref[...] = r2
        r2t_ref[...] = turned(r2)
        grd = mm(cot_ref[...], a_ref[...]).astype(BF)
        grd_ref[...] = grd
        grdt_ref[...] = turned(grd)
        ffn_ref[...] = jnp.zeros_like(ffn_ref)
        g2_ref[...] = jnp.zeros_like(g2_ref)
        rd_ref[...] = jnp.zeros_like(rd_ref)
        gr_ref[...] = jnp.zeros_like(gr_ref)

    def feed_forward(at, carry):
        slot = lax.rem(at, slots)

        @pl.when((at >= 1) & (at + slots - 1 < steps))
        def _():
            for copy in copies(at + slots - 1, lax.rem(at + slots - 1, slots)):
                copy.start()

        n2, r2, cot = n2_ref[...], r2_ref[...], cot_ref[...]
        b_gu, b_d = b_ref[at, :, : 2 * ff], b_ref[at, :, 2 * ff :]
        arrivals = copies(at, slot)
        weight_rows = wv_ref.shape[1] * wv_ref.shape[2]
        for copy in arrivals[:tensor_count]:
            copy.wait()
        w_d = wv_ref[slot, :, :, 2 * ff :].reshape(weight_rows, ff)
        grad_hidden = (mm(cot, w_d) + mm(grd_ref[...], b_d)).astype(BF).astype(F32)
        for copy in arrivals[tensor_count:]:
            copy.wait()
        w_gu = wv_ref[slot, :, :, : 2 * ff].reshape(weight_rows, 2 * ff)
        lin = mm(n2, w_gu) + mm(r2, b_gu)
        gate, up = lin[:, :ff], lin[:, ff:]
        square = gate * gate
        th = jnp.tanh(GELU_C * (gate + GELU_A * square * gate))
        half = 0.5 * (1.0 + th)
        act = gate * half
        slope = half + 0.5 * gate * (1.0 - th * th) * (GELU_C * (1.0 + 3.0 * GELU_A * square))
        hidden = (act * up).astype(BF)
        grad_gate = (grad_hidden * up * slope).astype(BF)
        grad_up = (grad_hidden * act).astype(BF)
        grads = jnp.concatenate([grad_gate, grad_up], axis=1)
        ffn_ref[...] += mm_nt(hidden, w_d)
        rd_ref[...] += mm_nt(hidden, b_d)
        g2_ref[...] += mm_nt(grads, w_gu)
        gr_ref[...] += mm_nt(grads, b_gu)
        terms = (
            mm(r2t_ref[rows_of(SLOT_G)], grad_gate), mm(r2t_ref[rows_of(SLOT_U)], grad_up),
            mm(grdt_ref[rows_of(SLOT_D)], hidden),
        )
        for kind, term in enumerate(terms):
            target = pl.multiple_of((kind * steps + at) * part_cols, LANES)
            for t in range(tensor_count):
                early_ref[t, :, pl.ds(target, part_cols)] = term[:, t * part_cols : (t + 1) * part_cols].astype(BF)
        return carry

    @pl.when(step == tensor_count)
    def _():
        lax.fori_loop(0, steps, feed_forward, 0)
        res, cot = res_ref[...], cot_ref[...]
        out_ref[...] = (res + (ffn_ref[...] + mm_nt(rd_ref[...].astype(BF), a_ref[...]))).astype(BF)
        grad_two = g2_ref[...] + mm_nt(gr_ref[...].astype(BF), a_ref[...])
        grad_res = cot.astype(F32) + rms_back(res, gain_ref[...], grad_two)
        gres_ref[...] = grad_res
        grad_branch = grad_res.astype(BF)
        gb_ref[...] = grad_branch
        gro = mm(grad_branch, a_ref[...])
        gro_ref[...] = gro.astype(BF)
        grot = gro.T[rows_of(SLOT_O)].astype(BF)
        first = 3 * steps * part_cols
        for t in range(tensor_count):
            early_ref[t, :, first:] = mm(grot, all_mixed_ref[t]).astype(BF)
        for j, rank in enumerate((gr_ref, rd_ref, ro_ref)):
            ranks_ref[j] = rank[...].astype(BF)


def attn_back_kernel(
    tensor_ref, kv_ref, gb_ref, gro_ref, r1_ref, cos_ref, sin_ref, ranks_ref, n2_ref, cot_ref,
    q_ref, mixed_ref, p_ref, inv_ref, wo_ref, bo_ref, wq_ref, bq_ref,
    dkva_ref, dkvb_ref, dkvc_ref, dkvd_ref, dkve_ref, q0_ref, g1_ref, gr_ref, wide_ref,
    ds_ref, dk_ref, dv_ref, kt_ref, r1t_ref, gq_ref, gm_ref, qs_ref, gs_ref,
):
    step = pl.program_id(0)
    rows = q_ref.shape[0]
    chunks = kv_ref.shape[0] // rows

    @pl.when(step == 0)
    def _():
        kt_ref[...] = turned(kv_ref[:, :HD])
        r1t_ref[...] = turned(r1_ref[...])
        dk_ref[...] = jnp.zeros_like(dk_ref)
        dv_ref[...] = jnp.zeros_like(dv_ref)
        g1_ref[...] = jnp.zeros_like(g1_ref)
        gr_ref[...] = jnp.zeros_like(gr_ref)

    gm_ref[...] = (mm(gb_ref[...], flat(wo_ref)) + mm(gro_ref[...], bo_ref[0])).astype(BF)
    heads = q_ref.shape[1] // HD
    deltas = []
    for h in range(heads):
        part, span = slice(h * HD, (h + 1) * HD), slice(h * rows, (h + 1) * rows)
        grad = gm_ref[:, part]
        qs_ref[span] = q_ref[:, part]
        gs_ref[span] = grad
        delta = grad.astype(F32) * mixed_ref[:, part].astype(F32)
        deltas.append(jnp.sum(delta.T, axis=0, keepdims=True))
    delta, inv = jnp.concatenate(deltas, axis=1), inv_ref[0, 0:1]
    queries, grads = qs_ref[...], gs_ref[...]
    for c in range(chunks):
        span = slice(c * rows, (c + 1) * rows)
        p = p_ref[0, span].astype(F32) * inv
        dp = mm_nt(kv_ref[span, HD:], grads)
        ds = (p * (dp - delta)).astype(BF)
        ds_ref[span] = ds
        dk_ref[span] += mm(ds, queries)
        dv_ref[span] += mm(p.astype(BF), grads)
    dq = mm(kt_ref[...], ds_ref[...]) * SCALE
    for h in range(heads):
        part, span = slice(h * HD, (h + 1) * HD), slice(h * rows, (h + 1) * rows)
        gq_ref[:, part] = rope_back(dq[:, span].T, cos_ref[...], sin_ref[...]).astype(BF)

    gq = gq_ref[...]
    grad_bq = mm(r1t_ref[rows_of(SLOT_Q)], gq).astype(BF)
    away = lax.rem(tensor_ref[0] + pl.num_programs(0) - step, pl.num_programs(0))

    @pl.when(away == 0)
    def _():
        q0_ref[...] = grad_bq

    for d, dkv_ref in ((1, dkvd_ref), (2, dkvc_ref), (3, dkvb_ref)):

        @pl.when(away == d)
        def _(dkv_ref=dkv_ref):
            dkv_ref[rows : rows + RANK] = grad_bq[:, : 2 * HD]
            dkv_ref[rows + RANK :, :HD] = grad_bq[:, 2 * HD :]
            dkv_ref[rows + RANK :, HD:] = jnp.zeros((RANK, HD), BF)

    gr_ref[...] += mm_nt(gq, bq_ref[0])
    g1_ref[...] += mm_nt(gq, flat(wq_ref))

    @pl.when(step == pl.num_programs(0) - 1)
    def _():
        wide = mm(turned(ranks_ref[0]), n2_ref[...]) + mm(turned(ranks_ref[1]), cot_ref[...])
        wide_ref[...] = wide + mm(turned(ranks_ref[2]), gb_ref[...])
        for c, dkv_ref in enumerate((dkva_ref, dkvb_ref, dkvc_ref, dkvd_ref, dkve_ref)):
            span = slice(c * rows, (c + 1) * rows)
            dkv_ref[:rows, :HD] = (dk_ref[span] * (1.0 / LOG2E)).astype(BF)
            dkv_ref[:rows, HD:] = dv_ref[span].astype(BF)


def shared_back_kernel(
    chips, core_ref, n1_ref, r1_ref, bkv_ref, cos_ref, sin_ref, own_ref, back1_ref, back2_ref, back3_ref, back4_ref,
    q0_ref, gr_ref, widef_ref,
    mine_ref, theirs_ref, gk_ref, gv_ref, grt_ref,
):
    rows = own_ref.shape[0]
    gkv = own_ref[...].astype(F32)
    for back_ref in (back1_ref, back2_ref, back3_ref, back4_ref):
        gkv = gkv + back_ref[:rows].astype(F32)
    queries = [q0_ref[:, j * LANES : (j + 1) * LANES].astype(F32) for j in range(3)]
    for back_ref in (back1_ref, back2_ref, back3_ref):
        queries[0] = queries[0] + back_ref[rows : rows + RANK, :HD].astype(F32)
        queries[1] = queries[1] + back_ref[rows : rows + RANK, HD:].astype(F32)
        queries[2] = queries[2] + back_ref[rows + RANK :, :HD].astype(F32)
    gk = rope_back(gkv[:, :HD], cos_ref[...], sin_ref[...]).astype(BF)
    gv = gkv[:, HD:].astype(BF)
    gk_ref[...] = gk
    gv_ref[...] = gv
    gr = gr_ref[...] + mm_nt(gk, bkv_ref[0]) + mm_nt(gv, bkv_ref[1])
    grt_ref[...] = gr.astype(BF)
    wide = (mm(gr.T.astype(BF), n1_ref[...]) + widef_ref[...]).T.astype(BF)
    share = mine_ref.shape[0] - 5 * RANK
    wide = wide.reshape(chips, 2, share // chips, LANES)
    first = core_ref[0] == 0
    mine_ref[:share] = jnp.where(first, wide[:, 0], wide[:, 1]).reshape(share, LANES)
    theirs_ref[:share] = jnp.where(first, wide[:, 1], wide[:, 0]).reshape(share, LANES)
    r1t = turned(r1_ref[...])
    for j, (slot, grad) in enumerate(((SLOT_K, gk), (SLOT_V, gv))):
        term = mm(r1t[rows_of(slot)], grad).astype(BF)
        part = slice(share + j * RANK, share + (j + 1) * RANK)
        mine_ref[part] = term
        theirs_ref[part] = term
    for j, term in enumerate(queries):
        part = slice(share + (2 + j) * RANK, share + (3 + j) * RANK)
        mine_ref[part] = term.astype(BF)
        theirs_ref[part] = term.astype(BF)


def payload_kernel(core_ref, mine_ref, other_ref, out_ref, q_ref):
    first = core_ref[0] == 0
    total = mine_ref[...].astype(F32) + other_ref[...].astype(F32)
    count = out_ref.shape[0]
    own_rows = (total.shape[0] - 5 * RANK) // count
    queries = total[total.shape[0] - 3 * RANK :].astype(BF)
    for n in range(q_ref.shape[0]):
        for j in range(3):
            q_ref[n, :, j * LANES : (j + 1) * LANES] = queries[j * RANK : (j + 1) * RANK]
    tensor_count = RANK // 4
    blank = jnp.zeros((RANK - own_rows - 2, LANES), F32)
    for n in range(count):
        pieces = [total[n * own_rows : (n + 1) * own_rows]]
        row = (2 * (n // tensor_count) * tensor_count + n % tensor_count) % RANK
        for j in range(2):
            at = count * own_rows + j * RANK + row
            low, high = total[at : at + 1], total[at + tensor_count : at + tensor_count + 1]
            pieces.append(jnp.where(first, low, high))
        out_ref[n] = jnp.concatenate(pieces + [blank], axis=0).astype(BF)


def input_kernel(
    x_ref, gain_ref, a_ref, wk_ref, wv_ref, gk_ref, gv_ref, gr_ref, g1_ref, gres_ref, grad_ref,
):
    g1 = g1_ref[...] + mm_nt(gk_ref[...], wk_ref[...]) + mm_nt(gv_ref[...], wv_ref[...])
    g1 = g1 + mm_nt(gr_ref[...], a_ref[...])
    x = x_ref[...].astype(F32)
    grad_ref[...] = gres_ref[...] + rms_back(x, gain_ref[...], g1)


def sum_hidden_kernel(
    ids_ref, terms_hbm, gu_hbm, down_hbm, out_hbm, terms_ref, acc_ref, gu_ref, down_ref, out_ref, sems, out_sems,
):
    adapters, rank, cols = acc_ref.shape
    ff = gu_ref.shape[2]
    groups = (slice(2 * ff, cols), slice(0, ff), slice(ff, 2 * ff))
    arrivals = []
    for j, group in enumerate(groups):
        part = pl.ds(group.start, group.stop - group.start)
        arrivals.append(pltpu.make_async_copy(terms_hbm.at[:, :, part], terms_ref.at[:, :, part], sems.at[j]))
        arrivals[j].start()
    acc_ref[...] = jnp.zeros_like(acc_ref)

    def added(group):
        for s in range(terms_ref.shape[0] // 2):
            pair = terms_ref[2 * s, :, group].astype(F32) + terms_ref[2 * s + 1, :, group].astype(F32)
            acc_ref[ids_ref[s], :, group] += pair

    sent = [
        pltpu.make_async_copy(down_ref, down_hbm, out_sems.at[0]),
        pltpu.make_async_copy(out_ref, out_hbm, out_sems.at[1]),
        pltpu.make_async_copy(gu_ref.at[0], gu_hbm.at[0], out_sems.at[2]),
        pltpu.make_async_copy(gu_ref.at[1], gu_hbm.at[1], out_sems.at[3]),
    ]
    arrivals[0].wait()
    added(groups[0])
    down_ref[...] = acc_ref[:, :, 2 * ff : 3 * ff].reshape(adapters * rank, ff).T
    sent[0].start()
    out_ref[...] = acc_ref[:, :, 3 * ff :].reshape(adapters * rank, cols - 3 * ff).T
    sent[1].start()
    for j in range(2):
        arrivals[1 + j].wait()
        added(groups[1 + j])
        gu_ref[j] = acc_ref[:, :, groups[1 + j]].reshape(adapters * rank, ff)
        sent[2 + j].start()
    for copy in sent:
        copy.wait()


def sum_wide_kernel(ids_ref, own_ref, terms_ref, *rest):
    q_refs, (wide_ref, kv_ref, q_ref, acc_ref, accq_ref) = rest[:-5], rest[-5:]
    acc_ref[...] = jnp.zeros_like(acc_ref)
    accq_ref[...] = jnp.zeros_like(accq_ref)
    y_count, x_count = len(q_refs), q_refs[0].shape[0]
    for away_y, terms in enumerate(q_refs):
        y = lax.rem(own_ref[1] + away_y, y_count)
        for away_x in range(x_count):
            x = lax.rem(own_ref[2] + away_x, x_count)
            accq_ref[ids_ref[y * x_count + x]] += terms[away_x].astype(F32)
    q_ref[...] = accq_ref[...].reshape(q_ref.shape)
    seqs, parts = terms_ref.shape[:2]
    for s in range(seqs):
        term = terms_ref[s, 0].astype(F32)
        for part in range(1, parts):
            term = term + terms_ref[s, part].astype(F32)
        acc_ref[ids_ref[s]] += term
    adapters, rank, _ = acc_ref.shape
    lane = lax.broadcasted_iota(jnp.int32, (rank, LANES), 1) // RANK
    own_rows, slots = wide_ref.shape[:2]
    for j in range(slots):
        total = jnp.zeros((rank, LANES), F32)
        for a in range(adapters):
            moved = pltpu.roll(acc_ref[a], ((a - j) * RANK) % LANES, 1)
            total = jnp.where(lane == a, moved, total)
        wide_ref[:, j] = total[:own_rows]
    mine = acc_ref[own_ref[0]]
    for j in range(2):
        kv_ref[j] = mine[own_rows + j : own_rows + j + 1]


def sds(shape, dtype):
    return jax.ShapeDtypeStruct(shape, dtype)


def scalars():
    return pl.BlockSpec(memory_space=pltpu.SMEM)


def whole(array):
    rank = len(array.shape)
    return pl.BlockSpec(array.shape, lambda *_: (0,) * rank)


def wholes(*arrays):
    return [whole(v) for v in arrays]


def by_step(*shape):
    return pl.BlockSpec((1,) + shape, lambda t: (t,) + (0,) * len(shape))


def call(kernel, name, steps, args, specs, outs, scratch, flops, nbytes):
    shapes = [shape for shape, _ in outs]
    return pl.pallas_call(
        kernel,
        name=name,
        grid=(steps,),
        in_specs=specs,
        out_specs=[whole(shape) if spec is None else spec for shape, spec in outs],
        out_shape=shapes,
        scratch_shapes=scratch,
        compiler_params=pltpu.CompilerParams(
            dimension_semantics=("arbitrary",), vmem_limit_bytes=VMEM_LIMIT
        ),
        cost_estimate=pl.CostEstimate(flops=flops, bytes_accessed=nbytes, transcendentals=0),
    )(*args)


def rope_tables(positions):
    half = HD // 2
    frequency = 10000.0 ** (-(jnp.arange(half).astype(F32) / half))
    angles = positions.astype(F32)[:, None] * frequency[None, :]
    cos, sin = jnp.cos(angles), jnp.sin(angles)
    return jnp.concatenate([cos, cos], axis=1), jnp.concatenate([-sin, sin], axis=1)


def on_device(
    tokens, cotangent, segments, adapter_ids, norm_gains, q_weight, kv_weight, out_weight,
    gate_up_weight, down_weight, wide_adapters, kv_adapter, q_adapter, out_adapter,
    gate_up_adapter, down_adapter,
):
    rows, width = tokens.shape
    tensor_count = lax.axis_size("tensor")
    dp_count = lax.axis_size("y") * lax.axis_size("x") * 2
    devices = dp_count * tensor_count
    group_rows = rows * tensor_count
    seq_length = 2 * group_rows
    shard_rows = q_weight.shape[0]
    q_cols, ff_cols = q_weight.shape[1], gate_up_weight.shape[2]
    heads_cols = tensor_count * q_cols
    seqs = adapter_ids.shape[0]
    adapters = wide_adapters.shape[2] // RANK
    dp = lax.axis_index(DP)
    tensor = lax.axis_index("tensor")
    my_core = lax.axis_index("core")
    adapter = lax.dynamic_index_in_dim(adapter_ids, dp // 2, keepdims=False)
    column = adapter * RANK
    f3 = 3 * ff_cols

    args = (gate_up_weight, down_weight.T, q_weight, out_weight.T)
    (pack,) = call(
        pack_kernel, "pack", 1, args, wholes(*args), [(sds((shard_rows, f3 + 2 * q_cols), BF), None)], [],
        0, 4 * shard_rows * (f3 + 2 * q_cols),
    )
    pack, wide_adapters = lax.optimization_barrier((pack, wide_adapters))
    weights = lax.all_gather(pack, ALL, axis=0, tiled=False)
    weights = weights.reshape(dp_count, tensor_count, shard_rows, f3 + 2 * q_cols)

    wide = wide_adapters.reshape(7, shard_rows, adapters, RANK)
    wide = jnp.take(wide, adapter_ids, axis=2).transpose(2, 1, 0, 3)
    wide = wide.reshape(seqs, shard_rows, 7 * RANK)
    wide = jnp.pad(wide, ((0, 0), (0, 0), (0, LANES - 7 * RANK)))
    shared = jnp.broadcast_to(kv_weight[:, None], (2, seqs, shard_rows, HD))
    wide = jnp.concatenate([wide, shared[0], shared[1]], axis=2)

    def from_other_core(value):
        return lax.ppermute(value, "core", [(0, 1), (1, 0)])

    a_own = lax.all_to_all(wide, ("y", "x"), 0, 0, tiled=True)
    a_other = from_other_core(a_own)
    a_all = jnp.where(my_core == 0, jnp.stack([a_own, a_other], 1), jnp.stack([a_other, a_own], 1))
    a_all = a_all.reshape(width, 3 * LANES)

    def take_rows(matrix):
        return lax.dynamic_slice_in_dim(matrix, column, RANK, matrix.ndim - 2)

    def take_cols(matrix):
        return lax.dynamic_slice_in_dim(matrix, column, RANK, matrix.ndim - 1)

    def in_slot(block, slot):
        pads = [(0, 0)] * block.ndim
        pads[-2] = (slot * RANK, LANES - (slot + 1) * RANK)
        return jnp.pad(block, pads)

    gu_rows = take_rows(gate_up_adapter)
    b_own = jnp.concatenate(
        [gu_rows[0], gu_rows[1], take_cols(down_adapter).T, take_rows(q_adapter), take_cols(out_adapter).T], axis=1
    )
    kv_rows = take_rows(kv_adapter)
    b_kv = jnp.stack([in_slot(kv_rows[0], SLOT_K), in_slot(kv_rows[1], SLOT_V)])

    start = dp * group_rows + tensor * rows
    span = WINDOW + rows
    cos_window, sin_window = rope_tables((start - WINDOW + jnp.arange(span)) % seq_length)
    cos, sin = cos_window[WINDOW:], sin_window[WINDOW:]
    padded = jnp.concatenate([jnp.full((WINDOW,), -1, jnp.int32), segments])
    kseg = lax.dynamic_slice_in_dim(padded, start, span, 0)
    qseg = kseg[WINDOW:].reshape(1, rows)
    kseg = kseg.reshape(span, 1)

    gain_one, gain_two = norm_gains[0:1], norm_gains[1:2]
    q_block = f3 // q_cols

    def weight_spec(block):
        return pl.BlockSpec((dp_count, 1, shard_rows, q_cols), lambda t: (0, t, 0, block))

    def adapter_spec(block):
        return pl.BlockSpec((1, LANES, q_cols), lambda t: (t, 0, block))

    def lane_block(block):
        return pl.BlockSpec((width, LANES), lambda *_: (0, block))

    head_specs = [weight_spec(q_block), adapter_spec(0), weight_spec(q_block + 1), adapter_spec(1)]
    q_spec, qb_spec, o_spec, ob_spec = head_specs
    a_spec, wk_spec, wv_spec = lane_block(0), lane_block(1), lane_block(2)
    token_cols = pl.BlockSpec((rows, q_cols), lambda t: (0, t))
    tok_bf, tok_f32, rank_bf = sds((rows, width), BF), sds((rows, width), F32), sds((rows, LANES), BF)

    args = (tokens, gain_one, a_all, a_all, a_all, b_kv, cos, sin)
    normed_one, rank_one, kv_own = call(
        shared_kernel, "keys_values", 1, args,
        wholes(*args[:2]) + [a_spec, wk_spec, wv_spec] + wholes(*args[5:]),
        [(tok_bf, None), (rank_bf, None), (sds((rows, 2 * HD), BF), None)],
        [], 2 * rows * width * 384, 6 * rows * width,
    )
    parts = seq_length // rows
    reach = WINDOW // rows

    def moved(value, steps):
        return lax.ppermute(value, SEQ, [(c, c + steps) for c in range(parts) if 0 <= c + steps < parts])

    kv_window = jnp.concatenate([moved(kv_own, d) for d in range(reach, 0, -1)] + [kv_own])

    b_own, kv_own = lax.optimization_barrier((b_own, kv_own))
    b_parts = [b_own] + [
        lax.ppermute(b_own, "tensor", [((z + d) % tensor_count, z) for z in range(tensor_count)])
        for d in range(1, tensor_count)
    ]
    b_all = jnp.roll(jnp.stack(b_parts), tensor, axis=0)
    b_heads = jnp.concatenate(
        [in_slot(b_all[:, :, f3 : f3 + q_cols], SLOT_Q), in_slot(b_all[:, :, f3 + q_cols :], SLOT_O)], axis=2
    )
    steps, slots = ff_cols // LANES, 2
    part_cols = ff_cols // steps
    b_hidden = b_all[:, :, :f3].reshape(tensor_count, RANK, 3, steps, part_cols).transpose(3, 2, 1, 0, 4)
    b_hidden = b_hidden.reshape(steps, 3, RANK, tensor_count * part_cols)
    b_hidden = jnp.concatenate(
        [in_slot(b_hidden[:, kind], slot) for kind, slot in enumerate((SLOT_G, SLOT_U, SLOT_D))], axis=2
    )

    heads = q_cols // HD
    last = tensor_count - 1

    def until_last(spec):
        return pl.BlockSpec(spec.block_shape, lambda t: spec.index_map(jnp.minimum(t, last)))

    p_spec, norm_spec = by_step(span, heads * rows), by_step(8, heads * rows)
    args = (
        kv_window, kseg, qseg, normed_one, rank_one, cos, sin, gain_two, a_all,
        weights, b_heads, weights, b_heads, tokens, cotangent, b_hidden, weights,
    )
    (
        queries, mixed, probs, norms, block_output, grad_residual, grad_branch, normed_two, ranks, grad_ro, early
    ) = call(
        forward_kernel, "forward", tensor_count + 1, args,
        wholes(*args[:8]) + [a_spec] + [until_last(spec) for spec in head_specs]
        + [pl.BlockSpec(memory_space=pl.ANY)] * 4,
        [
            (sds((rows, heads_cols), BF), until_last(token_cols)), (sds((rows, heads_cols), BF), until_last(token_cols)),
            (sds((tensor_count, span, heads * rows), BF), until_last(p_spec)),
            (sds((tensor_count, 8, heads * rows), F32), until_last(norm_spec)),
            (tok_bf, None), (tok_f32, None), (tok_bf, None), (tok_bf, None), (sds((3, rows, LANES), BF), None),
            (rank_bf, None), (sds((tensor_count, RANK, f3 + q_cols), BF), None),
        ],
        [
            pltpu.VMEM((span, rows), F32), pltpu.VMEM((span, heads * rows), F32), pltpu.VMEM((HD, span), BF),
            pltpu.VMEM((rows, width), F32), pltpu.VMEM((rows, width), F32), pltpu.VMEM((rows, LANES), F32),
            pltpu.VMEM((rows, LANES), F32), pltpu.VMEM((rows, LANES), F32), pltpu.VMEM((heads * rows, HD), BF),
            pltpu.VMEM((tensor_count, rows, q_cols), BF), pltpu.VMEM((rows, width), F32),
            pltpu.VMEM((rows, LANES), BF), pltpu.VMEM((LANES, rows), BF),
            pltpu.VMEM((rows, LANES), BF), pltpu.VMEM((LANES, rows), BF),
            pltpu.VMEM((slots, dp_count, shard_rows, 3 * tensor_count * part_cols), BF),
            pltpu.VMEM((rows, width), BF), pltpu.VMEM((rows, width), BF), pltpu.VMEM(b_hidden.shape, BF),
            pltpu.SemaphoreType.DMA((slots, 3 * tensor_count)), pltpu.SemaphoreType.DMA((3,)),
        ],
        4 * rows * heads_cols * (span + width) + 12 * rows * width * tensor_count * ff_cols,
        4 * width * heads_cols + 6 * width * tensor_count * ff_cols,
    )
    early = lax.psum_scatter(early, "tensor", scatter_dimension=0, tiled=True).reshape(RANK, -1)

    args = (
        tensor.astype(jnp.int32).reshape(1), kv_window, grad_branch, grad_ro, rank_one, cos, sin,
        ranks, normed_two, cotangent, queries, mixed, probs, norms, weights, b_heads, weights, b_heads,
    )
    *dkv, q_own, grad_one, grad_rank, wide_ffn = call(
        attn_back_kernel, "attention_back", tensor_count, args,
        [scalars()] + wholes(*args[1:10]) + [token_cols, token_cols, p_spec, norm_spec, o_spec, ob_spec, q_spec, qb_spec],
        [
            *[(sds((rows + (2 * RANK if 0 < w < reach else 0), 2 * HD), BF), None) for w in range(reach + 1)],
            (sds((RANK, q_cols), BF), None), (tok_f32, None), (sds((rows, LANES), F32), None),
            (sds((LANES, width), F32), None),
        ],
        [
            pltpu.VMEM((span, heads * rows), BF),
            pltpu.VMEM((span, HD), F32), pltpu.VMEM((span, HD), F32), pltpu.VMEM((HD, span), BF),
            pltpu.VMEM((LANES, rows), BF), pltpu.VMEM((rows, q_cols), BF), pltpu.VMEM((rows, q_cols), BF),
            pltpu.VMEM((heads * rows, HD), BF), pltpu.VMEM((heads * rows, HD), BF),
        ],
        2 * rows * heads_cols * (4 * span + 2 * width), 4 * width * heads_cols,
    )

    early, grad_one = lax.optimization_barrier((early, grad_one))
    early = lax.all_gather(early, DP, axis=0, tiled=False)

    def around(value, steps):
        return lax.ppermute(value, SEQ, [(c, (c - steps) % parts) for c in range(parts)])

    backs = [around(dkv[reach - d], d) for d in range(1, reach)] + [moved(dkv[0], -reach)]
    core = my_core.astype(jnp.int32).reshape(1)
    chips = dp_count // 2
    share = width // 2 + 5 * RANK
    args = (
        core, normed_one, rank_one, b_kv, cos, sin, dkv[reach], *backs, q_own, grad_rank, wide_ffn,
    )
    mine, theirs, grad_key, grad_value, grad_rank = call(
        functools.partial(shared_back_kernel, chips), "shared_back", 1, args,
        [scalars()] + wholes(*args[1:]),
        [
            (sds((share, LANES), BF), None), (sds((share, LANES), BF), None),
            (sds((rows, HD), BF), None), (sds((rows, HD), BF), None), (rank_bf, None),
        ],
        [], 4 * rows * width * LANES, 6 * rows * width,
    )
    own_rows = width // devices
    planes = chips * tensor_count
    args = (core, mine, from_other_core(theirs))
    payload, q_terms = call(
        payload_kernel, "payload", 1, args, [scalars()] + wholes(*args[1:]),
        [(sds((planes, RANK, LANES), BF), None), (sds((1, RANK, q_cols), BF), None)], [],
        0, 2 * planes * RANK * LANES,
    )
    payload, grad_key = lax.optimization_barrier((payload, grad_key))
    terms = lax.all_to_all(payload, PLANES, 0, 0, tiled=True)

    def with_others(value, axis):
        count = lax.axis_size(axis)
        return [value] + [
            lax.ppermute(value, axis, [((i + d) % count, i) for i in range(count)]) for d in range(1, count)
        ]

    q_terms = with_others(jnp.concatenate(with_others(q_terms, "x")), "y")
    terms = terms.reshape(seqs, tensor_count, RANK, LANES)

    args = (
        tokens, gain_one, a_all, a_all, a_all, grad_key, grad_value, grad_rank, grad_one, grad_residual,
    )
    (input_grad,) = call(
        input_kernel, "input_gradient", 1, args,
        wholes(*args[:2]) + [a_spec, wk_spec, wv_spec] + wholes(*args[5:]),
        [(tok_f32, None)], [], 2 * rows * width * 384, 16 * rows * width,
    )

    terms, input_grad = lax.optimization_barrier((terms, input_grad))
    own = jnp.stack([(dp * tensor_count + tensor) // RANK, lax.axis_index("y"), lax.axis_index("x")]).astype(jnp.int32)
    wide_grad, kv_adapter_grad, q_adapter_grad = call(
        sum_wide_kernel, "sum_wide", 1, (adapter_ids, own, terms, *q_terms),
        [scalars(), scalars()] + wholes(terms, *q_terms),
        [(sds((own_rows, 7, LANES), F32), None), (sds((2, 1, HD), F32), None), (sds((LANES, q_cols), F32), None)],
        [pltpu.VMEM((adapters, RANK, LANES), F32), pltpu.VMEM((adapters, RANK, q_cols), F32)], 0, 4 * LANES * f3,
    )
    shapes = [(2, LANES, ff_cols), (ff_cols, LANES), (q_cols, LANES)]
    gate_up_adapter_grad, down_adapter_grad, out_adapter_grad = call(
        sum_hidden_kernel, "sum_hidden", 1, (adapter_ids, early),
        [scalars(), pl.BlockSpec(memory_space=pl.ANY)],
        [(sds(shape, F32), pl.BlockSpec(memory_space=pl.ANY)) for shape in shapes],
        [pltpu.VMEM(early.shape, BF), pltpu.VMEM((adapters, RANK, f3 + q_cols), F32)]
        + [pltpu.VMEM(shape, F32) for shape in shapes]
        + [pltpu.SemaphoreType.DMA((3,)), pltpu.SemaphoreType.DMA((4,))],
        0, 4 * LANES * f3,
    )
    return (
        block_output, input_grad, wide_grad.transpose(1, 0, 2), kv_adapter_grad,
        q_adapter_grad, out_adapter_grad, gate_up_adapter_grad, down_adapter_grad,
    )


def solution(mesh):
    dp_count, tensor_count = mesh.shape["dp"], mesh.shape["tensor"]
    chips = dp_count // 2
    x_count = math.isqrt(chips)
    devices = mesh.devices.reshape(chips // x_count, x_count, 2, tensor_count)
    return jax.shard_map(
        on_device,
        mesh=Mesh(devices, ALL),
        in_specs=(
            P(ALL, None), P(ALL, None), P(), P(), P(), P(DP, "tensor"), P(None, DP, None),
            P("tensor", DP), P(None, DP, "tensor"), P("tensor", DP), P(None, DP, None), P(),
            P(None, "tensor"), P("tensor", None), P(None, None, "tensor"), P("tensor", None),
        ),
        out_specs=(
            P(ALL, None), P(ALL, None), P(None, ALL, None), P(None, ALL, None),
            P(None, "tensor"), P("tensor", None), P(None, None, "tensor"), P("tensor", None),
        ),
        check_vma=False,
    )
```

```python
import functools
import math

import jax
import jax.numpy as jnp
from jax import lax
from jax.experimental import pallas as pl
from jax.experimental.pallas import tpu as pltpu
from jax.sharding import Mesh, PartitionSpec as P

HD = 128
WINDOW = 1024
RANK = 16
LANES = 128
EPS = 1e-06
MASKED = -1e30
SCALE = HD ** (-0.5)
LOG2E = math.log2(math.e)
GELU_C = 0.7978845608028654
GELU_A = 0.044715
VMEM_LIMIT = 58 * 1024 * 1024
BF = jnp.bfloat16
F32 = jnp.float32
DP = ("y", "x", "core")
SEQ = ("core", "tensor")
PLANES = ("y", "x", "tensor")
ALL = ("y", "x", "core", "tensor")

SLOT_Q, SLOT_K, SLOT_V, SLOT_G, SLOT_U, SLOT_O, SLOT_D = range(7)


def rows_of(slot):
    return slice(slot * RANK, (slot + 1) * RANK)


def mm(a, b):
    return lax.dot_general(a, b, (((1,), (0,)), ((), ())), preferred_element_type=F32)


def mm_nt(a, b):
    return lax.dot_general(a, b, (((1,), (1,)), ((), ())), preferred_element_type=F32)


def turned(a):
    return a.astype(F32).T.astype(BF)


def rope(v, cos, sin):
    return v * cos + pltpu.roll(v, HD // 2, 1) * sin


def rope_back(g, cos, sin):
    return g * cos - pltpu.roll(g, HD // 2, 1) * sin


def flat(ref):
    block = ref[...]
    return block.reshape(block.shape[0] * block.shape[2], block.shape[3])


def rms(v, gain):
    return v * lax.rsqrt(jnp.mean(v * v, axis=-1, keepdims=True) + EPS) * gain


def rms_back(v, gain, grad):
    inv = lax.rsqrt(jnp.mean(v * v, axis=-1, keepdims=True) + EPS)
    scaled = grad * gain
    dot = jnp.mean(v * scaled, axis=-1, keepdims=True)
    return inv * scaled - v * (inv * inv * inv * dot)


def pack_kernel(gu_ref, down_ref, q_ref, o_ref, out_ref):
    ff, cols = gu_ref.shape[2], q_ref.shape[1]
    out_ref[:, :ff] = gu_ref[0]
    out_ref[:, ff : 2 * ff] = gu_ref[1]
    out_ref[:, 2 * ff : 3 * ff] = down_ref[...]
    out_ref[:, 3 * ff : 3 * ff + cols] = q_ref[...]
    out_ref[:, 3 * ff + cols :] = o_ref[...]


def shared_kernel(x_ref, gain_ref, a_ref, wk_ref, wv_ref, bkv_ref, cos_ref, sin_ref, n1_ref, r1_ref, kv_ref):
    n1 = rms(x_ref[...].astype(F32), gain_ref[...]).astype(BF)
    n1_ref[...] = n1
    r1 = mm(n1, a_ref[...]).astype(BF)
    r1_ref[...] = r1
    key = mm(n1, wk_ref[...]) + mm(r1, bkv_ref[0])
    kv_ref[:, :HD] = rope(key, cos_ref[...], sin_ref[...]).astype(BF)
    kv_ref[:, HD:] = (mm(n1, wv_ref[...]) + mm(r1, bkv_ref[1])).astype(BF)


def forward_kernel(
    kv_ref, kseg_ref, qseg_ref, n1_ref, r1_ref, cos_ref, sin_ref, gain_ref, a_ref,
    wq_ref, bq_ref, wo_ref, bo_ref, x_hbm, cot_hbm, b_hbm, w_ref,
    q_ref, mixed_ref, p_ref, inv_ref, out_ref, gres_ref, gb_ref, n2_ref, ranks_ref, gro_ref, early_ref,
    bias_ref, s_ref, vt_ref, ffn_ref, g2_ref, ro_ref, rd_ref, gr_ref, qs_ref,
    all_mixed_ref, res_ref, r2_ref, r2t_ref, grd_ref, grdt_ref, wv_ref, x_ref, cot_ref, b_ref, sems, late_sems,
):
    step = pl.program_id(0)
    slots, tensor_count = wv_ref.shape[0], w_ref.shape[1]
    steps = b_ref.shape[0]
    rows = q_ref.shape[0]
    chunks = kv_ref.shape[0] // rows
    ff = b_ref.shape[2] // 3
    part_cols = ff // tensor_count

    def copies(at, to):
        moves = []
        for kind in (2, 0, 1):
            for t in range(tensor_count):
                source = pl.multiple_of((kind * steps + at) * part_cols, LANES)
                target = (kind * tensor_count + t) * part_cols
                moves.append(
                    pltpu.make_async_copy(
                        w_ref.at[:, t, :, pl.ds(source, part_cols)],
                        wv_ref.at[to, :, :, pl.ds(target, part_cols)],
                        sems.at[to, len(moves)],
                    )
                )
        return moves

    late = [
        pltpu.make_async_copy(source, target, late_sems.at[j])
        for j, (source, target) in enumerate(((x_hbm, x_ref), (cot_hbm, cot_ref), (b_hbm, b_ref)))
    ]

    @pl.when(step == 0)
    def _():
        for copy in late:
            copy.start()
        key = lax.broadcasted_iota(jnp.int32, bias_ref.shape, 0)
        query = lax.broadcasted_iota(jnp.int32, bias_ref.shape, 1)
        allowed = (key >= query) & (key <= query + WINDOW) & (kseg_ref[...] == qseg_ref[...])
        bias_ref[...] = jnp.where(allowed, 0.0, MASKED)
        vt_ref[...] = turned(kv_ref[:, HD:])
        ffn_ref[...] = jnp.zeros_like(ffn_ref)
        ro_ref[...] = jnp.zeros_like(ro_ref)

    @pl.when((step >= 1) & (step < 1 + slots))
    def _():
        for copy in copies(step - 1, step - 1):
            copy.start()

    @pl.when(step < tensor_count)
    def _():
        lin = mm(n1_ref[...], flat(wq_ref)) + mm(r1_ref[...], bq_ref[0])
        heads = q_ref.shape[1] // HD
        for h in range(heads):
            part = slice(h * HD, (h + 1) * HD)
            query = (rope(lin[:, part], cos_ref[...], sin_ref[...]) * (SCALE * LOG2E)).astype(BF)
            q_ref[:, part] = query
            qs_ref[h * rows : (h + 1) * rows] = query
        queries = qs_ref[...]
        top = jnp.full((1, heads * rows), MASKED, F32)
        for c in range(chunks):
            span = slice(c * rows, (c + 1) * rows)
            s = mm_nt(kv_ref[span, :HD], queries)
            bias = bias_ref[span]
            s = jnp.concatenate([s[:, h * rows : (h + 1) * rows] + bias for h in range(heads)], axis=1)
            s_ref[span] = s
            top = jnp.maximum(top, jnp.max(s, axis=0, keepdims=True))
        total = jnp.zeros((1, heads * rows), F32)
        for c in range(chunks):
            span = slice(c * rows, (c + 1) * rows)
            p = jnp.exp2(s_ref[span] - top)
            total = total + jnp.sum(p, axis=0, keepdims=True)
            p_ref[0, span] = p.astype(BF)
        inv = 1.0 / total
        inv_ref[0, 0:1] = inv
        out = mm(vt_ref[...], p_ref[0]) * inv
        for h in range(heads):
            mixed_ref[:, h * HD : (h + 1) * HD] = out[:, h * rows : (h + 1) * rows].T.astype(BF)
        mixed = mixed_ref[...]
        all_mixed_ref[step] = mixed
        ffn_ref[...] += mm_nt(mixed, flat(wo_ref))
        ro_ref[...] += mm_nt(mixed, bo_ref[0])

    @pl.when(step == tensor_count - 1)
    def _():
        for copy in late:
            copy.wait()
        res = x_ref[...].astype(F32) + (ffn_ref[...] + mm_nt(ro_ref[...].astype(BF), a_ref[...]))
        res_ref[...] = res
        n2 = rms(res, gain_ref[...]).astype(BF)
        n2_ref[...] = n2
        r2 = mm(n2, a_ref[...]).astype(BF)
        r2_ref[...] = r2
        r2t_ref[...] = turned(r2)
        grd = mm(cot_ref[...], a_ref[...]).astype(BF)
        grd_ref[...] = grd
        grdt_ref[...] = turned(grd)
        ffn_ref[...] = jnp.zeros_like(ffn_ref)
        g2_ref[...] = jnp.zeros_like(g2_ref)
        rd_ref[...] = jnp.zeros_like(rd_ref)
        gr_ref[...] = jnp.zeros_like(gr_ref)

    def feed_forward(at, carry):
        slot = lax.rem(at, slots)

        @pl.when((at >= 1) & (at + slots - 1 < steps))
        def _():
            for copy in copies(at + slots - 1, lax.rem(at + slots - 1, slots)):
                copy.start()

        n2, r2, cot = n2_ref[...], r2_ref[...], cot_ref[...]
        b_gu, b_d = b_ref[at, :, : 2 * ff], b_ref[at, :, 2 * ff :]
        arrivals = copies(at, slot)
        weight_rows = wv_ref.shape[1] * wv_ref.shape[2]
        for copy in arrivals[:tensor_count]:
            copy.wait()
        w_d = wv_ref[slot, :, :, 2 * ff :].reshape(weight_rows, ff)
        grad_hidden = (mm(cot, w_d) + mm(grd_ref[...], b_d)).astype(BF).astype(F32)
        for copy in arrivals[tensor_count:]:
            copy.wait()
        w_gu = wv_ref[slot, :, :, : 2 * ff].reshape(weight_rows, 2 * ff)
        lin = mm(n2, w_gu) + mm(r2, b_gu)
        gate, up = lin[:, :ff], lin[:, ff:]
        square = gate * gate
        th = jnp.tanh(GELU_C * (gate + GELU_A * square * gate))
        half = 0.5 * (1.0 + th)
        act = gate * half
        slope = half + 0.5 * gate * (1.0 - th * th) * (GELU_C * (1.0 + 3.0 * GELU_A * square))
        hidden = (act * up).astype(BF)
        grad_gate = (grad_hidden * up * slope).astype(BF)
        grad_up = (grad_hidden * act).astype(BF)
        grads = jnp.concatenate([grad_gate, grad_up], axis=1)
        ffn_ref[...] += mm_nt(hidden, w_d)
        rd_ref[...] += mm_nt(hidden, b_d)
        g2_ref[...] += mm_nt(grads, w_gu)
        gr_ref[...] += mm_nt(grads, b_gu)
        terms = (
            mm(r2t_ref[rows_of(SLOT_G)], grad_gate), mm(r2t_ref[rows_of(SLOT_U)], grad_up),
            mm(grdt_ref[rows_of(SLOT_D)], hidden),
        )
        for kind, term in enumerate(terms):
            target = pl.multiple_of((kind * steps + at) * part_cols, LANES)
            for t in range(tensor_count):
                early_ref[t, :, pl.ds(target, part_cols)] = term[:, t * part_cols : (t + 1) * part_cols].astype(BF)
        return carry

    @pl.when(step == tensor_count)
    def _():
        lax.fori_loop(0, steps, feed_forward, 0)
        res, cot = res_ref[...], cot_ref[...]
        out_ref[...] = (res + (ffn_ref[...] + mm_nt(rd_ref[...].astype(BF), a_ref[...]))).astype(BF)
        grad_two = g2_ref[...] + mm_nt(gr_ref[...].astype(BF), a_ref[...])
        grad_res = cot.astype(F32) + rms_back(res, gain_ref[...], grad_two)
        gres_ref[...] = grad_res
        grad_branch = grad_res.astype(BF)
        gb_ref[...] = grad_branch
        gro = mm(grad_branch, a_ref[...])
        gro_ref[...] = gro.astype(BF)
        grot = gro.T[rows_of(SLOT_O)].astype(BF)
        first = 3 * steps * part_cols
        for t in range(tensor_count):
            early_ref[t, :, first:] = mm(grot, all_mixed_ref[t]).astype(BF)
        for j, rank in enumerate((gr_ref, rd_ref, ro_ref)):
            ranks_ref[j] = rank[...].astype(BF)


def attn_back_kernel(
    tensor_ref, kv_ref, gb_ref, gro_ref, r1_ref, cos_ref, sin_ref, ranks_ref, n2_ref, cot_ref,
    q_ref, mixed_ref, p_ref, inv_ref, wo_ref, bo_ref, wq_ref, bq_ref,
    dkva_ref, dkvb_ref, dkvc_ref, dkvd_ref, dkve_ref, q0_ref, g1_ref, gr_ref, wide_ref,
    ds_ref, dk_ref, dv_ref, kt_ref, r1t_ref, gq_ref, gm_ref, qs_ref, gs_ref,
):
    step = pl.program_id(0)
    rows = q_ref.shape[0]
    chunks = kv_ref.shape[0] // rows

    @pl.when(step == 0)
    def _():
        kt_ref[...] = turned(kv_ref[:, :HD])
        r1t_ref[...] = turned(r1_ref[...])
        dk_ref[...] = jnp.zeros_like(dk_ref)
        dv_ref[...] = jnp.zeros_like(dv_ref)
        g1_ref[...] = jnp.zeros_like(g1_ref)
        gr_ref[...] = jnp.zeros_like(gr_ref)

    gm_ref[...] = (mm(gb_ref[...], flat(wo_ref)) + mm(gro_ref[...], bo_ref[0])).astype(BF)
    heads = q_ref.shape[1] // HD
    deltas = []
    for h in range(heads):
        part, span = slice(h * HD, (h + 1) * HD), slice(h * rows, (h + 1) * rows)
        grad = gm_ref[:, part]
        qs_ref[span] = q_ref[:, part]
        gs_ref[span] = grad
        delta = grad.astype(F32) * mixed_ref[:, part].astype(F32)
        deltas.append(jnp.sum(delta.T, axis=0, keepdims=True))
    delta, inv = jnp.concatenate(deltas, axis=1), inv_ref[0, 0:1]
    queries, grads = qs_ref[...], gs_ref[...]
    for c in range(chunks):
        span = slice(c * rows, (c + 1) * rows)
        p = p_ref[0, span].astype(F32) * inv
        dp = mm_nt(kv_ref[span, HD:], grads)
        ds = (p * (dp - delta)).astype(BF)
        ds_ref[span] = ds
        dk_ref[span] += mm(ds, queries)
        dv_ref[span] += mm(p.astype(BF), grads)
    dq = mm(kt_ref[...], ds_ref[...]) * SCALE
    for h in range(heads):
        part, span = slice(h * HD, (h + 1) * HD), slice(h * rows, (h + 1) * rows)
        gq_ref[:, part] = rope_back(dq[:, span].T, cos_ref[...], sin_ref[...]).astype(BF)

    gq = gq_ref[...]
    grad_bq = mm(r1t_ref[rows_of(SLOT_Q)], gq).astype(BF)
    away = lax.rem(tensor_ref[0] + pl.num_programs(0) - step, pl.num_programs(0))

    @pl.when(away == 0)
    def _():
        q0_ref[...] = grad_bq

    for d, dkv_ref in ((1, dkvd_ref), (2, dkvc_ref), (3, dkvb_ref)):

        @pl.when(away == d)
        def _(dkv_ref=dkv_ref):
            dkv_ref[rows : rows + RANK] = grad_bq[:, : 2 * HD]
            dkv_ref[rows + RANK :, :HD] = grad_bq[:, 2 * HD :]
            dkv_ref[rows + RANK :, HD:] = jnp.zeros((RANK, HD), BF)

    gr_ref[...] += mm_nt(gq, bq_ref[0])
    g1_ref[...] += mm_nt(gq, flat(wq_ref))

    @pl.when(step == pl.num_programs(0) - 1)
    def _():
        wide = mm(turned(ranks_ref[0]), n2_ref[...]) + mm(turned(ranks_ref[1]), cot_ref[...])
        wide_ref[...] = wide + mm(turned(ranks_ref[2]), gb_ref[...])
        for c, dkv_ref in enumerate((dkva_ref, dkvb_ref, dkvc_ref, dkvd_ref, dkve_ref)):
            span = slice(c * rows, (c + 1) * rows)
            dkv_ref[:rows, :HD] = (dk_ref[span] * (1.0 / LOG2E)).astype(BF)
            dkv_ref[:rows, HD:] = dv_ref[span].astype(BF)


def shared_back_kernel(
    chips, core_ref, n1_ref, r1_ref, bkv_ref, cos_ref, sin_ref, own_ref, back1_ref, back2_ref, back3_ref, back4_ref,
    q0_ref, gr_ref, widef_ref,
    mine_ref, theirs_ref, gk_ref, gv_ref, grt_ref,
):
    rows = own_ref.shape[0]
    gkv = own_ref[...].astype(F32)
    for back_ref in (back1_ref, back2_ref, back3_ref, back4_ref):
        gkv = gkv + back_ref[:rows].astype(F32)
    queries = [q0_ref[:, j * LANES : (j + 1) * LANES].astype(F32) for j in range(3)]
    for back_ref in (back1_ref, back2_ref, back3_ref):
        queries[0] = queries[0] + back_ref[rows : rows + RANK, :HD].astype(F32)
        queries[1] = queries[1] + back_ref[rows : rows + RANK, HD:].astype(F32)
        queries[2] = queries[2] + back_ref[rows + RANK :, :HD].astype(F32)
    gk = rope_back(gkv[:, :HD], cos_ref[...], sin_ref[...]).astype(BF)
    gv = gkv[:, HD:].astype(BF)
    gk_ref[...] = gk
    gv_ref[...] = gv
    gr = gr_ref[...] + mm_nt(gk, bkv_ref[0]) + mm_nt(gv, bkv_ref[1])
    grt_ref[...] = gr.astype(BF)
    wide = (mm(gr.T.astype(BF), n1_ref[...]) + widef_ref[...]).T.astype(BF)
    share = mine_ref.shape[0] - 5 * RANK
    wide = wide.reshape(chips, 2, share // chips, LANES)
    first = core_ref[0] == 0
    mine_ref[:share] = jnp.where(first, wide[:, 0], wide[:, 1]).reshape(share, LANES)
    theirs_ref[:share] = jnp.where(first, wide[:, 1], wide[:, 0]).reshape(share, LANES)
    r1t = turned(r1_ref[...])
    for j, (slot, grad) in enumerate(((SLOT_K, gk), (SLOT_V, gv))):
        term = mm(r1t[rows_of(slot)], grad).astype(BF)
        part = slice(share + j * RANK, share + (j + 1) * RANK)
        mine_ref[part] = term
        theirs_ref[part] = term
    for j, term in enumerate(queries):
        part = slice(share + (2 + j) * RANK, share + (3 + j) * RANK)
        mine_ref[part] = term.astype(BF)
        theirs_ref[part] = term.astype(BF)


def payload_kernel(core_ref, mine_ref, other_ref, out_ref, q_ref):
    first = core_ref[0] == 0
    total = mine_ref[...].astype(F32) + other_ref[...].astype(F32)
    count = out_ref.shape[0]
    own_rows = (total.shape[0] - 5 * RANK) // count
    queries = total[total.shape[0] - 3 * RANK :].astype(BF)
    for n in range(q_ref.shape[0]):
        for j in range(3):
            q_ref[n, :, j * LANES : (j + 1) * LANES] = queries[j * RANK : (j + 1) * RANK]
    tensor_count = RANK // 4
    blank = jnp.zeros((RANK - own_rows - 2, LANES), F32)
    for n in range(count):
        pieces = [total[n * own_rows : (n + 1) * own_rows]]
        row = (2 * (n // tensor_count) * tensor_count + n % tensor_count) % RANK
        for j in range(2):
            at = count * own_rows + j * RANK + row
            low, high = total[at : at + 1], total[at + tensor_count : at + tensor_count + 1]
            pieces.append(jnp.where(first, low, high))
        out_ref[n] = jnp.concatenate(pieces + [blank], axis=0).astype(BF)


def input_kernel(
    x_ref, gain_ref, a_ref, wk_ref, wv_ref, gk_ref, gv_ref, gr_ref, g1_ref, gres_ref, grad_ref,
):
    g1 = g1_ref[...] + mm_nt(gk_ref[...], wk_ref[...]) + mm_nt(gv_ref[...], wv_ref[...])
    g1 = g1 + mm_nt(gr_ref[...], a_ref[...])
    x = x_ref[...].astype(F32)
    grad_ref[...] = gres_ref[...] + rms_back(x, gain_ref[...], g1)


def sum_hidden_kernel(
    ids_ref, terms_hbm, gu_hbm, down_hbm, out_hbm, terms_ref, acc_ref, gu_ref, down_ref, out_ref, sems, out_sems,
):
    adapters, rank, cols = acc_ref.shape
    ff = gu_ref.shape[2]
    groups = (slice(2 * ff, cols), slice(0, ff), slice(ff, 2 * ff))
    arrivals = []
    for j, group in enumerate(groups):
        part = pl.ds(group.start, group.stop - group.start)
        arrivals.append(pltpu.make_async_copy(terms_hbm.at[:, :, part], terms_ref.at[:, :, part], sems.at[j]))
        arrivals[j].start()
    acc_ref[...] = jnp.zeros_like(acc_ref)

    def added(group):
        for s in range(terms_ref.shape[0] // 2):
            pair = terms_ref[2 * s, :, group].astype(F32) + terms_ref[2 * s + 1, :, group].astype(F32)
            acc_ref[ids_ref[s], :, group] += pair

    sent = [
        pltpu.make_async_copy(down_ref, down_hbm, out_sems.at[0]),
        pltpu.make_async_copy(out_ref, out_hbm, out_sems.at[1]),
        pltpu.make_async_copy(gu_ref.at[0], gu_hbm.at[0], out_sems.at[2]),
        pltpu.make_async_copy(gu_ref.at[1], gu_hbm.at[1], out_sems.at[3]),
    ]
    arrivals[0].wait()
    added(groups[0])
    down_ref[...] = acc_ref[:, :, 2 * ff : 3 * ff].reshape(adapters * rank, ff).T
    sent[0].start()
    out_ref[...] = acc_ref[:, :, 3 * ff :].reshape(adapters * rank, cols - 3 * ff).T
    sent[1].start()
    for j in range(2):
        arrivals[1 + j].wait()
        added(groups[1 + j])
        gu_ref[j] = acc_ref[:, :, groups[1 + j]].reshape(adapters * rank, ff)
        sent[2 + j].start()
    for copy in sent:
        copy.wait()


def sum_wide_kernel(ids_ref, own_ref, terms_ref, *rest):
    q_refs, (wide_ref, kv_ref, q_ref, acc_ref, accq_ref) = rest[:-5], rest[-5:]
    acc_ref[...] = jnp.zeros_like(acc_ref)
    accq_ref[...] = jnp.zeros_like(accq_ref)
    y_count, x_count = len(q_refs), q_refs[0].shape[0]
    for away_y, terms in enumerate(q_refs):
        y = lax.rem(own_ref[1] + away_y, y_count)
        for away_x in range(x_count):
            x = lax.rem(own_ref[2] + away_x, x_count)
            accq_ref[ids_ref[y * x_count + x]] += terms[away_x].astype(F32)
    q_ref[...] = accq_ref[...].reshape(q_ref.shape)
    seqs, parts = terms_ref.shape[:2]
    for s in range(seqs):
        term = terms_ref[s, 0].astype(F32)
        for part in range(1, parts):
            term = term + terms_ref[s, part].astype(F32)
        acc_ref[ids_ref[s]] += term
    adapters, rank, _ = acc_ref.shape
    lane = lax.broadcasted_iota(jnp.int32, (rank, LANES), 1) // RANK
    own_rows, slots = wide_ref.shape[:2]
    for j in range(slots):
        total = jnp.zeros((rank, LANES), F32)
        for a in range(adapters):
            moved = pltpu.roll(acc_ref[a], ((a - j) * RANK) % LANES, 1)
            total = jnp.where(lane == a, moved, total)
        wide_ref[:, j] = total[:own_rows]
    mine = acc_ref[own_ref[0]]
    for j in range(2):
        kv_ref[j] = mine[own_rows + j : own_rows + j + 1]


def sds(shape, dtype):
    return jax.ShapeDtypeStruct(shape, dtype)


def scalars():
    return pl.BlockSpec(memory_space=pltpu.SMEM)


def whole(array):
    rank = len(array.shape)
    return pl.BlockSpec(array.shape, lambda *_: (0,) * rank)


def wholes(*arrays):
    return [whole(v) for v in arrays]


def by_step(*shape):
    return pl.BlockSpec((1,) + shape, lambda t: (t,) + (0,) * len(shape))


def call(kernel, name, steps, args, specs, outs, scratch, flops, nbytes):
    shapes = [shape for shape, _ in outs]
    return pl.pallas_call(
        kernel,
        name=name,
        grid=(steps,),
        in_specs=specs,
        out_specs=[whole(shape) if spec is None else spec for shape, spec in outs],
        out_shape=shapes,
        scratch_shapes=scratch,
        compiler_params=pltpu.CompilerParams(
            dimension_semantics=("arbitrary",), vmem_limit_bytes=VMEM_LIMIT
        ),
        cost_estimate=pl.CostEstimate(flops=flops, bytes_accessed=nbytes, transcendentals=0),
    )(*args)


def rope_tables(positions):
    half = HD // 2
    frequency = 10000.0 ** (-(jnp.arange(half).astype(F32) / half))
    angles = positions.astype(F32)[:, None] * frequency[None, :]
    cos, sin = jnp.cos(angles), jnp.sin(angles)
    return jnp.concatenate([cos, cos], axis=1), jnp.concatenate([-sin, sin], axis=1)


def on_device(
    tokens, cotangent, segments, adapter_ids, norm_gains, q_weight, kv_weight, out_weight,
    gate_up_weight, down_weight, wide_adapters, kv_adapter, q_adapter, out_adapter,
    gate_up_adapter, down_adapter,
):
    rows, width = tokens.shape
    tensor_count = lax.axis_size("tensor")
    dp_count = lax.axis_size("y") * lax.axis_size("x") * 2
    devices = dp_count * tensor_count
    group_rows = rows * tensor_count
    seq_length = 2 * group_rows
    shard_rows = q_weight.shape[0]
    q_cols, ff_cols = q_weight.shape[1], gate_up_weight.shape[2]
    heads_cols = tensor_count * q_cols
    seqs = adapter_ids.shape[0]
    adapters = wide_adapters.shape[2] // RANK
    dp = lax.axis_index(DP)
    tensor = lax.axis_index("tensor")
    my_core = lax.axis_index("core")
    adapter = lax.dynamic_index_in_dim(adapter_ids, dp // 2, keepdims=False)
    column = adapter * RANK
    f3 = 3 * ff_cols

    args = (gate_up_weight, down_weight.T, q_weight, out_weight.T)
    (pack,) = call(
        pack_kernel, "pack", 1, args, wholes(*args), [(sds((shard_rows, f3 + 2 * q_cols), BF), None)], [],
        0, 4 * shard_rows * (f3 + 2 * q_cols),
    )
    pack, wide_adapters = lax.optimization_barrier((pack, wide_adapters))
    weights = lax.all_gather(pack, ALL, axis=0, tiled=False)
    weights = weights.reshape(dp_count, tensor_count, shard_rows, f3 + 2 * q_cols)

    wide = wide_adapters.reshape(7, shard_rows, adapters, RANK)
    wide = jnp.take(wide, adapter_ids, axis=2).transpose(2, 1, 0, 3)
    wide = wide.reshape(seqs, shard_rows, 7 * RANK)
    wide = jnp.pad(wide, ((0, 0), (0, 0), (0, LANES - 7 * RANK)))
    shared = jnp.broadcast_to(kv_weight[:, None], (2, seqs, shard_rows, HD))
    wide = jnp.concatenate([wide, shared[0], shared[1]], axis=2)

    def from_other_core(value):
        return lax.ppermute(value, "core", [(0, 1), (1, 0)])

    a_own = lax.all_to_all(wide, ("y", "x"), 0, 0, tiled=True)
    a_other = from_other_core(a_own)
    a_all = jnp.where(my_core == 0, jnp.stack([a_own, a_other], 1), jnp.stack([a_other, a_own], 1))
    a_all = a_all.reshape(width, 3 * LANES)

    def take_rows(matrix):
        return lax.dynamic_slice_in_dim(matrix, column, RANK, matrix.ndim - 2)

    def take_cols(matrix):
        return lax.dynamic_slice_in_dim(matrix, column, RANK, matrix.ndim - 1)

    def in_slot(block, slot):
        pads = [(0, 0)] * block.ndim
        pads[-2] = (slot * RANK, LANES - (slot + 1) * RANK)
        return jnp.pad(block, pads)

    gu_rows = take_rows(gate_up_adapter)
    b_own = jnp.concatenate(
        [gu_rows[0], gu_rows[1], take_cols(down_adapter).T, take_rows(q_adapter), take_cols(out_adapter).T], axis=1
    )
    kv_rows = take_rows(kv_adapter)
    b_kv = jnp.stack([in_slot(kv_rows[0], SLOT_K), in_slot(kv_rows[1], SLOT_V)])

    start = dp * group_rows + tensor * rows
    span = WINDOW + rows
    cos_window, sin_window = rope_tables((start - WINDOW + jnp.arange(span)) % seq_length)
    cos, sin = cos_window[WINDOW:], sin_window[WINDOW:]
    padded = jnp.concatenate([jnp.full((WINDOW,), -1, jnp.int32), segments])
    kseg = lax.dynamic_slice_in_dim(padded, start, span, 0)
    qseg = kseg[WINDOW:].reshape(1, rows)
    kseg = kseg.reshape(span, 1)

    gain_one, gain_two = norm_gains[0:1], norm_gains[1:2]
    q_block = f3 // q_cols

    def weight_spec(block):
        return pl.BlockSpec((dp_count, 1, shard_rows, q_cols), lambda t: (0, t, 0, block))

    def adapter_spec(block):
        return pl.BlockSpec((1, LANES, q_cols), lambda t: (t, 0, block))

    def lane_block(block):
        return pl.BlockSpec((width, LANES), lambda *_: (0, block))

    head_specs = [weight_spec(q_block), adapter_spec(0), weight_spec(q_block + 1), adapter_spec(1)]
    q_spec, qb_spec, o_spec, ob_spec = head_specs
    a_spec, wk_spec, wv_spec = lane_block(0), lane_block(1), lane_block(2)
    token_cols = pl.BlockSpec((rows, q_cols), lambda t: (0, t))
    tok_bf, tok_f32, rank_bf = sds((rows, width), BF), sds((rows, width), F32), sds((rows, LANES), BF)

    args = (tokens, gain_one, a_all, a_all, a_all, b_kv, cos, sin)
    normed_one, rank_one, kv_own = call(
        shared_kernel, "keys_values", 1, args,
        wholes(*args[:2]) + [a_spec, wk_spec, wv_spec] + wholes(*args[5:]),
        [(tok_bf, None), (rank_bf, None), (sds((rows, 2 * HD), BF), None)],
        [], 2 * rows * width * 384, 6 * rows * width,
    )
    parts = seq_length // rows
    reach = WINDOW // rows

    def moved(value, steps):
        return lax.ppermute(value, SEQ, [(c, c + steps) for c in range(parts) if 0 <= c + steps < parts])

    kv_window = jnp.concatenate([moved(kv_own, d) for d in range(reach, 0, -1)] + [kv_own])

    b_own, kv_own = lax.optimization_barrier((b_own, kv_own))
    b_parts = [b_own] + [
        lax.ppermute(b_own, "tensor", [((z + d) % tensor_count, z) for z in range(tensor_count)])
        for d in range(1, tensor_count)
    ]
    b_all = jnp.roll(jnp.stack(b_parts), tensor, axis=0)
    b_heads = jnp.concatenate(
        [in_slot(b_all[:, :, f3 : f3 + q_cols], SLOT_Q), in_slot(b_all[:, :, f3 + q_cols :], SLOT_O)], axis=2
    )
    steps, slots = ff_cols // LANES, 2
    part_cols = ff_cols // steps
    b_hidden = b_all[:, :, :f3].reshape(tensor_count, RANK, 3, steps, part_cols).transpose(3, 2, 1, 0, 4)
    b_hidden = b_hidden.reshape(steps, 3, RANK, tensor_count * part_cols)
    b_hidden = jnp.concatenate(
        [in_slot(b_hidden[:, kind], slot) for kind, slot in enumerate((SLOT_G, SLOT_U, SLOT_D))], axis=2
    )

    heads = q_cols // HD
    last = tensor_count - 1

    def until_last(spec):
        return pl.BlockSpec(spec.block_shape, lambda t: spec.index_map(jnp.minimum(t, last)))

    p_spec, norm_spec = by_step(span, heads * rows), by_step(8, heads * rows)
    args = (
        kv_window, kseg, qseg, normed_one, rank_one, cos, sin, gain_two, a_all,
        weights, b_heads, weights, b_heads, tokens, cotangent, b_hidden, weights,
    )
    (
        queries, mixed, probs, norms, block_output, grad_residual, grad_branch, normed_two, ranks, grad_ro, early
    ) = call(
        forward_kernel, "forward", tensor_count + 1, args,
        wholes(*args[:8]) + [a_spec] + [until_last(spec) for spec in head_specs]
        + [pl.BlockSpec(memory_space=pl.ANY)] * 4,
        [
            (sds((rows, heads_cols), BF), until_last(token_cols)), (sds((rows, heads_cols), BF), until_last(token_cols)),
            (sds((tensor_count, span, heads * rows), BF), until_last(p_spec)),
            (sds((tensor_count, 8, heads * rows), F32), until_last(norm_spec)),
            (tok_bf, None), (tok_f32, None), (tok_bf, None), (tok_bf, None), (sds((3, rows, LANES), BF), None),
            (rank_bf, None), (sds((tensor_count, RANK, f3 + q_cols), BF), None),
        ],
        [
            pltpu.VMEM((span, rows), F32), pltpu.VMEM((span, heads * rows), F32), pltpu.VMEM((HD, span), BF),
            pltpu.VMEM((rows, width), F32), pltpu.VMEM((rows, width), F32), pltpu.VMEM((rows, LANES), F32),
            pltpu.VMEM((rows, LANES), F32), pltpu.VMEM((rows, LANES), F32), pltpu.VMEM((heads * rows, HD), BF),
            pltpu.VMEM((tensor_count, rows, q_cols), BF), pltpu.VMEM((rows, width), F32),
            pltpu.VMEM((rows, LANES), BF), pltpu.VMEM((LANES, rows), BF),
            pltpu.VMEM((rows, LANES), BF), pltpu.VMEM((LANES, rows), BF),
            pltpu.VMEM((slots, dp_count, shard_rows, 3 * tensor_count * part_cols), BF),
            pltpu.VMEM((rows, width), BF), pltpu.VMEM((rows, width), BF), pltpu.VMEM(b_hidden.shape, BF),
            pltpu.SemaphoreType.DMA((slots, 3 * tensor_count)), pltpu.SemaphoreType.DMA((3,)),
        ],
        4 * rows * heads_cols * (span + width) + 12 * rows * width * tensor_count * ff_cols,
        4 * width * heads_cols + 6 * width * tensor_count * ff_cols,
    )
    early = lax.psum_scatter(early, "tensor", scatter_dimension=0, tiled=True).reshape(RANK, -1)

    args = (
        tensor.astype(jnp.int32).reshape(1), kv_window, grad_branch, grad_ro, rank_one, cos, sin,
        ranks, normed_two, cotangent, queries, mixed, probs, norms, weights, b_heads, weights, b_heads,
    )
    *dkv, q_own, grad_one, grad_rank, wide_ffn = call(
        attn_back_kernel, "attention_back", tensor_count, args,
        [scalars()] + wholes(*args[1:10]) + [token_cols, token_cols, p_spec, norm_spec, o_spec, ob_spec, q_spec, qb_spec],
        [
            *[(sds((rows + (2 * RANK if 0 < w < reach else 0), 2 * HD), BF), None) for w in range(reach + 1)],
            (sds((RANK, q_cols), BF), None), (tok_f32, None), (sds((rows, LANES), F32), None),
            (sds((LANES, width), F32), None),
        ],
        [
            pltpu.VMEM((span, heads * rows), BF),
            pltpu.VMEM((span, HD), F32), pltpu.VMEM((span, HD), F32), pltpu.VMEM((HD, span), BF),
            pltpu.VMEM((LANES, rows), BF), pltpu.VMEM((rows, q_cols), BF), pltpu.VMEM((rows, q_cols), BF),
            pltpu.VMEM((heads * rows, HD), BF), pltpu.VMEM((heads * rows, HD), BF),
        ],
        2 * rows * heads_cols * (4 * span + 2 * width), 4 * width * heads_cols,
    )

    early, grad_one = lax.optimization_barrier((early, grad_one))
    early = lax.all_gather(early, DP, axis=0, tiled=False)

    def around(value, steps):
        return lax.ppermute(value, SEQ, [(c, (c - steps) % parts) for c in range(parts)])

    backs = [around(dkv[reach - d], d) for d in range(1, reach)] + [moved(dkv[0], -reach)]
    core = my_core.astype(jnp.int32).reshape(1)
    chips = dp_count // 2
    share = width // 2 + 5 * RANK
    args = (
        core, normed_one, rank_one, b_kv, cos, sin, dkv[reach], *backs, q_own, grad_rank, wide_ffn,
    )
    mine, theirs, grad_key, grad_value, grad_rank = call(
        functools.partial(shared_back_kernel, chips), "shared_back", 1, args,
        [scalars()] + wholes(*args[1:]),
        [
            (sds((share, LANES), BF), None), (sds((share, LANES), BF), None),
            (sds((rows, HD), BF), None), (sds((rows, HD), BF), None), (rank_bf, None),
        ],
        [], 4 * rows * width * LANES, 6 * rows * width,
    )
    own_rows = width // devices
    planes = chips * tensor_count
    args = (core, mine, from_other_core(theirs))
    payload, q_terms = call(
        payload_kernel, "payload", 1, args, [scalars()] + wholes(*args[1:]),
        [(sds((planes, RANK, LANES), BF), None), (sds((1, RANK, q_cols), BF), None)], [],
        0, 2 * planes * RANK * LANES,
    )
    payload, grad_key = lax.optimization_barrier((payload, grad_key))
    terms = lax.all_to_all(payload, PLANES, 0, 0, tiled=True)

    def with_others(value, axis):
        count = lax.axis_size(axis)
        return [value] + [
            lax.ppermute(value, axis, [((i + d) % count, i) for i in range(count)]) for d in range(1, count)
        ]

    terms = terms.reshape(seqs, tensor_count, RANK, LANES)

    args = (
        tokens, gain_one, a_all, a_all, a_all, grad_key, grad_value, grad_rank, grad_one, grad_residual,
    )
    (input_grad,) = call(
        input_kernel, "input_gradient", 1, args,
        wholes(*args[:2]) + [a_spec, wk_spec, wv_spec] + wholes(*args[5:]),
        [(tok_f32, None)], [], 2 * rows * width * 384, 16 * rows * width,
    )

    q_terms, input_grad = lax.optimization_barrier((q_terms, input_grad))
    q_terms = with_others(jnp.concatenate(with_others(q_terms, "x")), "y")
    terms, input_grad = lax.optimization_barrier((terms, input_grad))
    own = jnp.stack([(dp * tensor_count + tensor) // RANK, lax.axis_index("y"), lax.axis_index("x")]).astype(jnp.int32)
    wide_grad, kv_adapter_grad, q_adapter_grad = call(
        sum_wide_kernel, "sum_wide", 1, (adapter_ids, own, terms, *q_terms),
        [scalars(), scalars()] + wholes(terms, *q_terms),
        [(sds((own_rows, 7, LANES), F32), None), (sds((2, 1, HD), F32), None), (sds((LANES, q_cols), F32), None)],
        [pltpu.VMEM((adapters, RANK, LANES), F32), pltpu.VMEM((adapters, RANK, q_cols), F32)], 0, 4 * LANES * f3,
    )
    shapes = [(2, LANES, ff_cols), (ff_cols, LANES), (q_cols, LANES)]
    gate_up_adapter_grad, down_adapter_grad, out_adapter_grad = call(
        sum_hidden_kernel, "sum_hidden", 1, (adapter_ids, early),
        [scalars(), pl.BlockSpec(memory_space=pl.ANY)],
        [(sds(shape, F32), pl.BlockSpec(memory_space=pl.ANY)) for shape in shapes],
        [pltpu.VMEM(early.shape, BF), pltpu.VMEM((adapters, RANK, f3 + q_cols), F32)]
        + [pltpu.VMEM(shape, F32) for shape in shapes]
        + [pltpu.SemaphoreType.DMA((3,)), pltpu.SemaphoreType.DMA((4,))],
        0, 4 * LANES * f3,
    )
    return (
        block_output, input_grad, wide_grad.transpose(1, 0, 2), kv_adapter_grad,
        q_adapter_grad, out_adapter_grad, gate_up_adapter_grad, down_adapter_grad,
    )


def solution(mesh):
    dp_count, tensor_count = mesh.shape["dp"], mesh.shape["tensor"]
    chips = dp_count // 2
    x_count = math.isqrt(chips)
    devices = mesh.devices.reshape(chips // x_count, x_count, 2, tensor_count)
    return jax.shard_map(
        on_device,
        mesh=Mesh(devices, ALL),
        in_specs=(
            P(ALL, None), P(ALL, None), P(), P(), P(), P(DP, "tensor"), P(None, DP, None),
            P("tensor", DP), P(None, DP, "tensor"), P("tensor", DP), P(None, DP, None), P(),
            P(None, "tensor"), P("tensor", None), P(None, None, "tensor"), P("tensor", None),
        ),
        out_specs=(
            P(ALL, None), P(ALL, None), P(None, ALL, None), P(None, ALL, None),
            P(None, "tensor"), P("tensor", None), P(None, None, "tensor"), P("tensor", None),
        ),
        check_vma=False,
    )
```
